32 devices in a mesh: gx: 4 (over y, x), gy: 8 (over z, core).
Axes of the slice: x: 2, y: 2, z: 4, core: 2. Of those that a mesh axis runs over, the one named last changes fastest.
Arguments:
- field: float32 [3, 16, 256, 1024], P(None, None, 'gx', 'gy'), may hold values from -6 to 6
- masks: int32 [2, 7, 8, 32], P(None, None, 'gx', 'gy'), may hold values 0 or 1
Outputs:
- restored: float32 [3, 16, 256, 1024], P(None, None, 'gx', 'gy')
- coarse: float32 [3, 4, 64, 256], replicated
The draws below stay inside these ranges and needn't reach their ends.
All inputs are finite; a program needn't handle non-finite values. No bound on the sum of `masks` on one device may be relied on, other than what follows from the above.
Results may differ from the reference program's by a relative error of at most 0.00002.
Values sent between devices are 32-bit elements; how exact they have to be, the bound alone decides.
No kernel may reach another device: no remote copies, remote signals or barrier semaphores. Data moves between devices by JAX's collectives and lax.ppermute only.
A program may use at most 128 MiB of HBM per device.

```python
import jax
import jax.numpy as jnp
from jax import lax

VARS = 3
NZ = 16
BLOCK = 32
LEVELS = 2
NX = 256
NY = 1024


def with_ends(array, stream_key, smallest, largest):
    place = [jax.random.randint(jax.random.fold_in(stream_key, axis), (), 0, length) for axis, length in enumerate(array.shape)]
    longest = array.shape.index(max(array.shape))
    beside = place[:longest] + [(place[longest] + 1) % array.shape[longest]] + place[longest + 1:]
    return array.at[tuple(place)].set(smallest).at[tuple(beside)].set(largest)


def shard_levels(stream_key, shape, cuts, low, largest):
    loudness = 1.0
    for dim, shards_of in cuts:
        heights = jax.random.uniform(jax.random.fold_in(jax.random.fold_in(stream_key, 6), dim), (shards_of,), jnp.float32, low / len(cuts), largest / len(cuts))
        loudness = loudness * jnp.repeat(jnp.exp(heights), shape[dim] // shards_of).reshape((-1,) + (1,) * (len(shape) - 1 - dim))
    return loudness


def bell_draw(rng, shape, scale, limit, split=(), held_as=jnp.bfloat16):
    result = jax.random.normal(rng, shape, jnp.float32) * scale
    if len(split) > 0:
        result = shard_levels(rng, shape, split, -0.22, 0.18) * result
    return jnp.clip(result, min=-limit, max=limit).astype(held_as)


def setup_inputs(seed: int = 0) -> dict:
    seeds = jax.random.split(jax.random.key(seed), 3)
    field = bell_draw(seeds[0], (VARS, NZ, NX, NY), 1.0, 6.0, ((2, 4), (3, 8)), jnp.float32)
    masks = with_ends((jax.random.randint(seeds[1], (LEVELS, 7, NX // BLOCK, NY // BLOCK), 0, 2) < 1).astype(jnp.int32), jax.random.fold_in(seeds[1], 1), 0, 1)
    return {"field": field, "masks": masks}


def take_slice(volume, start, stop, stride, direction):
    return lax.slice_in_dim(volume, start, stop, stride, direction)


def lift_forward(padded, direction):
    length = padded.shape[direction] - 4
    even_cells = take_slice(padded, 2, length + 2, 2, direction)
    odd_cells = take_slice(padded, 3, length + 3, 2, direction)
    next_even = take_slice(padded, 4, length + 4, 2, direction)
    detail = odd_cells - 0.5 * (even_cells + next_even)
    first_detail = take_slice(padded, 1, 2, 1, direction) - 0.5 * (take_slice(padded, 0, 1, 1, direction) + take_slice(padded, 2, 3, 1, direction))
    previous = jnp.concatenate([first_detail, take_slice(detail, 0, length // 2 - 1, 1, direction)], direction)
    smooth = even_cells + 0.25 * (previous + detail)
    return jnp.concatenate([smooth, detail], 0)


def lift_inverse(padded, direction):
    middle = padded.shape[0] // 2
    smooth_pad = padded[:middle]
    detail_pad = padded[middle:]
    length = padded.shape[direction] - 2
    even_ext = take_slice(smooth_pad, 1, length + 2, 1, direction) - 0.25 * (take_slice(detail_pad, 0, length + 1, 1, direction) + take_slice(detail_pad, 1, length + 2, 1, direction))
    even_cells = take_slice(even_ext, 0, length, 1, direction)
    next_even = take_slice(even_ext, 1, length + 1, 1, direction)
    odd_cells = take_slice(detail_pad, 1, length + 1, 1, direction) + 0.5 * (even_cells + next_even)
    target_shape = list(even_cells.shape)
    target_shape[direction] = 2 * length
    return jnp.stack([even_cells, odd_cells], direction + 1).reshape(target_shape)


def wrap_local(volume, direction, margin):
    length = volume.shape[direction]
    return jnp.concatenate([take_slice(volume, length - margin, length, 1, direction), volume, take_slice(volume, 0, margin, 1, direction)], direction)


def mirror_forward(volume, direction):
    length = volume.shape[direction]
    return jnp.concatenate([take_slice(volume, 2, 3, 1, direction), take_slice(volume, 1, 2, 1, direction), volume, take_slice(volume, length - 2, length - 1, 1, direction), take_slice(volume, length - 3, length - 2, 1, direction)], direction)


def mirror_inverse(volume, direction):
    middle = volume.shape[0] // 2
    length = volume.shape[direction]
    smooth = volume[:middle]
    detail = volume[middle:]
    smooth_pad = jnp.concatenate([take_slice(smooth, 0, 1, 1, direction), smooth, take_slice(smooth, length - 1, length, 1, direction)], direction)
    detail_pad = jnp.concatenate([take_slice(detail, 0, 1, 1, direction), detail, take_slice(detail, length - 2, length - 1, 1, direction)], direction)
    return jnp.concatenate([smooth_pad, detail_pad], 0)


def expand_mask(mask_block, block_width):
    return jnp.repeat(jnp.repeat(mask_block, block_width, 1), block_width, 2).astype(jnp.float32)


def forward_level(volume):
    volume = lift_forward(wrap_local(volume, 3, 2), 3)
    volume = lift_forward(wrap_local(volume, 4, 2), 4)
    return lift_forward(mirror_forward(volume, 2), 2)


def inverse_level(volume):
    volume = lift_inverse(mirror_inverse(volume, 2), 2)
    volume = lift_inverse(wrap_local(volume, 4, 1), 4)
    return lift_inverse(wrap_local(volume, 3, 1), 3)


def reference(field, masks):
    def one_variable(values):
        volume = values[None, None]
        detail_list = []
        for level_index in range(LEVELS):
            volume = forward_level(volume)
            kept_mask = expand_mask(masks[level_index], BLOCK >> (level_index + 1))
            detail_list.append(volume[1:] * kept_mask[:, None, None, :, :])
            volume = volume[:1]
        coarse = volume[0, 0]
        for level_index in range(LEVELS - 1, -1, -1):
            volume = inverse_level(jnp.concatenate([volume, detail_list[level_index]], 0))
        return volume[0, 0], coarse

    restored, coarse = lax.map(one_variable, field)
    return restored, coarse
```

```python
import functools

import jax
import jax.numpy as jnp
import ml_dtypes
import numpy as np
from jax import lax
from jax.experimental import pallas as pl
from jax.experimental.pallas import tpu as pltpu
from jax.sharding import PartitionSpec as P

F32 = jnp.float32
BF16 = jnp.bfloat16
VMEM_LIMIT = 48 * 1024 * 1024

NV, NZ, NR, NL = 3, 16, 64, 128
HALO = 8


def detail_row(k):
    return {2 * k + 1: 1.0, 2 * k: -0.5, 2 * k + 2: -0.5}


def smooth_row(k):
    row = {2 * k: 1.0}
    for j in (k - 1, k):
        for cell, value in detail_row(j).items():
            row[cell] = row.get(cell, 0.0) + 0.25 * value
    return row


def even_row(k):
    return {("s", k): 1.0, ("d", k - 1): -0.25, ("d", k): -0.25}


def odd_row(k):
    row = {("d", k): 1.0}
    for j in (k, k + 1):
        for name, value in even_row(j).items():
            row[name] = row.get(name, 0.0) + 0.5 * value
    return row


def as_bf16(matrix):
    cast = matrix.astype(ml_dtypes.bfloat16)
    assert (cast.astype(np.float64) == matrix).all()
    return cast


def cell_place(y):
    return y if 0 <= y < NL else (y + HALO + NL if y < 0 else y + HALO)


def fill_forward(matrix, place_in, column, row):
    for cell, value in row.items():
        matrix[place_in(cell), column] += value


def level_one_columns():
    names = {("s", k): k for k in range(65)}
    names.update({("d", k): 128 + k for k in range(65)})
    names[("d", -1)] = 128 + 65
    return names


def level_two_columns():
    names = {("s", k): k for k in range(33)}
    names.update({("d", k): 64 + k for k in range(33)})
    names[("d", -1)] = 64 + 33
    return names


def smooth_place(k):
    return k + 2


@functools.lru_cache(maxsize=None)
def weights():
    w = {}
    names = level_one_columns()
    forward = np.zeros((144, 256))
    inverse = np.zeros((256, 128))
    for (kind, k), column in names.items():
        fill_forward(forward, cell_place, column, smooth_row(k) if kind == "s" else detail_row(k))
    for k in range(64):
        for y, row in ((2 * k, even_row(k)), (2 * k + 1, odd_row(k))):
            for name, value in row.items():
                inverse[names[name], y] += value
    w["forward"], w["inverse"] = forward, inverse
    smooth = np.zeros((256, 128))
    for k in range(-2, 67):
        fill_forward(smooth, cell_place, smooth_place(k), smooth_row(k))
    w["smooth"] = smooth
    names2 = level_two_columns()
    forward2 = np.zeros((128, 128))
    inverse2 = np.zeros((128, 128))
    for (kind, k), column in names2.items():
        fill_forward(forward2, smooth_place, column, smooth_row(k) if kind == "s" else detail_row(k))
    for k in range(33):
        rows = [(2 * k, even_row(k))] + ([(2 * k + 1, odd_row(k))] if k < 32 else [])
        for y, row in rows:
            for name, value in row.items():
                inverse2[names2[name], y] += value
    w["forward2"], w["inverse2"] = forward2, inverse2
    back = np.zeros((256, 128))
    back[:65] = inverse[:65]
    back[128 : 128 + 65] = inverse[:65]
    w["back"] = back
    plane = np.zeros((2, 8, NZ))

    def mirrored(z):
        return -z if z < 0 else (2 * (NZ - 1) - z if z > NZ - 1 else z)

    for k in range(8):
        for z, value in smooth_row(k).items():
            plane[0, k, mirrored(z)] += value
        for z, value in detail_row(k).items():
            plane[1, k, mirrored(z)] += value
    halo = np.zeros((4, 128, 2, 8, 16))
    for bz in range(2):
        for k in range(8):
            for z in range(NZ):
                for c in range(HALO):
                    left = 8 * ((z - 1) % NZ) + c
                    right = 8 * z + c
                    halo[0:2, left, bz, k, c] = plane[bz, k, z]
                    halo[2:4, right, bz, k, 8 + c] = plane[bz, k, z]
    w["halo"] = halo.reshape(512, 256)
    spread = np.zeros((3, 128, 2, 128))
    for k in range(64):
        spread[0, k, 0, k] = 1
    spread[1, 0, 0, 64] = 1
    spread[2, 63, 0, 65] = 1
    for k in range(32):
        spread[0, 64 + k, 1, k] = 1
        spread[0, 64 + k, 1, 64 + k] = 1
    for base in (0, 64):
        spread[1, 64, 1, base + 32] = 1
        spread[2, 95, 1, base + 33] = 1
    w["spread"] = spread.reshape(384, 256)
    expand = np.zeros((2, 4, 128))
    for j in range(4):
        expand[0, j, 16 * j : 16 * j + 16] = 1
        expand[1, j, 64 + 8 * j : 64 + 8 * j + 8] = 1
    w["expand"] = expand
    twice = {}
    for k, value in smooth_row(0).items():
        for y, other in smooth_row(k).items():
            twice[y] = twice.get(y, 0.0) + value * other
    columns = np.zeros((NV, 2, 128, 128))
    for m in range(-1, 34):
        for t, value in twice.items():
            if 0 <= 4 * m + t < NL:
                for v in range(NV):
                    columns[v, :, 4 * m + t, 40 * v + m + 1] = value
    w["part_columns"] = columns.reshape(NV * 256, 128)
    rows = np.zeros((24, 2, 64))
    for m in range(-1, 18):
        for t, value in twice.items():
            if 0 <= 4 * m + t < NR:
                rows[m % 24, :, 4 * m + t] = value
    w["part_rows"] = rows.reshape(24, 128)
    return {name: as_bf16(matrix) for name, matrix in w.items()}


def two_terms(x):
    high = x.astype(BF16)
    low = (x - high.astype(F32)).astype(BF16)
    return high, low


def dot(a, b):
    return jnp.dot(a, b, preferred_element_type=F32)


def lift_planes(cells):
    half = len(cells) // 2
    even, odd = cells[0::2], cells[1::2]
    detail = [odd[k] - 0.5 * (even[k] + even[min(k + 1, half - 1)]) for k in range(half)]
    smooth = [even[k] + 0.25 * (detail[max(k - 1, 0)] + detail[k]) for k in range(half)]
    return smooth, detail


def unlift_planes(smooth, detail):
    half = len(smooth)
    even = [smooth[k] - 0.25 * (detail[max(k - 1, 0)] + detail[k]) for k in range(half)]
    out = []
    for k in range(half):
        out += [even[k], detail[k] + 0.5 * (even[k] + even[min(k + 1, half - 1)])]
    return out


def lift_rows(load, start):
    even, odd, after = load(start), load(start + 1), load(start + 2)
    before, odd_before = load(start - 2), load(start - 1)
    detail = odd - 0.5 * (even + after)
    detail_before = odd_before - 0.5 * (before + even)
    return even + 0.25 * (detail_before + detail), detail


def unlift_rows(smooth, detail, row):
    here, after = detail(row), detail(row + 1)
    even = smooth(row) - 0.25 * (detail(row - 1) + here)
    next_even = smooth(row + 1) - 0.25 * (here + after)
    return even, here + 0.5 * (even + next_even)


def pack_kernel(field, masks, expand, part_columns, part_rows, top, bottom, left, right, own_masks, share, wide):
    lane = lax.broadcasted_iota(jnp.int32, (8, NL), 1) // 8

    def pack_rows(step, _):
        v, t = step // 8, step % 8
        rows = pl.ds(pl.multiple_of(t * 8, 8), 8)
        low = jnp.zeros((8, NL), F32)
        high = jnp.zeros((8, NL), F32)
        for z in range(NZ):
            x = field[v, z, rows, :]
            turned = pltpu.roll(x, 8 * z, 1) if z else x
            low = jnp.where(lane == z, turned, low)
            high = jnp.where(lane == (z - 1) % NZ, turned, high)
        left[v, rows, :] = low
        right[v, rows, :] = high
        return 0

    lax.fori_loop(0, NV * 8, pack_rows, 0)
    for v in range(NV):
        top[v] = left[v, 0:8, :]
        top[3 + v] = right[v, 0:8, :]
        bottom[v] = left[v, NR - 8 : NR, :]
        bottom[3 + v] = right[v, NR - 8 : NR, :]
        top[8 + v * NZ : 8 + (v + 1) * NZ] = field[v, :, 0:8, :]
        bottom[8 + v * NZ : 8 + (v + 1) * NZ] = field[v, :, NR - 8 : NR, :]
    for i, out in ((0, top), (1, bottom)):
        tile = jnp.zeros((7, NL), F32)
        for l in range(2):
            flags = masks[l, i].astype(F32).astype(BF16)
            tile += lax.dot_general(flags, expand[l], (((0,), (0,)), ((), ())), preferred_element_type=F32)
        own_masks[i] = jnp.concatenate([tile, jnp.zeros((1, NL), F32)], 0)
        out[6] = own_masks[i]
        out[7] = jnp.zeros((8, NL), F32)

    def columns(step, _):
        planes = pl.ds(step * 4, 4)
        terms = []
        for v in range(NV):
            terms += list(two_terms(field[v, planes].reshape(4 * NR, NL)))
        wide[planes] = dot(jnp.concatenate(terms, 1), part_columns[...]).reshape(4, NR, NL)
        return 0

    lax.fori_loop(0, NZ // 4, columns, 0)
    smooth, _ = lift_planes([wide[z] for z in range(NZ)])
    smooth, _ = lift_planes(smooth)
    high, low = two_terms(jnp.concatenate(smooth, 1))
    part = dot(part_rows[...], jnp.concatenate([high, low], 0))
    for z in range(4):
        share[z * 24 : (z + 1) * 24, :] = part[:, z * NL : (z + 1) * NL]


def pack(field, masks):
    w = weights()
    shapes = [(56, 8, NL), (56, 8, NL), (NV, NR, NL), (NV, NR, NL), (2, 8, NL), (96, NL)]
    vmem = pl.BlockSpec(memory_space=pltpu.VMEM)
    return pl.pallas_call(
        pack_kernel,
        out_shape=[jax.ShapeDtypeStruct(s, F32) for s in shapes],
        in_specs=[vmem] * 5,
        out_specs=[vmem] * 6,
        scratch_shapes=[pltpu.VMEM((NZ, NR, NL), F32)],
        compiler_params=pltpu.CompilerParams(vmem_limit_bytes=VMEM_LIMIT),
    )(field, masks.transpose(0, 2, 3, 1), w["expand"], w["part_columns"], w["part_rows"])


def join_kernel(left, right, own_masks, north, south, to_left, to_right):
    for v in range(NV):
        for side, tile, out in ((left, v, to_left), (right, 3 + v, to_right)):
            out[v * 80 : v * 80 + 64, :] = side[v]
            out[v * 80 + 64 : v * 80 + 72, :] = south[tile]
            out[v * 80 + 72 : v * 80 + 80, :] = north[tile]
    for out in (to_left, to_right):
        out[240:248, :] = north[6]
        out[248:256, :] = own_masks[0]
        out[256:264, :] = own_masks[1]
        out[264:272, :] = south[6]


def join(left, right, own_masks, north, south):
    whole = pl.BlockSpec((NV, NR, NL), lambda i: (0, 0, 0))
    edge = pl.BlockSpec((8, 8, NL), lambda i: (0, 0, 0))
    out = pl.BlockSpec((272, NL), lambda i: (0, 0))
    return pl.pallas_call(
        join_kernel,
        grid=(1,),
        out_shape=[jax.ShapeDtypeStruct((272, NL), F32)] * 2,
        in_specs=[whole, whole, pl.BlockSpec((2, 8, NL), lambda i: (0, 0, 0)), edge, edge],
        out_specs=[out, out],
        compiler_params=pltpu.CompilerParams(vmem_limit_bytes=VMEM_LIMIT),
    )(left, right, own_masks, north, south)


def wave_kernel(
    field, north, south, west, east, own_masks,
    forward, inverse, smooth_w, forward2, inverse2, back, halo_w, spread,
    out,
    cells, first, halo_x, halo, gain, gain2, low, second, kept2, low_back, kept, sems,
):
    copies = []
    for v in range(NV):
        planes = pl.ds(8 + v * NZ, NZ)
        pairs = [
            (field.at[v], cells.at[v, 0:NZ, 8:72, :]),
            (north.at[planes], cells.at[v, 0:NZ, 0:8, :]),
            (north.at[planes], cells.at[v, 0:NZ, 80:88, :]),
            (south.at[planes], cells.at[v, 0:NZ, 72:80, :]),
            (field.at[v, :, 0:8, :], cells.at[v, 0:NZ, 88:96, :]),
        ]
        for p, ref in ((NZ, west), (NZ + 1, east)):
            pairs += [
                (ref.at[v * 80 : v * 80 + 80, :], cells.at[v, p, 8:88, :]),
                (ref.at[v * 80 + 72 : v * 80 + 80, :], cells.at[v, p, 0:8, :]),
                (ref.at[v * 80 : v * 80 + 8, :], cells.at[v, p, 88:96, :]),
            ]
        copies.append([
            pltpu.make_async_copy(source, target, sems.at[v, n]) for n, (source, target) in enumerate(pairs)
        ])
        for copy in copies[-1]:
            copy.start()
    tiles = [pltpu.make_async_copy(ref.at[240:272, :], cells.at[0, 18 + n, 0:32, :], sems.at[3, n])
             for n, ref in enumerate((west, east))]
    tiles += [pltpu.make_async_copy(north.at[6], cells.at[0, 20, 0:8, :], sems.at[3, 2]),
              pltpu.make_async_copy(south.at[6], cells.at[0, 20, 24:32, :], sems.at[3, 3])]
    for copy in tiles:
        copy.start()
    for copy in tiles:
        copy.wait()

    own = jnp.concatenate([cells[0, 20, 0:8, :], own_masks[0], own_masks[1], cells[0, 20, 24:32, :]], 0)
    flags = jnp.concatenate([own, cells[0, 19, 0:32, :], cells[0, 18, 0:32, :]], 1).astype(BF16)
    lanes = dot(flags, spread[...])
    lane64 = lax.broadcasted_iota(jnp.int32, (1, NL), 1) < 64
    zero, one = jnp.zeros((1, NL), F32), jnp.ones((1, NL), F32)
    forward_f, forward2_f = forward[...].astype(F32), forward2[...].astype(F32)
    for ib in range(4):
        for bz in range(2):
            for bx in range(2):
                n = 2 * bz + bx
                b = 8 * ib + 4 * bz + bx - 1
                smooth_one = lanes[b : b + 1, 0:NL] if n else zero
                detail_one = lanes[b + 2 : b + 3, 0:NL]
                row = jnp.concatenate([smooth_one, detail_one], 1)
                gain[ib, n, 0:144, :] = dot((forward_f * row).astype(BF16), inverse[...]).astype(BF16)
                gain[ib, n, 144:256, :] = jnp.zeros((112, NL), BF16)
                smooth_two = lanes[b : b + 1, NL:] if n else one
                row = jnp.where(lane64, smooth_two, lanes[b + 2 : b + 3, NL:])
                both = dot((forward2_f * row).astype(BF16), inverse2[...]).astype(BF16)
                gain2[ib, n, 0:128, :] = both
                gain2[ib, n, 128:256, :] = both

    for v in range(NV):
        for copy in copies[v]:
            copy.wait()

        def rows_one(t, _):
            at = pl.multiple_of(t * 8, 8)
            lifted = [
                lift_rows(lambda s: cells[v, p, pl.ds(16 * t + s, 8, stride=2), :], 8) for p in range(NZ + 2)
            ]
            for bx in range(2):
                smooth, detail = lift_planes([pair[bx] for pair in lifted[:NZ]])
                for bz, part in ((0, smooth), (1, detail)):
                    for z in range(8):
                        first[2 * bz + bx, v * 8 + z, pl.ds(at, 8), :] = part[z]
                halo_x[bx, v, pl.ds(at, 8), 0:NL] = lifted[NZ][bx]
                halo_x[bx, v, pl.ds(at, 8), NL:] = lifted[NZ + 1][bx]
            return 0

        lax.fori_loop(0, 5, rows_one, 0)
    for bx in range(2):
        high, low_term = two_terms(halo_x[bx].reshape(NV * 40, 256))
        terms = jnp.concatenate([high[:, :NL], low_term[:, :NL], high[:, NL:], low_term[:, NL:]], 1)
        halo[bx] = dot(terms, halo_w[...]).reshape(NV, 40, 256)

    def operand(n, v, at, count):
        bz, bx = n // 2, n % 2
        rows = pl.ds(at, count)
        main = first[n, pl.ds(v * 8, 8), rows, :].reshape(8 * count, NL)
        beside = halo[bx, v, rows, bz * NL : (bz + 1) * NL]
        sides = jnp.concatenate([pltpu.roll(beside, (NL - 16 * z) % NL, 1) if z else beside for z in range(8)], 0)
        return two_terms(jnp.concatenate([main, sides], 1))

    def smooth_part(v, _):
        planes = pl.ds(v * 8, 8)
        for at, count in ((0, 16), (16, 16), (32, 8)):
            high, low_term = operand(0, v, at, count)
            part = (dot(high, smooth_w[...]) + dot(low_term, smooth_w[...])).reshape(8, count, NL)
            if at < 32:
                low[planes, 8 + at : 8 + at + count, :] = part
                if at == 0:
                    low[planes, 56:64, :] = part[:, 0:8]
            else:
                low[planes, 0:8, :] = part
                low[planes, 40:48, :] = part
                low[planes, 48:56, :] = part
        return 0

    lax.fori_loop(0, NV, smooth_part, 0)

    def rows_two(v, _):
        for t in range(3):
            lifted = [
                lift_rows(lambda s: low[v * 8 + p, pl.ds(16 * t + s, 8, stride=2), :], 8) for p in range(8)
            ]
            for bx in range(2):
                smooth, detail = lift_planes([pair[bx] for pair in lifted])
                for bz, part in ((0, smooth), (1, detail)):
                    for z in range(4):
                        second[2 * bz + bx, t, pl.ds(pl.multiple_of((v * 4 + z) * 8, 8), 8), :] = part[z]
        return 0

    lax.fori_loop(0, NV, rows_two, 0)
    ext_two = lax.broadcasted_iota(jnp.int32, (NV * 4, 8, NL), 1) < 4
    for n in range(4):
        for t in range(3):
            terms = jnp.concatenate(two_terms(second[n, t]), 1)
            if t < 2:
                kept2[n, :, 8 + 8 * t : 16 + 8 * t, :] = dot(terms, gain2[t + 1, n]).reshape(NV * 4, 8, NL)
            else:
                below = dot(terms, gain2[3, n]).reshape(NV * 4, 8, NL)
                above = dot(terms, gain2[0, n]).reshape(NV * 4, 8, NL)
                part = jnp.where(ext_two, below, above)
                kept2[n, :, 0:8, :] = part
                kept2[n, :, 24:32, :] = part

    def back_two(v, _):
        for t in range(3):
            pairs = {}
            for bz in range(2):
                for z in range(4):
                    p = v * 4 + z
                    if t < 2:
                        pairs[bz, z] = unlift_rows(
                            lambda r: kept2[2 * bz, p, pl.ds(r, 8), :],
                            lambda r: kept2[2 * bz + 1, p, pl.ds(r, 8), :],
                            8 + 8 * t,
                        )
                    else:
                        even = kept2[2 * bz, p, 24:32, :] - 0.25 * (
                            kept2[2 * bz + 1, p, 23:31, :] + kept2[2 * bz + 1, p, 24:32, :]
                        )
                        pairs[bz, z] = (even, even)
            for parity in range(2 if t < 2 else 1):
                planes = unlift_planes([pairs[0, z][parity] for z in range(4)], [pairs[1, z][parity] for z in range(4)])
                for z in range(8):
                    low_back[v * 8 + z, pl.ds(16 * t + parity, 8, stride=2), :] = planes[z]
        return 0

    lax.fori_loop(0, NV, back_two, 0)

    ext_one = lax.broadcasted_iota(jnp.int32, (8, 8, NL), 1) < 4

    def keep(v, _):
        planes = pl.ds(v * 8, 8)
        for n in range(4):
            for ib in range(3):
                at, count = 16 * ib, 16 if ib < 2 else 8
                high, low_term = operand(n, v, at, count)
                if n == 0:
                    terms = jnp.concatenate(two_terms(low_back[planes, at : at + count, :].reshape(8 * count, NL)), 1)
                    base = dot(terms, back[...])
                if ib < 2:
                    part = dot(high, gain[ib + 1, n]) + dot(low_term, gain[ib + 1, n])
                    if n == 0:
                        part = part + base
                    kept[n, planes, 8 + at : 24 + at, :] = part.reshape(8, count, NL)
                else:
                    below = dot(high, gain[3, n]) + dot(low_term, gain[3, n])
                    above = dot(high, gain[0, n]) + dot(low_term, gain[0, n])
                    if n == 0:
                        below = below + base
                    part = jnp.where(ext_one, below.reshape(8, 8, NL), above.reshape(8, 8, NL))
                    kept[n, planes, 0:8, :] = part
                    kept[n, planes, 40:48, :] = part
        return 0

    lax.fori_loop(0, NV, keep, 0)

    def back_one(step, _):
        v, t = step // 4, step % 4
        pairs = {}
        for bz in range(2):
            for z in range(8):
                p = v * 8 + z
                pairs[bz, z] = unlift_rows(
                    lambda r: kept[2 * bz, p, pl.ds(8 * t + r, 8), :],
                    lambda r: kept[2 * bz + 1, p, pl.ds(8 * t + r, 8), :],
                    8,
                )
        for parity in range(2):
            planes = unlift_planes([pairs[0, z][parity] for z in range(8)], [pairs[1, z][parity] for z in range(8)])
            for z in range(NZ):
                out[v, z, pl.ds(16 * t + parity, 8, stride=2), :] = planes[z]
        return 0

    lax.fori_loop(0, NV * 4, back_one, 0)


def wave(field, north, south, west, east, own_masks):
    w = weights()
    vmem = pl.BlockSpec(memory_space=pltpu.VMEM)
    anywhere = pl.BlockSpec(memory_space=pl.ANY)
    names = ["forward", "inverse", "smooth", "forward2", "inverse2", "back", "halo", "spread"]
    return pl.pallas_call(
        wave_kernel,
        out_shape=jax.ShapeDtypeStruct((NV, NZ, NR, NL), F32),
        in_specs=[anywhere] * 5 + [vmem] * (1 + len(names)),
        out_specs=vmem,
        scratch_shapes=[
            pltpu.VMEM((NV, 21, 96, NL), F32),
            pltpu.VMEM((4, NV * 8, 40, NL), F32),
            pltpu.VMEM((2, NV, 40, 256), F32),
            pltpu.VMEM((2, NV, 40, 256), F32),
            pltpu.VMEM((4, 4, 256, NL), BF16),
            pltpu.VMEM((4, 4, 256, NL), BF16),
            pltpu.VMEM((NV * 8, 64, NL), F32),
            pltpu.VMEM((4, 3, NV * 32, NL), F32),
            pltpu.VMEM((4, NV * 4, 40, NL), F32),
            pltpu.VMEM((NV * 8, 48, NL), F32),
            pltpu.VMEM((4, NV * 8, 48, NL), F32),
            pltpu.SemaphoreType.DMA((4, 11)),
        ],
        compiler_params=pltpu.CompilerParams(vmem_limit_bytes=VMEM_LIMIT),
    )(field, north, south, west, east, own_masks, *[w[name] for name in names])


def coarse_kernel(count_x, count_y, shares, out):
    lane = lax.broadcasted_iota(jnp.int32, (16, NL), 1)
    row = lax.broadcasted_iota(jnp.int32, (8, NL), 0)

    def block(i, _):
        before, after = lax.rem(i + count_x - 1, count_x), lax.rem(i + 1, count_x)
        for z in range(4):
            pieces = []
            for j in range(count_y):
                first = shares[i, j, 24 * z : 24 * z + 8, :]
                second = shares[i, j, 24 * z + 8 : 24 * z + 16, :]
                first += jnp.where(row < 4, shares[before, j, 24 * z + 16 : 24 * z + 24, :], 0.0)
                second += jnp.where(row < 4, 0.0, shares[after, j, 24 * z + 16 : 24 * z + 24, :])
                pieces.append(jnp.concatenate([first, second], 0))
            for v in range(NV):
                for t in range(count_y // 4):
                    total = jnp.zeros((16, NL), F32)
                    for q in range(-1, 5):
                        start = 32 * q - 1
                        turned = pltpu.roll(pieces[(4 * t + q) % count_y], (start - 40 * v) % NL, 1)
                        total += jnp.where((lane >= start) & (lane < start + 35), turned, 0.0)
                    out[v, z, pl.ds(pl.multiple_of(16 * i, 16), 16), NL * t : NL * (t + 1)] = total
        return 0

    lax.fori_loop(0, count_x, block, 0)


def coarse_of(shares, count_x, count_y):
    vmem = pl.BlockSpec(memory_space=pltpu.VMEM)
    return pl.pallas_call(
        functools.partial(coarse_kernel, count_x, count_y),
        out_shape=jax.ShapeDtypeStruct((NV, 4, 16 * count_x, 32 * count_y), F32),
        in_specs=[vmem],
        out_specs=vmem,
        compiler_params=pltpu.CompilerParams(vmem_limit_bytes=VMEM_LIMIT),
    )(shares.reshape(count_x, count_y, 96, NL))


def shifts(axis):
    count = lax.axis_size(axis)
    up = [(i, (i + 1) % count) for i in range(count)]
    return up, [(j, i) for i, j in up]


def body(field, masks):
    count_x, count_y = lax.axis_size("gx"), lax.axis_size("gy")
    top, bottom, left, right, own_masks, share = pack(field, masks)
    shares = lax.all_gather(share, ("gx", "gy"), axis=0, tiled=True)
    up, down = shifts("gx")
    north = lax.ppermute(bottom, "gx", up)
    south = lax.ppermute(top, "gx", down)
    to_left, to_right = join(left, right, own_masks, north, south)
    up, down = shifts("gy")
    west = lax.ppermute(to_right, "gy", up)
    east = lax.ppermute(to_left, "gy", down)
    restored = wave(field, north, south, west, east, own_masks)
    return restored, coarse_of(shares, count_x, count_y)


def solution(mesh):
    placed = P(None, None, "gx", "gy")
    return jax.shard_map(
        body,
        mesh=mesh,
        in_specs=(placed, placed),
        out_specs=(placed, P()),
        check_vma=False,
    )
```

```python
import functools

import jax
import jax.numpy as jnp
import ml_dtypes
import numpy as np
from jax import lax
from jax.experimental import pallas as pl
from jax.experimental.pallas import tpu as pltpu
from jax.sharding import PartitionSpec as P

F32 = jnp.float32
BF16 = jnp.bfloat16
VMEM_LIMIT = 48 * 1024 * 1024

NV, NZ, NR, NL = 3, 16, 64, 128
HALO = 8


def detail_row(k):
    return {2 * k + 1: 1.0, 2 * k: -0.5, 2 * k + 2: -0.5}


def smooth_row(k):
    row = {2 * k: 1.0}
    for j in (k - 1, k):
        for cell, value in detail_row(j).items():
            row[cell] = row.get(cell, 0.0) + 0.25 * value
    return row


def even_row(k):
    return {("s", k): 1.0, ("d", k - 1): -0.25, ("d", k): -0.25}


def odd_row(k):
    row = {("d", k): 1.0}
    for j in (k, k + 1):
        for name, value in even_row(j).items():
            row[name] = row.get(name, 0.0) + 0.5 * value
    return row


def as_bf16(matrix):
    cast = matrix.astype(ml_dtypes.bfloat16)
    assert (cast.astype(np.float64) == matrix).all()
    return cast


def cell_place(y):
    return y if 0 <= y < NL else (y + HALO + NL if y < 0 else y + HALO)


def fill_forward(matrix, place_in, column, row):
    for cell, value in row.items():
        matrix[place_in(cell), column] += value


def level_one_columns():
    names = {("s", k): k for k in range(65)}
    names.update({("d", k): 128 + k for k in range(65)})
    names[("d", -1)] = 128 + 65
    return names


def level_two_columns():
    names = {("s", k): k for k in range(33)}
    names.update({("d", k): 64 + k for k in range(33)})
    names[("d", -1)] = 64 + 33
    return names


def smooth_place(k):
    return k + 2


@functools.lru_cache(maxsize=None)
def weights():
    w = {}
    names = level_one_columns()
    forward = np.zeros((144, 256))
    inverse = np.zeros((256, 128))
    for (kind, k), column in names.items():
        fill_forward(forward, cell_place, column, smooth_row(k) if kind == "s" else detail_row(k))
    for k in range(64):
        for y, row in ((2 * k, even_row(k)), (2 * k + 1, odd_row(k))):
            for name, value in row.items():
                inverse[names[name], y] += value
    w["forward"], w["inverse"] = forward, inverse
    smooth = np.zeros((256, 128))
    for k in range(-2, 67):
        fill_forward(smooth, cell_place, smooth_place(k), smooth_row(k))
    w["smooth"] = smooth
    names2 = level_two_columns()
    forward2 = np.zeros((128, 128))
    inverse2 = np.zeros((128, 128))
    for (kind, k), column in names2.items():
        fill_forward(forward2, smooth_place, column, smooth_row(k) if kind == "s" else detail_row(k))
    for k in range(33):
        rows = [(2 * k, even_row(k))] + ([(2 * k + 1, odd_row(k))] if k < 32 else [])
        for y, row in rows:
            for name, value in row.items():
                inverse2[names2[name], y] += value
    w["forward2"], w["inverse2"] = forward2, inverse2
    back = np.zeros((256, 128))
    back[:65] = inverse[:65]
    back[128 : 128 + 65] = inverse[:65]
    w["back"] = back
    plane = np.zeros((2, 8, NZ))

    def mirrored(z):
        return -z if z < 0 else (2 * (NZ - 1) - z if z > NZ - 1 else z)

    for k in range(8):
        for z, value in smooth_row(k).items():
            plane[0, k, mirrored(z)] += value
        for z, value in detail_row(k).items():
            plane[1, k, mirrored(z)] += value
    halo = np.zeros((4, 128, 2, 8, 16))
    for bz in range(2):
        for k in range(8):
            for z in range(NZ):
                for c in range(HALO):
                    left = 8 * ((z - 1) % NZ) + c
                    right = 8 * z + c
                    halo[0:2, left, bz, k, c] = plane[bz, k, z]
                    halo[2:4, right, bz, k, 8 + c] = plane[bz, k, z]
    w["halo"] = halo.reshape(512, 256)
    spread = np.zeros((3, 128, 2, 128))
    for k in range(64):
        spread[0, k, 0, k] = 1
    spread[1, 0, 0, 64] = 1
    spread[2, 63, 0, 65] = 1
    for k in range(32):
        spread[0, 64 + k, 1, k] = 1
        spread[0, 64 + k, 1, 64 + k] = 1
    for base in (0, 64):
        spread[1, 64, 1, base + 32] = 1
        spread[2, 95, 1, base + 33] = 1
    w["spread"] = spread.reshape(384, 256)
    expand = np.zeros((2, 4, 128))
    for j in range(4):
        expand[0, j, 16 * j : 16 * j + 16] = 1
        expand[1, j, 64 + 8 * j : 64 + 8 * j + 8] = 1
    w["expand"] = expand
    last = np.zeros((256, 128))
    last[:128, :32] = forward2[:, :32]
    last[128:, :32] = forward2[:, :32]
    w["last"] = last
    return {name: as_bf16(matrix) for name, matrix in w.items()}


def two_terms(x):
    high = x.astype(BF16)
    low = (x - high.astype(F32)).astype(BF16)
    return high, low


def dot(a, b):
    return jnp.dot(a, b, preferred_element_type=F32)


def lift_planes(cells):
    half = len(cells) // 2
    even, odd = cells[0::2], cells[1::2]
    detail = [odd[k] - 0.5 * (even[k] + even[min(k + 1, half - 1)]) for k in range(half)]
    smooth = [even[k] + 0.25 * (detail[max(k - 1, 0)] + detail[k]) for k in range(half)]
    return smooth, detail


def unlift_planes(smooth, detail):
    half = len(smooth)
    even = [smooth[k] - 0.25 * (detail[max(k - 1, 0)] + detail[k]) for k in range(half)]
    out = []
    for k in range(half):
        out += [even[k], detail[k] + 0.5 * (even[k] + even[min(k + 1, half - 1)])]
    return out


def lift_rows(load, start):
    even, odd, after = load(start), load(start + 1), load(start + 2)
    before, odd_before = load(start - 2), load(start - 1)
    detail = odd - 0.5 * (even + after)
    detail_before = odd_before - 0.5 * (before + even)
    return even + 0.25 * (detail_before + detail), detail


def unlift_rows(smooth, detail, row):
    here, after = detail(row), detail(row + 1)
    even = smooth(row) - 0.25 * (detail(row - 1) + here)
    next_even = smooth(row + 1) - 0.25 * (here + after)
    return even, here + 0.5 * (even + next_even)


def pack_kernel(field, masks, expand, top, bottom, left, right, own_masks):
    lane = lax.broadcasted_iota(jnp.int32, (8, NL), 1) // 8

    def pack_rows(step, _):
        v, t = step // 8, step % 8
        rows = pl.ds(pl.multiple_of(t * 8, 8), 8)
        low = jnp.zeros((8, NL), F32)
        high = jnp.zeros((8, NL), F32)
        for z in range(NZ):
            x = field[v, z, rows, :]
            turned = pltpu.roll(x, 8 * z, 1) if z else x
            low = jnp.where(lane == z, turned, low)
            high = jnp.where(lane == (z - 1) % NZ, turned, high)
        left[v, rows, :] = low
        right[v, rows, :] = high
        return 0

    lax.fori_loop(0, NV * 8, pack_rows, 0)
    for v in range(NV):
        top[v] = left[v, 0:8, :]
        top[3 + v] = right[v, 0:8, :]
        bottom[v] = left[v, NR - 8 : NR, :]
        bottom[3 + v] = right[v, NR - 8 : NR, :]
        top[8 + v * NZ : 8 + (v + 1) * NZ] = field[v, :, 0:8, :]
        bottom[8 + v * NZ : 8 + (v + 1) * NZ] = field[v, :, NR - 8 : NR, :]
    for i, out in ((0, top), (1, bottom)):
        tile = jnp.zeros((7, NL), F32)
        for l in range(2):
            flags = masks[l, i].astype(F32).astype(BF16)
            tile += lax.dot_general(flags, expand[l], (((0,), (0,)), ((), ())), preferred_element_type=F32)
        own_masks[i] = jnp.concatenate([tile, jnp.zeros((1, NL), F32)], 0)
        out[6] = own_masks[i]
        out[7] = jnp.zeros((8, NL), F32)


def pack(field, masks):
    w = weights()
    shapes = [(56, 8, NL), (56, 8, NL), (NV, NR, NL), (NV, NR, NL), (2, 8, NL)]
    vmem = pl.BlockSpec(memory_space=pltpu.VMEM)
    return pl.pallas_call(
        pack_kernel,
        out_shape=[jax.ShapeDtypeStruct(s, F32) for s in shapes],
        in_specs=[vmem] * 3,
        out_specs=[vmem] * 5,
        compiler_params=pltpu.CompilerParams(vmem_limit_bytes=VMEM_LIMIT),
    )(field, masks.transpose(0, 2, 3, 1), w["expand"])


def join_kernel(left, right, own_masks, north, south, to_left, to_right):
    for v in range(NV):
        for side, tile, out in ((left, v, to_left), (right, 3 + v, to_right)):
            out[v * 80 : v * 80 + 64, :] = side[v]
            out[v * 80 + 64 : v * 80 + 72, :] = south[tile]
            out[v * 80 + 72 : v * 80 + 80, :] = north[tile]
    for out in (to_left, to_right):
        out[240:248, :] = north[6]
        out[248:256, :] = own_masks[0]
        out[256:264, :] = own_masks[1]
        out[264:272, :] = south[6]


def join(left, right, own_masks, north, south):
    whole = pl.BlockSpec((NV, NR, NL), lambda i: (0, 0, 0))
    edge = pl.BlockSpec((8, 8, NL), lambda i: (0, 0, 0))
    out = pl.BlockSpec((272, NL), lambda i: (0, 0))
    return pl.pallas_call(
        join_kernel,
        grid=(1,),
        out_shape=[jax.ShapeDtypeStruct((272, NL), F32)] * 2,
        in_specs=[whole, whole, pl.BlockSpec((2, 8, NL), lambda i: (0, 0, 0)), edge, edge],
        out_specs=[out, out],
        compiler_params=pltpu.CompilerParams(vmem_limit_bytes=VMEM_LIMIT),
    )(left, right, own_masks, north, south)


def wave_kernel(
    field, north, south, west, east, own_masks,
    forward, inverse, smooth_w, forward2, inverse2, back, halo_w, spread, last,
    out, share,
    cells, first, halo_x, halo, gain, gain2, low, second, kept2, low_back, kept, sems,
):
    copies = []
    for v in range(NV):
        planes = pl.ds(8 + v * NZ, NZ)
        pairs = [
            (field.at[v], cells.at[v, 0:NZ, 8:72, :]),
            (north.at[planes], cells.at[v, 0:NZ, 0:8, :]),
            (north.at[planes], cells.at[v, 0:NZ, 80:88, :]),
            (south.at[planes], cells.at[v, 0:NZ, 72:80, :]),
            (field.at[v, :, 0:8, :], cells.at[v, 0:NZ, 88:96, :]),
        ]
        for p, ref in ((NZ, west), (NZ + 1, east)):
            pairs += [
                (ref.at[v * 80 : v * 80 + 80, :], cells.at[v, p, 8:88, :]),
                (ref.at[v * 80 + 72 : v * 80 + 80, :], cells.at[v, p, 0:8, :]),
                (ref.at[v * 80 : v * 80 + 8, :], cells.at[v, p, 88:96, :]),
            ]
        copies.append([
            pltpu.make_async_copy(source, target, sems.at[v, n]) for n, (source, target) in enumerate(pairs)
        ])
        for copy in copies[-1]:
            copy.start()
    tiles = [pltpu.make_async_copy(ref.at[240:272, :], cells.at[0, 18 + n, 0:32, :], sems.at[3, n])
             for n, ref in enumerate((west, east))]
    tiles += [pltpu.make_async_copy(north.at[6], cells.at[0, 20, 0:8, :], sems.at[3, 2]),
              pltpu.make_async_copy(south.at[6], cells.at[0, 20, 24:32, :], sems.at[3, 3])]
    for copy in tiles:
        copy.start()
    for copy in tiles:
        copy.wait()

    own = jnp.concatenate([cells[0, 20, 0:8, :], own_masks[0], own_masks[1], cells[0, 20, 24:32, :]], 0)
    flags = jnp.concatenate([own, cells[0, 19, 0:32, :], cells[0, 18, 0:32, :]], 1).astype(BF16)
    lanes = dot(flags, spread[...])
    lane64 = lax.broadcasted_iota(jnp.int32, (1, NL), 1) < 64
    zero, one = jnp.zeros((1, NL), F32), jnp.ones((1, NL), F32)
    forward_f, forward2_f = forward[...].astype(F32), forward2[...].astype(F32)
    for ib in range(4):
        for bz in range(2):
            for bx in range(2):
                n = 2 * bz + bx
                b = 8 * ib + 4 * bz + bx - 1
                smooth_one = lanes[b : b + 1, 0:NL] if n else zero
                detail_one = lanes[b + 2 : b + 3, 0:NL]
                row = jnp.concatenate([smooth_one, detail_one], 1)
                gain[ib, n, 0:144, :] = dot((forward_f * row).astype(BF16), inverse[...]).astype(BF16)
                gain[ib, n, 144:256, :] = jnp.zeros((112, NL), BF16)
                smooth_two = lanes[b : b + 1, NL:] if n else one
                row = jnp.where(lane64, smooth_two, lanes[b + 2 : b + 3, NL:])
                both = dot((forward2_f * row).astype(BF16), inverse2[...]).astype(BF16)
                gain2[ib, n, 0:128, :] = both
                gain2[ib, n, 128:256, :] = both

    for v in range(NV):
        for copy in copies[v]:
            copy.wait()

        def rows_one(t, _):
            at = pl.multiple_of(t * 8, 8)
            lifted = [
                lift_rows(lambda s: cells[v, p, pl.ds(16 * t + s, 8, stride=2), :], 8) for p in range(NZ + 2)
            ]
            for bx in range(2):
                smooth, detail = lift_planes([pair[bx] for pair in lifted[:NZ]])
                for bz, part in ((0, smooth), (1, detail)):
                    for z in range(8):
                        first[2 * bz + bx, v * 8 + z, pl.ds(at, 8), :] = part[z]
                halo_x[bx, v, pl.ds(at, 8), 0:NL] = lifted[NZ][bx]
                halo_x[bx, v, pl.ds(at, 8), NL:] = lifted[NZ + 1][bx]
            return 0

        lax.fori_loop(0, 5, rows_one, 0)
    for bx in range(2):
        high, low_term = two_terms(halo_x[bx].reshape(NV * 40, 256))
        terms = jnp.concatenate([high[:, :NL], low_term[:, :NL], high[:, NL:], low_term[:, NL:]], 1)
        halo[bx] = dot(terms, halo_w[...]).reshape(NV, 40, 256)

    def operand(n, v, at, count):
        bz, bx = n // 2, n % 2
        rows = pl.ds(at, count)
        main = first[n, pl.ds(v * 8, 8), rows, :].reshape(8 * count, NL)
        beside = halo[bx, v, rows, bz * NL : (bz + 1) * NL]
        sides = jnp.concatenate([pltpu.roll(beside, (NL - 16 * z) % NL, 1) if z else beside for z in range(8)], 0)
        return two_terms(jnp.concatenate([main, sides], 1))

    def smooth_part(v, _):
        planes = pl.ds(v * 8, 8)
        for at, count in ((0, 16), (16, 16), (32, 8)):
            high, low_term = operand(0, v, at, count)
            part = (dot(high, smooth_w[...]) + dot(low_term, smooth_w[...])).reshape(8, count, NL)
            if at < 32:
                low[planes, 8 + at : 8 + at + count, :] = part
                if at == 0:
                    low[planes, 56:64, :] = part[:, 0:8]
            else:
                low[planes, 0:8, :] = part
                low[planes, 40:48, :] = part
                low[planes, 48:56, :] = part
        return 0

    lax.fori_loop(0, NV, smooth_part, 0)

    def rows_two(v, _):
        for t in range(3):
            lifted = [
                lift_rows(lambda s: low[v * 8 + p, pl.ds(16 * t + s, 8, stride=2), :], 8) for p in range(8)
            ]
            for bx in range(2):
                smooth, detail = lift_planes([pair[bx] for pair in lifted])
                for bz, part in ((0, smooth), (1, detail)):
                    for z in range(4):
                        second[2 * bz + bx, t, pl.ds(pl.multiple_of((v * 4 + z) * 8, 8), 8), :] = part[z]
        return 0

    lax.fori_loop(0, NV, rows_two, 0)
    ext_two = lax.broadcasted_iota(jnp.int32, (NV * 4, 8, NL), 1) < 4
    for n in range(4):
        for t in range(3):
            terms = jnp.concatenate(two_terms(second[n, t]), 1)
            if n == 0 and t < 2:
                part = dot(terms, last[...]).reshape(NV, 4, 8, NL)
                for v in range(NV):
                    share[16 * v + 8 * t : 16 * v + 8 * t + 8, :] = part[v, 0] + sum(
                        pltpu.roll(part[v, z], 32 * z, 1) for z in range(1, 4)
                    )
            if t < 2:
                kept2[n, :, 8 + 8 * t : 16 + 8 * t, :] = dot(terms, gain2[t + 1, n]).reshape(NV * 4, 8, NL)
            else:
                below = dot(terms, gain2[3, n]).reshape(NV * 4, 8, NL)
                above = dot(terms, gain2[0, n]).reshape(NV * 4, 8, NL)
                part = jnp.where(ext_two, below, above)
                kept2[n, :, 0:8, :] = part
                kept2[n, :, 24:32, :] = part

    def back_two(v, _):
        for t in range(3):
            pairs = {}
            for bz in range(2):
                for z in range(4):
                    p = v * 4 + z
                    if t < 2:
                        pairs[bz, z] = unlift_rows(
                            lambda r: kept2[2 * bz, p, pl.ds(r, 8), :],
                            lambda r: kept2[2 * bz + 1, p, pl.ds(r, 8), :],
                            8 + 8 * t,
                        )
                    else:
                        even = kept2[2 * bz, p, 24:32, :] - 0.25 * (
                            kept2[2 * bz + 1, p, 23:31, :] + kept2[2 * bz + 1, p, 24:32, :]
                        )
                        pairs[bz, z] = (even, even)
            for parity in range(2 if t < 2 else 1):
                planes = unlift_planes([pairs[0, z][parity] for z in range(4)], [pairs[1, z][parity] for z in range(4)])
                for z in range(8):
                    low_back[v * 8 + z, pl.ds(16 * t + parity, 8, stride=2), :] = planes[z]
        return 0

    lax.fori_loop(0, NV, back_two, 0)

    ext_one = lax.broadcasted_iota(jnp.int32, (8, 8, NL), 1) < 4

    def keep(v, _):
        planes = pl.ds(v * 8, 8)
        for n in range(4):
            for ib in range(3):
                at, count = 16 * ib, 16 if ib < 2 else 8
                high, low_term = operand(n, v, at, count)
                if n == 0:
                    terms = jnp.concatenate(two_terms(low_back[planes, at : at + count, :].reshape(8 * count, NL)), 1)
                    base = dot(terms, back[...])
                if ib < 2:
                    part = dot(high, gain[ib + 1, n]) + dot(low_term, gain[ib + 1, n])
                    if n == 0:
                        part = part + base
                    kept[n, planes, 8 + at : 24 + at, :] = part.reshape(8, count, NL)
                else:
                    below = dot(high, gain[3, n]) + dot(low_term, gain[3, n])
                    above = dot(high, gain[0, n]) + dot(low_term, gain[0, n])
                    if n == 0:
                        below = below + base
                    part = jnp.where(ext_one, below.reshape(8, 8, NL), above.reshape(8, 8, NL))
                    kept[n, planes, 0:8, :] = part
                    kept[n, planes, 40:48, :] = part
        return 0

    lax.fori_loop(0, NV, keep, 0)

    def back_one(step, _):
        v, t = step // 4, step % 4
        pairs = {}
        for bz in range(2):
            for z in range(8):
                p = v * 8 + z
                pairs[bz, z] = unlift_rows(
                    lambda r: kept[2 * bz, p, pl.ds(8 * t + r, 8), :],
                    lambda r: kept[2 * bz + 1, p, pl.ds(8 * t + r, 8), :],
                    8,
                )
        for parity in range(2):
            planes = unlift_planes([pairs[0, z][parity] for z in range(8)], [pairs[1, z][parity] for z in range(8)])
            for z in range(NZ):
                out[v, z, pl.ds(16 * t + parity, 8, stride=2), :] = planes[z]
        return 0

    lax.fori_loop(0, NV * 4, back_one, 0)


def wave(field, north, south, west, east, own_masks):
    w = weights()
    vmem = pl.BlockSpec(memory_space=pltpu.VMEM)
    anywhere = pl.BlockSpec(memory_space=pl.ANY)
    names = ["forward", "inverse", "smooth", "forward2", "inverse2", "back", "halo", "spread", "last"]
    return pl.pallas_call(
        wave_kernel,
        out_shape=[jax.ShapeDtypeStruct((NV, NZ, NR, NL), F32), jax.ShapeDtypeStruct((48, NL), F32)],
        in_specs=[anywhere] * 5 + [vmem] * (1 + len(names)),
        out_specs=[vmem, vmem],
        scratch_shapes=[
            pltpu.VMEM((NV, 21, 96, NL), F32),
            pltpu.VMEM((4, NV * 8, 40, NL), F32),
            pltpu.VMEM((2, NV, 40, 256), F32),
            pltpu.VMEM((2, NV, 40, 256), F32),
            pltpu.VMEM((4, 4, 256, NL), BF16),
            pltpu.VMEM((4, 4, 256, NL), BF16),
            pltpu.VMEM((NV * 8, 64, NL), F32),
            pltpu.VMEM((4, 3, NV * 32, NL), F32),
            pltpu.VMEM((4, NV * 4, 40, NL), F32),
            pltpu.VMEM((NV * 8, 48, NL), F32),
            pltpu.VMEM((4, NV * 8, 48, NL), F32),
            pltpu.SemaphoreType.DMA((4, 11)),
        ],
        compiler_params=pltpu.CompilerParams(vmem_limit_bytes=VMEM_LIMIT),
    )(field, north, south, west, east, own_masks, *[w[name] for name in names])


def coarse_kernel(count_x, count_y, shares, out):
    lane = lax.broadcasted_iota(jnp.int32, (16, NL), 1) // 32

    def block(i, _):
        rows = pl.ds(pl.multiple_of(16 * i, 16), 16)
        for v in range(NV):
            for t in range(count_y // 4):
                parts = [shares[i, 4 * t + q, 16 * v : 16 * v + 16, :] for q in range(4)]
                for z in range(4):
                    turned = [pltpu.roll(p, (32 * (q - z)) % NL, 1) if q != z else p for q, p in enumerate(parts)]
                    low = jnp.where(lane == 0, turned[0], turned[1])
                    high = jnp.where(lane == 2, turned[2], turned[3])
                    out[v, z, rows, NL * t : NL * (t + 1)] = jnp.where(lane < 2, low, high)
        return 0

    lax.fori_loop(0, count_x, block, 0)


def coarse_of(shares, count_x, count_y):
    vmem = pl.BlockSpec(memory_space=pltpu.VMEM)
    return pl.pallas_call(
        functools.partial(coarse_kernel, count_x, count_y),
        out_shape=jax.ShapeDtypeStruct((NV, 4, 16 * count_x, 32 * count_y), F32),
        in_specs=[vmem],
        out_specs=vmem,
        compiler_params=pltpu.CompilerParams(vmem_limit_bytes=VMEM_LIMIT),
    )(shares.reshape(count_x, count_y, 48, NL))


def shifts(axis):
    count = lax.axis_size(axis)
    up = [(i, (i + 1) % count) for i in range(count)]
    return up, [(j, i) for i, j in up]


def body(field, masks):
    count_x, count_y = lax.axis_size("gx"), lax.axis_size("gy")
    top, bottom, left, right, own_masks = pack(field, masks)
    up, down = shifts("gx")
    north = lax.ppermute(bottom, "gx", up)
    south = lax.ppermute(top, "gx", down)
    to_left, to_right = join(left, right, own_masks, north, south)
    up, down = shifts("gy")
    west = lax.ppermute(to_right, "gy", up)
    east = lax.ppermute(to_left, "gy", down)
    restored, share = wave(field, north, south, west, east, own_masks)
    shares = lax.all_gather(share, ("gx", "gy"), axis=0, tiled=True)
    return restored, coarse_of(shares, count_x, count_y)


def solution(mesh):
    placed = P(None, None, "gx", "gy")
    return jax.shard_map(
        body,
        mesh=mesh,
        in_specs=(placed, placed),
        out_specs=(placed, P()),
        check_vma=False,
    )
```

```python
import functools

import jax
import jax.numpy as jnp
import ml_dtypes
import numpy as np
from jax import lax
from jax.experimental import pallas as pl
from jax.experimental.pallas import tpu as pltpu
from jax.sharding import PartitionSpec as P

F32 = jnp.float32
BF16 = jnp.bfloat16
VMEM_LIMIT = 48 * 1024 * 1024

NV, NZ, NR, NL = 3, 16, 64, 128
HALO = 8


def detail_row(k):
    return {2 * k + 1: 1.0, 2 * k: -0.5, 2 * k + 2: -0.5}


def smooth_row(k):
    row = {2 * k: 1.0}
    for j in (k - 1, k):
        for cell, value in detail_row(j).items():
            row[cell] = row.get(cell, 0.0) + 0.25 * value
    return row


def even_row(k):
    return {("s", k): 1.0, ("d", k - 1): -0.25, ("d", k): -0.25}


def odd_row(k):
    row = {("d", k): 1.0}
    for j in (k, k + 1):
        for name, value in even_row(j).items():
            row[name] = row.get(name, 0.0) + 0.5 * value
    return row


def as_bf16(matrix):
    cast = matrix.astype(ml_dtypes.bfloat16)
    assert (cast.astype(np.float64) == matrix).all()
    return cast


def cell_place(y):
    return y if 0 <= y < NL else (y + HALO + NL if y < 0 else y + HALO)


def fill_forward(matrix, place_in, column, row):
    for cell, value in row.items():
        matrix[place_in(cell), column] += value


def level_one_columns():
    names = {("s", k): k for k in range(65)}
    names.update({("d", k): 128 + k for k in range(65)})
    names[("d", -1)] = 128 + 65
    return names


def level_two_columns():
    names = {("s", k): k for k in range(33)}
    names.update({("d", k): 64 + k for k in range(33)})
    names[("d", -1)] = 64 + 33
    return names


def smooth_place(k):
    return k + 2


@functools.lru_cache(maxsize=None)
def weights():
    w = {}
    names = level_one_columns()
    forward = np.zeros((144, 256))
    inverse = np.zeros((256, 128))
    for (kind, k), column in names.items():
        fill_forward(forward, cell_place, column, smooth_row(k) if kind == "s" else detail_row(k))
    for k in range(64):
        for y, row in ((2 * k, even_row(k)), (2 * k + 1, odd_row(k))):
            for name, value in row.items():
                inverse[names[name], y] += value
    w["forward"], w["inverse"] = forward, inverse
    smooth = np.zeros((256, 128))
    for k in range(-2, 67):
        fill_forward(smooth, cell_place, smooth_place(k), smooth_row(k))
    w["smooth"] = smooth
    names2 = level_two_columns()
    forward2 = np.zeros((128, 128))
    inverse2 = np.zeros((128, 128))
    for (kind, k), column in names2.items():
        fill_forward(forward2, smooth_place, column, smooth_row(k) if kind == "s" else detail_row(k))
    for k in range(33):
        rows = [(2 * k, even_row(k))] + ([(2 * k + 1, odd_row(k))] if k < 32 else [])
        for y, row in rows:
            for name, value in row.items():
                inverse2[names2[name], y] += value
    w["forward2"], w["inverse2"] = forward2, inverse2
    back = np.zeros((256, 128))
    back[:65] = inverse[:65]
    back[128 : 128 + 65] = inverse[:65]
    w["back"] = back
    plane = np.zeros((2, 8, NZ))

    def mirrored(z):
        return -z if z < 0 else (2 * (NZ - 1) - z if z > NZ - 1 else z)

    for k in range(8):
        for z, value in smooth_row(k).items():
            plane[0, k, mirrored(z)] += value
        for z, value in detail_row(k).items():
            plane[1, k, mirrored(z)] += value
    halo = np.zeros((4, 128, 2, 8, 16))
    for bz in range(2):
        for k in range(8):
            for z in range(NZ):
                for c in range(HALO):
                    left = 8 * ((z - 1) % NZ) + c
                    right = 8 * z + c
                    halo[0:2, left, bz, k, c] = plane[bz, k, z]
                    halo[2:4, right, bz, k, 8 + c] = plane[bz, k, z]
    w["halo"] = halo.reshape(512, 256)
    spread = np.zeros((3, 128, 2, 128))
    for k in range(64):
        spread[0, k, 0, k] = 1
    spread[1, 0, 0, 64] = 1
    spread[2, 63, 0, 65] = 1
    for k in range(32):
        spread[0, 64 + k, 1, k] = 1
        spread[0, 64 + k, 1, 64 + k] = 1
    for base in (0, 64):
        spread[1, 64, 1, base + 32] = 1
        spread[2, 95, 1, base + 33] = 1
    w["spread"] = spread.reshape(384, 256)
    expand = np.zeros((2, 4, 128))
    for j in range(4):
        expand[0, j, 16 * j : 16 * j + 16] = 1
        expand[1, j, 64 + 8 * j : 64 + 8 * j + 8] = 1
    w["expand"] = expand
    last = np.zeros((256, 128))
    last[:128, :32] = forward2[:, :32]
    last[128:, :32] = forward2[:, :32]
    w["last"] = last
    return {name: as_bf16(matrix) for name, matrix in w.items()}


def two_terms(x):
    high = x.astype(BF16)
    low = (x - high.astype(F32)).astype(BF16)
    return high, low


def dot(a, b):
    return jnp.dot(a, b, preferred_element_type=F32)


def lift_planes(cells):
    half = len(cells) // 2
    even, odd = cells[0::2], cells[1::2]
    detail = [odd[k] - 0.5 * (even[k] + even[min(k + 1, half - 1)]) for k in range(half)]
    smooth = [even[k] + 0.25 * (detail[max(k - 1, 0)] + detail[k]) for k in range(half)]
    return smooth, detail


def unlift_planes(smooth, detail):
    half = len(smooth)
    even = [smooth[k] - 0.25 * (detail[max(k - 1, 0)] + detail[k]) for k in range(half)]
    out = []
    for k in range(half):
        out += [even[k], detail[k] + 0.5 * (even[k] + even[min(k + 1, half - 1)])]
    return out


def lift_rows(load, start):
    even, odd, after = load(start), load(start + 1), load(start + 2)
    before, odd_before = load(start - 2), load(start - 1)
    detail = odd - 0.5 * (even + after)
    detail_before = odd_before - 0.5 * (before + even)
    return even + 0.25 * (detail_before + detail), detail


def unlift_rows(smooth, detail, row):
    here, after = detail(row), detail(row + 1)
    even = smooth(row) - 0.25 * (detail(row - 1) + here)
    next_even = smooth(row + 1) - 0.25 * (here + after)
    return even, here + 0.5 * (even + next_even)


def pack_kernel(field, masks, expand, top, bottom, left, right, own_masks):
    lane = lax.broadcasted_iota(jnp.int32, (8, NL), 1) // 8

    def pack_rows(step, _):
        v, t = step // 8, step % 8
        rows = pl.ds(pl.multiple_of(t * 8, 8), 8)
        low = jnp.zeros((8, NL), F32)
        high = jnp.zeros((8, NL), F32)
        for z in range(NZ):
            x = field[v, z, rows, :]
            turned = pltpu.roll(x, 8 * z, 1) if z else x
            low = jnp.where(lane == z, turned, low)
            high = jnp.where(lane == (z - 1) % NZ, turned, high)
        left[v, rows, :] = low
        right[v, rows, :] = high
        return 0

    lax.fori_loop(0, NV * 8, pack_rows, 0)
    for v in range(NV):
        top[v] = left[v, 0:8, :]
        top[3 + v] = right[v, 0:8, :]
        bottom[v] = left[v, NR - 8 : NR, :]
        bottom[3 + v] = right[v, NR - 8 : NR, :]
        top[8 + v * NZ : 8 + (v + 1) * NZ] = field[v, :, 0:8, :]
        bottom[8 + v * NZ : 8 + (v + 1) * NZ] = field[v, :, NR - 8 : NR, :]
    for i, out in ((0, top), (1, bottom)):
        tile = jnp.zeros((7, NL), F32)
        for l in range(2):
            flags = masks[l, i].astype(F32).astype(BF16)
            tile += lax.dot_general(flags, expand[l], (((0,), (0,)), ((), ())), preferred_element_type=F32)
        own_masks[i] = jnp.concatenate([tile, jnp.zeros((1, NL), F32)], 0)
        out[6] = own_masks[i]
        out[7] = jnp.zeros((8, NL), F32)


def pack(field, masks):
    w = weights()
    shapes = [(56, 8, NL), (56, 8, NL), (NV, NR, NL), (NV, NR, NL), (2, 8, NL)]
    vmem = pl.BlockSpec(memory_space=pltpu.VMEM)
    return pl.pallas_call(
        pack_kernel,
        out_shape=[jax.ShapeDtypeStruct(s, F32) for s in shapes],
        in_specs=[vmem] * 3,
        out_specs=[vmem] * 5,
        compiler_params=pltpu.CompilerParams(vmem_limit_bytes=VMEM_LIMIT),
    )(field, masks.transpose(0, 2, 3, 1), w["expand"])


def join_kernel(left, right, own_masks, north, south, to_left, to_right):
    for v in range(NV):
        for side, tile, out in ((left, v, to_left), (right, 3 + v, to_right)):
            out[v * 80 : v * 80 + 64, :] = side[v]
            out[v * 80 + 64 : v * 80 + 72, :] = south[tile]
            out[v * 80 + 72 : v * 80 + 80, :] = north[tile]
    for out in (to_left, to_right):
        out[240:248, :] = north[6]
        out[248:256, :] = own_masks[0]
        out[256:264, :] = own_masks[1]
        out[264:272, :] = south[6]


def join(left, right, own_masks, north, south):
    whole = pl.BlockSpec((NV, NR, NL), lambda i: (0, 0, 0))
    edge = pl.BlockSpec((8, 8, NL), lambda i: (0, 0, 0))
    out = pl.BlockSpec((272, NL), lambda i: (0, 0))
    return pl.pallas_call(
        join_kernel,
        grid=(1,),
        out_shape=[jax.ShapeDtypeStruct((272, NL), F32)] * 2,
        in_specs=[whole, whole, pl.BlockSpec((2, 8, NL), lambda i: (0, 0, 0)), edge, edge],
        out_specs=[out, out],
        compiler_params=pltpu.CompilerParams(vmem_limit_bytes=VMEM_LIMIT),
    )(left, right, own_masks, north, south)


def wave_kernel(
    field, north, south, west, east, own_masks,
    forward, inverse, smooth_w, forward2, inverse2, back, halo_w, spread, last,
    out, share,
    cells, first, halo_x, halo, gain, gain2, low, second, kept2, low_back, kept, sems,
):
    copies = []
    for v in range(NV):
        planes = pl.ds(8 + v * NZ, NZ)
        pairs = [
            (field.at[v], cells.at[v, 0:NZ, 8:72, :]),
            (north.at[planes], cells.at[v, 0:NZ, 0:8, :]),
            (north.at[planes], cells.at[v, 0:NZ, 80:88, :]),
            (south.at[planes], cells.at[v, 0:NZ, 72:80, :]),
            (field.at[v, :, 0:8, :], cells.at[v, 0:NZ, 88:96, :]),
        ]
        for p, ref in ((NZ, west), (NZ + 1, east)):
            pairs += [
                (ref.at[v * 80 : v * 80 + 80, :], cells.at[v, p, 8:88, :]),
                (ref.at[v * 80 + 72 : v * 80 + 80, :], cells.at[v, p, 0:8, :]),
                (ref.at[v * 80 : v * 80 + 8, :], cells.at[v, p, 88:96, :]),
            ]
        copies.append([
            pltpu.make_async_copy(source, target, sems.at[v, n]) for n, (source, target) in enumerate(pairs)
        ])
        for copy in copies[-1]:
            copy.start()
    tiles = [pltpu.make_async_copy(ref.at[240:272, :], cells.at[0, 18 + n, 0:32, :], sems.at[3, n])
             for n, ref in enumerate((west, east))]
    tiles += [pltpu.make_async_copy(north.at[6], cells.at[0, 20, 0:8, :], sems.at[3, 2]),
              pltpu.make_async_copy(south.at[6], cells.at[0, 20, 24:32, :], sems.at[3, 3])]
    for copy in tiles:
        copy.start()
    for copy in tiles:
        copy.wait()

    own = jnp.concatenate([cells[0, 20, 0:8, :], own_masks[0], own_masks[1], cells[0, 20, 24:32, :]], 0)
    flags = jnp.concatenate([own, cells[0, 19, 0:32, :], cells[0, 18, 0:32, :]], 1).astype(BF16)
    lanes = dot(flags, spread[...])
    lane64 = lax.broadcasted_iota(jnp.int32, (1, NL), 1) < 64
    zero, one = jnp.zeros((1, NL), F32), jnp.ones((1, NL), F32)
    forward_f, forward2_f = forward[...].astype(F32), forward2[...].astype(F32)
    for ib in range(4):
        for bz in range(2):
            for bx in range(2):
                n = 2 * bz + bx
                b = 8 * ib + 4 * bz + bx - 1
                smooth_one = lanes[b : b + 1, 0:NL] if n else zero
                detail_one = lanes[b + 2 : b + 3, 0:NL]
                row = jnp.concatenate([smooth_one, detail_one], 1)
                gain[ib, n, 0:144, :] = dot((forward_f * row).astype(BF16), inverse[...]).astype(BF16)
                gain[ib, n, 144:256, :] = jnp.zeros((112, NL), BF16)
                smooth_two = lanes[b : b + 1, NL:] if n else one
                row = jnp.where(lane64, smooth_two, lanes[b + 2 : b + 3, NL:])
                both = dot((forward2_f * row).astype(BF16), inverse2[...]).astype(BF16)
                gain2[ib, n, 0:128, :] = both
                gain2[ib, n, 128:256, :] = both

    for v in range(NV):
        for copy in copies[v]:
            copy.wait()

        def rows_one(t, _):
            at = pl.multiple_of(t * 8, 8)
            lifted = [
                lift_rows(lambda s: cells[v, p, pl.ds(16 * t + s, 8, stride=2), :], 8) for p in range(NZ + 2)
            ]
            for bx in range(2):
                smooth, detail = lift_planes([pair[bx] for pair in lifted[:NZ]])
                for bz, part in ((0, smooth), (1, detail)):
                    for z in range(8):
                        first[2 * bz + bx, v * 8 + z, pl.ds(at, 8), :] = part[z]
                halo_x[bx, v, pl.ds(at, 8), 0:NL] = lifted[NZ][bx]
                halo_x[bx, v, pl.ds(at, 8), NL:] = lifted[NZ + 1][bx]
            return 0

        lax.fori_loop(0, 5, rows_one, 0)
    for bx in range(2):
        high, low_term = two_terms(halo_x[bx].reshape(NV * 40, 256))
        terms = jnp.concatenate([high[:, :NL], low_term[:, :NL], high[:, NL:], low_term[:, NL:]], 1)
        halo[bx] = dot(terms, halo_w[...]).reshape(NV, 40, 256)

    def operand(n, v, at, count):
        bz, bx = n // 2, n % 2
        rows = pl.ds(at, count)
        main = first[n, pl.ds(v * 8, 8), rows, :].reshape(8 * count, NL)
        beside = halo[bx, v, rows, bz * NL : (bz + 1) * NL]
        sides = jnp.concatenate([pltpu.roll(beside, (NL - 16 * z) % NL, 1) if z else beside for z in range(8)], 0)
        return two_terms(jnp.concatenate([main, sides], 1))

    def smooth_part(v, _):
        planes = pl.ds(v * 8, 8)
        for at, count in ((0, 16), (16, 16), (32, 8)):
            high, low_term = operand(0, v, at, count)
            part = (dot(high, smooth_w[...]) + dot(low_term, smooth_w[...])).reshape(8, count, NL)
            if at < 32:
                low[planes, 8 + at : 8 + at + count, :] = part
                if at == 0:
                    low[planes, 56:64, :] = part[:, 0:8]
            else:
                low[planes, 0:8, :] = part
                low[planes, 40:48, :] = part
                low[planes, 48:56, :] = part
        return 0

    lax.fori_loop(0, NV, smooth_part, 0)

    def rows_two(v, _):
        for t in range(3):
            lifted = [
                lift_rows(lambda s: low[v * 8 + p, pl.ds(16 * t + s, 8, stride=2), :], 8) for p in range(8)
            ]
            for bx in range(2):
                smooth, detail = lift_planes([pair[bx] for pair in lifted])
                for bz, part in ((0, smooth), (1, detail)):
                    for z in range(4):
                        second[2 * bz + bx, t, pl.ds(pl.multiple_of((v * 4 + z) * 8, 8), 8), :] = part[z]
        return 0

    lax.fori_loop(0, NV, rows_two, 0)
    ext_two = lax.broadcasted_iota(jnp.int32, (NV * 4, 8, NL), 1) < 4
    for n in range(4):
        for t in range(3):
            terms = jnp.concatenate(two_terms(second[n, t]), 1)
            if n == 0 and t < 2:
                part = dot(terms, last[...]).reshape(NV, 4, 8, NL)
                for v in range(NV):
                    share[16 * v + 8 * t : 16 * v + 8 * t + 8, :] = part[v, 0] + sum(
                        pltpu.roll(part[v, z], 32 * z, 1) for z in range(1, 4)
                    )
            if t < 2:
                kept2[n, :, 8 + 8 * t : 16 + 8 * t, :] = dot(terms, gain2[t + 1, n]).reshape(NV * 4, 8, NL)
            else:
                below = dot(terms, gain2[3, n]).reshape(NV * 4, 8, NL)
                above = dot(terms, gain2[0, n]).reshape(NV * 4, 8, NL)
                part = jnp.where(ext_two, below, above)
                kept2[n, :, 0:8, :] = part
                kept2[n, :, 24:32, :] = part

    def back_two(v, _):
        for t in range(3):
            pairs = {}
            for bz in range(2):
                for z in range(4):
                    p = v * 4 + z
                    if t < 2:
                        pairs[bz, z] = unlift_rows(
                            lambda r: kept2[2 * bz, p, pl.ds(r, 8), :],
                            lambda r: kept2[2 * bz + 1, p, pl.ds(r, 8), :],
                            8 + 8 * t,
                        )
                    else:
                        even = kept2[2 * bz, p, 24:32, :] - 0.25 * (
                            kept2[2 * bz + 1, p, 23:31, :] + kept2[2 * bz + 1, p, 24:32, :]
                        )
                        pairs[bz, z] = (even, even)
            for parity in range(2 if t < 2 else 1):
                planes = unlift_planes([pairs[0, z][parity] for z in range(4)], [pairs[1, z][parity] for z in range(4)])
                for z in range(8):
                    low_back[v * 8 + z, pl.ds(16 * t + parity, 8, stride=2), :] = planes[z]
        return 0

    lax.fori_loop(0, NV, back_two, 0)

    ext_one = lax.broadcasted_iota(jnp.int32, (8, 8, NL), 1) < 4

    def keep(v, _):
        planes = pl.ds(v * 8, 8)
        for n in range(4):
            for ib in range(3):
                at, count = 16 * ib, 16 if ib < 2 else 8
                high, low_term = operand(n, v, at, count)
                if n == 0:
                    terms = jnp.concatenate(two_terms(low_back[planes, at : at + count, :].reshape(8 * count, NL)), 1)
                    base = dot(terms, back[...])
                if ib < 2:
                    part = dot(high, gain[ib + 1, n]) + dot(low_term, gain[ib + 1, n])
                    if n == 0:
                        part = part + base
                    kept[n, planes, 8 + at : 24 + at, :] = part.reshape(8, count, NL)
                else:
                    below = dot(high, gain[3, n]) + dot(low_term, gain[3, n])
                    above = dot(high, gain[0, n]) + dot(low_term, gain[0, n])
                    if n == 0:
                        below = below + base
                    part = jnp.where(ext_one, below.reshape(8, 8, NL), above.reshape(8, 8, NL))
                    kept[n, planes, 0:8, :] = part
                    kept[n, planes, 40:48, :] = part
        return 0

    lax.fori_loop(0, NV, keep, 0)

    def back_one(step, _):
        v, t = step // 4, step % 4
        pairs = {}
        for bz in range(2):
            for z in range(8):
                p = v * 8 + z
                pairs[bz, z] = unlift_rows(
                    lambda r: kept[2 * bz, p, pl.ds(8 * t + r, 8), :],
                    lambda r: kept[2 * bz + 1, p, pl.ds(8 * t + r, 8), :],
                    8,
                )
        for parity in range(2):
            planes = unlift_planes([pairs[0, z][parity] for z in range(8)], [pairs[1, z][parity] for z in range(8)])
            for z in range(NZ):
                out[v, z, pl.ds(16 * t + parity, 8, stride=2), :] = planes[z]
        return 0

    lax.fori_loop(0, NV * 4, back_one, 0)


def wave(field, north, south, west, east, own_masks):
    w = weights()
    vmem = pl.BlockSpec(memory_space=pltpu.VMEM)
    anywhere = pl.BlockSpec(memory_space=pl.ANY)
    names = ["forward", "inverse", "smooth", "forward2", "inverse2", "back", "halo", "spread", "last"]
    return pl.pallas_call(
        wave_kernel,
        out_shape=[jax.ShapeDtypeStruct((NV, NZ, NR, NL), F32), jax.ShapeDtypeStruct((48, NL), F32)],
        in_specs=[anywhere] * 5 + [vmem] * (1 + len(names)),
        out_specs=[vmem, vmem],
        scratch_shapes=[
            pltpu.VMEM((NV, 21, 96, NL), F32),
            pltpu.VMEM((4, NV * 8, 40, NL), F32),
            pltpu.VMEM((2, NV, 40, 256), F32),
            pltpu.VMEM((2, NV, 40, 256), F32),
            pltpu.VMEM((4, 4, 256, NL), BF16),
            pltpu.VMEM((4, 4, 256, NL), BF16),
            pltpu.VMEM((NV * 8, 64, NL), F32),
            pltpu.VMEM((4, 3, NV * 32, NL), F32),
            pltpu.VMEM((4, NV * 4, 40, NL), F32),
            pltpu.VMEM((NV * 8, 48, NL), F32),
            pltpu.VMEM((4, NV * 8, 48, NL), F32),
            pltpu.SemaphoreType.DMA((4, 11)),
        ],
        compiler_params=pltpu.CompilerParams(vmem_limit_bytes=VMEM_LIMIT),
    )(field, north, south, west, east, own_masks, *[w[name] for name in names])


def coarse_kernel(count_x, count_y, shares, out):
    lane = lax.broadcasted_iota(jnp.int32, (16, NL), 1) // 32

    def block(i, _):
        rows = pl.ds(pl.multiple_of(16 * i, 16), 16)
        for v in range(NV):
            for t in range(count_y // 4):
                parts = [shares[4 * t + q, i, 16 * v : 16 * v + 16, :] for q in range(4)]
                for z in range(4):
                    turned = [pltpu.roll(p, (32 * (q - z)) % NL, 1) if q != z else p for q, p in enumerate(parts)]
                    low = jnp.where(lane == 0, turned[0], turned[1])
                    high = jnp.where(lane == 2, turned[2], turned[3])
                    out[v, z, rows, NL * t : NL * (t + 1)] = jnp.where(lane < 2, low, high)
        return 0

    lax.fori_loop(0, count_x, block, 0)


def coarse_of(shares, count_x, count_y):
    vmem = pl.BlockSpec(memory_space=pltpu.VMEM)
    return pl.pallas_call(
        functools.partial(coarse_kernel, count_x, count_y),
        out_shape=jax.ShapeDtypeStruct((NV, 4, 16 * count_x, 32 * count_y), F32),
        in_specs=[vmem],
        out_specs=vmem,
        compiler_params=pltpu.CompilerParams(vmem_limit_bytes=VMEM_LIMIT),
    )(shares.reshape(count_y, count_x, 48, NL))


def shifts(axis):
    count = lax.axis_size(axis)
    up = [(i, (i + 1) % count) for i in range(count)]
    return up, [(j, i) for i, j in up]


def body(field, masks):
    count_x, count_y = lax.axis_size("gx"), lax.axis_size("gy")
    top, bottom, left, right, own_masks = pack(field, masks)
    up, down = shifts("gx")
    north = lax.ppermute(bottom, "gx", up)
    south = lax.ppermute(top, "gx", down)
    to_left, to_right = join(left, right, own_masks, north, south)
    up, down = shifts("gy")
    west = lax.ppermute(to_right, "gy", up)
    east = lax.ppermute(to_left, "gy", down)
    restored, share = wave(field, north, south, west, east, own_masks)
    shares = lax.all_gather(lax.all_gather(share, "gx", axis=0, tiled=True), "gy", axis=0, tiled=True)
    return restored, coarse_of(shares, count_x, count_y)


def solution(mesh):
    placed = P(None, None, "gx", "gy")
    return jax.shard_map(
        body,
        mesh=mesh,
        in_specs=(placed, placed),
        out_specs=(placed, P()),
        check_vma=False,
    )
```

```python
import functools

import jax
import jax.numpy as jnp
import ml_dtypes
import numpy as np
from jax import lax
from jax.experimental import pallas as pl
from jax.experimental.pallas import tpu as pltpu
from jax.sharding import PartitionSpec as P

F32 = jnp.float32
BF16 = jnp.bfloat16
VMEM_LIMIT = 32 * 1024 * 1024

NV, NZ, NR, NL = 3, 16, 64, 128


def detail_row(k):
    return {2 * k + 1: 1.0, 2 * k: -0.5, 2 * k + 2: -0.5}


def smooth_row(k):
    row = {2 * k: 1.0}
    for j in (k - 1, k):
        for cell, value in detail_row(j).items():
            row[cell] = row.get(cell, 0.0) + 0.25 * value
    return row


def even_row(k):
    return {("s", k): 1.0, ("d", k - 1): -0.25, ("d", k): -0.25}


def odd_row(k):
    row = {("d", k): 1.0}
    for j in (k, k + 1):
        for name, value in even_row(j).items():
            row[name] = row.get(name, 0.0) + 0.5 * value
    return row


def as_bf16(matrix):
    cast = matrix.astype(ml_dtypes.bfloat16)
    assert (cast.astype(np.float64) == matrix).all()
    return cast


def combine(*terms):
    total = {}
    for factor, row in terms:
        for cell, value in row.items():
            total[cell] = total.get(cell, 0.0) + factor * value
    return total


def level_one_columns():
    names = {("s", k): k for k in range(65)}
    names.update({("d", k): 128 + k for k in range(65)})
    names[("d", -1)] = 128 + 65
    return names


def level_two_columns():
    names = {("s", k): k for k in range(33)}
    names.update({("d", k): 64 + k for k in range(33)})
    names[("d", -1)] = 64 + 33
    return names


def smooth_place(k):
    return k + 2


def beyond(n):
    return {"cell": 24 * n, "after": 24 * n + 8, "before": 24 * n + 16}


BEYOND_SMOOTH = {65: 96, 66: 104, -2: 112, -1: 120}


def own_row(kind, k, n):
    place = {name: 128 + lane for name, lane in beyond(n).items()}
    if kind == "d":
        if k == -1:
            return {place["before"]: 1.0, 0: -0.5}
        if k == 64:
            return {place["after"]: 1.0}
        return {(place["cell"] if y == 128 else y): value for y, value in detail_row(k).items()}
    if k in BEYOND_SMOOTH:
        row = {128 + BEYOND_SMOOTH[k]: 1.0}
        return combine((1.0, row), (1.0, {0: -0.125})) if k == -1 else row
    even = place["cell"] if k == 64 else 2 * k
    return combine((1.0, {even: 1.0}), (0.25, own_row("d", k - 1, n)), (0.25, own_row("d", k, n)))


def group_start(n):
    return 16 * (24 * n // 16)


@functools.lru_cache(maxsize=None)
def weights():
    w = {}
    names = level_one_columns()
    forward = np.zeros((4, 256, 256))
    inverse = np.zeros((256, 128))
    for (kind, k), column in names.items():
        for n in range(4):
            for place, value in own_row(kind, k, n).items():
                forward[n, place, column] += value
    for k in range(64):
        for y, row in ((2 * k, even_row(k)), (2 * k + 1, odd_row(k))):
            for name, value in row.items():
                inverse[names[name], y] += value
    short = np.zeros((4, 160, 256))
    for n in range(4):
        at = 128 + group_start(n)
        short[n, :128], short[n, 128:] = forward[n, :128], forward[n, at : at + 32]
        assert abs(short[n]).sum() == abs(forward[n]).sum()
    smooth = np.zeros((256, 128))
    for k in range(-2, 67):
        for place, value in own_row("s", k, 0).items():
            smooth[place, smooth_place(k)] += value
    names2 = level_two_columns()
    forward2 = np.zeros((128, 128))
    inverse2 = np.zeros((128, 128))
    for (kind, k), column in names2.items():
        for cell, value in (smooth_row(k) if kind == "s" else detail_row(k)).items():
            forward2[smooth_place(cell), column] += value
    for k in range(33):
        rows = [(2 * k, even_row(k))] + ([(2 * k + 1, odd_row(k))] if k < 32 else [])
        for y, row in rows:
            for name, value in row.items():
                inverse2[names2[name], y] += value
    back = np.zeros((256, 128))
    back[:65] = inverse[:65]
    back[128 : 128 + 65] = inverse[:65]
    spread = np.zeros((3, 128, 2, 128))
    for k in range(64):
        spread[0, k, 0, k] = 1
    spread[1, 0, 0, 64] = 1
    spread[2, 63, 0, 65] = 1
    for k in range(32):
        spread[0, 64 + k, 1, k] = 1
        spread[0, 64 + k, 1, 64 + k] = 1
    for base in (0, 64):
        spread[1, 64, 1, base + 32] = 1
        spread[2, 95, 1, base + 33] = 1
    w["wide"] = np.concatenate([short.reshape(640, 256), spread.reshape(384, 256)], 0)
    w["narrow"] = np.concatenate([inverse, smooth, back, forward2, inverse2], 0)
    edge = np.zeros((4, 2, 128, 2, 128))

    def put(n, side, lane, row):
        for z in range(8):
            for y, value in row.items():
                j = y - 120 if y >= 120 else y + 8
                edge[n, :, 16 * z + j, side, lane + z] += value

    part = {127: 1.0, 126: -0.5}
    for n in range(4):
        put(n, 0, beyond(n)["cell"], {0: 1.0})
        put(n, 0, beyond(n)["after"], detail_row(0))
        put(n, 1, beyond(n)["before"], part)
    put(0, 0, BEYOND_SMOOTH[65], smooth_row(1))
    put(0, 0, BEYOND_SMOOTH[66], smooth_row(2))
    put(0, 1, BEYOND_SMOOTH[-2], smooth_row(62))
    put(0, 1, BEYOND_SMOOTH[-1], combine((1.0, {126: 1.0}), (0.25, detail_row(62)), (0.25, part)))
    w["edge"] = edge.reshape(1024, 256)
    expand = np.zeros((2, 4, 128))
    for j in range(4):
        expand[0, j, 16 * j : 16 * j + 16] = 1
        expand[1, j, 64 + 8 * j : 64 + 8 * j + 8] = 1
    twice = combine(*[(value, smooth_row(k)) for k, value in smooth_row(0).items()])
    columns = np.zeros((2, 128, 128))
    for m in range(-1, 34):
        for t, value in twice.items():
            if 0 <= 4 * m + t < NL:
                columns[:, 4 * m + t, m + 1] = value
    rows = np.zeros((4, 32, 2, 64))
    for z in range(4):
        places = {m: m for m in range(16)}
        places.update({16: 16 + 2 * z, 17: 17 + 2 * z, -1: 16 + 15 - z})
        for m, place in places.items():
            for t, value in twice.items():
                if 0 <= 4 * m + t < NR:
                    rows[z, place, :, 4 * m + t] = value
    pad = np.zeros((8, 128))
    w["first"] = np.concatenate([columns.reshape(256, 128), rows.reshape(128, 128), expand.reshape(8, 128), pad], 0)
    return {name: as_bf16(matrix) for name, matrix in w.items()}


def two_terms(x):
    high = x.astype(BF16)
    low = (x - high.astype(F32)).astype(BF16)
    return high, low


def dot(a, b):
    return jnp.dot(a, b, preferred_element_type=F32)


def lift_planes(cells):
    half = len(cells) // 2
    even, odd = cells[0::2], cells[1::2]
    detail = [odd[k] - 0.5 * (even[k] + even[min(k + 1, half - 1)]) for k in range(half)]
    smooth = [even[k] + 0.25 * (detail[max(k - 1, 0)] + detail[k]) for k in range(half)]
    return smooth, detail


def unlift_planes(smooth, detail):
    half = len(smooth)
    even = [smooth[k] - 0.25 * (detail[max(k - 1, 0)] + detail[k]) for k in range(half)]
    out = []
    for k in range(half):
        out += [even[k], detail[k] + 0.5 * (even[k] + even[min(k + 1, half - 1)])]
    return out


def lift_rows(load, start):
    even, odd, after = load(start), load(start + 1), load(start + 2)
    before, odd_before = load(start - 2), load(start - 1)
    detail = odd - 0.5 * (even + after)
    detail_before = odd_before - 0.5 * (before + even)
    return even + 0.25 * (detail_before + detail), detail


def unlift_rows(smooth, detail, row):
    here, after = detail(row), detail(row + 1)
    even = smooth(row) - 0.25 * (detail(row - 1) + here)
    next_even = smooth(row + 1) - 0.25 * (here + after)
    return even, here + 0.5 * (even + next_even)


PITCH = 80


def first_kernel(field, masks, table, lifted, up, down, own_masks, share, cells, twice, sems):
    copies = [pltpu.make_async_copy(field.at[v], cells.at[v], sems.at[v]) for v in range(NV)]
    for copy in copies:
        copy.start()
    for i, out, tile in ((0, up, 18), (1, down, 12)):
        total = jnp.zeros((7, NL), F32)
        for l in range(2):
            flags = masks[l, i].astype(F32).astype(BF16)
            spread = table[384 + 4 * l : 388 + 4 * l, :]
            total += lax.dot_general(flags, spread, (((0,), (0,)), ((), ())), preferred_element_type=F32)
        own_masks[i] = jnp.concatenate([total, jnp.zeros((1, NL), F32)], 0)
        out[tile] = own_masks[i]
    for p in range(NV * NZ):
        lifted[p * PITCH : p * PITCH + 8, :] = jnp.zeros((8, NL), F32)
        lifted[p * PITCH + 72 : p * PITCH + 80, :] = jnp.zeros((8, NL), F32)

    for v in range(NV):
        copies[v].wait()

        def planes(t, _):
            at = pl.multiple_of(t * 8, 8)
            smooth, detail = lift_planes([cells[v, z, pl.ds(at, 8), :] for z in range(NZ)])
            for k, tile in enumerate(smooth + detail):
                lifted[pl.ds((v * NZ + k) * PITCH + 8 + at, 8), :] = tile
            for k, tile in enumerate(lift_planes(smooth)[0]):
                twice[v * 4 + k, pl.ds(at, 8), :] = tile
            return 0

        lax.fori_loop(0, 8, planes, 0)
        for bz in range(2):

            def row(x):
                return lifted[pl.ds((v * NZ + bz * 8) * PITCH + 8 + x, 8, stride=PITCH), :]

            x = [row(j) for j in range(7 if bz == 0 else 3)]
            first = x[1] - 0.5 * (x[0] + x[2])
            up[v * 6 + bz] = x[0]
            up[v * 6 + 2 + bz] = first
            y = {j: row(j) for j in (range(58, 64) if bz == 0 else (62, 63))}
            part = y[63] - 0.5 * y[62]
            down[v * 4 + bz] = part
            if bz == 0:
                second = x[3] - 0.5 * (x[2] + x[4])
                third = x[5] - 0.5 * (x[4] + x[6])
                up[v * 6 + 4] = x[2] + 0.25 * (first + second)
                up[v * 6 + 5] = x[4] + 0.25 * (second + third)
                before = y[59] - 0.5 * (y[58] + y[60])
                last = y[61] - 0.5 * (y[60] + y[62])
                down[v * 4 + 2] = y[60] + 0.25 * (before + last)
                down[v * 4 + 3] = y[62] + 0.25 * (last + part)

    total = jnp.zeros((80, NL), F32)
    for v in range(NV):
        main, extra = [], jnp.zeros((16, NL), F32)
        for z in range(4):
            terms = jnp.concatenate(two_terms(twice[v * 4 + z]), 0)
            part = dot(table[256 + 32 * z : 288 + 32 * z, :], terms)
            main.append(part[:16])
            extra += part[16:]
        terms = jnp.concatenate(two_terms(jnp.concatenate(main + [extra], 0)), 1)
        part = dot(terms, table[0:256, :])
        total += pltpu.roll(part, 35 * v, 1) if v else part
    share[...] = total


def first_step(field, masks):
    vmem = pl.BlockSpec(memory_space=pltpu.VMEM)
    shapes = [(NV * NZ * PITCH, NL), (19, 8, NL), (13, 8, NL), (2, 8, NL), (80, NL)]
    return pl.pallas_call(
        first_kernel,
        out_shape=[jax.ShapeDtypeStruct(s, F32) for s in shapes],
        in_specs=[pl.BlockSpec(memory_space=pl.ANY), vmem, vmem],
        out_specs=[vmem] * 5,
        scratch_shapes=[
            pltpu.VMEM((NV, NZ, NR, NL), F32),
            pltpu.VMEM((NV * 4, NR, NL), F32),
            pltpu.SemaphoreType.DMA((NV,)),
        ],
        compiler_params=pltpu.CompilerParams(vmem_limit_bytes=VMEM_LIMIT),
    )(field, masks.transpose(0, 2, 3, 1), weights()["first"])


ROWS = 40


def edge_kernel(lifted, north, south, own_masks, table, *rest):
    count = len(rest) - 5
    shares, (parts, to_left, to_right, joined, packed) = rest[:count], rest[count:]

    def lift(step, _):
        v, bz = step // 2, lax.rem(step, 2)
        for z in range(8):
            start = pl.multiple_of((step * 8 + z) * PITCH, 8)
            for t in range(4):
                pair = lift_rows(lambda s: lifted[pl.ds(start + 16 * t + s, 8, stride=2), :], 8)
                for bx in range(2):
                    plane = (2 * bz + bx) * 24 + v * 8 + z
                    parts[pl.ds(pl.multiple_of(plane * ROWS + 8 * t, 8), 8), :] = pair[bx]
        return 0

    lax.fori_loop(0, NV * 2, lift, 0)
    for p in range(4 * NV * 8):
        parts[p * ROWS + 32 : p * ROWS + 40, :] = jnp.zeros((8, NL), F32)
    for v in range(NV):
        for bz in range(2):

            def cell(x):
                return lifted[pl.ds((v * NZ + bz * 8) * PITCH + 8 + x, 8, stride=PITCH), :]

            def at(bx, r):
                return pl.ds(((2 * bz + bx) * 24 + v * 8) * ROWS + r, 8, stride=ROWS)

            before, after, detail = north[v * 4 + bz], south[v * 6 + bz], south[v * 6 + 2 + bz]
            start = cell(0)
            last = cell(63) - 0.5 * (cell(62) + after)
            parts[at(0, 0), :] = parts[at(0, 0), :] + 0.25 * before
            parts[at(0, 31), :] = parts[at(0, 31), :] - 0.125 * after
            parts[at(1, 31), :] = parts[at(1, 31), :] - 0.5 * after
            parts[at(0, 32), :] = after + 0.25 * (last + detail)
            parts[at(1, 32), :] = detail
            parts[at(1, 39), :] = before - 0.5 * start
            if bz == 0:
                parts[at(0, 33), :] = south[v * 6 + 4]
                parts[at(0, 34), :] = south[v * 6 + 5]
                parts[at(0, 38), :] = north[v * 4 + 2]
                parts[at(0, 39), :] = north[v * 4 + 3] - 0.125 * start

    lane = lax.broadcasted_iota(jnp.int32, (8, NL), 1) // 16

    def pack(step, _):
        for t in range(5):
            tile = jnp.zeros((8, NL), F32)
            for z in range(8):
                x = parts[pl.ds(pl.multiple_of((step * 8 + z) * ROWS + 8 * t, 8), 8), :]
                tile = jnp.where(lane == z, pltpu.roll(x, (8 + 16 * z) % NL, 1), tile)
            packed[pl.ds(pl.multiple_of(step * ROWS + 8 * t, 8), 8), :] = tile
        return 0

    lax.fori_loop(0, 4 * NV, pack, 0)
    terms = []
    for n in range(4):
        terms += list(two_terms(packed[n * 120 : (n + 1) * 120, :]))
    sides = dot(jnp.concatenate(terms, 1), table[...])
    to_left[0:120, :] = sides[:, :NL]
    to_right[0:120, :] = sides[:, NL:]
    for out in (to_left, to_right):
        out[120:128, :] = north[12]
        out[128:136, :] = own_masks[0]
        out[136:144, :] = own_masks[1]
        out[144:152, :] = south[18]
    for n, piece in enumerate(shares):
        joined[80 * n : 80 * (n + 1), :] = piece[...]


def edge_step(lifted, north, south, own_masks, shares):
    vmem = pl.BlockSpec(memory_space=pltpu.VMEM)
    shapes = [(4 * NV * 8 * ROWS, NL), (152, NL), (152, NL), (80 * len(shares), NL)]
    return pl.pallas_call(
        edge_kernel,
        out_shape=[jax.ShapeDtypeStruct(s, F32) for s in shapes],
        in_specs=[vmem] * (5 + len(shares)),
        out_specs=[vmem] * 4,
        scratch_shapes=[pltpu.VMEM((480, NL), F32)],
        compiler_params=pltpu.CompilerParams(vmem_limit_bytes=VMEM_LIMIT),
    )(lifted, north, south, own_masks, weights()["edge"], *shares)


def wave_kernel(
    parts, west, east, own_masks, north_mask, south_mask, wide, narrow,
    out,
    gain, gain2, low, second, kept2, low_back, kept,
):
    inverse, smooth_w, back = narrow.at[0:256], narrow.at[256:512], narrow.at[512:768]
    forward2, inverse2 = narrow.at[768:896], narrow.at[896:1024]

    masks = [jnp.concatenate([ref[120 + 8 * i : 128 + 8 * i, :] for i in range(4)], 0) for ref in (east, west)]
    own = jnp.concatenate([north_mask[0], own_masks[0], own_masks[1], south_mask[0]], 0)
    flags = jnp.concatenate([own] + masks, 1).astype(BF16)
    lanes = dot(flags, wide[640:1024, :])
    lane64 = lax.broadcasted_iota(jnp.int32, (1, NL), 1) < 64
    zero, one = jnp.zeros((1, NL), F32), jnp.ones((1, NL), F32)
    forward_f = [wide[160 * n : 160 * (n + 1), :].astype(F32) for n in range(4)]
    forward2_f = forward2[...].astype(F32)
    for ib in range(4):
        for bz in range(2):
            for bx in range(2):
                n = 2 * bz + bx
                b = 8 * ib + 4 * bz + bx - 1
                smooth_one = lanes[b : b + 1, 0:NL] if n else zero
                detail_one = lanes[b + 2 : b + 3, 0:NL]
                row = jnp.concatenate([smooth_one, detail_one], 1)
                both = dot((forward_f[n] * row).astype(BF16), inverse[...]).astype(BF16)
                at = 128 + group_start(n)
                gain[ib, n, 0:128, :] = both[0:128]
                gain[ib, n, 128:256, :] = jnp.zeros((128, NL), BF16)
                gain[ib, n, at : at + 32, :] = both[128:160]
                smooth_two = lanes[b : b + 1, NL:] if n else one
                row = jnp.where(lane64, smooth_two, lanes[b + 2 : b + 3, NL:])
                both = dot((forward2_f * row).astype(BF16), inverse2[...]).astype(BF16)
                gain2[ib, n, 0:128, :] = both
                gain2[ib, n, 128:256, :] = both

    def sides(v, at, count):
        rows = pl.ds(pl.multiple_of(v * ROWS + at, 8), count)
        beside = west[rows, :] + east[rows, :]
        tiles = [pltpu.roll(beside, NL - z, 1) if z else beside for z in range(8)]
        return two_terms(jnp.concatenate(tiles, 0))

    def operand(n, v, at, count, beside):
        main = two_terms(parts[n, pl.ds(v * 8, 8), pl.ds(at, count), :].reshape(8 * count, NL))
        return [jnp.concatenate(pair, 1) for pair in zip(main, beside)]

    def smooth_part(v, _):
        planes = pl.ds(v * 8, 8)
        for at, count in ((0, 16), (16, 16), (32, 8)):
            high, low_term = operand(0, v, at, count, sides(v, at, count))
            part = (dot(high, smooth_w[...]) + dot(low_term, smooth_w[...])).reshape(8, count, NL)
            if at < 32:
                low[planes, 8 + at : 8 + at + count, :] = part
                if at == 0:
                    low[planes, 56:64, :] = part[:, 0:8]
            else:
                low[planes, 0:8, :] = part
                low[planes, 40:48, :] = part
                low[planes, 48:56, :] = part
        return 0

    lax.fori_loop(0, NV, smooth_part, 0)

    def rows_two(v, _):
        for t in range(3):
            lifted = [
                lift_rows(lambda s: low[v * 8 + p, pl.ds(16 * t + s, 8, stride=2), :], 8) for p in range(8)
            ]
            for bx in range(2):
                smooth, detail = lift_planes([pair[bx] for pair in lifted])
                for bz, part in ((0, smooth), (1, detail)):
                    for z in range(4):
                        second[2 * bz + bx, t, pl.ds(pl.multiple_of((v * 4 + z) * 8, 8), 8), :] = part[z]
        return 0

    lax.fori_loop(0, NV, rows_two, 0)
    ext_two = lax.broadcasted_iota(jnp.int32, (NV * 4, 8, NL), 1) < 4
    for n in range(4):
        for t in range(3):
            terms = jnp.concatenate(two_terms(second[n, t]), 1)
            if t < 2:
                kept2[n, :, 8 + 8 * t : 16 + 8 * t, :] = dot(terms, gain2[t + 1, n]).reshape(NV * 4, 8, NL)
            else:
                below = dot(terms, gain2[3, n]).reshape(NV * 4, 8, NL)
                above = dot(terms, gain2[0, n]).reshape(NV * 4, 8, NL)
                part = jnp.where(ext_two, below, above)
                kept2[n, :, 0:8, :] = part
                kept2[n, :, 24:32, :] = part

    def back_two(v, _):
        for t in range(3):
            pairs = {}
            for bz in range(2):
                for z in range(4):
                    p = v * 4 + z
                    if t < 2:
                        pairs[bz, z] = unlift_rows(
                            lambda r: kept2[2 * bz, p, pl.ds(r, 8), :],
                            lambda r: kept2[2 * bz + 1, p, pl.ds(r, 8), :],
                            8 + 8 * t,
                        )
                    else:
                        even = kept2[2 * bz, p, 24:32, :] - 0.25 * (
                            kept2[2 * bz + 1, p, 23:31, :] + kept2[2 * bz + 1, p, 24:32, :]
                        )
                        pairs[bz, z] = (even, even)
            for parity in range(2 if t < 2 else 1):
                planes = unlift_planes([pairs[0, z][parity] for z in range(4)], [pairs[1, z][parity] for z in range(4)])
                for z in range(8):
                    low_back[v * 8 + z, pl.ds(16 * t + parity, 8, stride=2), :] = planes[z]
        return 0

    lax.fori_loop(0, NV, back_two, 0)

    ext_one = lax.broadcasted_iota(jnp.int32, (8, 8, NL), 1) < 4

    def keep(v, _):
        planes = pl.ds(v * 8, 8)
        for ib in range(3):
            at, count = 16 * ib, 16 if ib < 2 else 8
            beside = sides(v, at, count)
            for n in range(4):
                high, low_term = operand(n, v, at, count, beside)
                if n == 0:
                    terms = jnp.concatenate(two_terms(low_back[planes, at : at + count, :].reshape(8 * count, NL)), 1)
                    base = dot(terms, back[...])
                if ib < 2:
                    part = dot(high, gain[ib + 1, n]) + dot(low_term, gain[ib + 1, n])
                    if n == 0:
                        part = part + base
                    kept[n, planes, 8 + at : 24 + at, :] = part.reshape(8, count, NL)
                else:
                    below = dot(high, gain[3, n]) + dot(low_term, gain[3, n])
                    above = dot(high, gain[0, n]) + dot(low_term, gain[0, n])
                    if n == 0:
                        below = below + base
                    part = jnp.where(ext_one, below.reshape(8, 8, NL), above.reshape(8, 8, NL))
                    kept[n, planes, 0:8, :] = part
                    kept[n, planes, 40:48, :] = part
        return 0

    lax.fori_loop(0, NV, keep, 0)

    def back_one(step, _):
        v, t = step // 4, step % 4
        pairs = {}
        for bz in range(2):
            for z in range(8):
                p = v * 8 + z
                pairs[bz, z] = unlift_rows(
                    lambda r: kept[2 * bz, p, pl.ds(8 * t + r, 8), :],
                    lambda r: kept[2 * bz + 1, p, pl.ds(8 * t + r, 8), :],
                    8,
                )
        for parity in range(2):
            planes = unlift_planes([pairs[0, z][parity] for z in range(8)], [pairs[1, z][parity] for z in range(8)])
            for z in range(NZ):
                out[v, z, pl.ds(16 * t + parity, 8, stride=2), :] = planes[z]
        return 0

    lax.fori_loop(0, NV * 4, back_one, 0)


def wave(parts, west, east, own_masks, north, south):
    w = weights()
    vmem = pl.BlockSpec(memory_space=pltpu.VMEM)
    whole = lambda *shape: pl.BlockSpec(shape, lambda i: (0,) * len(shape))
    out = (NV, NZ, NR, NL)
    return pl.pallas_call(
        wave_kernel,
        grid=(1,),
        out_shape=jax.ShapeDtypeStruct(out, F32),
        in_specs=[
            vmem, vmem, vmem, vmem,
            pl.BlockSpec((1, 8, NL), lambda i: (12, 0, 0)), pl.BlockSpec((1, 8, NL), lambda i: (18, 0, 0)),
            vmem, vmem,
        ],
        out_specs=whole(*out),
        scratch_shapes=[
            pltpu.VMEM((4, 4, 256, NL), BF16),
            pltpu.VMEM((4, 4, 256, NL), BF16),
            pltpu.VMEM((NV * 8, 64, NL), F32),
            pltpu.VMEM((4, 3, NV * 32, NL), F32),
            pltpu.VMEM((4, NV * 4, 40, NL), F32),
            pltpu.VMEM((NV * 8, 48, NL), F32),
            pltpu.VMEM((4, NV * 8, 48, NL), F32),
        ],
        compiler_params=pltpu.CompilerParams(vmem_limit_bytes=VMEM_LIMIT),
    )(parts.reshape(4, NV * 8, ROWS, NL), west, east, own_masks, north, south, w["wide"], w["narrow"])


def rows_kernel(count_x, count_z, *refs):
    shares, out = refs[:count_x], refs[count_x]
    me = lax.axis_index("gx")
    row = lax.broadcasted_iota(jnp.int32, (8, NL), 0)
    for r in range(count_x):
        at = pl.multiple_of(16 * (me ^ r), 16)
        for j in range(count_z):
            for z in range(4):
                out[j, z, pl.ds(at, 16), :] = shares[r][80 * j + 16 * z : 80 * j + 16 * z + 16, :]
    for r in range(count_x):
        i = me ^ r
        below = pl.multiple_of(16 * lax.rem(i + 1, count_x), 16)
        above = pl.multiple_of(16 * lax.rem(i + count_x - 1, count_x) + 8, 8)
        for j in range(count_z):
            low = shares[r][80 * j + 64 : 80 * j + 72, :]
            high = shares[r][80 * j + 72 : 80 * j + 80, :]
            for z in range(4):
                first = pltpu.roll(low, 8 - 2 * z, 0) if z else low
                last = pltpu.roll(high, z, 0) if z else high
                out[j, z, pl.ds(below, 8), :] += jnp.where(row < 2, first, 0.0)
                out[j, z, pl.ds(above, 8), :] += jnp.where(row == 7, last, 0.0)


def rows_step(pieces, count_z):
    vmem = pl.BlockSpec(memory_space=pltpu.VMEM)
    count_x = len(pieces)
    return pl.pallas_call(
        functools.partial(rows_kernel, count_x, count_z),
        out_shape=jax.ShapeDtypeStruct((count_z, 4, 16 * count_x, NL), F32),
        in_specs=[vmem] * count_x,
        out_specs=vmem,
        compiler_params=pltpu.CompilerParams(vmem_limit_bytes=VMEM_LIMIT),
    )(*pieces)


def coarse_kernel(count_x, count_y, own, other, out):
    me = lax.axis_index("gy")
    me_z, is_even = lax.shift_right_logical(me, 1), lax.rem(me, 2) == 0
    lane = lax.broadcasted_iota(jnp.int32, (8, NL), 1)

    def block(i, _):
        rows = pl.ds(pl.multiple_of(8 * i, 8), 8)
        for z in range(4):
            pieces = []
            for j in range(count_y // 2):
                mine, theirs = own[j ^ me_z, z, rows, :], other[j ^ me_z, z, rows, :]
                pieces += [jnp.where(is_even, mine, theirs), jnp.where(is_even, theirs, mine)]
            for v in range(NV):
                for t in range(count_y // 4):
                    total = jnp.zeros((8, NL), F32)
                    for q in range(-1, 5):
                        start = 32 * q - 1
                        shift = (start - 35 * v) % NL
                        piece = pieces[(4 * t + q) % count_y]
                        turned = pltpu.roll(piece, shift, 1) if shift else piece
                        total += jnp.where((lane >= start) & (lane < start + 35), turned, 0.0)
                    out[v, z, rows, NL * t : NL * (t + 1)] = total
        return 0

    lax.fori_loop(0, 2 * count_x, block, 0)


def coarse_step(own, other, count_x, count_y):
    vmem = pl.BlockSpec(memory_space=pltpu.VMEM)
    return pl.pallas_call(
        functools.partial(coarse_kernel, count_x, count_y),
        out_shape=jax.ShapeDtypeStruct((NV, 4, 16 * count_x, 32 * count_y), F32),
        in_specs=[vmem, vmem],
        out_specs=vmem,
        compiler_params=pltpu.CompilerParams(vmem_limit_bytes=VMEM_LIMIT),
    )(own, other)


def shifted(x, axis, step):
    count = lax.axis_size(axis)
    return lax.ppermute(x, axis, [(i, (i + step) % count) for i in range(count)])


def swapped(x, axis, distance):
    return lax.ppermute(x, axis, [(i, i ^ distance) for i in range(lax.axis_size(axis))])


def body(field, masks):
    count_x, count_y = lax.axis_size("gx"), lax.axis_size("gy")
    lifted, up, down, own_masks, share = first_step(field, masks)
    south = shifted(up, "gx", -1)
    north = shifted(down, "gx", 1)
    shares = [share] + [swapped(share, "gy", r) for r in range(2, count_y, 2)]
    parts, to_left, to_right, joined = edge_step(lifted, north, south, own_masks, shares)
    west = shifted(to_right, "gy", 1)
    east = shifted(to_left, "gy", -1)
    pieces = [joined] + [swapped(joined, "gx", r) for r in range(1, count_x)]
    restored = wave(parts, west, east, own_masks, north, south)
    own = rows_step(pieces, count_y // 2)
    other = swapped(own, "gy", 1)
    return restored, coarse_step(own, other, count_x, count_y)


def solution(mesh):
    placed = P(None, None, "gx", "gy")
    return jax.shard_map(
        body,
        mesh=mesh,
        in_specs=(placed, placed),
        out_specs=(placed, P()),
        check_vma=False,
    )
```

```python
import functools

import jax
import jax.numpy as jnp
import ml_dtypes
import numpy as np
from jax import lax
from jax.experimental import pallas as pl
from jax.experimental.pallas import tpu as pltpu
from jax.sharding import PartitionSpec as P

F32 = jnp.float32
BF16 = jnp.bfloat16
VMEM_LIMIT = 32 * 1024 * 1024

NV, NZ, NR, NL = 3, 16, 64, 128


def detail_row(k):
    return {2 * k + 1: 1.0, 2 * k: -0.5, 2 * k + 2: -0.5}


def smooth_row(k):
    row = {2 * k: 1.0}
    for j in (k - 1, k):
        for cell, value in detail_row(j).items():
            row[cell] = row.get(cell, 0.0) + 0.25 * value
    return row


def even_row(k):
    return {("s", k): 1.0, ("d", k - 1): -0.25, ("d", k): -0.25}


def odd_row(k):
    row = {("d", k): 1.0}
    for j in (k, k + 1):
        for name, value in even_row(j).items():
            row[name] = row.get(name, 0.0) + 0.5 * value
    return row


def as_bf16(matrix):
    cast = matrix.astype(ml_dtypes.bfloat16)
    assert (cast.astype(np.float64) == matrix).all()
    return cast


def combine(*terms):
    total = {}
    for factor, row in terms:
        for cell, value in row.items():
            total[cell] = total.get(cell, 0.0) + factor * value
    return total


def level_one_columns():
    names = {("s", k): k for k in range(65)}
    names.update({("d", k): 128 + k for k in range(65)})
    names[("d", -1)] = 128 + 65
    return names


def level_two_columns():
    names = {("s", k): k for k in range(33)}
    names.update({("d", k): 64 + k for k in range(33)})
    names[("d", -1)] = 64 + 33
    return names


def smooth_place(k):
    return k + 2


def beyond(n):
    return {"cell": 24 * n, "after": 24 * n + 8, "before": 24 * n + 16}


BEYOND_SMOOTH = {65: 96, 66: 104, -2: 112, -1: 120}


def own_row(kind, k, n):
    place = {name: 128 + lane for name, lane in beyond(n).items()}
    if kind == "d":
        if k == -1:
            return {place["before"]: 1.0, 0: -0.5}
        if k == 64:
            return {place["after"]: 1.0}
        return {(place["cell"] if y == 128 else y): value for y, value in detail_row(k).items()}
    if k in BEYOND_SMOOTH:
        row = {128 + BEYOND_SMOOTH[k]: 1.0}
        return combine((1.0, row), (1.0, {0: -0.125})) if k == -1 else row
    even = place["cell"] if k == 64 else 2 * k
    return combine((1.0, {even: 1.0}), (0.25, own_row("d", k - 1, n)), (0.25, own_row("d", k, n)))


def group_start(n):
    return 16 * (24 * n // 16)


@functools.lru_cache(maxsize=None)
def weights():
    w = {}
    names = level_one_columns()
    forward = np.zeros((4, 256, 256))
    inverse = np.zeros((256, 128))
    for (kind, k), column in names.items():
        for n in range(4):
            for place, value in own_row(kind, k, n).items():
                forward[n, place, column] += value
    for k in range(64):
        for y, row in ((2 * k, even_row(k)), (2 * k + 1, odd_row(k))):
            for name, value in row.items():
                inverse[names[name], y] += value
    short = np.zeros((4, 160, 256))
    for n in range(4):
        at = 128 + group_start(n)
        short[n, :128], short[n, 128:] = forward[n, :128], forward[n, at : at + 32]
        assert abs(short[n]).sum() == abs(forward[n]).sum()
    smooth = np.zeros((256, 128))
    for k in range(-2, 67):
        for place, value in own_row("s", k, 0).items():
            smooth[place, smooth_place(k)] += value
    names2 = level_two_columns()
    forward2 = np.zeros((128, 128))
    inverse2 = np.zeros((128, 128))
    for (kind, k), column in names2.items():
        for cell, value in (smooth_row(k) if kind == "s" else detail_row(k)).items():
            forward2[smooth_place(cell), column] += value
    for k in range(33):
        rows = [(2 * k, even_row(k))] + ([(2 * k + 1, odd_row(k))] if k < 32 else [])
        for y, row in rows:
            for name, value in row.items():
                inverse2[names2[name], y] += value
    back = np.zeros((256, 128))
    back[:65] = inverse[:65]
    back[128 : 128 + 65] = inverse[:65]
    spread = np.zeros((3, 128, 2, 128))
    for k in range(64):
        spread[0, k, 0, k] = 1
    spread[1, 0, 0, 64] = 1
    spread[2, 63, 0, 65] = 1
    for k in range(32):
        spread[0, 64 + k, 1, k] = 1
        spread[0, 64 + k, 1, 64 + k] = 1
    for base in (0, 64):
        spread[1, 64, 1, base + 32] = 1
        spread[2, 95, 1, base + 33] = 1
    w["wide"] = np.concatenate([short.reshape(640, 256), spread.reshape(384, 256)], 0)
    w["narrow"] = np.concatenate([inverse, smooth, back, forward2, inverse2], 0)
    edge = np.zeros((4, 2, 128, 2, 128))

    def put(n, side, lane, row):
        for z in range(8):
            for y, value in row.items():
                j = y - 120 if y >= 120 else y + 8
                edge[n, :, 16 * z + j, side, lane + z] += value

    part = {127: 1.0, 126: -0.5}
    for n in range(4):
        put(n, 0, beyond(n)["cell"], {0: 1.0})
        put(n, 0, beyond(n)["after"], detail_row(0))
        put(n, 1, beyond(n)["before"], part)
    put(0, 0, BEYOND_SMOOTH[65], smooth_row(1))
    put(0, 0, BEYOND_SMOOTH[66], smooth_row(2))
    put(0, 1, BEYOND_SMOOTH[-2], smooth_row(62))
    put(0, 1, BEYOND_SMOOTH[-1], combine((1.0, {126: 1.0}), (0.25, detail_row(62)), (0.25, part)))
    w["edge"] = edge.reshape(1024, 256)
    expand = np.zeros((2, 4, 128))
    for j in range(4):
        expand[0, j, 16 * j : 16 * j + 16] = 1
        expand[1, j, 64 + 8 * j : 64 + 8 * j + 8] = 1
    twice = combine(*[(value, smooth_row(k)) for k, value in smooth_row(0).items()])
    columns = np.zeros((2, 128, 128))
    for m in range(-1, 34):
        for t, value in twice.items():
            if 0 <= 4 * m + t < NL:
                columns[:, 4 * m + t, m + 1] = value
    rows = np.zeros((4, 32, 2, 64))
    for z in range(4):
        places = {m: m for m in range(16)}
        places.update({16: 16 + 2 * z, 17: 17 + 2 * z, -1: 16 + 15 - z})
        for m, place in places.items():
            for t, value in twice.items():
                if 0 <= 4 * m + t < NR:
                    rows[z, place, :, 4 * m + t] = value
    pad = np.zeros((8, 128))
    w["first"] = np.concatenate([columns.reshape(256, 128), rows.reshape(128, 128), expand.reshape(8, 128), pad], 0)
    return {name: as_bf16(matrix) for name, matrix in w.items()}


def two_terms(x):
    high = x.astype(BF16)
    low = (x - high.astype(F32)).astype(BF16)
    return high, low


def dot(a, b):
    return jnp.dot(a, b, preferred_element_type=F32)


def lift_planes(cells):
    half = len(cells) // 2
    even, odd = cells[0::2], cells[1::2]
    detail = [odd[k] - 0.5 * (even[k] + even[min(k + 1, half - 1)]) for k in range(half)]
    smooth = [even[k] + 0.25 * (detail[max(k - 1, 0)] + detail[k]) for k in range(half)]
    return smooth, detail


def unlift_planes(smooth, detail):
    half = len(smooth)
    even = [smooth[k] - 0.25 * (detail[max(k - 1, 0)] + detail[k]) for k in range(half)]
    out = []
    for k in range(half):
        out += [even[k], detail[k] + 0.5 * (even[k] + even[min(k + 1, half - 1)])]
    return out


def lift_rows(load, start):
    even, odd, after = load(start), load(start + 1), load(start + 2)
    before, odd_before = load(start - 2), load(start - 1)
    detail = odd - 0.5 * (even + after)
    detail_before = odd_before - 0.5 * (before + even)
    return even + 0.25 * (detail_before + detail), detail


def unlift_rows(smooth, detail, row):
    here, after = detail(row), detail(row + 1)
    even = smooth(row) - 0.25 * (detail(row - 1) + here)
    next_even = smooth(row + 1) - 0.25 * (here + after)
    return even, here + 0.5 * (even + next_even)


PITCH = 80


def first_kernel(
    field, masks_hbm, table_hbm, lifted, up, down, own_masks, share, cells, twice, masks, table, sems
):
    copies = []
    for v in range(NV):
        for h in range(2):
            part = pl.ds(8 * h, 8)
            copies.append(pltpu.make_async_copy(field.at[v, part], cells.at[v, part], sems.at[2 * v + h]))
    copies.append(pltpu.make_async_copy(masks_hbm, masks, sems.at[2 * NV]))
    copies.append(pltpu.make_async_copy(table_hbm, table, sems.at[2 * NV + 1]))
    for copy in copies:
        copy.start()
    for p in range(NV * NZ):
        lifted[p * PITCH : p * PITCH + 8, :] = jnp.zeros((8, NL), F32)
        lifted[p * PITCH + 72 : p * PITCH + 80, :] = jnp.zeros((8, NL), F32)

    for v in range(NV):
        for copy in copies[2 * v : 2 * v + 2]:
            copy.wait()

        def planes(t, _):
            at = pl.multiple_of(t * 8, 8)
            smooth, detail = lift_planes([cells[v, z, pl.ds(at, 8), :] for z in range(NZ)])
            for k, tile in enumerate(smooth + detail):
                lifted[pl.ds((v * NZ + k) * PITCH + 8 + at, 8), :] = tile
            for k, tile in enumerate(lift_planes(smooth)[0]):
                twice[v * 4 + k, pl.ds(at, 8), :] = tile
            return 0

        lax.fori_loop(0, 8, planes, 0)
        for bz in range(2):

            def row(x):
                return lifted[pl.ds((v * NZ + bz * 8) * PITCH + 8 + x, 8, stride=PITCH), :]

            x = [row(j) for j in range(7 if bz == 0 else 3)]
            first = x[1] - 0.5 * (x[0] + x[2])
            up[v * 6 + bz] = x[0]
            up[v * 6 + 2 + bz] = first
            y = {j: row(j) for j in (range(58, 64) if bz == 0 else (62, 63))}
            part = y[63] - 0.5 * y[62]
            down[v * 4 + bz] = part
            if bz == 0:
                second = x[3] - 0.5 * (x[2] + x[4])
                third = x[5] - 0.5 * (x[4] + x[6])
                up[v * 6 + 4] = x[2] + 0.25 * (first + second)
                up[v * 6 + 5] = x[4] + 0.25 * (second + third)
                before = y[59] - 0.5 * (y[58] + y[60])
                last = y[61] - 0.5 * (y[60] + y[62])
                down[v * 4 + 2] = y[60] + 0.25 * (before + last)
                down[v * 4 + 3] = y[62] + 0.25 * (last + part)

    for copy in copies[2 * NV :]:
        copy.wait()
    for i, out, tile in ((0, up, 18), (1, down, 12)):
        total = jnp.zeros((7, NL), F32)
        for l in range(2):
            flags = masks[l, i].astype(F32).astype(BF16)
            spread = table[384 + 4 * l : 388 + 4 * l, :]
            total += lax.dot_general(flags, spread, (((0,), (0,)), ((), ())), preferred_element_type=F32)
        own_masks[i] = jnp.concatenate([total, jnp.zeros((1, NL), F32)], 0)
        out[tile] = own_masks[i]
    total = jnp.zeros((80, NL), F32)
    for v in range(NV):
        main, extra = [], jnp.zeros((16, NL), F32)
        for z in range(4):
            terms = jnp.concatenate(two_terms(twice[v * 4 + z]), 0)
            part = dot(table[256 + 32 * z : 288 + 32 * z, :], terms)
            main.append(part[:16])
            extra += part[16:]
        terms = jnp.concatenate(two_terms(jnp.concatenate(main + [extra], 0)), 1)
        part = dot(terms, table[0:256, :])
        total += pltpu.roll(part, 35 * v, 1) if v else part
    share[...] = total


def in_hbm(x):
    return pltpu.with_memory_space_constraint(x, pltpu.HBM)


def first_step(field, masks):
    vmem = pl.BlockSpec(memory_space=pltpu.VMEM)
    shapes = [(NV * NZ * PITCH, NL), (19, 8, NL), (13, 8, NL), (2, 8, NL), (80, NL)]
    return pl.pallas_call(
        first_kernel,
        out_shape=[jax.ShapeDtypeStruct(s, F32) for s in shapes],
        in_specs=[pl.BlockSpec(memory_space=pltpu.HBM)] * 3,
        out_specs=[vmem] * 5,
        scratch_shapes=[
            pltpu.VMEM((NV, NZ, NR, NL), F32),
            pltpu.VMEM((NV * 4, NR, NL), F32),
            pltpu.VMEM((2, 2, 4, 7), jnp.int32),
            pltpu.VMEM((400, NL), BF16),
            pltpu.SemaphoreType.DMA((2 * NV + 2,)),
        ],
        compiler_params=pltpu.CompilerParams(vmem_limit_bytes=VMEM_LIMIT),
    )(*[in_hbm(x) for x in (field, masks.transpose(0, 2, 3, 1), jnp.asarray(weights()["first"]))])


ROWS = 40


def edge_kernel(lifted, north, south, own_masks, table, parts, to_left, to_right, packed):
    def lift(step, _):
        v, bz = step // 2, lax.rem(step, 2)
        for z in range(8):
            start = pl.multiple_of((step * 8 + z) * PITCH, 8)
            for t in range(4):
                pair = lift_rows(lambda s: lifted[pl.ds(start + 16 * t + s, 8, stride=2), :], 8)
                for bx in range(2):
                    plane = (2 * bz + bx) * 24 + v * 8 + z
                    parts[pl.ds(pl.multiple_of(plane * ROWS + 8 * t, 8), 8), :] = pair[bx]
        return 0

    lax.fori_loop(0, NV * 2, lift, 0)
    for p in range(4 * NV * 8):
        parts[p * ROWS + 32 : p * ROWS + 40, :] = jnp.zeros((8, NL), F32)
    for v in range(NV):
        for bz in range(2):

            def cell(x):
                return lifted[pl.ds((v * NZ + bz * 8) * PITCH + 8 + x, 8, stride=PITCH), :]

            def at(bx, r):
                return pl.ds(((2 * bz + bx) * 24 + v * 8) * ROWS + r, 8, stride=ROWS)

            before, after, detail = north[v * 4 + bz], south[v * 6 + bz], south[v * 6 + 2 + bz]
            start = cell(0)
            last = cell(63) - 0.5 * (cell(62) + after)
            parts[at(0, 0), :] = parts[at(0, 0), :] + 0.25 * before
            parts[at(0, 31), :] = parts[at(0, 31), :] - 0.125 * after
            parts[at(1, 31), :] = parts[at(1, 31), :] - 0.5 * after
            parts[at(0, 32), :] = after + 0.25 * (last + detail)
            parts[at(1, 32), :] = detail
            parts[at(1, 39), :] = before - 0.5 * start
            if bz == 0:
                parts[at(0, 33), :] = south[v * 6 + 4]
                parts[at(0, 34), :] = south[v * 6 + 5]
                parts[at(0, 38), :] = north[v * 4 + 2]
                parts[at(0, 39), :] = north[v * 4 + 3] - 0.125 * start

    lane = lax.broadcasted_iota(jnp.int32, (8, NL), 1) // 16

    def pack(step, _):
        for t in range(5):
            tile = jnp.zeros((8, NL), F32)
            for z in range(8):
                x = parts[pl.ds(pl.multiple_of((step * 8 + z) * ROWS + 8 * t, 8), 8), :]
                tile = jnp.where(lane == z, pltpu.roll(x, (8 + 16 * z) % NL, 1), tile)
            packed[pl.ds(pl.multiple_of(step * ROWS + 8 * t, 8), 8), :] = tile
        return 0

    lax.fori_loop(0, 4 * NV, pack, 0)
    terms = []
    for n in range(4):
        terms += list(two_terms(packed[n * 120 : (n + 1) * 120, :]))
    sides = dot(jnp.concatenate(terms, 1), table[...])
    to_left[0:120, :] = sides[:, :NL]
    to_right[0:120, :] = sides[:, NL:]
    for out in (to_left, to_right):
        out[120:128, :] = north[12]
        out[128:136, :] = own_masks[0]
        out[136:144, :] = own_masks[1]
        out[144:152, :] = south[18]


def edge_step(lifted, north, south, own_masks):
    vmem = pl.BlockSpec(memory_space=pltpu.VMEM)
    shapes = [(4 * NV * 8 * ROWS, NL), (152, NL), (152, NL)]
    return pl.pallas_call(
        edge_kernel,
        out_shape=[jax.ShapeDtypeStruct(s, F32) for s in shapes],
        in_specs=[vmem] * 5,
        out_specs=[vmem] * 3,
        scratch_shapes=[pltpu.VMEM((480, NL), F32)],
        compiler_params=pltpu.CompilerParams(vmem_limit_bytes=VMEM_LIMIT),
    )(lifted, north, south, own_masks, weights()["edge"])


def join_kernel(*refs):
    shares, out = refs[:-2], refs[-1]
    for n, piece in enumerate(shares):
        out[80 * n : 80 * (n + 1), :] = piece[...]


def join_step(shares, after):
    vmem = pl.BlockSpec(memory_space=pltpu.VMEM)
    return pl.pallas_call(
        join_kernel,
        out_shape=jax.ShapeDtypeStruct((80 * len(shares), NL), F32),
        in_specs=[vmem] * len(shares) + [pl.BlockSpec(memory_space=pl.ANY)],
        out_specs=vmem,
        compiler_params=pltpu.CompilerParams(vmem_limit_bytes=VMEM_LIMIT),
    )(*shares, after)


def mask_lanes(west, east, own_masks, north_mask, south_mask, wide):
    masks = [jnp.concatenate([ref[120 + 8 * i : 128 + 8 * i, :] for i in range(4)], 0) for ref in (east, west)]
    own = jnp.concatenate([north_mask[0], own_masks[0], own_masks[1], south_mask[0]], 0)
    flags = jnp.concatenate([own] + masks, 1).astype(BF16)
    return dot(flags, wide[640:1024, :])


def sides(west, east, v, at, count):
    rows = pl.ds(pl.multiple_of(v * ROWS + at, 8), count)
    beside = west[rows, :] + east[rows, :]
    tiles = [pltpu.roll(beside, NL - z, 1) if z else beside for z in range(8)]
    return two_terms(jnp.concatenate(tiles, 0))


def operand(parts, n, v, at, count, beside):
    main = two_terms(parts[n, pl.ds(v * 8, 8), pl.ds(at, count), :].reshape(8 * count, NL))
    return [jnp.concatenate(pair, 1) for pair in zip(main, beside)]


def low_kernel(
    parts, west, east, own_masks, north_mask, south_mask, wide, narrow, low_back, gain2, low, second, kept2
):
    smooth_w, forward2, inverse2 = narrow.at[256:512], narrow.at[768:896], narrow.at[896:1024]
    lanes = mask_lanes(west, east, own_masks, north_mask, south_mask, wide)
    lane64 = lax.broadcasted_iota(jnp.int32, (1, NL), 1) < 64
    forward2_f = forward2[...].astype(F32)
    for ib in range(4):
        for n in range(4):
            b = 8 * ib + 4 * (n // 2) + n % 2 - 1
            smooth_two = lanes[b : b + 1, NL:] if n else jnp.ones((1, NL), F32)
            row = jnp.where(lane64, smooth_two, lanes[b + 2 : b + 3, NL:])
            both = dot((forward2_f * row).astype(BF16), inverse2[...]).astype(BF16)
            gain2[ib, n, 0:128, :] = both
            gain2[ib, n, 128:256, :] = both

    def smooth_part(v, _):
        planes = pl.ds(v * 8, 8)
        for at, count in ((0, 16), (16, 16), (32, 8)):
            high, low_term = operand(parts, 0, v, at, count, sides(west, east, v, at, count))
            part = (dot(high, smooth_w[...]) + dot(low_term, smooth_w[...])).reshape(8, count, NL)
            if at < 32:
                low[planes, 8 + at : 8 + at + count, :] = part
                if at == 0:
                    low[planes, 56:64, :] = part[:, 0:8]
            else:
                low[planes, 0:8, :] = part
                low[planes, 40:48, :] = part
                low[planes, 48:56, :] = part
        return 0

    lax.fori_loop(0, NV, smooth_part, 0)

    def rows_two(v, _):
        for t in range(3):
            lifted = [
                lift_rows(lambda s: low[v * 8 + p, pl.ds(16 * t + s, 8, stride=2), :], 8) for p in range(8)
            ]
            for bx in range(2):
                smooth, detail = lift_planes([pair[bx] for pair in lifted])
                for bz, part in ((0, smooth), (1, detail)):
                    for z in range(4):
                        second[2 * bz + bx, t, pl.ds(pl.multiple_of((v * 4 + z) * 8, 8), 8), :] = part[z]
        return 0

    lax.fori_loop(0, NV, rows_two, 0)
    ext_two = lax.broadcasted_iota(jnp.int32, (NV * 4, 8, NL), 1) < 4
    for n in range(4):
        for t in range(3):
            terms = jnp.concatenate(two_terms(second[n, t]), 1)
            if t < 2:
                kept2[n, :, 8 + 8 * t : 16 + 8 * t, :] = dot(terms, gain2[t + 1, n]).reshape(NV * 4, 8, NL)
            else:
                below = dot(terms, gain2[3, n]).reshape(NV * 4, 8, NL)
                above = dot(terms, gain2[0, n]).reshape(NV * 4, 8, NL)
                part = jnp.where(ext_two, below, above)
                kept2[n, :, 0:8, :] = part
                kept2[n, :, 24:32, :] = part

    def back_two(v, _):
        for t in range(3):
            pairs = {}
            for bz in range(2):
                for z in range(4):
                    p = v * 4 + z
                    if t < 2:
                        pairs[bz, z] = unlift_rows(
                            lambda r: kept2[2 * bz, p, pl.ds(r, 8), :],
                            lambda r: kept2[2 * bz + 1, p, pl.ds(r, 8), :],
                            8 + 8 * t,
                        )
                    else:
                        even = kept2[2 * bz, p, 24:32, :] - 0.25 * (
                            kept2[2 * bz + 1, p, 23:31, :] + kept2[2 * bz + 1, p, 24:32, :]
                        )
                        pairs[bz, z] = (even, even)
            for parity in range(2 if t < 2 else 1):
                planes = unlift_planes([pairs[0, z][parity] for z in range(4)], [pairs[1, z][parity] for z in range(4)])
                for z in range(8):
                    low_back[v * 8 + z, pl.ds(16 * t + parity, 8, stride=2), :] = planes[z]
        return 0

    lax.fori_loop(0, NV, back_two, 0)


def high_kernel(
    parts, west, east, own_masks, north_mask, south_mask, wide, narrow, low_back, out, gain, kept, cells, sems
):
    inverse, back = narrow.at[0:256], narrow.at[512:768]
    lanes = mask_lanes(west, east, own_masks, north_mask, south_mask, wide)
    forward_f = [wide[160 * n : 160 * (n + 1), :].astype(F32) for n in range(4)]
    for ib in range(4):
        for n in range(4):
            b = 8 * ib + 4 * (n // 2) + n % 2 - 1
            smooth_one = lanes[b : b + 1, 0:NL] if n else jnp.zeros((1, NL), F32)
            row = jnp.concatenate([smooth_one, lanes[b + 2 : b + 3, 0:NL]], 1)
            both = dot((forward_f[n] * row).astype(BF16), inverse[...]).astype(BF16)
            at = 128 + group_start(n)
            gain[ib, n, 0:128, :] = both[0:128]
            gain[ib, n, 128:256, :] = jnp.zeros((128, NL), BF16)
            gain[ib, n, at : at + 32, :] = both[128:160]

    ext_one = lax.broadcasted_iota(jnp.int32, (8, 8, NL), 1) < 4

    def keep(v, _):
        planes = pl.ds(v * 8, 8)
        for ib in range(3):
            at, count = 16 * ib, 16 if ib < 2 else 8
            beside = sides(west, east, v, at, count)
            for n in range(4):
                high, low_term = operand(parts, n, v, at, count, beside)
                if n == 0:
                    terms = jnp.concatenate(two_terms(low_back[planes, at : at + count, :].reshape(8 * count, NL)), 1)
                    base = dot(terms, back[...])
                if ib < 2:
                    part = dot(high, gain[ib + 1, n]) + dot(low_term, gain[ib + 1, n])
                    if n == 0:
                        part = part + base
                    kept[n, planes, 8 + at : 24 + at, :] = part.reshape(8, count, NL)
                else:
                    below = dot(high, gain[3, n]) + dot(low_term, gain[3, n])
                    above = dot(high, gain[0, n]) + dot(low_term, gain[0, n])
                    if n == 0:
                        below = below + base
                    part = jnp.where(ext_one, below.reshape(8, 8, NL), above.reshape(8, 8, NL))
                    kept[n, planes, 0:8, :] = part
                    kept[n, planes, 40:48, :] = part
        return 0

    def back_one(step, _):
        v, t = step // 4, step % 4
        pairs = {}
        for bz in range(2):
            for z in range(8):
                p = v * 8 + z
                pairs[bz, z] = unlift_rows(
                    lambda r: kept[2 * bz, p, pl.ds(8 * t + r, 8), :],
                    lambda r: kept[2 * bz + 1, p, pl.ds(8 * t + r, 8), :],
                    8,
                )
        for parity in range(2):
            planes = unlift_planes([pairs[0, z][parity] for z in range(8)], [pairs[1, z][parity] for z in range(8)])
            for z in range(NZ):
                cells[v, z, pl.ds(16 * t + parity, 8, stride=2), :] = planes[z]
        return 0

    def one(v, _):
        keep(v, 0)
        lax.fori_loop(v * 4, v * 4 + 4, back_one, 0)
        pltpu.make_async_copy(cells.at[v], out.at[v], sems.at[v]).start()
        return 0

    lax.fori_loop(0, NV, one, 0)
    for v in range(NV):
        pltpu.make_async_copy(cells.at[v], out.at[v], sems.at[v]).wait()


def main_specs():
    vmem = pl.BlockSpec(memory_space=pltpu.VMEM)
    return [
        vmem, vmem, vmem, vmem,
        pl.BlockSpec((1, 8, NL), lambda i: (12, 0, 0)), pl.BlockSpec((1, 8, NL), lambda i: (18, 0, 0)),
        vmem, vmem,
    ]


def low_step(*operands):
    w = weights()
    return pl.pallas_call(
        low_kernel,
        grid=(1,),
        out_shape=jax.ShapeDtypeStruct((NV * 8, 48, NL), F32),
        in_specs=main_specs(),
        out_specs=pl.BlockSpec((NV * 8, 48, NL), lambda i: (0, 0, 0)),
        scratch_shapes=[
            pltpu.VMEM((4, 4, 256, NL), BF16),
            pltpu.VMEM((NV * 8, 64, NL), F32),
            pltpu.VMEM((4, 3, NV * 32, NL), F32),
            pltpu.VMEM((4, NV * 4, 40, NL), F32),
        ],
        compiler_params=pltpu.CompilerParams(vmem_limit_bytes=VMEM_LIMIT),
    )(*operands, w["wide"], w["narrow"])


def high_step(low_back, *operands):
    w = weights()
    return pl.pallas_call(
        high_kernel,
        grid=(1,),
        out_shape=jax.ShapeDtypeStruct((NV, NZ, NR, NL), F32),
        in_specs=main_specs() + [pl.BlockSpec((NV * 8, 48, NL), lambda i: (0, 0, 0))],
        out_specs=pl.BlockSpec(memory_space=pltpu.HBM),
        scratch_shapes=[
            pltpu.VMEM((4, 4, 256, NL), BF16),
            pltpu.VMEM((4, NV * 8, 48, NL), F32),
            pltpu.VMEM((NV, NZ, NR, NL), F32),
            pltpu.SemaphoreType.DMA((NV,)),
        ],
        compiler_params=pltpu.CompilerParams(vmem_limit_bytes=VMEM_LIMIT),
    )(*operands, w["wide"], w["narrow"], low_back)


def rows_kernel(count_x, count_z, *refs):
    shares, out = refs[:count_x], refs[count_x + 1]
    me = lax.axis_index("gx")
    row = lax.broadcasted_iota(jnp.int32, (8, NL), 0)
    for r in range(count_x):
        at = pl.multiple_of(16 * (me ^ r), 16)
        for j in range(count_z):
            for z in range(4):
                out[j, z, pl.ds(at, 16), :] = shares[r][80 * j + 16 * z : 80 * j + 16 * z + 16, :]
    for r in range(count_x):
        i = me ^ r
        below = pl.multiple_of(16 * lax.rem(i + 1, count_x), 16)
        above = pl.multiple_of(16 * lax.rem(i + count_x - 1, count_x) + 8, 8)
        for j in range(count_z):
            low = shares[r][80 * j + 64 : 80 * j + 72, :]
            high = shares[r][80 * j + 72 : 80 * j + 80, :]
            for z in range(4):
                first = pltpu.roll(low, 8 - 2 * z, 0) if z else low
                last = pltpu.roll(high, z, 0) if z else high
                out[j, z, pl.ds(below, 8), :] += jnp.where(row < 2, first, 0.0)
                out[j, z, pl.ds(above, 8), :] += jnp.where(row == 7, last, 0.0)


def rows_step(pieces, count_z, after):
    vmem = pl.BlockSpec(memory_space=pltpu.VMEM)
    count_x = len(pieces)
    return pl.pallas_call(
        functools.partial(rows_kernel, count_x, count_z),
        out_shape=jax.ShapeDtypeStruct((count_z, 4, 16 * count_x, NL), F32),
        in_specs=[vmem] * count_x + [pl.BlockSpec(memory_space=pl.ANY)],
        out_specs=vmem,
        compiler_params=pltpu.CompilerParams(vmem_limit_bytes=VMEM_LIMIT),
    )(*pieces, after)


def coarse_kernel(count_x, count_y, own, other, out_hbm, out, sems):
    me = lax.axis_index("gy")
    me_z, is_even = lax.shift_right_logical(me, 1), lax.rem(me, 2) == 0
    lane = lax.broadcasted_iota(jnp.int32, (8, NL), 1)

    def block(i, _):
        rows = pl.ds(pl.multiple_of(8 * i, 8), 8)
        for z in range(4):
            pieces = []
            for j in range(count_y // 2):
                mine, theirs = own[j ^ me_z, z, rows, :], other[j ^ me_z, z, rows, :]
                pieces += [jnp.where(is_even, mine, theirs), jnp.where(is_even, theirs, mine)]
            for v in range(NV):
                for t in range(count_y // 4):
                    total = jnp.zeros((8, NL), F32)
                    for q in range(-1, 5):
                        start = 32 * q - 1
                        shift = (start - 35 * v) % NL
                        piece = pieces[(4 * t + q) % count_y]
                        turned = pltpu.roll(piece, shift, 1) if shift else piece
                        total += jnp.where((lane >= start) & (lane < start + 35), turned, 0.0)
                    out[v, z, rows, NL * t : NL * (t + 1)] = total
        return 0

    def copy(i):
        rows = pl.ds(pl.multiple_of(16 * i, 16), 16)
        return pltpu.make_async_copy(out.at[:, :, rows], out_hbm.at[:, :, rows], sems.at[i])

    def pair(i, _):
        block(2 * i, 0)
        block(2 * i + 1, 0)
        copy(i).start()
        return 0

    lax.fori_loop(0, count_x, pair, 0)
    for i in range(count_x):
        copy(i).wait()


def coarse_step(own, other, count_x, count_y):
    vmem = pl.BlockSpec(memory_space=pltpu.VMEM)
    shape = (NV, 4, 16 * count_x, 32 * count_y)
    return pl.pallas_call(
        functools.partial(coarse_kernel, count_x, count_y),
        out_shape=jax.ShapeDtypeStruct(shape, F32),
        in_specs=[vmem, vmem],
        out_specs=pl.BlockSpec(memory_space=pltpu.HBM),
        scratch_shapes=[pltpu.VMEM(shape, F32), pltpu.SemaphoreType.DMA((count_x,))],
        compiler_params=pltpu.CompilerParams(vmem_limit_bytes=VMEM_LIMIT),
    )(own, other)


def shifted(x, axis, step):
    count = lax.axis_size(axis)
    return lax.ppermute(x, axis, [(i, (i + step) % count) for i in range(count)])


def swapped(x, axis, distance):
    return lax.ppermute(x, axis, [(i, i ^ distance) for i in range(lax.axis_size(axis))])


def body(field, masks):
    count_x, count_y = lax.axis_size("gx"), lax.axis_size("gy")
    lifted, up, down, own_masks, share = first_step(field, masks)
    south = shifted(up, "gx", -1)
    north = shifted(down, "gx", 1)
    shares = [share] + [swapped(share, "gy", r) for r in range(2, count_y, 2)]
    parts, to_left, to_right = edge_step(lifted, north, south, own_masks)
    west = shifted(to_right, "gy", 1)
    east = shifted(to_left, "gy", -1)
    joined = join_step(shares, to_left)
    pieces = [joined] + [swapped(joined, "gx", r) for r in range(1, count_x)]
    operands = (parts.reshape(4, NV * 8, ROWS, NL), west, east, own_masks, north, south)
    low_back = low_step(*operands)
    own = rows_step(pieces, count_y // 2, low_back)
    other = swapped(own, "gy", 1)
    restored = high_step(low_back, *operands)
    return restored, coarse_step(own, other, count_x, count_y)


def solution(mesh):
    placed = P(None, None, "gx", "gy")
    return jax.shard_map(
        body,
        mesh=mesh,
        in_specs=(placed, placed),
        out_specs=(placed, P()),
        check_vma=False,
    )
```

```python
import functools

import jax
import jax.numpy as jnp
import ml_dtypes
import numpy as np
from jax import lax
from jax.experimental import pallas as pl
from jax.experimental.pallas import tpu as pltpu
from jax.sharding import PartitionSpec as P

F32 = jnp.float32
BF16 = jnp.bfloat16
VMEM_LIMIT = 32 * 1024 * 1024

NV, NZ, NR, NL = 3, 16, 64, 128


def detail_row(k):
    return {2 * k + 1: 1.0, 2 * k: -0.5, 2 * k + 2: -0.5}


def smooth_row(k):
    row = {2 * k: 1.0}
    for j in (k - 1, k):
        for cell, value in detail_row(j).items():
            row[cell] = row.get(cell, 0.0) + 0.25 * value
    return row


def even_row(k):
    return {("s", k): 1.0, ("d", k - 1): -0.25, ("d", k): -0.25}


def odd_row(k):
    row = {("d", k): 1.0}
    for j in (k, k + 1):
        for name, value in even_row(j).items():
            row[name] = row.get(name, 0.0) + 0.5 * value
    return row


def as_bf16(matrix):
    cast = matrix.astype(ml_dtypes.bfloat16)
    assert (cast.astype(np.float64) == matrix).all()
    return cast


def combine(*terms):
    total = {}
    for factor, row in terms:
        for cell, value in row.items():
            total[cell] = total.get(cell, 0.0) + factor * value
    return total


def level_one_columns():
    names = {("s", k): k for k in range(65)}
    names.update({("d", k): 128 + k for k in range(65)})
    names[("d", -1)] = 128 + 65
    return names


def level_two_columns():
    names = {("s", k): k for k in range(33)}
    names.update({("d", k): 64 + k for k in range(33)})
    names[("d", -1)] = 64 + 33
    return names


def smooth_place(k):
    return k + 2


def beyond(n):
    return {"cell": 24 * n, "after": 24 * n + 8, "before": 24 * n + 16}


BEYOND_SMOOTH = {65: 96, 66: 104, -2: 112, -1: 120}


def own_row(kind, k, n):
    place = {name: 128 + lane for name, lane in beyond(n).items()}
    if kind == "d":
        if k == -1:
            return {place["before"]: 1.0, 0: -0.5}
        if k == 64:
            return {place["after"]: 1.0}
        return {(place["cell"] if y == 128 else y): value for y, value in detail_row(k).items()}
    if k in BEYOND_SMOOTH:
        row = {128 + BEYOND_SMOOTH[k]: 1.0}
        return combine((1.0, row), (1.0, {0: -0.125})) if k == -1 else row
    even = place["cell"] if k == 64 else 2 * k
    return combine((1.0, {even: 1.0}), (0.25, own_row("d", k - 1, n)), (0.25, own_row("d", k, n)))


@functools.lru_cache(maxsize=None)
def weights():
    w = {}
    names = level_one_columns()
    forward = np.zeros((4, 256, 256))
    inverse = np.zeros((256, 128))
    for (kind, k), column in names.items():
        for n in range(4):
            for place, value in own_row(kind, k, n).items():
                forward[n, place, column] += value
    for k in range(64):
        for y, row in ((2 * k, even_row(k)), (2 * k + 1, odd_row(k))):
            for name, value in row.items():
                inverse[names[name], y] += value
    short = np.zeros((144, 256))
    short[:128] = forward[0, :128]
    for i, lane in enumerate(beyond(0).values()):
        short[128 + i] = forward[0, 128 + lane]
    smooth = np.zeros((256, 128))
    for k in range(-2, 67):
        for place, value in own_row("s", k, 0).items():
            smooth[place, smooth_place(k)] += value
    names2 = level_two_columns()
    forward2 = np.zeros((128, 128))
    inverse2 = np.zeros((128, 128))
    for (kind, k), column in names2.items():
        for cell, value in (smooth_row(k) if kind == "s" else detail_row(k)).items():
            forward2[smooth_place(cell), column] += value
    for k in range(33):
        rows = [(2 * k, even_row(k))] + ([(2 * k + 1, odd_row(k))] if k < 32 else [])
        for y, row in rows:
            for name, value in row.items():
                inverse2[names2[name], y] += value
    back = np.zeros((256, 128))
    back[:65] = inverse[:65]
    back[128 : 128 + 65] = inverse[:65]
    spread = np.zeros((3, 128, 2, 128))
    for k in range(64):
        spread[0, k, 0, k] = 1
    spread[1, 0, 0, 64] = 1
    spread[2, 63, 0, 65] = 1
    for k in range(32):
        spread[0, 64 + k, 1, k] = 1
        spread[0, 64 + k, 1, 64 + k] = 1
    for base in (0, 64):
        spread[1, 64, 1, base + 32] = 1
        spread[2, 95, 1, base + 33] = 1
    w["wide"] = np.concatenate([short, spread.reshape(384, 256)], 0)
    w["narrow"] = np.concatenate([inverse, smooth, back, forward2, inverse2], 0)
    edge = np.zeros((4, 2, 128, 2, 128))

    def put(n, side, lane, row):
        for z in range(8):
            for y, value in row.items():
                j = y - 120 if y >= 120 else y + 8
                edge[n, :, 16 * z + j, side, lane + z] += value

    part = {127: 1.0, 126: -0.5}
    for n in range(4):
        put(n, 0, beyond(n)["cell"], {0: 1.0})
        put(n, 0, beyond(n)["after"], detail_row(0))
        put(n, 1, beyond(n)["before"], part)
    put(0, 0, BEYOND_SMOOTH[65], smooth_row(1))
    put(0, 0, BEYOND_SMOOTH[66], smooth_row(2))
    put(0, 1, BEYOND_SMOOTH[-2], smooth_row(62))
    put(0, 1, BEYOND_SMOOTH[-1], combine((1.0, {126: 1.0}), (0.25, detail_row(62)), (0.25, part)))
    w["edge"] = edge.reshape(1024, 256)
    expand = np.zeros((2, 4, 128))
    for j in range(4):
        expand[0, j, 16 * j : 16 * j + 16] = 1
        expand[1, j, 64 + 8 * j : 64 + 8 * j + 8] = 1
    twice = combine(*[(value, smooth_row(k)) for k, value in smooth_row(0).items()])
    columns = np.zeros((2, 128, 128))
    for m in range(-1, 34):
        for t, value in twice.items():
            if 0 <= 4 * m + t < NL:
                columns[:, 4 * m + t, m + 1] = value
    rows = np.zeros((4, 32, 2, 64))
    for z in range(4):
        places = {m: m for m in range(16)}
        places.update({16: 16 + 2 * z, 17: 17 + 2 * z, -1: 16 + 15 - z})
        for m, place in places.items():
            for t, value in twice.items():
                if 0 <= 4 * m + t < NR:
                    rows[z, place, :, 4 * m + t] = value
    pad = np.zeros((8, 128))
    w["first"] = np.concatenate([columns.reshape(256, 128), rows.reshape(128, 128), expand.reshape(8, 128), pad], 0)
    return {name: as_bf16(matrix) for name, matrix in w.items()}


def two_terms(x):
    high = x.astype(BF16)
    low = (x - high.astype(F32)).astype(BF16)
    return high, low


def dot(a, b):
    return jnp.dot(a, b, preferred_element_type=F32)


def lift_planes(cells):
    half = len(cells) // 2
    even, odd = cells[0::2], cells[1::2]
    detail = [odd[k] - 0.5 * (even[k] + even[min(k + 1, half - 1)]) for k in range(half)]
    smooth = [even[k] + 0.25 * (detail[max(k - 1, 0)] + detail[k]) for k in range(half)]
    return smooth, detail


def unlift_planes(smooth, detail):
    half = len(smooth)
    even = [smooth[k] - 0.25 * (detail[max(k - 1, 0)] + detail[k]) for k in range(half)]
    out = []
    for k in range(half):
        out += [even[k], detail[k] + 0.5 * (even[k] + even[min(k + 1, half - 1)])]
    return out


def lift_rows(load, start):
    even, odd, after = load(start), load(start + 1), load(start + 2)
    before, odd_before = load(start - 2), load(start - 1)
    detail = odd - 0.5 * (even + after)
    detail_before = odd_before - 0.5 * (before + even)
    return even + 0.25 * (detail_before + detail), detail


def unlift_rows(smooth, detail, row):
    here, after = detail(row), detail(row + 1)
    even = smooth(row) - 0.25 * (detail(row - 1) + here)
    next_even = smooth(row + 1) - 0.25 * (here + after)
    return even, here + 0.5 * (even + next_even)


PITCH = 80


def first_kernel(
    field, masks_hbm, table_hbm, lifted, up, down, own_masks, share, cells, twice, masks, table, sems
):
    copies = []
    for v in range(NV):
        for h in range(2):
            part = pl.ds(8 * h, 8)
            copies.append(pltpu.make_async_copy(field.at[v, part], cells.at[v, part], sems.at[2 * v + h]))
    copies.append(pltpu.make_async_copy(masks_hbm, masks, sems.at[2 * NV]))
    copies.append(pltpu.make_async_copy(table_hbm, table, sems.at[2 * NV + 1]))
    for copy in copies:
        copy.start()
    for p in range(NV * NZ):
        lifted[p * PITCH : p * PITCH + 8, :] = jnp.zeros((8, NL), F32)
        lifted[p * PITCH + 72 : p * PITCH + 80, :] = jnp.zeros((8, NL), F32)

    for v in range(NV):
        for copy in copies[2 * v : 2 * v + 2]:
            copy.wait()

        def planes(t, _):
            at = pl.multiple_of(t * 8, 8)
            smooth, detail = lift_planes([cells[v, z, pl.ds(at, 8), :] for z in range(NZ)])
            for k, tile in enumerate(smooth + detail):
                lifted[pl.ds((v * NZ + k) * PITCH + 8 + at, 8), :] = tile
            for k, tile in enumerate(lift_planes(smooth)[0]):
                twice[v * 4 + k, pl.ds(at, 8), :] = tile
            return 0

        lax.fori_loop(0, 8, planes, 0)
        for bz in range(2):

            def row(x):
                return lifted[pl.ds((v * NZ + bz * 8) * PITCH + 8 + x, 8, stride=PITCH), :]

            x = [row(j) for j in range(7 if bz == 0 else 3)]
            first = x[1] - 0.5 * (x[0] + x[2])
            up[v * 6 + bz] = x[0]
            up[v * 6 + 2 + bz] = first
            y = {j: row(j) for j in (range(58, 64) if bz == 0 else (62, 63))}
            part = y[63] - 0.5 * y[62]
            down[v * 4 + bz] = part
            if bz == 0:
                second = x[3] - 0.5 * (x[2] + x[4])
                third = x[5] - 0.5 * (x[4] + x[6])
                up[v * 6 + 4] = x[2] + 0.25 * (first + second)
                up[v * 6 + 5] = x[4] + 0.25 * (second + third)
                before = y[59] - 0.5 * (y[58] + y[60])
                last = y[61] - 0.5 * (y[60] + y[62])
                down[v * 4 + 2] = y[60] + 0.25 * (before + last)
                down[v * 4 + 3] = y[62] + 0.25 * (last + part)

    for copy in copies[2 * NV :]:
        copy.wait()
    for i, out, tile in ((0, up, 18), (1, down, 12)):
        total = jnp.zeros((7, NL), F32)
        for l in range(2):
            flags = masks[l, i].astype(F32).astype(BF16)
            spread = table[384 + 4 * l : 388 + 4 * l, :]
            total += lax.dot_general(flags, spread, (((0,), (0,)), ((), ())), preferred_element_type=F32)
        own_masks[i] = jnp.concatenate([total, jnp.zeros((1, NL), F32)], 0)
        out[tile] = own_masks[i]
    total = jnp.zeros((80, NL), F32)
    for v in range(NV):
        main, extra = [], jnp.zeros((16, NL), F32)
        for z in range(4):
            terms = jnp.concatenate(two_terms(twice[v * 4 + z]), 0)
            part = dot(table[256 + 32 * z : 288 + 32 * z, :], terms)
            main.append(part[:16])
            extra += part[16:]
        terms = jnp.concatenate(two_terms(jnp.concatenate(main + [extra], 0)), 1)
        part = dot(terms, table[0:256, :])
        total += pltpu.roll(part, 35 * v, 1) if v else part
    share[...] = total


def in_hbm(x):
    return pltpu.with_memory_space_constraint(x, pltpu.HBM)


def first_step(field, masks):
    vmem = pl.BlockSpec(memory_space=pltpu.VMEM)
    shapes = [(NV * NZ * PITCH, NL), (19, 8, NL), (13, 8, NL), (2, 8, NL), (80, NL)]
    return pl.pallas_call(
        first_kernel,
        out_shape=[jax.ShapeDtypeStruct(s, F32) for s in shapes],
        in_specs=[pl.BlockSpec(memory_space=pltpu.HBM)] * 3,
        out_specs=[vmem] * 5,
        scratch_shapes=[
            pltpu.VMEM((NV, NZ, NR, NL), F32),
            pltpu.VMEM((NV * 4, NR, NL), F32),
            pltpu.VMEM((2, 2, 4, 7), jnp.int32),
            pltpu.VMEM((400, NL), BF16),
            pltpu.SemaphoreType.DMA((2 * NV + 2,)),
        ],
        compiler_params=pltpu.CompilerParams(vmem_limit_bytes=VMEM_LIMIT),
    )(*[in_hbm(x) for x in (field, masks.transpose(0, 2, 3, 1), jnp.asarray(weights()["first"]))])


ROWS = 40


def lift_kernel(lifted, parts):
    def lift(step, _):
        v, bz = step // 2, lax.rem(step, 2)
        for z in range(8):
            start = pl.multiple_of((step * 8 + z) * PITCH, 8)
            for t in range(4):
                pair = lift_rows(lambda s: lifted[pl.ds(start + 16 * t + s, 8, stride=2), :], 8)
                for bx in range(2):
                    plane = (2 * bz + bx) * 24 + v * 8 + z
                    parts[pl.ds(pl.multiple_of(plane * ROWS + 8 * t, 8), 8), :] = pair[bx]
        return 0

    lax.fori_loop(0, NV * 2, lift, 0)


def lift_step(lifted):
    vmem = pl.BlockSpec(memory_space=pltpu.VMEM)
    return pl.pallas_call(
        lift_kernel,
        out_shape=jax.ShapeDtypeStruct((4 * NV * 8 * ROWS, NL), F32),
        in_specs=[vmem],
        out_specs=vmem,
        cost_estimate=pl.CostEstimate(flops=2 * 10**9, bytes_accessed=4 * 10**6, transcendentals=0),
        compiler_params=pltpu.CompilerParams(vmem_limit_bytes=VMEM_LIMIT),
    )(lifted)


def edge_kernel(parts_in, lifted, north, south, own_masks, table, *rest):
    count = len(rest) - 5
    shares, (parts, to_left, to_right, joined, packed) = rest[:count], rest[count:]
    for n, piece in enumerate(shares):
        joined[80 * n : 80 * (n + 1), :] = piece[...]
    for p in range(4 * NV * 8):
        parts[p * ROWS + 32 : p * ROWS + 40, :] = jnp.zeros((8, NL), F32)
    for v in range(NV):
        for bz in range(2):

            def cell(x):
                return lifted[pl.ds((v * NZ + bz * 8) * PITCH + 8 + x, 8, stride=PITCH), :]

            def at(bx, r):
                return pl.ds(((2 * bz + bx) * 24 + v * 8) * ROWS + r, 8, stride=ROWS)

            before, after, detail = north[v * 4 + bz], south[v * 6 + bz], south[v * 6 + 2 + bz]
            start = cell(0)
            last = cell(63) - 0.5 * (cell(62) + after)
            parts[at(0, 0), :] = parts[at(0, 0), :] + 0.25 * before
            parts[at(0, 31), :] = parts[at(0, 31), :] - 0.125 * after
            parts[at(1, 31), :] = parts[at(1, 31), :] - 0.5 * after
            parts[at(0, 32), :] = after + 0.25 * (last + detail)
            parts[at(1, 32), :] = detail
            parts[at(1, 39), :] = before - 0.5 * start
            if bz == 0:
                parts[at(0, 33), :] = south[v * 6 + 4]
                parts[at(0, 34), :] = south[v * 6 + 5]
                parts[at(0, 38), :] = north[v * 4 + 2]
                parts[at(0, 39), :] = north[v * 4 + 3] - 0.125 * start

    lane = lax.broadcasted_iota(jnp.int32, (8, NL), 1) // 16

    def pack(step, _):
        for t in range(5):
            tile = jnp.zeros((8, NL), F32)
            for z in range(8):
                x = parts[pl.ds(pl.multiple_of((step * 8 + z) * ROWS + 8 * t, 8), 8), :]
                tile = jnp.where(lane == z, pltpu.roll(x, (8 + 16 * z) % NL, 1), tile)
            packed[pl.ds(pl.multiple_of(step * ROWS + 8 * t, 8), 8), :] = tile
        return 0

    lax.fori_loop(0, 4 * NV, pack, 0)
    terms = []
    for n in range(4):
        terms += list(two_terms(packed[n * 120 : (n + 1) * 120, :]))
    sides = dot(jnp.concatenate(terms, 1), table[...])
    to_left[0:120, :] = sides[:, :NL]
    to_right[0:120, :] = sides[:, NL:]
    for out in (to_left, to_right):
        out[120:128, :] = north[12]
        out[128:136, :] = own_masks[0]
        out[136:144, :] = own_masks[1]
        out[144:152, :] = south[18]


def edge_step(parts, lifted, north, south, own_masks, shares):
    vmem = pl.BlockSpec(memory_space=pltpu.VMEM)
    shapes = [(4 * NV * 8 * ROWS, NL), (152, NL), (152, NL), (80 * len(shares), NL)]
    return pl.pallas_call(
        edge_kernel,
        out_shape=[jax.ShapeDtypeStruct(s, F32) for s in shapes],
        in_specs=[vmem] * (6 + len(shares)),
        out_specs=[vmem] * 4,
        input_output_aliases={0: 0},
        scratch_shapes=[pltpu.VMEM((480, NL), F32)],
        compiler_params=pltpu.CompilerParams(vmem_limit_bytes=VMEM_LIMIT),
    )(parts, lifted, north, south, own_masks, weights()["edge"], *shares)


def mask_lanes(west, east, own_masks, north_mask, south_mask, wide):
    masks = [jnp.concatenate([ref[120 + 8 * i : 128 + 8 * i, :] for i in range(4)], 0) for ref in (east, west)]
    own = jnp.concatenate([north_mask[0], own_masks[0], own_masks[1], south_mask[0]], 0)
    flags = jnp.concatenate([own] + masks, 1).astype(BF16)
    return dot(flags, wide[144:528, :])


def sides(west, east, v, at, count):
    rows = pl.ds(pl.multiple_of(v * ROWS + at, 8), count)
    beside = west[rows, :] + east[rows, :]
    tiles = [pltpu.roll(beside, NL - z, 1) if z else beside for z in range(8)]
    return two_terms(jnp.concatenate(tiles, 0))


def operand(parts, n, v, at, count, beside):
    main = two_terms(parts[n, pl.ds(v * 8, 8), pl.ds(at, count), :].reshape(8 * count, NL))
    return [jnp.concatenate(pair, 1) for pair in zip(main, beside)]


def low_kernel(
    parts, west, east, own_masks, north_mask, south_mask, wide, narrow, low_back, gain2, low, second, kept2
):
    smooth_w, forward2, inverse2 = narrow.at[256:512], narrow.at[768:896], narrow.at[896:1024]
    lanes = mask_lanes(west, east, own_masks, north_mask, south_mask, wide)
    lane64 = lax.broadcasted_iota(jnp.int32, (1, NL), 1) < 64
    forward2_f = forward2[...].astype(F32)
    for ib in range(4):
        for n in range(4):
            b = 8 * ib + 4 * (n // 2) + n % 2 - 1
            smooth_two = lanes[b : b + 1, NL:] if n else jnp.ones((1, NL), F32)
            row = jnp.where(lane64, smooth_two, lanes[b + 2 : b + 3, NL:])
            both = dot((forward2_f * row).astype(BF16), inverse2[...]).astype(BF16)
            gain2[ib, n, 0:128, :] = both
            gain2[ib, n, 128:256, :] = both

    def smooth_part(v, _):
        planes = pl.ds(v * 8, 8)
        for at, count in ((0, 16), (16, 16), (32, 8)):
            high, low_term = operand(parts, 0, v, at, count, sides(west, east, v, at, count))
            part = (dot(high, smooth_w[...]) + dot(low_term, smooth_w[...])).reshape(8, count, NL)
            if at < 32:
                low[planes, 8 + at : 8 + at + count, :] = part
                if at == 0:
                    low[planes, 56:64, :] = part[:, 0:8]
            else:
                low[planes, 0:8, :] = part
                low[planes, 40:48, :] = part
                low[planes, 48:56, :] = part
        return 0

    lax.fori_loop(0, NV, smooth_part, 0)

    def rows_two(v, _):
        for t in range(3):
            lifted = [
                lift_rows(lambda s: low[v * 8 + p, pl.ds(16 * t + s, 8, stride=2), :], 8) for p in range(8)
            ]
            for bx in range(2):
                smooth, detail = lift_planes([pair[bx] for pair in lifted])
                for bz, part in ((0, smooth), (1, detail)):
                    for z in range(4):
                        second[2 * bz + bx, t, pl.ds(pl.multiple_of((v * 4 + z) * 8, 8), 8), :] = part[z]
        return 0

    lax.fori_loop(0, NV, rows_two, 0)
    for n in range(4):
        for t in range(3):
            terms = jnp.concatenate(two_terms(second[n, t]), 1)
            if t < 2:
                kept2[n, :, 8 + 8 * t : 16 + 8 * t, :] = dot(terms, gain2[t + 1, n]).reshape(NV * 4, 8, NL)
            else:
                kept2[n, :, 0:8, :] = dot(terms, gain2[0, n]).reshape(NV * 4, 8, NL)
                kept2[n, :, 24:32, :] = dot(terms, gain2[3, n]).reshape(NV * 4, 8, NL)

    def back_two(v, _):
        for t in range(3):
            pairs = {}
            for bz in range(2):
                for z in range(4):
                    p = v * 4 + z
                    if t < 2:
                        pairs[bz, z] = unlift_rows(
                            lambda r: kept2[2 * bz, p, pl.ds(r, 8), :],
                            lambda r: kept2[2 * bz + 1, p, pl.ds(r, 8), :],
                            8 + 8 * t,
                        )
                    else:
                        even = kept2[2 * bz, p, 24:32, :] - 0.25 * (
                            kept2[2 * bz + 1, p, 23:31, :] + kept2[2 * bz + 1, p, 24:32, :]
                        )
                        pairs[bz, z] = (even, even)
            for parity in range(2 if t < 2 else 1):
                planes = unlift_planes([pairs[0, z][parity] for z in range(4)], [pairs[1, z][parity] for z in range(4)])
                for z in range(8):
                    low_back[v * 8 + z, pl.ds(16 * t + parity, 8, stride=2), :] = planes[z]
        return 0

    lax.fori_loop(0, NV, back_two, 0)


def high_kernel(
    parts, west, east, own_masks, north_mask, south_mask, wide, narrow, low_back, out, gain, gain_beyond, kept, cells, sems
):
    inverse, back = narrow.at[0:256], narrow.at[512:768]
    lanes = mask_lanes(west, east, own_masks, north_mask, south_mask, wide)
    forward_f = wide[0:144, :].astype(F32)
    for ib in range(4):
        for n in range(4):
            b = 8 * ib + 4 * (n // 2) + n % 2 - 1
            smooth_one = lanes[b : b + 1, 0:NL] if n else jnp.zeros((1, NL), F32)
            row = jnp.concatenate([smooth_one, lanes[b + 2 : b + 3, 0:NL]], 1)
            both = dot((forward_f * row).astype(BF16), inverse[...])
            main = both[0:128].astype(BF16)
            gain[ib, n, 0:128, :] = main
            gain[ib, n, 128:256, :] = main
            gain_beyond[ib, n] = both[128:136]

    def keep(n, _):
        turn = lax.rem(NL - 24 * n, NL)
        for ib in range(3):
            at, count = 16 * ib, 16 if ib < 2 else 8
            terms = jnp.concatenate(two_terms(parts[n, :, at : at + count, :].reshape(24 * count, NL)), 1)
            for place, first in (((8 + at, ib + 1),) if ib < 2 else ((40, 3), (0, 0))):
                product = dot(terms, gain[first, n]).reshape(24, count, NL)
                rows = [gain_beyond[first, n, i : i + 1, :] for i in range(3)]
                for v in range(NV):
                    beside = west[v * ROWS + at : v * ROWS + at + count, :] + east[v * ROWS + at : v * ROWS + at + count, :]
                    beside = pltpu.roll(beside, turn, 1)
                    for z in range(8):
                        part = product[v * 8 + z]
                        for i in range(3):
                            part += beside[:, 8 * i + z : 8 * i + z + 1] * rows[i]
                        kept[n, v * 8 + z, place : place + count, :] = part
        return 0

    lax.fori_loop(0, 4, keep, 0)
    for at, count in ((0, 16), (16, 16), (32, 8)):
        terms = jnp.concatenate(two_terms(low_back[:, at : at + count, :].reshape(24 * count, NL)), 1)
        kept[0, :, 8 + at : 8 + at + count, :] += dot(terms, back[...]).reshape(24, count, NL)

    def back_one(step, _):
        v, t = step // 4, step % 4
        pairs = {}
        for bz in range(2):
            for z in range(8):
                p = v * 8 + z
                pairs[bz, z] = unlift_rows(
                    lambda r: kept[2 * bz, p, pl.ds(8 * t + r, 8), :],
                    lambda r: kept[2 * bz + 1, p, pl.ds(8 * t + r, 8), :],
                    8,
                )
        for parity in range(2):
            planes = unlift_planes([pairs[0, z][parity] for z in range(8)], [pairs[1, z][parity] for z in range(8)])
            for z in range(NZ):
                cells[v, z, pl.ds(16 * t + parity, 8, stride=2), :] = planes[z]
        return 0

    def one(v, _):
        lax.fori_loop(v * 4, v * 4 + 4, back_one, 0)
        pltpu.make_async_copy(cells.at[v], out.at[v], sems.at[v]).start()
        return 0

    lax.fori_loop(0, NV, one, 0)
    for v in range(NV):
        pltpu.make_async_copy(cells.at[v], out.at[v], sems.at[v]).wait()


def main_specs():
    vmem = pl.BlockSpec(memory_space=pltpu.VMEM)
    return [
        vmem, vmem, vmem, vmem,
        pl.BlockSpec((1, 8, NL), lambda i: (12, 0, 0)), pl.BlockSpec((1, 8, NL), lambda i: (18, 0, 0)),
        vmem, vmem,
    ]


def low_step(*operands):
    w = weights()
    return pl.pallas_call(
        low_kernel,
        grid=(1,),
        out_shape=jax.ShapeDtypeStruct((NV * 8, 48, NL), F32),
        in_specs=main_specs(),
        out_specs=pl.BlockSpec((NV * 8, 48, NL), lambda i: (0, 0, 0)),
        scratch_shapes=[
            pltpu.VMEM((4, 4, 256, NL), BF16),
            pltpu.VMEM((NV * 8, 64, NL), F32),
            pltpu.VMEM((4, 3, NV * 32, NL), F32),
            pltpu.VMEM((4, NV * 4, 40, NL), F32),
        ],
        cost_estimate=pl.CostEstimate(flops=4 * 10**9, bytes_accessed=8 * 10**6, transcendentals=0),
        compiler_params=pltpu.CompilerParams(vmem_limit_bytes=VMEM_LIMIT),
    )(*operands, w["wide"], w["narrow"])


def high_step(low_back, *operands):
    w = weights()
    return pl.pallas_call(
        high_kernel,
        grid=(1,),
        out_shape=jax.ShapeDtypeStruct((NV, NZ, NR, NL), F32),
        in_specs=main_specs() + [pl.BlockSpec((NV * 8, 48, NL), lambda i: (0, 0, 0))],
        out_specs=pl.BlockSpec(memory_space=pltpu.HBM),
        scratch_shapes=[
            pltpu.VMEM((4, 4, 256, NL), BF16),
            pltpu.VMEM((4, 4, 8, NL), F32),
            pltpu.VMEM((4, NV * 8, 48, NL), F32),
            pltpu.VMEM((NV, NZ, NR, NL), F32),
            pltpu.SemaphoreType.DMA((NV,)),
        ],
        cost_estimate=pl.CostEstimate(flops=4 * 10**9, bytes_accessed=8 * 10**6, transcendentals=0),
        compiler_params=pltpu.CompilerParams(vmem_limit_bytes=VMEM_LIMIT),
    )(*operands, w["wide"], w["narrow"], low_back)


def rows_kernel(count_x, count_z, *refs):
    shares, out = refs[:count_x], refs[count_x + 1]
    me = lax.axis_index("gx")
    row = lax.broadcasted_iota(jnp.int32, (8, NL), 0)
    for r in range(count_x):
        at = pl.multiple_of(16 * (me ^ r), 16)
        for j in range(count_z):
            for z in range(4):
                out[j, z, pl.ds(at, 16), :] = shares[r][80 * j + 16 * z : 80 * j + 16 * z + 16, :]
    for r in range(count_x):
        i = me ^ r
        below = pl.multiple_of(16 * lax.rem(i + 1, count_x), 16)
        above = pl.multiple_of(16 * lax.rem(i + count_x - 1, count_x) + 8, 8)
        for j in range(count_z):
            low = shares[r][80 * j + 64 : 80 * j + 72, :]
            high = shares[r][80 * j + 72 : 80 * j + 80, :]
            for z in range(4):
                first = pltpu.roll(low, 8 - 2 * z, 0) if z else low
                last = pltpu.roll(high, z, 0) if z else high
                out[j, z, pl.ds(below, 8), :] += jnp.where(row < 2, first, 0.0)
                out[j, z, pl.ds(above, 8), :] += jnp.where(row == 7, last, 0.0)


def rows_step(pieces, count_z, after):
    vmem = pl.BlockSpec(memory_space=pltpu.VMEM)
    count_x = len(pieces)
    return pl.pallas_call(
        functools.partial(rows_kernel, count_x, count_z),
        out_shape=jax.ShapeDtypeStruct((count_z, 4, 16 * count_x, NL), F32),
        in_specs=[vmem] * count_x + [pl.BlockSpec(memory_space=pl.ANY)],
        out_specs=vmem,
        compiler_params=pltpu.CompilerParams(vmem_limit_bytes=VMEM_LIMIT),
    )(*pieces, after)


def coarse_kernel(count_x, count_y, own, other, out_hbm, out, sems):
    me = lax.axis_index("gy")
    me_z, is_even = lax.shift_right_logical(me, 1), lax.rem(me, 2) == 0
    lane = lax.broadcasted_iota(jnp.int32, (8, NL), 1)

    def block(i, _):
        rows = pl.ds(pl.multiple_of(8 * i, 8), 8)
        for z in range(4):
            pieces = []
            for j in range(count_y // 2):
                mine, theirs = own[j ^ me_z, z, rows, :], other[j ^ me_z, z, rows, :]
                pieces += [jnp.where(is_even, mine, theirs), jnp.where(is_even, theirs, mine)]
            for v in range(NV):
                turned = []
                for j, piece in enumerate(pieces):
                    shift = (32 * j - 1 - 35 * v) % NL
                    turned.append(pltpu.roll(piece, shift, 1) if shift else piece)
                for t in range(count_y // 4):
                    total = jnp.where(lane < 2, turned[4 * t - 1], 0.0)
                    total += jnp.where(lane == NL - 1, turned[(4 * t + 4) % count_y], 0.0)
                    for q in range(4):
                        inside = (lane >= 32 * q - 1) & (lane < 32 * q + 34)
                        total += jnp.where(inside, turned[4 * t + q], 0.0)
                    out[v, z, rows, NL * t : NL * (t + 1)] = total
        return 0

    def copy(i):
        rows = pl.ds(pl.multiple_of(16 * i, 16), 16)
        return pltpu.make_async_copy(out.at[:, :, rows], out_hbm.at[:, :, rows], sems.at[i])

    def pair(i, _):
        block(2 * i, 0)
        block(2 * i + 1, 0)
        copy(i).start()
        return 0

    lax.fori_loop(0, count_x, pair, 0)
    for i in range(count_x):
        copy(i).wait()


def coarse_step(own, other, count_x, count_y):
    vmem = pl.BlockSpec(memory_space=pltpu.VMEM)
    shape = (NV, 4, 16 * count_x, 32 * count_y)
    return pl.pallas_call(
        functools.partial(coarse_kernel, count_x, count_y),
        out_shape=jax.ShapeDtypeStruct(shape, F32),
        in_specs=[vmem, vmem],
        out_specs=pl.BlockSpec(memory_space=pltpu.HBM),
        scratch_shapes=[pltpu.VMEM(shape, F32), pltpu.SemaphoreType.DMA((count_x,))],
        compiler_params=pltpu.CompilerParams(vmem_limit_bytes=VMEM_LIMIT),
    )(own, other)


def shifted(x, axis, step):
    count = lax.axis_size(axis)
    return lax.ppermute(x, axis, [(i, (i + step) % count) for i in range(count)])


def swapped(x, axis, distance):
    return lax.ppermute(x, axis, [(i, i ^ distance) for i in range(lax.axis_size(axis))])


def body(field, masks):
    count_x, count_y = lax.axis_size("gx"), lax.axis_size("gy")
    lifted, up, down, own_masks, share = first_step(field, masks)
    south = shifted(up, "gx", -1)
    north = shifted(down, "gx", 1)
    shares = [share] + [swapped(share, "gy", r) for r in range(2, count_y, 2)]
    parts, to_left, to_right, joined = edge_step(lift_step(lifted), lifted, north, south, own_masks, shares)
    west = shifted(to_right, "gy", 1)
    east = shifted(to_left, "gy", -1)
    pieces = [joined] + [swapped(joined, "gx", r) for r in range(1, count_x)]
    operands = (parts.reshape(4, NV * 8, ROWS, NL), west, east, own_masks, north, south)
    low_back = low_step(*operands)
    own = rows_step(pieces, count_y // 2, low_back)
    other = swapped(own, "gy", 1)
    restored = high_step(low_back, *operands)
    return restored, coarse_step(own, other, count_x, count_y)


def solution(mesh):
    placed = P(None, None, "gx", "gy")
    return jax.shard_map(
        body,
        mesh=mesh,
        in_specs=(placed, placed),
        out_specs=(placed, P()),
        check_vma=False,
    )
```

```python
import functools

import jax
import jax.numpy as jnp
import ml_dtypes
import numpy as np
from jax import lax
from jax.experimental import pallas as pl
from jax.experimental.pallas import tpu as pltpu
from jax.sharding import PartitionSpec as P

F32 = jnp.float32
BF16 = jnp.bfloat16
VMEM_LIMIT = 32 * 1024 * 1024

NV, NZ, NR, NL = 3, 16, 64, 128


def detail_row(k):
    return {2 * k + 1: 1.0, 2 * k: -0.5, 2 * k + 2: -0.5}


def smooth_row(k):
    row = {2 * k: 1.0}
    for j in (k - 1, k):
        for cell, value in detail_row(j).items():
            row[cell] = row.get(cell, 0.0) + 0.25 * value
    return row


def even_row(k):
    return {("s", k): 1.0, ("d", k - 1): -0.25, ("d", k): -0.25}


def odd_row(k):
    row = {("d", k): 1.0}
    for j in (k, k + 1):
        for name, value in even_row(j).items():
            row[name] = row.get(name, 0.0) + 0.5 * value
    return row


def as_bf16(matrix):
    cast = matrix.astype(ml_dtypes.bfloat16)
    assert (cast.astype(np.float64) == matrix).all()
    return cast


def combine(*terms):
    total = {}
    for factor, row in terms:
        for cell, value in row.items():
            total[cell] = total.get(cell, 0.0) + factor * value
    return total


def level_one_columns():
    names = {("s", k): k for k in range(65)}
    names.update({("d", k): 128 + k for k in range(65)})
    names[("d", -1)] = 128 + 65
    return names


def level_two_columns():
    names = {("s", k): k for k in range(33)}
    names.update({("d", k): 64 + k for k in range(33)})
    names[("d", -1)] = 64 + 33
    return names


def smooth_place(k):
    return k + 2


def beyond(n):
    return {"cell": 24 * n, "after": 24 * n + 8, "before": 24 * n + 16}


BEYOND_SMOOTH = {65: 96, 66: 104, -2: 112, -1: 120}


def own_row(kind, k, n):
    place = {name: 128 + lane for name, lane in beyond(n).items()}
    if kind == "d":
        if k == -1:
            return {place["before"]: 1.0, 0: -0.5}
        if k == 64:
            return {place["after"]: 1.0}
        return {(place["cell"] if y == 128 else y): value for y, value in detail_row(k).items()}
    if k in BEYOND_SMOOTH:
        row = {128 + BEYOND_SMOOTH[k]: 1.0}
        return combine((1.0, row), (1.0, {0: -0.125})) if k == -1 else row
    even = place["cell"] if k == 64 else 2 * k
    return combine((1.0, {even: 1.0}), (0.25, own_row("d", k - 1, n)), (0.25, own_row("d", k, n)))


@functools.lru_cache(maxsize=None)
def weights():
    w = {}
    names = level_one_columns()
    forward = np.zeros((4, 256, 256))
    inverse = np.zeros((256, 128))
    for (kind, k), column in names.items():
        for n in range(4):
            for place, value in own_row(kind, k, n).items():
                forward[n, place, column] += value
    for k in range(64):
        for y, row in ((2 * k, even_row(k)), (2 * k + 1, odd_row(k))):
            for name, value in row.items():
                inverse[names[name], y] += value
    short = np.zeros((144, 256))
    short[:128] = forward[0, :128]
    for i, lane in enumerate(beyond(0).values()):
        short[128 + i] = forward[0, 128 + lane]
    smooth = np.zeros((256, 128))
    for k in range(-2, 67):
        for place, value in own_row("s", k, 0).items():
            smooth[place, smooth_place(k)] += value
    names2 = level_two_columns()
    forward2 = np.zeros((128, 128))
    inverse2 = np.zeros((128, 128))
    for (kind, k), column in names2.items():
        for cell, value in (smooth_row(k) if kind == "s" else detail_row(k)).items():
            forward2[smooth_place(cell), column] += value
    for k in range(33):
        rows = [(2 * k, even_row(k))] + ([(2 * k + 1, odd_row(k))] if k < 32 else [])
        for y, row in rows:
            for name, value in row.items():
                inverse2[names2[name], y] += value
    back = np.zeros((256, 128))
    back[:65] = inverse[:65]
    back[128 : 128 + 65] = inverse[:65]
    spread = np.zeros((3, 128, 2, 128))
    for k in range(64):
        spread[0, k, 0, k] = 1
    spread[1, 0, 0, 64] = 1
    spread[2, 63, 0, 65] = 1
    for k in range(32):
        spread[0, 64 + k, 1, k] = 1
        spread[0, 64 + k, 1, 64 + k] = 1
    for base in (0, 64):
        spread[1, 64, 1, base + 32] = 1
        spread[2, 95, 1, base + 33] = 1
    w["wide"] = np.concatenate([short, spread.reshape(384, 256)], 0)
    w["narrow"] = np.concatenate([inverse, smooth, back, forward2, inverse2], 0)
    edge = np.zeros((4, 2, 128, 2, 128))

    def put(n, side, lane, row):
        for z in range(8):
            for y, value in row.items():
                j = y - 120 if y >= 120 else y + 8
                edge[n, :, 16 * z + j, side, lane + z] += value

    part = {127: 1.0, 126: -0.5}
    for n in range(4):
        put(n, 0, beyond(n)["cell"], {0: 1.0})
        put(n, 0, beyond(n)["after"], detail_row(0))
        put(n, 1, beyond(n)["before"], part)
    put(0, 0, BEYOND_SMOOTH[65], smooth_row(1))
    put(0, 0, BEYOND_SMOOTH[66], smooth_row(2))
    put(0, 1, BEYOND_SMOOTH[-2], smooth_row(62))
    put(0, 1, BEYOND_SMOOTH[-1], combine((1.0, {126: 1.0}), (0.25, detail_row(62)), (0.25, part)))
    w["edge"] = edge.reshape(1024, 256)
    expand = np.zeros((2, 4, 128))
    for j in range(4):
        expand[0, j, 16 * j : 16 * j + 16] = 1
        expand[1, j, 64 + 8 * j : 64 + 8 * j + 8] = 1
    twice = combine(*[(value, smooth_row(k)) for k, value in smooth_row(0).items()])
    columns = np.zeros((2, 128, 128))
    for m in range(-1, 34):
        for t, value in twice.items():
            if 0 <= 4 * m + t < NL:
                columns[:, 4 * m + t, m + 1] = value
    rows = np.zeros((4, 32, 2, 64))
    for z in range(4):
        places = {m: m for m in range(16)}
        places.update({16: 16 + 2 * z, 17: 17 + 2 * z, -1: 16 + 15 - z})
        for m, place in places.items():
            for t, value in twice.items():
                if 0 <= 4 * m + t < NR:
                    rows[z, place, :, 4 * m + t] = value
    pad = np.zeros((8, 128))
    w["first"] = np.concatenate([columns.reshape(256, 128), rows.reshape(128, 128), expand.reshape(8, 128), pad], 0)
    return {name: as_bf16(matrix) for name, matrix in w.items()}


def two_terms(x):
    high = x.astype(BF16)
    low = (x - high.astype(F32)).astype(BF16)
    return high, low


def cost(gigaflops):
    return pl.CostEstimate(flops=gigaflops * 10**9, bytes_accessed=8 * 10**6, transcendentals=0)


def dot(a, b):
    return jnp.dot(a, b, preferred_element_type=F32)


def lift_planes(cells):
    half = len(cells) // 2
    even, odd = cells[0::2], cells[1::2]
    detail = [odd[k] - 0.5 * (even[k] + even[min(k + 1, half - 1)]) for k in range(half)]
    smooth = [even[k] + 0.25 * (detail[max(k - 1, 0)] + detail[k]) for k in range(half)]
    return smooth, detail


def unlift_planes(smooth, detail):
    half = len(smooth)
    even = [smooth[k] - 0.25 * (detail[max(k - 1, 0)] + detail[k]) for k in range(half)]
    out = []
    for k in range(half):
        out += [even[k], detail[k] + 0.5 * (even[k] + even[min(k + 1, half - 1)])]
    return out


def lift_rows(load, start):
    even, odd, after = load(start), load(start + 1), load(start + 2)
    before, odd_before = load(start - 2), load(start - 1)
    detail = odd - 0.5 * (even + after)
    detail_before = odd_before - 0.5 * (before + even)
    return even + 0.25 * (detail_before + detail), detail


def unlift_rows(smooth, detail, row):
    here, after = detail(row), detail(row + 1)
    even = smooth(row) - 0.25 * (detail(row - 1) + here)
    next_even = smooth(row + 1) - 0.25 * (here + after)
    return even, here + 0.5 * (even + next_even)


PITCH = 80


def first_kernel(
    field, masks_hbm, table_hbm, lifted, up, down, own_masks, share, cells, twice, masks, table, sems
):
    copies = []
    for v in range(NV):
        for h in range(2):
            part = pl.ds(8 * h, 8)
            copies.append(pltpu.make_async_copy(field.at[v, part], cells.at[v, part], sems.at[2 * v + h]))
    copies.append(pltpu.make_async_copy(masks_hbm, masks, sems.at[2 * NV]))
    copies.append(pltpu.make_async_copy(table_hbm, table, sems.at[2 * NV + 1]))
    for copy in copies:
        copy.start()
    for p in range(NV * NZ):
        lifted[p * PITCH : p * PITCH + 8, :] = jnp.zeros((8, NL), F32)
        lifted[p * PITCH + 72 : p * PITCH + 80, :] = jnp.zeros((8, NL), F32)

    for v in range(NV):
        for copy in copies[2 * v : 2 * v + 2]:
            copy.wait()

        def planes(t, _):
            at = pl.multiple_of(t * 8, 8)
            smooth, detail = lift_planes([cells[v, z, pl.ds(at, 8), :] for z in range(NZ)])
            for k, tile in enumerate(smooth + detail):
                lifted[pl.ds((v * NZ + k) * PITCH + 8 + at, 8), :] = tile
            for k, tile in enumerate(lift_planes(smooth)[0]):
                twice[v * 4 + k, pl.ds(at, 8), :] = tile
            return 0

        lax.fori_loop(0, 8, planes, 0)
        for bz in range(2):

            def row(x):
                return lifted[pl.ds((v * NZ + bz * 8) * PITCH + 8 + x, 8, stride=PITCH), :]

            x = [row(j) for j in range(7 if bz == 0 else 3)]
            first = x[1] - 0.5 * (x[0] + x[2])
            up[v * 6 + bz] = x[0]
            up[v * 6 + 2 + bz] = first
            y = {j: row(j) for j in (range(58, 64) if bz == 0 else (62, 63))}
            part = y[63] - 0.5 * y[62]
            down[v * 4 + bz] = part
            if bz == 0:
                second = x[3] - 0.5 * (x[2] + x[4])
                third = x[5] - 0.5 * (x[4] + x[6])
                up[v * 6 + 4] = x[2] + 0.25 * (first + second)
                up[v * 6 + 5] = x[4] + 0.25 * (second + third)
                before = y[59] - 0.5 * (y[58] + y[60])
                last = y[61] - 0.5 * (y[60] + y[62])
                down[v * 4 + 2] = y[60] + 0.25 * (before + last)
                down[v * 4 + 3] = y[62] + 0.25 * (last + part)

    for copy in copies[2 * NV :]:
        copy.wait()
    for i, out, tile in ((0, up, 18), (1, down, 12)):
        total = jnp.zeros((7, NL), F32)
        for l in range(2):
            flags = masks[l, i].astype(F32).astype(BF16)
            spread = table[384 + 4 * l : 388 + 4 * l, :]
            total += lax.dot_general(flags, spread, (((0,), (0,)), ((), ())), preferred_element_type=F32)
        own_masks[i] = jnp.concatenate([total, jnp.zeros((1, NL), F32)], 0)
        out[tile] = own_masks[i]
    total = jnp.zeros((80, NL), F32)
    for v in range(NV):
        main, extra = [], jnp.zeros((16, NL), F32)
        for z in range(4):
            terms = jnp.concatenate(two_terms(twice[v * 4 + z]), 0)
            part = dot(table[256 + 32 * z : 288 + 32 * z, :], terms)
            main.append(part[:16])
            extra += part[16:]
        terms = jnp.concatenate(two_terms(jnp.concatenate(main + [extra], 0)), 1)
        part = dot(terms, table[0:256, :])
        total += pltpu.roll(part, 35 * v, 1) if v else part
    share[...] = total


def in_hbm(x):
    return pltpu.with_memory_space_constraint(x, pltpu.HBM)


def first_step(field, masks):
    vmem = pl.BlockSpec(memory_space=pltpu.VMEM)
    shapes = [(NV * NZ * PITCH, NL), (19, 8, NL), (13, 8, NL), (2, 8, NL), (80, NL)]
    return pl.pallas_call(
        first_kernel,
        out_shape=[jax.ShapeDtypeStruct(s, F32) for s in shapes],
        in_specs=[pl.BlockSpec(memory_space=pltpu.HBM)] * 3,
        out_specs=[vmem] * 5,
        scratch_shapes=[
            pltpu.VMEM((NV, NZ, NR, NL), F32),
            pltpu.VMEM((NV * 4, NR, NL), F32),
            pltpu.VMEM((2, 2, 4, 7), jnp.int32),
            pltpu.VMEM((400, NL), BF16),
            pltpu.SemaphoreType.DMA((2 * NV + 2,)),
        ],
        compiler_params=pltpu.CompilerParams(vmem_limit_bytes=VMEM_LIMIT),
    )(*[in_hbm(x) for x in (field, masks.transpose(0, 2, 3, 1), jnp.asarray(weights()["first"]))])


ROWS = 40


def lift_kernel(lifted, parts):
    def lift(step, _):
        v, bz = step // 2, lax.rem(step, 2)
        for z in range(8):
            start = pl.multiple_of((step * 8 + z) * PITCH, 8)
            for t in range(4):
                pair = lift_rows(lambda s: lifted[pl.ds(start + 16 * t + s, 8, stride=2), :], 8)
                for bx in range(2):
                    plane = (2 * bz + bx) * 24 + v * 8 + z
                    parts[pl.ds(pl.multiple_of(plane * ROWS + 8 * t, 8), 8), :] = pair[bx]
        return 0

    lax.fori_loop(0, NV * 2, lift, 0)


def lift_step(lifted):
    vmem = pl.BlockSpec(memory_space=pltpu.VMEM)
    return pl.pallas_call(
        lift_kernel,
        out_shape=jax.ShapeDtypeStruct((4 * NV * 8 * ROWS, NL), F32),
        in_specs=[vmem],
        out_specs=vmem,
        compiler_params=pltpu.CompilerParams(vmem_limit_bytes=VMEM_LIMIT),
    )(lifted)


def edge_kernel(parts_in, lifted, north, south, own_masks, table, parts, to_left, to_right, packed):
    for p in range(4 * NV * 8):
        parts[p * ROWS + 32 : p * ROWS + 40, :] = jnp.zeros((8, NL), F32)
    for v in range(NV):
        for bz in range(2):

            def cell(x):
                return lifted[pl.ds((v * NZ + bz * 8) * PITCH + 8 + x, 8, stride=PITCH), :]

            def at(bx, r):
                return pl.ds(((2 * bz + bx) * 24 + v * 8) * ROWS + r, 8, stride=ROWS)

            before, after, detail = north[v * 4 + bz], south[v * 6 + bz], south[v * 6 + 2 + bz]
            start = cell(0)
            last = cell(63) - 0.5 * (cell(62) + after)
            parts[at(0, 0), :] = parts[at(0, 0), :] + 0.25 * before
            parts[at(0, 31), :] = parts[at(0, 31), :] - 0.125 * after
            parts[at(1, 31), :] = parts[at(1, 31), :] - 0.5 * after
            parts[at(0, 32), :] = after + 0.25 * (last + detail)
            parts[at(1, 32), :] = detail
            parts[at(1, 39), :] = before - 0.5 * start
            if bz == 0:
                parts[at(0, 33), :] = south[v * 6 + 4]
                parts[at(0, 34), :] = south[v * 6 + 5]
                parts[at(0, 38), :] = north[v * 4 + 2]
                parts[at(0, 39), :] = north[v * 4 + 3] - 0.125 * start

    lane = lax.broadcasted_iota(jnp.int32, (8, NL), 1) // 16

    def pack(step, _):
        for t in range(5):
            tile = jnp.zeros((8, NL), F32)
            for z in range(8):
                x = parts[pl.ds(pl.multiple_of((step * 8 + z) * ROWS + 8 * t, 8), 8), :]
                tile = jnp.where(lane == z, pltpu.roll(x, (8 + 16 * z) % NL, 1), tile)
            packed[pl.ds(pl.multiple_of(step * ROWS + 8 * t, 8), 8), :] = tile
        return 0

    lax.fori_loop(0, 4 * NV, pack, 0)
    terms = []
    for n in range(4):
        terms += list(two_terms(packed[n * 120 : (n + 1) * 120, :]))
    sides = dot(jnp.concatenate(terms, 1), table[...])
    to_left[0:120, :] = sides[:, :NL]
    to_right[0:120, :] = sides[:, NL:]
    for out in (to_left, to_right):
        out[120:128, :] = north[12]
        out[128:136, :] = own_masks[0]
        out[136:144, :] = own_masks[1]
        out[144:152, :] = south[18]


def edge_step(parts, lifted, north, south, own_masks):
    vmem = pl.BlockSpec(memory_space=pltpu.VMEM)
    shapes = [(4 * NV * 8 * ROWS, NL), (152, NL), (152, NL)]
    return pl.pallas_call(
        edge_kernel,
        out_shape=[jax.ShapeDtypeStruct(s, F32) for s in shapes],
        in_specs=[vmem] * 6,
        out_specs=[vmem] * 3,
        input_output_aliases={0: 0},
        cost_estimate=cost(20),
        scratch_shapes=[pltpu.VMEM((480, NL), F32)],
        compiler_params=pltpu.CompilerParams(vmem_limit_bytes=VMEM_LIMIT),
    )(parts, lifted, north, south, own_masks, weights()["edge"])


def join_kernel(*refs):
    shares, out = refs[:-2], refs[-1]
    for n, piece in enumerate(shares):
        out[80 * n : 80 * (n + 1), :] = piece[...]


def join_step(shares, after):
    vmem = pl.BlockSpec(memory_space=pltpu.VMEM)
    return pl.pallas_call(
        join_kernel,
        out_shape=jax.ShapeDtypeStruct((80 * len(shares), NL), F32),
        in_specs=[vmem] * len(shares) + [pl.BlockSpec(memory_space=pl.ANY)],
        out_specs=vmem,
        cost_estimate=cost(20),
        compiler_params=pltpu.CompilerParams(vmem_limit_bytes=VMEM_LIMIT),
    )(*shares, after)


def mask_lanes(west, east, own_masks, north_mask, south_mask, wide):
    masks = [jnp.concatenate([ref[120 + 8 * i : 128 + 8 * i, :] for i in range(4)], 0) for ref in (east, west)]
    own = jnp.concatenate([north_mask[0], own_masks[0], own_masks[1], south_mask[0]], 0)
    flags = jnp.concatenate([own] + masks, 1).astype(BF16)
    return dot(flags, wide[144:528, :])


def sides(west, east, v, at, count):
    rows = pl.ds(pl.multiple_of(v * ROWS + at, 8), count)
    beside = west[rows, :] + east[rows, :]
    tiles = [pltpu.roll(beside, NL - z, 1) if z else beside for z in range(8)]
    return two_terms(jnp.concatenate(tiles, 0))


def operand(parts, n, v, at, count, beside):
    main = two_terms(parts[n, pl.ds(v * 8, 8), pl.ds(at, count), :].reshape(8 * count, NL))
    return [jnp.concatenate(pair, 1) for pair in zip(main, beside)]


def low_kernel(
    parts, west, east, own_masks, north_mask, south_mask, wide, narrow, low_back, gain2, low, second, kept2
):
    smooth_w, forward2, inverse2 = narrow.at[256:512], narrow.at[768:896], narrow.at[896:1024]
    lanes = mask_lanes(west, east, own_masks, north_mask, south_mask, wide)
    lane64 = lax.broadcasted_iota(jnp.int32, (1, NL), 1) < 64
    forward2_f = forward2[...].astype(F32)
    for ib in range(4):
        for n in range(4):
            b = 8 * ib + 4 * (n // 2) + n % 2 - 1
            smooth_two = lanes[b : b + 1, NL:] if n else jnp.ones((1, NL), F32)
            row = jnp.where(lane64, smooth_two, lanes[b + 2 : b + 3, NL:])
            both = dot((forward2_f * row).astype(BF16), inverse2[...]).astype(BF16)
            gain2[ib, n, 0:128, :] = both
            gain2[ib, n, 128:256, :] = both

    def smooth_part(v, _):
        planes = pl.ds(v * 8, 8)
        for at, count in ((0, 16), (16, 16), (32, 8)):
            high, low_term = operand(parts, 0, v, at, count, sides(west, east, v, at, count))
            part = (dot(high, smooth_w[...]) + dot(low_term, smooth_w[...])).reshape(8, count, NL)
            if at < 32:
                low[planes, 8 + at : 8 + at + count, :] = part
                if at == 0:
                    low[planes, 56:64, :] = part[:, 0:8]
            else:
                low[planes, 0:8, :] = part
                low[planes, 40:48, :] = part
                low[planes, 48:56, :] = part
        return 0

    lax.fori_loop(0, NV, smooth_part, 0)

    def rows_two(v, _):
        for t in range(3):
            lifted = [
                lift_rows(lambda s: low[v * 8 + p, pl.ds(16 * t + s, 8, stride=2), :], 8) for p in range(8)
            ]
            for bx in range(2):
                smooth, detail = lift_planes([pair[bx] for pair in lifted])
                for bz, part in ((0, smooth), (1, detail)):
                    for z in range(4):
                        second[2 * bz + bx, t, pl.ds(pl.multiple_of((v * 4 + z) * 8, 8), 8), :] = part[z]
        return 0

    lax.fori_loop(0, NV, rows_two, 0)
    for n in range(4):
        for t in range(3):
            terms = jnp.concatenate(two_terms(second[n, t]), 1)
            if t < 2:
                kept2[n, :, 8 + 8 * t : 16 + 8 * t, :] = dot(terms, gain2[t + 1, n]).reshape(NV * 4, 8, NL)
            else:
                kept2[n, :, 0:8, :] = dot(terms, gain2[0, n]).reshape(NV * 4, 8, NL)
                kept2[n, :, 24:32, :] = dot(terms, gain2[3, n]).reshape(NV * 4, 8, NL)

    def back_two(v, _):
        for t in range(3):
            pairs = {}
            for bz in range(2):
                for z in range(4):
                    p = v * 4 + z
                    if t < 2:
                        pairs[bz, z] = unlift_rows(
                            lambda r: kept2[2 * bz, p, pl.ds(r, 8), :],
                            lambda r: kept2[2 * bz + 1, p, pl.ds(r, 8), :],
                            8 + 8 * t,
                        )
                    else:
                        even = kept2[2 * bz, p, 24:32, :] - 0.25 * (
                            kept2[2 * bz + 1, p, 23:31, :] + kept2[2 * bz + 1, p, 24:32, :]
                        )
                        pairs[bz, z] = (even, even)
            for parity in range(2 if t < 2 else 1):
                planes = unlift_planes([pairs[0, z][parity] for z in range(4)], [pairs[1, z][parity] for z in range(4)])
                for z in range(8):
                    low_back[v * 8 + z, pl.ds(16 * t + parity, 8, stride=2), :] = planes[z]
        return 0

    lax.fori_loop(0, NV, back_two, 0)


def high_kernel(
    parts, west, east, own_masks, north_mask, south_mask, wide, narrow, low_back, kept, gain, sides_wide
):
    inverse, back = narrow.at[0:256], narrow.at[512:768]
    lanes = mask_lanes(west, east, own_masks, north_mask, south_mask, wide)
    forward_f = wide[0:144, :].astype(F32)
    for ib in range(4):
        sides_wide[ib] = jnp.zeros((NL, 4 * NL), F32)
    for ib in range(4):
        for n in range(4):
            b = 8 * ib + 4 * (n // 2) + n % 2 - 1
            smooth_one = lanes[b : b + 1, 0:NL] if n else jnp.zeros((1, NL), F32)
            row = jnp.concatenate([smooth_one, lanes[b + 2 : b + 3, 0:NL]], 1)
            both = dot((forward_f * row).astype(BF16), inverse[...])
            main = both[0:128].astype(BF16)
            gain[ib, n, 0:128, :] = main
            gain[ib, n, 128:256, :] = main
            for i in range(3):
                at = 24 * n + 8 * i
                sides_wide[ib, at : at + 1, n * NL : (n + 1) * NL] = both[128 + i : 129 + i]

    gain_sides = []
    for ib in range(4):
        side = sides_wide[ib].astype(BF16)
        gain_sides.append(jnp.concatenate([side, side], 0))
    for ib in range(3):
        at, count = 16 * ib, 16 if ib < 2 else 8
        tiles = []
        for v in range(NV):
            rows = slice(v * ROWS + at, v * ROWS + at + count)
            beside = west[rows, :] + east[rows, :]
            tiles += [pltpu.roll(beside, NL - z, 1) if z else beside for z in range(8)]
        terms = jnp.concatenate(two_terms(jnp.concatenate(tiles, 0)), 1)
        for place, first in (((8 + at, ib + 1),) if ib < 2 else ((40, 3), (0, 0))):
            product = dot(terms, gain_sides[first])
            for n in range(4):
                kept[n, :, place : place + count, :] = product[:, n * NL : (n + 1) * NL].reshape(24, count, NL)

    def keep(n, _):
        for ib in range(3):
            at, count = 16 * ib, 16 if ib < 2 else 8
            terms = jnp.concatenate(two_terms(parts[n, :, at : at + count, :].reshape(24 * count, NL)), 1)
            for place, first in (((8 + at, ib + 1),) if ib < 2 else ((40, 3), (0, 0))):
                kept[n, :, place : place + count, :] += dot(terms, gain[first, n]).reshape(24, count, NL)
        return 0

    lax.fori_loop(0, 4, keep, 0)
    for at, count in ((0, 16), (16, 16), (32, 8)):
        terms = jnp.concatenate(two_terms(low_back[:, at : at + count, :].reshape(24 * count, NL)), 1)
        kept[0, :, 8 + at : 8 + at + count, :] += dot(terms, back[...]).reshape(24, count, NL)


def cells_kernel(kept, out, cells, sems):
    def back_one(step, _):
        v, t = step // 4, step % 4
        pairs = {}
        for bz in range(2):
            for z in range(8):
                p = v * 8 + z
                pairs[bz, z] = unlift_rows(
                    lambda r: kept[2 * bz, p, pl.ds(8 * t + r, 8), :],
                    lambda r: kept[2 * bz + 1, p, pl.ds(8 * t + r, 8), :],
                    8,
                )
        for parity in range(2):
            planes = unlift_planes([pairs[0, z][parity] for z in range(8)], [pairs[1, z][parity] for z in range(8)])
            for z in range(NZ):
                cells[v, z, pl.ds(16 * t + parity, 8, stride=2), :] = planes[z]
        return 0

    def one(v, _):
        lax.fori_loop(v * 4, v * 4 + 4, back_one, 0)
        pltpu.make_async_copy(cells.at[v], out.at[v], sems.at[v]).start()
        return 0

    lax.fori_loop(0, NV, one, 0)
    for v in range(NV):
        pltpu.make_async_copy(cells.at[v], out.at[v], sems.at[v]).wait()


def main_specs():
    vmem = pl.BlockSpec(memory_space=pltpu.VMEM)
    return [
        vmem, vmem, vmem, vmem,
        pl.BlockSpec((1, 8, NL), lambda i: (12, 0, 0)), pl.BlockSpec((1, 8, NL), lambda i: (18, 0, 0)),
        vmem, vmem,
    ]


def low_step(*operands):
    w = weights()
    return pl.pallas_call(
        low_kernel,
        grid=(1,),
        out_shape=jax.ShapeDtypeStruct((NV * 8, 48, NL), F32),
        in_specs=main_specs(),
        out_specs=pl.BlockSpec((NV * 8, 48, NL), lambda i: (0, 0, 0)),
        scratch_shapes=[
            pltpu.VMEM((4, 4, 256, NL), BF16),
            pltpu.VMEM((NV * 8, 64, NL), F32),
            pltpu.VMEM((4, 3, NV * 32, NL), F32),
            pltpu.VMEM((4, NV * 4, 40, NL), F32),
        ],
        cost_estimate=cost(4),
        compiler_params=pltpu.CompilerParams(vmem_limit_bytes=VMEM_LIMIT),
    )(*operands, w["wide"], w["narrow"])


def high_step(low_back, *operands):
    w = weights()
    return pl.pallas_call(
        high_kernel,
        grid=(1,),
        out_shape=jax.ShapeDtypeStruct((4, NV * 8, 48, NL), F32),
        in_specs=main_specs() + [pl.BlockSpec((NV * 8, 48, NL), lambda i: (0, 0, 0))],
        out_specs=pl.BlockSpec((4, NV * 8, 48, NL), lambda i: (0, 0, 0, 0)),
        scratch_shapes=[
            pltpu.VMEM((4, 4, 256, NL), BF16),
            pltpu.VMEM((4, NL, 4 * NL), F32),
        ],
        cost_estimate=cost(4),
        compiler_params=pltpu.CompilerParams(vmem_limit_bytes=VMEM_LIMIT),
    )(*operands, w["wide"], w["narrow"], low_back)


def cells_step(kept):
    shape = (NV, NZ, NR, NL)
    return pl.pallas_call(
        cells_kernel,
        out_shape=jax.ShapeDtypeStruct(shape, F32),
        in_specs=[pl.BlockSpec(memory_space=pltpu.VMEM)],
        out_specs=pl.BlockSpec(memory_space=pltpu.HBM),
        scratch_shapes=[pltpu.VMEM(shape, F32), pltpu.SemaphoreType.DMA((NV,))],
        cost_estimate=cost(4),
        compiler_params=pltpu.CompilerParams(vmem_limit_bytes=VMEM_LIMIT),
    )(kept)


def rows_kernel(count_x, count_z, *refs):
    shares, out = refs[:count_x], refs[count_x + 1]
    me = lax.axis_index("gx")
    row = lax.broadcasted_iota(jnp.int32, (8, NL), 0)
    for r in range(count_x):
        at = pl.multiple_of(16 * (me ^ r), 16)
        for j in range(count_z):
            for z in range(4):
                out[j, z, pl.ds(at, 16), :] = shares[r][80 * j + 16 * z : 80 * j + 16 * z + 16, :]
    for r in range(count_x):
        i = me ^ r
        below = pl.multiple_of(16 * lax.rem(i + 1, count_x), 16)
        above = pl.multiple_of(16 * lax.rem(i + count_x - 1, count_x) + 8, 8)
        for j in range(count_z):
            low = shares[r][80 * j + 64 : 80 * j + 72, :]
            high = shares[r][80 * j + 72 : 80 * j + 80, :]
            for z in range(4):
                first = pltpu.roll(low, 8 - 2 * z, 0) if z else low
                last = pltpu.roll(high, z, 0) if z else high
                out[j, z, pl.ds(below, 8), :] += jnp.where(row < 2, first, 0.0)
                out[j, z, pl.ds(above, 8), :] += jnp.where(row == 7, last, 0.0)


def rows_step(pieces, count_z, after):
    vmem = pl.BlockSpec(memory_space=pltpu.VMEM)
    count_x = len(pieces)
    return pl.pallas_call(
        functools.partial(rows_kernel, count_x, count_z),
        out_shape=jax.ShapeDtypeStruct((count_z, 4, 16 * count_x, NL), F32),
        in_specs=[vmem] * count_x + [pl.BlockSpec(memory_space=pl.ANY)],
        out_specs=vmem,
        compiler_params=pltpu.CompilerParams(vmem_limit_bytes=VMEM_LIMIT),
    )(*pieces, after)


def coarse_kernel(count_x, count_y, own, other, out_hbm, out, sems):
    me = lax.axis_index("gy")
    me_z, is_even = lax.shift_right_logical(me, 1), lax.rem(me, 2) == 0
    lane = lax.broadcasted_iota(jnp.int32, (8, NL), 1)

    def block(i, _):
        rows = pl.ds(pl.multiple_of(8 * i, 8), 8)
        for z in range(4):
            pieces = []
            for j in range(count_y // 2):
                mine, theirs = own[j ^ me_z, z, rows, :], other[j ^ me_z, z, rows, :]
                pieces += [jnp.where(is_even, mine, theirs), jnp.where(is_even, theirs, mine)]
            for v in range(NV):
                turned = []
                for j, piece in enumerate(pieces):
                    shift = (32 * j - 1 - 35 * v) % NL
                    turned.append(pltpu.roll(piece, shift, 1) if shift else piece)
                for t in range(count_y // 4):
                    total = jnp.where(lane < 2, turned[4 * t - 1], 0.0)
                    total += jnp.where(lane == NL - 1, turned[(4 * t + 4) % count_y], 0.0)
                    for q in range(4):
                        inside = (lane >= 32 * q - 1) & (lane < 32 * q + 34)
                        total += jnp.where(inside, turned[4 * t + q], 0.0)
                    out[v, z, rows, NL * t : NL * (t + 1)] = total
        return 0

    def copy(i):
        rows = pl.ds(pl.multiple_of(16 * i, 16), 16)
        return pltpu.make_async_copy(out.at[:, :, rows], out_hbm.at[:, :, rows], sems.at[i])

    def pair(i, _):
        block(2 * i, 0)
        block(2 * i + 1, 0)
        copy(i).start()
        return 0

    lax.fori_loop(0, count_x, pair, 0)
    for i in range(count_x):
        copy(i).wait()


def coarse_step(own, other, count_x, count_y):
    vmem = pl.BlockSpec(memory_space=pltpu.VMEM)
    shape = (NV, 4, 16 * count_x, 32 * count_y)
    return pl.pallas_call(
        functools.partial(coarse_kernel, count_x, count_y),
        out_shape=jax.ShapeDtypeStruct(shape, F32),
        in_specs=[vmem, vmem],
        out_specs=pl.BlockSpec(memory_space=pltpu.HBM),
        scratch_shapes=[pltpu.VMEM(shape, F32), pltpu.SemaphoreType.DMA((count_x,))],
        compiler_params=pltpu.CompilerParams(vmem_limit_bytes=VMEM_LIMIT),
    )(own, other)


def shifted(x, axis, step):
    count = lax.axis_size(axis)
    return lax.ppermute(x, axis, [(i, (i + step) % count) for i in range(count)])


def swapped(x, axis, distance):
    return lax.ppermute(x, axis, [(i, i ^ distance) for i in range(lax.axis_size(axis))])


def body(field, masks):
    count_x, count_y = lax.axis_size("gx"), lax.axis_size("gy")
    lifted, up, down, own_masks, share = first_step(field, masks)
    south = shifted(up, "gx", -1)
    north = shifted(down, "gx", 1)
    shares = [share] + [swapped(share, "gy", r) for r in range(2, count_y, 2)]
    parts, to_left, to_right = edge_step(lift_step(lifted), lifted, north, south, own_masks)
    west = shifted(to_right, "gy", 1)
    east = shifted(to_left, "gy", -1)
    joined = join_step(shares, to_left)
    pieces = [joined] + [swapped(joined, "gx", r) for r in range(1, count_x)]
    operands = (parts.reshape(4, NV * 8, ROWS, NL), west, east, own_masks, north, south)
    kept = high_step(low_step(*operands), *operands)
    own = rows_step(pieces, count_y // 2, kept)
    other = swapped(own, "gy", 1)
    return cells_step(kept), coarse_step(own, other, count_x, count_y)


def solution(mesh):
    placed = P(None, None, "gx", "gy")
    return jax.shard_map(
        body,
        mesh=mesh,
        in_specs=(placed, placed),
        out_specs=(placed, P()),
        check_vma=False,
    )
```

```python
import functools

import jax
import jax.numpy as jnp
import ml_dtypes
import numpy as np
from jax import lax
from jax.experimental import pallas as pl
from jax.experimental.pallas import tpu as pltpu
from jax.sharding import PartitionSpec as P

F32 = jnp.float32
BF16 = jnp.bfloat16
VMEM_LIMIT = 32 * 1024 * 1024

NV, NZ, NR, NL = 3, 16, 64, 128


def detail_row(k):
    return {2 * k + 1: 1.0, 2 * k: -0.5, 2 * k + 2: -0.5}


def smooth_row(k):
    row = {2 * k: 1.0}
    for j in (k - 1, k):
        for cell, value in detail_row(j).items():
            row[cell] = row.get(cell, 0.0) + 0.25 * value
    return row


def even_row(k):
    return {("s", k): 1.0, ("d", k - 1): -0.25, ("d", k): -0.25}


def odd_row(k):
    row = {("d", k): 1.0}
    for j in (k, k + 1):
        for name, value in even_row(j).items():
            row[name] = row.get(name, 0.0) + 0.5 * value
    return row


def as_bf16(matrix):
    cast = matrix.astype(ml_dtypes.bfloat16)
    assert (cast.astype(np.float64) == matrix).all()
    return cast


def combine(*terms):
    total = {}
    for factor, row in terms:
        for cell, value in row.items():
            total[cell] = total.get(cell, 0.0) + factor * value
    return total


def level_one_columns():
    names = {("s", k): k for k in range(65)}
    names.update({("d", k): 128 + k for k in range(65)})
    names[("d", -1)] = 128 + 65
    return names


def level_two_columns():
    names = {("s", k): k for k in range(33)}
    names.update({("d", k): 64 + k for k in range(33)})
    names[("d", -1)] = 64 + 33
    return names


def smooth_place(k):
    return k + 2


def beyond(n):
    return {"cell": 24 * n, "after": 24 * n + 8, "before": 24 * n + 16}


BEYOND_SMOOTH = {65: 96, 66: 104, -2: 112, -1: 120}


def own_row(kind, k, n):
    place = {name: 128 + lane for name, lane in beyond(n).items()}
    if kind == "d":
        if k == -1:
            return {place["before"]: 1.0, 0: -0.5}
        if k == 64:
            return {place["after"]: 1.0}
        return {(place["cell"] if y == 128 else y): value for y, value in detail_row(k).items()}
    if k in BEYOND_SMOOTH:
        row = {128 + BEYOND_SMOOTH[k]: 1.0}
        return combine((1.0, row), (1.0, {0: -0.125})) if k == -1 else row
    even = place["cell"] if k == 64 else 2 * k
    return combine((1.0, {even: 1.0}), (0.25, own_row("d", k - 1, n)), (0.25, own_row("d", k, n)))


@functools.lru_cache(maxsize=None)
def weights():
    w = {}
    names = level_one_columns()
    forward = np.zeros((4, 256, 256))
    inverse = np.zeros((256, 128))
    for (kind, k), column in names.items():
        for n in range(4):
            for place, value in own_row(kind, k, n).items():
                forward[n, place, column] += value
    for k in range(64):
        for y, row in ((2 * k, even_row(k)), (2 * k + 1, odd_row(k))):
            for name, value in row.items():
                inverse[names[name], y] += value
    short = np.zeros((144, 256))
    short[:128] = forward[0, :128]
    for i, lane in enumerate(beyond(0).values()):
        short[128 + i] = forward[0, 128 + lane]
    smooth = np.zeros((256, 128))
    for k in range(-2, 67):
        for place, value in own_row("s", k, 0).items():
            smooth[place, smooth_place(k)] += value
    names2 = level_two_columns()
    forward2 = np.zeros((128, 128))
    inverse2 = np.zeros((128, 128))
    for (kind, k), column in names2.items():
        for cell, value in (smooth_row(k) if kind == "s" else detail_row(k)).items():
            forward2[smooth_place(cell), column] += value
    for k in range(33):
        rows = [(2 * k, even_row(k))] + ([(2 * k + 1, odd_row(k))] if k < 32 else [])
        for y, row in rows:
            for name, value in row.items():
                inverse2[names2[name], y] += value
    back = np.zeros((256, 128))
    back[:65] = inverse[:65]
    back[128 : 128 + 65] = inverse[:65]
    spread = np.zeros((3, 128, 2, 128))
    for k in range(64):
        spread[0, k, 0, k] = 1
    spread[1, 0, 0, 64] = 1
    spread[2, 63, 0, 65] = 1
    for k in range(32):
        spread[0, 64 + k, 1, k] = 1
        spread[0, 64 + k, 1, 64 + k] = 1
    for base in (0, 64):
        spread[1, 64, 1, base + 32] = 1
        spread[2, 95, 1, base + 33] = 1
    w["wide"] = np.concatenate([short, spread.reshape(384, 256)], 0)
    own, beside = smooth[:128], smooth[128:]
    w["narrow"] = np.concatenate([inverse, own, own, beside, beside, back, forward2, inverse2], 0)
    edge = np.zeros((4, 128, 128))

    def put(n, lane, row):
        for z in range(8):
            for y, value in row.items():
                j = y - 120 if y >= 120 else y + 8
                edge[n, 16 * z + j, lane + z] += value

    part = {127: 1.0, 126: -0.5}
    for n in range(4):
        put(n, beyond(n)["cell"], {0: 1.0})
        put(n, beyond(n)["after"], detail_row(0))
        put(n, beyond(n)["before"], part)
    put(0, BEYOND_SMOOTH[65], smooth_row(1))
    put(0, BEYOND_SMOOTH[66], smooth_row(2))
    put(0, BEYOND_SMOOTH[-2], smooth_row(62))
    put(0, BEYOND_SMOOTH[-1], combine((1.0, {126: 1.0}), (0.25, detail_row(62)), (0.25, part)))
    w["edge"] = edge.reshape(512, 128)
    expand = np.zeros((2, 4, 128))
    for j in range(4):
        expand[0, j, 16 * j : 16 * j + 16] = 1
        expand[1, j, 64 + 8 * j : 64 + 8 * j + 8] = 1
    twice = combine(*[(value, smooth_row(k)) for k, value in smooth_row(0).items()])
    columns = np.zeros((2, 128, 128))
    for m in range(-1, 34):
        for t, value in twice.items():
            if 0 <= 4 * m + t < NL:
                columns[:, 4 * m + t, m + 1] = value
    rows = np.zeros((4, 32, 2, 64))
    for z in range(4):
        places = {m: m for m in range(16)}
        places.update({16: 16 + 2 * z, 17: 17 + 2 * z, -1: 16 + 15 - z})
        for m, place in places.items():
            for t, value in twice.items():
                if 0 <= 4 * m + t < NR:
                    rows[z, place, :, 4 * m + t] = value
    pad = np.zeros((8, 128))
    w["first"] = np.concatenate([columns.reshape(256, 128), rows.reshape(128, 128), expand.reshape(8, 128), pad], 0)
    return {name: as_bf16(matrix) for name, matrix in w.items()}


def two_terms(x):
    high = x.astype(BF16)
    low = (x - high.astype(F32)).astype(BF16)
    return high, low


def cost(gigaflops):
    return pl.CostEstimate(flops=gigaflops * 10**9, bytes_accessed=8 * 10**6, transcendentals=0)


def dot(a, b):
    return jnp.dot(a, b, preferred_element_type=F32)


def lift_planes(cells):
    half = len(cells) // 2
    even, odd = cells[0::2], cells[1::2]
    detail = [odd[k] - 0.5 * (even[k] + even[min(k + 1, half - 1)]) for k in range(half)]
    smooth = [even[k] + 0.25 * (detail[max(k - 1, 0)] + detail[k]) for k in range(half)]
    return smooth, detail


def unlift_planes(smooth, detail):
    half = len(smooth)
    even = [smooth[k] - 0.25 * (detail[max(k - 1, 0)] + detail[k]) for k in range(half)]
    out = []
    for k in range(half):
        out += [even[k], detail[k] + 0.5 * (even[k] + even[min(k + 1, half - 1)])]
    return out


def lift_rows(load, start):
    even, odd, after = load(start), load(start + 1), load(start + 2)
    before, odd_before = load(start - 2), load(start - 1)
    detail = odd - 0.5 * (even + after)
    detail_before = odd_before - 0.5 * (before + even)
    return even + 0.25 * (detail_before + detail), detail


def unlift_rows(smooth, detail, row):
    here, after = detail(row), detail(row + 1)
    even = smooth(row) - 0.25 * (detail(row - 1) + here)
    next_even = smooth(row + 1) - 0.25 * (here + after)
    return even, here + 0.5 * (even + next_even)


PITCH = 80


def first_kernel(
    field, masks_hbm, table_hbm, lifted, up, down, own_masks, share, cells, twice, masks, table, sems
):
    copies = []
    for v in range(NV):
        for h in range(4):
            part = pl.ds(4 * h, 4)
            copies.append(pltpu.make_async_copy(field.at[v, part], cells.at[v, part], sems.at[4 * v + h]))
    copies.append(pltpu.make_async_copy(masks_hbm, masks, sems.at[4 * NV]))
    copies.append(pltpu.make_async_copy(table_hbm, table, sems.at[4 * NV + 1]))
    for copy in copies:
        copy.start()
    for p in range(NV * NZ):
        lifted[p * PITCH : p * PITCH + 8, :] = jnp.zeros((8, NL), F32)
        lifted[p * PITCH + 72 : p * PITCH + 80, :] = jnp.zeros((8, NL), F32)

    for v in range(NV):
        for copy in copies[4 * v : 4 * v + 4]:
            copy.wait()

        def planes(t, _):
            at = pl.multiple_of(t * 8, 8)
            smooth, detail = lift_planes([cells[v, z, pl.ds(at, 8), :] for z in range(NZ)])
            for k, tile in enumerate(smooth + detail):
                lifted[pl.ds((v * NZ + k) * PITCH + 8 + at, 8), :] = tile
            for k, tile in enumerate(lift_planes(smooth)[0]):
                twice[v * 4 + k, pl.ds(at, 8), :] = tile
            return 0

        lax.fori_loop(0, 8, planes, 0)
        for bz in range(2):

            def row(x):
                return lifted[pl.ds((v * NZ + bz * 8) * PITCH + 8 + x, 8, stride=PITCH), :]

            x = [row(j) for j in range(7 if bz == 0 else 3)]
            first = x[1] - 0.5 * (x[0] + x[2])
            up[v * 6 + bz] = x[0]
            up[v * 6 + 2 + bz] = first
            y = {j: row(j) for j in (range(58, 64) if bz == 0 else (62, 63))}
            part = y[63] - 0.5 * y[62]
            down[v * 4 + bz] = part
            if bz == 0:
                second = x[3] - 0.5 * (x[2] + x[4])
                third = x[5] - 0.5 * (x[4] + x[6])
                up[v * 6 + 4] = x[2] + 0.25 * (first + second)
                up[v * 6 + 5] = x[4] + 0.25 * (second + third)
                before = y[59] - 0.5 * (y[58] + y[60])
                last = y[61] - 0.5 * (y[60] + y[62])
                down[v * 4 + 2] = y[60] + 0.25 * (before + last)
                down[v * 4 + 3] = y[62] + 0.25 * (last + part)

    for copy in copies[4 * NV :]:
        copy.wait()
    for i, out, tile in ((0, up, 18), (1, down, 12)):
        total = jnp.zeros((7, NL), F32)
        for l in range(2):
            flags = masks[l, i].astype(F32).astype(BF16)
            spread = table[384 + 4 * l : 388 + 4 * l, :]
            total += lax.dot_general(flags, spread, (((0,), (0,)), ((), ())), preferred_element_type=F32)
        own_masks[i] = jnp.concatenate([total, jnp.zeros((1, NL), F32)], 0)
        out[tile] = own_masks[i]
    total = jnp.zeros((80, NL), F32)
    for v in range(NV):
        main, extra = [], jnp.zeros((16, NL), F32)
        for z in range(4):
            terms = jnp.concatenate(two_terms(twice[v * 4 + z]), 0)
            part = dot(table[256 + 32 * z : 288 + 32 * z, :], terms)
            main.append(part[:16])
            extra += part[16:]
        terms = jnp.concatenate(two_terms(jnp.concatenate(main + [extra], 0)), 1)
        part = dot(terms, table[0:256, :])
        total += pltpu.roll(part, 35 * v, 1) if v else part
    lane = lax.broadcasted_iota(jnp.int32, (8, NL), 1)
    spare = (lane >= 105) & (lane < 126)
    upper = lax.broadcasted_iota(jnp.int32, (8, NL), 0) < 4
    below, above = total[64:72], total[72:80]
    pieces = [pltpu.roll(above, 105 - 21 * p, 1) for p in range(5)]
    for g in range(8):
        if g < 5:
            extra = pltpu.roll(below, 105 - 21 * g, 1)
        else:
            extra = pltpu.roll(pieces[2 * g - 10], 4, 0)
            extra = jnp.where(upper, extra, pieces[2 * g - 9] if g < 7 else 0.0)
        share[8 * g : 8 * g + 8, :] = jnp.where(spare, extra, total[8 * g : 8 * g + 8])


def in_hbm(x):
    return pltpu.with_memory_space_constraint(x, pltpu.HBM)


def first_step(field, masks):
    vmem = pl.BlockSpec(memory_space=pltpu.VMEM)
    shapes = [(NV * NZ * PITCH, NL), (19, 8, NL), (13, 8, NL), (2, 8, NL), (64, NL)]
    return pl.pallas_call(
        first_kernel,
        out_shape=[jax.ShapeDtypeStruct(s, F32) for s in shapes],
        in_specs=[pl.BlockSpec(memory_space=pltpu.HBM)] * 3,
        out_specs=[vmem] * 5,
        scratch_shapes=[
            pltpu.VMEM((NV, NZ, NR, NL), F32),
            pltpu.VMEM((NV * 4, NR, NL), F32),
            pltpu.VMEM((2, 2, 4, 7), jnp.int32),
            pltpu.VMEM((400, NL), BF16),
            pltpu.SemaphoreType.DMA((4 * NV + 2,)),
        ],
        compiler_params=pltpu.CompilerParams(vmem_limit_bytes=VMEM_LIMIT),
    )(*[in_hbm(x) for x in (field, masks.transpose(0, 2, 3, 1), jnp.asarray(weights()["first"]))])


ROWS = 40


def lift_kernel(lifted, parts):
    def lift(step, _):
        v, bz = step // 2, lax.rem(step, 2)
        for z in range(8):
            start = pl.multiple_of((step * 8 + z) * PITCH, 8)
            for t in range(4):
                pair = lift_rows(lambda s: lifted[pl.ds(start + 16 * t + s, 8, stride=2), :], 8)
                for bx in range(2):
                    plane = (2 * bz + bx) * 24 + v * 8 + z
                    parts[pl.ds(pl.multiple_of(plane * ROWS + 8 * t, 8), 8), :] = pair[bx]
        return 0

    lax.fori_loop(0, NV * 2, lift, 0)


def lift_step(lifted):
    vmem = pl.BlockSpec(memory_space=pltpu.VMEM)
    return pl.pallas_call(
        lift_kernel,
        out_shape=jax.ShapeDtypeStruct((4 * NV * 8 * ROWS, NL), F32),
        in_specs=[vmem],
        out_specs=vmem,
        compiler_params=pltpu.CompilerParams(vmem_limit_bytes=VMEM_LIMIT),
    )(lifted)


def edge_kernel(parts_in, lifted, north, south, own_masks, table, parts, sides, packed):
    for p in range(4 * NV * 8):
        parts[p * ROWS + 32 : p * ROWS + 40, :] = jnp.zeros((8, NL), F32)
    for v in range(NV):
        for bz in range(2):

            def cell(x):
                return lifted[pl.ds((v * NZ + bz * 8) * PITCH + 8 + x, 8, stride=PITCH), :]

            def at(bx, r):
                return pl.ds(((2 * bz + bx) * 24 + v * 8) * ROWS + r, 8, stride=ROWS)

            before, after, detail = north[v * 4 + bz], south[v * 6 + bz], south[v * 6 + 2 + bz]
            start = cell(0)
            last = cell(63) - 0.5 * (cell(62) + after)
            parts[at(0, 0), :] = parts[at(0, 0), :] + 0.25 * before
            parts[at(0, 31), :] = parts[at(0, 31), :] - 0.125 * after
            parts[at(1, 31), :] = parts[at(1, 31), :] - 0.5 * after
            parts[at(0, 32), :] = after + 0.25 * (last + detail)
            parts[at(1, 32), :] = detail
            parts[at(1, 39), :] = before - 0.5 * start
            if bz == 0:
                parts[at(0, 33), :] = south[v * 6 + 4]
                parts[at(0, 34), :] = south[v * 6 + 5]
                parts[at(0, 38), :] = north[v * 4 + 2]
                parts[at(0, 39), :] = north[v * 4 + 3] - 0.125 * start

    lane = lax.broadcasted_iota(jnp.int32, (8, NL), 1) // 16

    def pack(step, _):
        for t in range(5):
            tile = jnp.zeros((8, NL), F32)
            for z in range(8):
                x = parts[pl.ds(pl.multiple_of((step * 8 + z) * ROWS + 8 * t, 8), 8), :]
                tile = jnp.where(lane == z, pltpu.roll(x, (8 + 16 * z) % NL, 1), tile)
            packed[pl.ds(pl.multiple_of(step * ROWS + 8 * t, 8), 8), :] = tile
        return 0

    lax.fori_loop(0, 4 * NV, pack, 0)
    terms = [two_terms(packed[n * 120 : (n + 1) * 120, :]) for n in range(4)]
    high, low = [jnp.concatenate(part, 1) for part in zip(*terms)]
    sides[0:120, :] = dot(high, table[...]) + dot(low, table[...])
    sides[120:128, :] = north[12]
    sides[128:136, :] = own_masks[0]
    sides[136:144, :] = own_masks[1]
    sides[144:152, :] = south[18]


def edge_step(parts, lifted, north, south, own_masks):
    vmem = pl.BlockSpec(memory_space=pltpu.VMEM)
    shapes = [(4 * NV * 8 * ROWS, NL), (152, NL)]
    return pl.pallas_call(
        edge_kernel,
        out_shape=[jax.ShapeDtypeStruct(s, F32) for s in shapes],
        in_specs=[vmem] * 6,
        out_specs=[vmem] * 2,
        input_output_aliases={0: 0},
        cost_estimate=cost(20),
        scratch_shapes=[pltpu.VMEM((480, NL), F32)],
        compiler_params=pltpu.CompilerParams(vmem_limit_bytes=VMEM_LIMIT),
    )(parts, lifted, north, south, own_masks, weights()["edge"])


def join_kernel(*refs):
    shares, out = refs[:-2], refs[-1]
    for n, piece in enumerate(shares):
        out[64 * n : 64 * (n + 1), :] = piece[...]


def join_step(shares, after):
    vmem = pl.BlockSpec(memory_space=pltpu.VMEM)
    return pl.pallas_call(
        join_kernel,
        out_shape=jax.ShapeDtypeStruct((64 * len(shares), NL), F32),
        in_specs=[vmem] * len(shares) + [pl.BlockSpec(memory_space=pl.ANY)],
        out_specs=vmem,
        cost_estimate=cost(20),
        compiler_params=pltpu.CompilerParams(vmem_limit_bytes=VMEM_LIMIT),
    )(*shares, after)


def mask_lanes(west, east, own_masks, north_mask, south_mask, wide):
    masks = [jnp.concatenate([ref[120 + 8 * i : 128 + 8 * i, :] for i in range(4)], 0) for ref in (east, west)]
    own = jnp.concatenate([north_mask[0], own_masks[0], own_masks[1], south_mask[0]], 0)
    flags = jnp.concatenate([own] + masks, 1).astype(BF16)
    return dot(flags, wide[144:528, :])


def beside_terms(west, east, at, count):
    lane = lax.broadcasted_iota(jnp.int32, (count, NL), 1)
    from_west = (lane >= 112) | ((lane < 96) & (lax.rem(lane, 24) >= 16))
    tiles = []
    for v in range(NV):
        rows = slice(v * ROWS + at, v * ROWS + at + count)
        beside = jnp.where(from_west, west[rows, :], east[rows, :])
        tiles += [pltpu.roll(beside, NL - z, 1) if z else beside for z in range(8)]
    return jnp.concatenate(two_terms(jnp.concatenate(tiles, 0)), 1)


def own_terms(planes, at, count):
    return jnp.concatenate(two_terms(planes[:, at : at + count, :].reshape(24 * count, NL)), 1)


def low_kernel(
    parts, west, east, own_masks, north_mask, south_mask, wide, narrow, low_back, gain2, low, second, kept2
):
    smooth_own, smooth_beside = narrow.at[256:512], narrow.at[512:768]
    forward2, inverse2 = narrow.at[1024:1152], narrow.at[1152:1280]
    lanes = mask_lanes(west, east, own_masks, north_mask, south_mask, wide)
    lane64 = lax.broadcasted_iota(jnp.int32, (1, NL), 1) < 64
    forward2_f = forward2[...].astype(F32)
    for ib in range(4):
        for n in range(4):
            b = 8 * ib + 4 * (n // 2) + n % 2 - 1
            smooth_two = lanes[b : b + 1, NL:] if n else jnp.ones((1, NL), F32)
            row = jnp.where(lane64, smooth_two, lanes[b + 2 : b + 3, NL:])
            both = dot((forward2_f * row).astype(BF16), inverse2[...]).astype(BF16)
            gain2[ib, n, 0:128, :] = both
            gain2[ib, n, 128:256, :] = both

    for at, count in ((0, 16), (16, 16), (32, 8)):
        part = dot(own_terms(parts.at[0], at, count), smooth_own[...])
        part += dot(beside_terms(west, east, at, count), smooth_beside[...])
        part = part.reshape(24, count, NL)
        if at < 32:
            low[:, 8 + at : 8 + at + count, :] = part
            if at == 0:
                low[:, 56:64, :] = part[:, 0:8]
        else:
            low[:, 0:8, :] = part
            low[:, 40:48, :] = part
            low[:, 48:56, :] = part

    def rows_two(v, _):
        for t in range(3):
            lifted = [
                lift_rows(lambda s: low[v * 8 + p, pl.ds(16 * t + s, 8, stride=2), :], 8) for p in range(8)
            ]
            for bx in range(2):
                smooth, detail = lift_planes([pair[bx] for pair in lifted])
                for bz, part in ((0, smooth), (1, detail)):
                    for z in range(4):
                        second[2 * bz + bx, t, pl.ds(pl.multiple_of((v * 4 + z) * 8, 8), 8), :] = part[z]
        return 0

    lax.fori_loop(0, NV, rows_two, 0)
    for n in range(4):
        for t in range(3):
            terms = jnp.concatenate(two_terms(second[n, t]), 1)
            if t < 2:
                kept2[n, :, 8 + 8 * t : 16 + 8 * t, :] = dot(terms, gain2[t + 1, n]).reshape(NV * 4, 8, NL)
            else:
                kept2[n, :, 0:8, :] = dot(terms, gain2[0, n]).reshape(NV * 4, 8, NL)
                kept2[n, :, 24:32, :] = dot(terms, gain2[3, n]).reshape(NV * 4, 8, NL)

    def back_two(v, _):
        for t in range(3):
            pairs = {}
            for bz in range(2):
                for z in range(4):
                    p = v * 4 + z
                    if t < 2:
                        pairs[bz, z] = unlift_rows(
                            lambda r: kept2[2 * bz, p, pl.ds(r, 8), :],
                            lambda r: kept2[2 * bz + 1, p, pl.ds(r, 8), :],
                            8 + 8 * t,
                        )
                    else:
                        even = kept2[2 * bz, p, 24:32, :] - 0.25 * (
                            kept2[2 * bz + 1, p, 23:31, :] + kept2[2 * bz + 1, p, 24:32, :]
                        )
                        pairs[bz, z] = (even, even)
            for parity in range(2 if t < 2 else 1):
                planes = unlift_planes([pairs[0, z][parity] for z in range(4)], [pairs[1, z][parity] for z in range(4)])
                for z in range(8):
                    low_back[v * 8 + z, pl.ds(16 * t + parity, 8, stride=2), :] = planes[z]
        return 0

    lax.fori_loop(0, NV, back_two, 0)


def high_kernel(
    parts, west, east, own_masks, north_mask, south_mask, wide, narrow, low_back, kept, gain, sides_wide
):
    inverse, back = narrow.at[0:256], narrow.at[768:1024]
    lanes = mask_lanes(west, east, own_masks, north_mask, south_mask, wide)
    forward_f = wide[0:144, :].astype(F32)
    for ib in range(4):
        sides_wide[ib] = jnp.zeros((NL, 4 * NL), F32)
    for ib in range(4):
        for n in range(4):
            b = 8 * ib + 4 * (n // 2) + n % 2 - 1
            smooth_one = lanes[b : b + 1, 0:NL] if n else jnp.zeros((1, NL), F32)
            row = jnp.concatenate([smooth_one, lanes[b + 2 : b + 3, 0:NL]], 1)
            both = dot((forward_f * row).astype(BF16), inverse[...])
            main = both[0:128].astype(BF16)
            gain[ib, n, 0:128, :] = main
            gain[ib, n, 128:256, :] = main
            for i in range(3):
                at = 24 * n + 8 * i
                sides_wide[ib, at : at + 1, n * NL : (n + 1) * NL] = both[128 + i : 129 + i]

    gain_sides = []
    for ib in range(4):
        side = sides_wide[ib].astype(BF16)
        gain_sides.append(jnp.concatenate([side, side], 0))
    for ib in range(3):
        at, count = 16 * ib, 16 if ib < 2 else 8
        terms = beside_terms(west, east, at, count)
        for place, first in (((8 + at, ib + 1),) if ib < 2 else ((40, 3), (0, 0))):
            product = dot(terms, gain_sides[first])
            for n in range(4):
                kept[n, :, place : place + count, :] = product[:, n * NL : (n + 1) * NL].reshape(24, count, NL)

    def keep(n, _):
        for ib in range(3):
            at, count = 16 * ib, 16 if ib < 2 else 8
            terms = own_terms(parts.at[n], at, count)
            for place, first in (((8 + at, ib + 1),) if ib < 2 else ((40, 3), (0, 0))):
                kept[n, :, place : place + count, :] += dot(terms, gain[first, n]).reshape(24, count, NL)
        return 0

    lax.fori_loop(0, 4, keep, 0)
    for at, count in ((0, 16), (16, 16), (32, 8)):
        kept[0, :, 8 + at : 8 + at + count, :] += dot(own_terms(low_back, at, count), back[...]).reshape(24, count, NL)


def cells_kernel(kept, out, cells, sems):
    def back_one(step, _):
        v, t = step // 4, step % 4
        pairs = {}
        for bz in range(2):
            for z in range(8):
                p = v * 8 + z
                pairs[bz, z] = unlift_rows(
                    lambda r: kept[2 * bz, p, pl.ds(8 * t + r, 8), :],
                    lambda r: kept[2 * bz + 1, p, pl.ds(8 * t + r, 8), :],
                    8,
                )
        for parity in range(2):
            planes = unlift_planes([pairs[0, z][parity] for z in range(8)], [pairs[1, z][parity] for z in range(8)])
            for z in range(NZ):
                cells[v, z, pl.ds(16 * t + parity, 8, stride=2), :] = planes[z]
        return 0

    def one(v, _):
        lax.fori_loop(v * 4, v * 4 + 4, back_one, 0)
        pltpu.make_async_copy(cells.at[v], out.at[v], sems.at[v]).start()
        return 0

    lax.fori_loop(0, NV, one, 0)
    for v in range(NV):
        pltpu.make_async_copy(cells.at[v], out.at[v], sems.at[v]).wait()


def main_specs():
    vmem = pl.BlockSpec(memory_space=pltpu.VMEM)
    return [
        vmem, vmem, vmem, vmem,
        pl.BlockSpec((1, 8, NL), lambda i: (12, 0, 0)), pl.BlockSpec((1, 8, NL), lambda i: (18, 0, 0)),
        vmem, vmem,
    ]


def low_step(*operands):
    w = weights()
    return pl.pallas_call(
        low_kernel,
        grid=(1,),
        out_shape=jax.ShapeDtypeStruct((NV * 8, 48, NL), F32),
        in_specs=main_specs(),
        out_specs=pl.BlockSpec((NV * 8, 48, NL), lambda i: (0, 0, 0)),
        scratch_shapes=[
            pltpu.VMEM((4, 4, 256, NL), BF16),
            pltpu.VMEM((NV * 8, 64, NL), F32),
            pltpu.VMEM((4, 3, NV * 32, NL), F32),
            pltpu.VMEM((4, NV * 4, 40, NL), F32),
        ],
        cost_estimate=cost(4),
        compiler_params=pltpu.CompilerParams(vmem_limit_bytes=VMEM_LIMIT),
    )(*operands, w["wide"], w["narrow"])


def high_step(low_back, *operands):
    w = weights()
    return pl.pallas_call(
        high_kernel,
        grid=(1,),
        out_shape=jax.ShapeDtypeStruct((4, NV * 8, 48, NL), F32),
        in_specs=main_specs() + [pl.BlockSpec((NV * 8, 48, NL), lambda i: (0, 0, 0))],
        out_specs=pl.BlockSpec((4, NV * 8, 48, NL), lambda i: (0, 0, 0, 0)),
        scratch_shapes=[
            pltpu.VMEM((4, 4, 256, NL), BF16),
            pltpu.VMEM((4, NL, 4 * NL), F32),
        ],
        cost_estimate=cost(4),
        compiler_params=pltpu.CompilerParams(vmem_limit_bytes=VMEM_LIMIT),
    )(*operands, w["wide"], w["narrow"], low_back)


def cells_step(kept):
    shape = (NV, NZ, NR, NL)
    return pl.pallas_call(
        cells_kernel,
        out_shape=jax.ShapeDtypeStruct(shape, F32),
        in_specs=[pl.BlockSpec(memory_space=pltpu.VMEM)],
        out_specs=pl.BlockSpec(memory_space=pltpu.HBM),
        scratch_shapes=[pltpu.VMEM(shape, F32), pltpu.SemaphoreType.DMA((NV,))],
        cost_estimate=cost(4),
        compiler_params=pltpu.CompilerParams(vmem_limit_bytes=VMEM_LIMIT),
    )(kept)


def rows_kernel(count_x, count_z, *refs):
    shares, out = refs[:count_x], refs[count_x + 1]
    me, me_y = lax.axis_index("gx"), lax.axis_index("gy")
    row = lax.broadcasted_iota(jnp.int32, (8, NL), 0)
    piece = lax.broadcasted_iota(jnp.int32, (8, NL), 1) // 21
    for r in range(count_x):
        at = pl.multiple_of(16 * (me ^ r), 16)
        for j in range(count_z):
            for z in range(4):
                out[j, z, pl.ds(at, 16), :] = shares[r][64 * j + 16 * z : 64 * j + 16 * z + 16, :]
    for r in range(count_x):
        i = me ^ r
        below = pl.multiple_of(16 * lax.rem(i + 1, count_x), 16)
        above = pl.multiple_of(16 * lax.rem(i + count_x - 1, count_x) + 8, 8)
        for j in range(count_z):
            tiles = [shares[r][64 * j + 8 * g : 64 * j + 8 * g + 8, :] for g in range(8)]
            low, high = jnp.zeros((8, NL), F32), jnp.zeros((8, NL), F32)
            for p in range(5):
                back = (21 * p - 105) % NL
                low = jnp.where(piece == p, pltpu.roll(tiles[p], back, 1), low)
                extra = tiles[5 + p // 2]
                extra = extra if p % 2 else pltpu.roll(extra, 4, 0)
                high = jnp.where(piece == p, pltpu.roll(extra, back, 1), high)
            for z in range(4):
                first = pltpu.roll(low, 8 - 2 * z, 0) if z else low
                last = pltpu.roll(high, z, 0) if z else high
                out[j, z, pl.ds(below, 8), :] += jnp.where(row < 2, first, 0.0)
                out[j, z, pl.ds(above, 8), :] += jnp.where(row == 7, last, 0.0)
    for j in range(count_z):
        place = lax.rem(2 * (lax.shift_right_logical(me_y, 1) ^ j) + lax.rem(me_y, 2), 4)
        turn = lax.rem(32 * place + NL - 1, NL)
        for z in range(4):
            for t in range(2 * count_x):
                rows = slice(8 * t, 8 * t + 8)
                out[j, z, rows, :] = pltpu.roll(out[j, z, rows, :], turn, 1)


def rows_step(pieces, count_z, after):
    vmem = pl.BlockSpec(memory_space=pltpu.VMEM)
    count_x = len(pieces)
    return pl.pallas_call(
        functools.partial(rows_kernel, count_x, count_z),
        out_shape=jax.ShapeDtypeStruct((count_z, 4, 16 * count_x, NL), F32),
        in_specs=[vmem] * count_x + [pl.BlockSpec(memory_space=pl.ANY)],
        out_specs=vmem,
        compiler_params=pltpu.CompilerParams(vmem_limit_bytes=VMEM_LIMIT),
    )(*pieces, after)


def coarse_kernel(count_x, count_y, own, other, out_hbm, out, sems):
    me = lax.axis_index("gy")
    me_z, is_even = lax.shift_right_logical(me, 1), lax.rem(me, 2) == 0
    lane = lax.broadcasted_iota(jnp.int32, (8, NL), 1)
    place = [lax.rem(lane + NL - 35 * v, NL) for v in range(NV)]

    def block(i, _):
        rows = pl.ds(pl.multiple_of(8 * i, 8), 8)
        for z in range(4):
            pieces = []
            for j in range(count_y // 2):
                mine, theirs = own[j ^ me_z, z, rows, :], other[j ^ me_z, z, rows, :]
                pieces += [jnp.where(is_even, mine, theirs), jnp.where(is_even, theirs, mine)]
            for v in range(NV):
                at = place[v]
                for t in range(count_y // 4):
                    total = jnp.where(at < 2, pieces[4 * t - 1], 0.0)
                    total += jnp.where(at == NL - 1, pieces[(4 * t + 4) % count_y], 0.0)
                    for q in range(4):
                        inside = (at >= 32 * q - 1) & (at < 32 * q + 34)
                        total += jnp.where(inside, pieces[4 * t + q], 0.0)
                    out[v, z, rows, NL * t : NL * (t + 1)] = pltpu.roll(total, NL - 35 * v, 1) if v else total
        return 0

    def copy(i):
        rows = pl.ds(pl.multiple_of(16 * i, 16), 16)
        return pltpu.make_async_copy(out.at[:, :, rows], out_hbm.at[:, :, rows], sems.at[i])

    def pair(i, _):
        block(2 * i, 0)
        block(2 * i + 1, 0)
        copy(i).start()
        return 0

    lax.fori_loop(0, count_x, pair, 0)
    for i in range(count_x):
        copy(i).wait()


def coarse_step(own, other, count_x, count_y):
    vmem = pl.BlockSpec(memory_space=pltpu.VMEM)
    shape = (NV, 4, 16 * count_x, 32 * count_y)
    return pl.pallas_call(
        functools.partial(coarse_kernel, count_x, count_y),
        out_shape=jax.ShapeDtypeStruct(shape, F32),
        in_specs=[vmem, vmem],
        out_specs=pl.BlockSpec(memory_space=pltpu.HBM),
        scratch_shapes=[pltpu.VMEM(shape, F32), pltpu.SemaphoreType.DMA((count_x,))],
        compiler_params=pltpu.CompilerParams(vmem_limit_bytes=VMEM_LIMIT),
    )(own, other)


def shifted(x, axis, step):
    count = lax.axis_size(axis)
    return lax.ppermute(x, axis, [(i, (i + step) % count) for i in range(count)])


def swapped(x, axis, distance):
    return lax.ppermute(x, axis, [(i, i ^ distance) for i in range(lax.axis_size(axis))])


def body(field, masks):
    count_x, count_y = lax.axis_size("gx"), lax.axis_size("gy")
    lifted, up, down, own_masks, share = first_step(field, masks)
    south = shifted(up, "gx", -1)
    north = shifted(down, "gx", 1)
    shares = [share] + [swapped(share, "gy", r) for r in range(2, count_y, 2)]
    parts, sides = edge_step(lift_step(lifted), lifted, north, south, own_masks)
    west = shifted(sides, "gy", 1)
    east = shifted(sides, "gy", -1)
    joined = join_step(shares, sides)
    pieces = [joined] + [swapped(joined, "gx", r) for r in range(1, count_x)]
    operands = (parts.reshape(4, NV * 8, ROWS, NL), west, east, own_masks, north, south)
    kept = high_step(low_step(*operands), *operands)
    own = rows_step(pieces, count_y // 2, kept)
    other = swapped(own, "gy", 1)
    return cells_step(kept), coarse_step(own, other, count_x, count_y)


def solution(mesh):
    placed = P(None, None, "gx", "gy")
    return jax.shard_map(
        body,
        mesh=mesh,
        in_specs=(placed, placed),
        out_specs=(placed, P()),
        check_vma=False,
    )
```

```python
import functools

import jax
import jax.numpy as jnp
import ml_dtypes
import numpy as np
from jax import lax
from jax.experimental import pallas as pl
from jax.experimental.pallas import tpu as pltpu
from jax.sharding import PartitionSpec as P

F32 = jnp.float32
BF16 = jnp.bfloat16
VMEM_LIMIT = 32 * 1024 * 1024

NV, NZ, NR, NL = 3, 16, 64, 128


def detail_row(k):
    return {2 * k + 1: 1.0, 2 * k: -0.5, 2 * k + 2: -0.5}


def smooth_row(k):
    row = {2 * k: 1.0}
    for j in (k - 1, k):
        for cell, value in detail_row(j).items():
            row[cell] = row.get(cell, 0.0) + 0.25 * value
    return row


def even_row(k):
    return {("s", k): 1.0, ("d", k - 1): -0.25, ("d", k): -0.25}


def odd_row(k):
    row = {("d", k): 1.0}
    for j in (k, k + 1):
        for name, value in even_row(j).items():
            row[name] = row.get(name, 0.0) + 0.5 * value
    return row


def as_bf16(matrix):
    cast = matrix.astype(ml_dtypes.bfloat16)
    assert (cast.astype(np.float64) == matrix).all()
    return cast


def combine(*terms):
    total = {}
    for factor, row in terms:
        for cell, value in row.items():
            total[cell] = total.get(cell, 0.0) + factor * value
    return total


def level_one_columns():
    names = {("s", k): k for k in range(65)}
    names.update({("d", k): 128 + k for k in range(65)})
    names[("d", -1)] = 128 + 65
    return names


def level_two_columns():
    names = {("s", k): k for k in range(33)}
    names.update({("d", k): 64 + k for k in range(33)})
    names[("d", -1)] = 64 + 33
    return names


def smooth_place(k):
    return k + 2


def beyond(n):
    return {"cell": 24 * n, "after": 24 * n + 8, "before": 24 * n + 16}


BEYOND_SMOOTH = {65: 96, 66: 104, -2: 112, -1: 120}


def own_row(kind, k, n):
    place = {name: 128 + lane for name, lane in beyond(n).items()}
    if kind == "d":
        if k == -1:
            return {place["before"]: 1.0, 0: -0.5}
        if k == 64:
            return {place["after"]: 1.0}
        return {(place["cell"] if y == 128 else y): value for y, value in detail_row(k).items()}
    if k in BEYOND_SMOOTH:
        row = {128 + BEYOND_SMOOTH[k]: 1.0}
        return combine((1.0, row), (1.0, {0: -0.125})) if k == -1 else row
    even = place["cell"] if k == 64 else 2 * k
    return combine((1.0, {even: 1.0}), (0.25, own_row("d", k - 1, n)), (0.25, own_row("d", k, n)))


@functools.lru_cache(maxsize=None)
def weights():
    w = {}
    names = level_one_columns()
    forward = np.zeros((4, 256, 256))
    inverse = np.zeros((256, 128))
    for (kind, k), column in names.items():
        for n in range(4):
            for place, value in own_row(kind, k, n).items():
                forward[n, place, column] += value
    for k in range(64):
        for y, row in ((2 * k, even_row(k)), (2 * k + 1, odd_row(k))):
            for name, value in row.items():
                inverse[names[name], y] += value
    short = np.zeros((144, 256))
    short[:128] = forward[0, :128]
    for i, lane in enumerate(beyond(0).values()):
        short[128 + i] = forward[0, 128 + lane]
    smooth = np.zeros((256, 128))
    for k in range(-2, 67):
        for place, value in own_row("s", k, 0).items():
            smooth[place, smooth_place(k)] += value
    names2 = level_two_columns()
    forward2 = np.zeros((128, 128))
    inverse2 = np.zeros((128, 128))
    for (kind, k), column in names2.items():
        for cell, value in (smooth_row(k) if kind == "s" else detail_row(k)).items():
            forward2[smooth_place(cell), column] += value
    for k in range(33):
        rows = [(2 * k, even_row(k))] + ([(2 * k + 1, odd_row(k))] if k < 32 else [])
        for y, row in rows:
            for name, value in row.items():
                inverse2[names2[name], y] += value
    back = np.zeros((256, 128))
    back[:65] = inverse[:65]
    back[128 : 128 + 65] = inverse[:65]
    spread = np.zeros((3, 128, 2, 128))
    for k in range(64):
        spread[0, k, 0, k] = 1
    spread[1, 0, 0, 64] = 1
    spread[2, 63, 0, 65] = 1
    for k in range(32):
        spread[0, 64 + k, 1, k] = 1
        spread[0, 64 + k, 1, 64 + k] = 1
    for base in (0, 64):
        spread[1, 64, 1, base + 32] = 1
        spread[2, 95, 1, base + 33] = 1
    w["wide"] = np.concatenate([short, spread.reshape(384, 256)], 0)
    own, beside = smooth[:128], smooth[128:]
    w["narrow"] = np.concatenate([inverse, own, own, beside, beside, back, forward2, inverse2], 0)
    edge = np.zeros((4, 128, 128))

    def put(n, lane, row):
        for z in range(8):
            for y, value in row.items():
                j = y - 120 if y >= 120 else y + 8
                edge[n, 16 * z + j, lane + z] += value

    part = {127: 1.0, 126: -0.5}
    for n in range(4):
        put(n, beyond(n)["cell"], {0: 1.0})
        put(n, beyond(n)["after"], detail_row(0))
        put(n, beyond(n)["before"], part)
    put(0, BEYOND_SMOOTH[65], smooth_row(1))
    put(0, BEYOND_SMOOTH[66], smooth_row(2))
    put(0, BEYOND_SMOOTH[-2], smooth_row(62))
    put(0, BEYOND_SMOOTH[-1], combine((1.0, {126: 1.0}), (0.25, detail_row(62)), (0.25, part)))
    w["edge"] = edge.reshape(512, 128)
    expand = np.zeros((2, 4, 128))
    for j in range(4):
        expand[0, j, 16 * j : 16 * j + 16] = 1
        expand[1, j, 64 + 8 * j : 64 + 8 * j + 8] = 1
    twice = combine(*[(value, smooth_row(k)) for k, value in smooth_row(0).items()])
    columns = np.zeros((2, 128, 128))
    for m in range(-1, 34):
        for t, value in twice.items():
            if 0 <= 4 * m + t < NL:
                columns[:, 4 * m + t, m + 1] = value
    rows = np.zeros((4, 32, 2, 64))
    for z in range(4):
        places = {m: m for m in range(16)}
        places.update({16: 16 + 2 * z, 17: 17 + 2 * z, -1: 16 + 15 - z})
        for m, place in places.items():
            for t, value in twice.items():
                if 0 <= 4 * m + t < NR:
                    rows[z, place, :, 4 * m + t] = value
    pad = np.zeros((8, 128))
    w["first"] = np.concatenate([columns.reshape(256, 128), rows.reshape(128, 128), expand.reshape(8, 128), pad], 0)
    return {name: as_bf16(matrix) for name, matrix in w.items()}


def two_terms(x):
    high = x.astype(BF16)
    low = (x - high.astype(F32)).astype(BF16)
    return high, low


def cost(gigaflops):
    return pl.CostEstimate(flops=gigaflops * 10**9, bytes_accessed=8 * 10**6, transcendentals=0)


def dot(a, b):
    return jnp.dot(a, b, preferred_element_type=F32)


def lift_planes(cells):
    half = len(cells) // 2
    even, odd = cells[0::2], cells[1::2]
    detail = [odd[k] - 0.5 * (even[k] + even[min(k + 1, half - 1)]) for k in range(half)]
    smooth = [even[k] + 0.25 * (detail[max(k - 1, 0)] + detail[k]) for k in range(half)]
    return smooth, detail


def unlift_planes(smooth, detail):
    half = len(smooth)
    even = [smooth[k] - 0.25 * (detail[max(k - 1, 0)] + detail[k]) for k in range(half)]
    out = []
    for k in range(half):
        out += [even[k], detail[k] + 0.5 * (even[k] + even[min(k + 1, half - 1)])]
    return out


def lift_rows(load, start):
    even, odd, after = load(start), load(start + 1), load(start + 2)
    before, odd_before = load(start - 2), load(start - 1)
    detail = odd - 0.5 * (even + after)
    detail_before = odd_before - 0.5 * (before + even)
    return even + 0.25 * (detail_before + detail), detail


def unlift_rows(smooth, detail, row):
    here, after = detail(row), detail(row + 1)
    even = smooth(row) - 0.25 * (detail(row - 1) + here)
    next_even = smooth(row + 1) - 0.25 * (here + after)
    return even, here + 0.5 * (even + next_even)


PITCH = 80


def first_kernel(
    field, masks_hbm, table_hbm, lifted, up, down, own_masks, share, cells, twice, masks, table, sems
):
    small = [
        pltpu.make_async_copy(masks_hbm, masks, sems.at[0]),
        pltpu.make_async_copy(table_hbm, table, sems.at[1]),
    ]
    copies = []
    for v in range(NV):
        for c in range(4):
            part = pl.ds(16 * c, 16)
            copies.append(pltpu.make_async_copy(field.at[v, :, part], cells.at[v, :, part], sems.at[2 + 4 * v + c]))
    for copy in small + copies:
        copy.start()
    for p in range(NV * NZ):
        lifted[p * PITCH : p * PITCH + 8, :] = jnp.zeros((8, NL), F32)
        lifted[p * PITCH + 72 : p * PITCH + 80, :] = jnp.zeros((8, NL), F32)
    for copy in small:
        copy.wait()
    for i, out, tile in ((0, up, 18), (1, down, 12)):
        total = jnp.zeros((7, NL), F32)
        for l in range(2):
            flags = masks[l, i].astype(F32).astype(BF16)
            spread = table[384 + 4 * l : 388 + 4 * l, :]
            total += lax.dot_general(flags, spread, (((0,), (0,)), ((), ())), preferred_element_type=F32)
        own_masks[i] = jnp.concatenate([total, jnp.zeros((1, NL), F32)], 0)
        out[tile] = own_masks[i]

    for v in range(NV):
        for t in range(8):
            if t % 2 == 0:
                copies[4 * v + t // 2].wait()
            smooth, detail = lift_planes([cells[v, z, 8 * t : 8 * t + 8, :] for z in range(NZ)])
            for k, tile in enumerate(smooth + detail):
                start = (v * NZ + k) * PITCH + 8 + 8 * t
                lifted[start : start + 8, :] = tile
            for k, tile in enumerate(lift_planes(smooth)[0]):
                twice[v * 4 + k, 8 * t : 8 * t + 8, :] = tile
        for bz in range(2):

            def row(x):
                return lifted[pl.ds((v * NZ + bz * 8) * PITCH + 8 + x, 8, stride=PITCH), :]

            x = [row(j) for j in range(7 if bz == 0 else 3)]
            first = x[1] - 0.5 * (x[0] + x[2])
            up[v * 6 + bz] = x[0]
            up[v * 6 + 2 + bz] = first
            y = {j: row(j) for j in (range(58, 64) if bz == 0 else (62, 63))}
            part = y[63] - 0.5 * y[62]
            down[v * 4 + bz] = part
            if bz == 0:
                second = x[3] - 0.5 * (x[2] + x[4])
                third = x[5] - 0.5 * (x[4] + x[6])
                up[v * 6 + 4] = x[2] + 0.25 * (first + second)
                up[v * 6 + 5] = x[4] + 0.25 * (second + third)
                before = y[59] - 0.5 * (y[58] + y[60])
                last = y[61] - 0.5 * (y[60] + y[62])
                down[v * 4 + 2] = y[60] + 0.25 * (before + last)
                down[v * 4 + 3] = y[62] + 0.25 * (last + part)

    total = jnp.zeros((80, NL), F32)
    for v in range(NV):
        main, extra = [], jnp.zeros((16, NL), F32)
        for z in range(4):
            terms = jnp.concatenate(two_terms(twice[v * 4 + z]), 0)
            part = dot(table[256 + 32 * z : 288 + 32 * z, :], terms)
            main.append(part[:16])
            extra += part[16:]
        terms = jnp.concatenate(two_terms(jnp.concatenate(main + [extra], 0)), 1)
        part = dot(terms, table[0:256, :])
        total += pltpu.roll(part, 35 * v, 1) if v else part
    lane = lax.broadcasted_iota(jnp.int32, (8, NL), 1)
    spare = (lane >= 105) & (lane < 126)
    upper = lax.broadcasted_iota(jnp.int32, (8, NL), 0) < 4
    below, above = total[64:72], total[72:80]
    pieces = [pltpu.roll(above, 105 - 21 * p, 1) for p in range(5)]
    for g in range(8):
        if g < 5:
            extra = pltpu.roll(below, 105 - 21 * g, 1)
        else:
            extra = pltpu.roll(pieces[2 * g - 10], 4, 0)
            extra = jnp.where(upper, extra, pieces[2 * g - 9] if g < 7 else 0.0)
        share[8 * g : 8 * g + 8, :] = jnp.where(spare, extra, total[8 * g : 8 * g + 8])


def in_hbm(x):
    return pltpu.with_memory_space_constraint(x, pltpu.HBM)


def first_step(field, masks):
    vmem = pl.BlockSpec(memory_space=pltpu.VMEM)
    shapes = [(NV * NZ * PITCH, NL), (19, 8, NL), (13, 8, NL), (2, 8, NL), (64, NL)]
    return pl.pallas_call(
        first_kernel,
        out_shape=[jax.ShapeDtypeStruct(s, F32) for s in shapes],
        in_specs=[pl.BlockSpec(memory_space=pltpu.HBM)] * 3,
        out_specs=[vmem] * 5,
        scratch_shapes=[
            pltpu.VMEM((NV, NZ, NR, NL), F32),
            pltpu.VMEM((NV * 4, NR, NL), F32),
            pltpu.VMEM((2, 2, 4, 7), jnp.int32),
            pltpu.VMEM((400, NL), BF16),
            pltpu.SemaphoreType.DMA((4 * NV + 2,)),
        ],
        compiler_params=pltpu.CompilerParams(vmem_limit_bytes=VMEM_LIMIT),
    )(*[in_hbm(x) for x in (field, masks.transpose(0, 2, 3, 1), jnp.asarray(weights()["first"]))])


ROWS = 40


def lift_kernel(lifted, parts):
    def lift(step, _):
        v, bz = step // 2, lax.rem(step, 2)
        for z in range(8):
            start = pl.multiple_of((step * 8 + z) * PITCH, 8)
            for t in range(4):
                pair = lift_rows(lambda s: lifted[pl.ds(start + 16 * t + s, 8, stride=2), :], 8)
                for bx in range(2):
                    plane = (2 * bz + bx) * 24 + v * 8 + z
                    parts[pl.ds(pl.multiple_of(plane * ROWS + 8 * t, 8), 8), :] = pair[bx]
        return 0

    lax.fori_loop(0, NV * 2, lift, 0)


def lift_step(lifted):
    vmem = pl.BlockSpec(memory_space=pltpu.VMEM)
    return pl.pallas_call(
        lift_kernel,
        out_shape=jax.ShapeDtypeStruct((4 * NV * 8 * ROWS, NL), F32),
        in_specs=[vmem],
        out_specs=vmem,
        compiler_params=pltpu.CompilerParams(vmem_limit_bytes=VMEM_LIMIT),
    )(lifted)


def edge_kernel(parts_in, lifted, north, south, own_masks, table_hbm, parts, sides, packed, table, sem):
    copy = pltpu.make_async_copy(table_hbm, table, sem.at[0])
    copy.start()
    for p in range(4 * NV * 8):
        parts[p * ROWS + 32 : p * ROWS + 40, :] = jnp.zeros((8, NL), F32)
    for v in range(NV):
        for bz in range(2):

            def cell(x):
                return lifted[pl.ds((v * NZ + bz * 8) * PITCH + 8 + x, 8, stride=PITCH), :]

            def at(bx, r):
                return pl.ds(((2 * bz + bx) * 24 + v * 8) * ROWS + r, 8, stride=ROWS)

            before, after, detail = north[v * 4 + bz], south[v * 6 + bz], south[v * 6 + 2 + bz]
            start = cell(0)
            last = cell(63) - 0.5 * (cell(62) + after)
            parts[at(0, 0), :] = parts[at(0, 0), :] + 0.25 * before
            parts[at(0, 31), :] = parts[at(0, 31), :] - 0.125 * after
            parts[at(1, 31), :] = parts[at(1, 31), :] - 0.5 * after
            parts[at(0, 32), :] = after + 0.25 * (last + detail)
            parts[at(1, 32), :] = detail
            parts[at(1, 39), :] = before - 0.5 * start
            if bz == 0:
                parts[at(0, 33), :] = south[v * 6 + 4]
                parts[at(0, 34), :] = south[v * 6 + 5]
                parts[at(0, 38), :] = north[v * 4 + 2]
                parts[at(0, 39), :] = north[v * 4 + 3] - 0.125 * start

    lane = lax.broadcasted_iota(jnp.int32, (8, NL), 1) // 16

    def pack(v, _):
        for n in range(4):
            for t in range(5):
                tile = jnp.zeros((8, NL), F32)
                for z in range(8):
                    start = (n * 24 + v * 8 + z) * ROWS + 8 * t
                    x = parts[pl.ds(pl.multiple_of(start, 8), 8), :]
                    tile = jnp.where(lane == z, pltpu.roll(x, (8 + 16 * z) % NL, 1), tile)
                packed[pl.ds(pl.multiple_of(n * 120 + v * ROWS + 8 * t, 8), 8), :] = tile
        return 0

    lax.fori_loop(0, NV, pack, 0)
    copy.wait()
    terms = [two_terms(packed[n * 120 : (n + 1) * 120, :]) for n in range(4)]
    high, low = [jnp.concatenate(part, 1) for part in zip(*terms)]
    sides[0:120, :] = dot(high, table[...]) + dot(low, table[...])
    sides[120:128, :] = north[12]
    sides[128:136, :] = own_masks[0]
    sides[136:144, :] = own_masks[1]
    sides[144:152, :] = south[18]


def edge_step(parts, lifted, north, south, own_masks):
    vmem = pl.BlockSpec(memory_space=pltpu.VMEM)
    shapes = [(4 * NV * 8 * ROWS, NL), (152, NL)]
    return pl.pallas_call(
        edge_kernel,
        out_shape=[jax.ShapeDtypeStruct(s, F32) for s in shapes],
        in_specs=[vmem] * 5 + [pl.BlockSpec(memory_space=pltpu.HBM)],
        out_specs=[vmem] * 2,
        input_output_aliases={0: 0},
        cost_estimate=cost(20),
        scratch_shapes=[pltpu.VMEM((480, NL), F32), pltpu.VMEM((512, NL), BF16), pltpu.SemaphoreType.DMA((1,))],
        compiler_params=pltpu.CompilerParams(vmem_limit_bytes=VMEM_LIMIT),
    )(parts, lifted, north, south, own_masks, in_hbm(jnp.asarray(weights()["edge"])))


def join_kernel(*refs):
    shares, out = refs[:-2], refs[-1]
    for n, piece in enumerate(shares):
        out[64 * n : 64 * (n + 1), :] = piece[...]


def join_step(shares, after):
    vmem = pl.BlockSpec(memory_space=pltpu.VMEM)
    return pl.pallas_call(
        join_kernel,
        out_shape=jax.ShapeDtypeStruct((64 * len(shares), NL), F32),
        in_specs=[vmem] * len(shares) + [pl.BlockSpec(memory_space=pl.ANY)],
        out_specs=vmem,
        cost_estimate=cost(20),
        compiler_params=pltpu.CompilerParams(vmem_limit_bytes=VMEM_LIMIT),
    )(*shares, after)


def mask_lanes(west, east, own_masks, north_mask, south_mask, wide):
    masks = [jnp.concatenate([ref[120 + 8 * i : 128 + 8 * i, :] for i in range(4)], 0) for ref in (east, west)]
    own = jnp.concatenate([north_mask[0], own_masks[0], own_masks[1], south_mask[0]], 0)
    flags = jnp.concatenate([own] + masks, 1).astype(BF16)
    return dot(flags, wide[144:528, :])


def beside_tiles(west, east, at, count):
    lane = lax.broadcasted_iota(jnp.int32, (count, NL), 1)
    from_west = (lane >= 112) | ((lane < 96) & (lax.rem(lane, 24) >= 16))
    tiles = []
    for v in range(NV):
        rows = slice(v * ROWS + at, v * ROWS + at + count)
        beside = jnp.where(from_west, west[rows, :], east[rows, :])
        tiles += [pltpu.roll(beside, NL - z, 1) if z else beside for z in range(8)]
    return tiles


def beside_terms(west, east, at, count):
    return jnp.concatenate(two_terms(jnp.concatenate(beside_tiles(west, east, at, count), 0)), 1)


def own_terms(planes, at, count):
    return jnp.concatenate(two_terms(planes[:, at : at + count, :].reshape(24 * count, NL)), 1)


def main_kernel(
    parts, flat, west, east, own_masks, north_mask, south_mask, wide, narrow,
    kept,
    gain2, low, second, kept2, low_back, gain, sides_wide, turned,
):
    inverse, smooth_own, smooth_beside = narrow.at[0:256], narrow.at[256:512], narrow.at[512:768]
    back, forward2, inverse2 = narrow.at[768:1024], narrow.at[1024:1152], narrow.at[1152:1280]
    lanes = mask_lanes(west, east, own_masks, north_mask, south_mask, wide)
    lane64 = lax.broadcasted_iota(jnp.int32, (1, NL), 1) < 64
    forward2_f = forward2[...].astype(F32)
    for ib in range(4):
        for n in range(4):
            b = 8 * ib + 4 * (n // 2) + n % 2 - 1
            smooth_two = lanes[b : b + 1, NL:] if n else jnp.ones((1, NL), F32)
            row = jnp.where(lane64, smooth_two, lanes[b + 2 : b + 3, NL:])
            both = dot((forward2_f * row).astype(BF16), inverse2[...]).astype(BF16)
            gain2[ib, n, 0:128, :] = both
            gain2[ib, n, 128:256, :] = both

    for at, count in ((0, 16), (16, 16), (32, 8)):
        part = dot(own_terms(parts.at[0], at, count), smooth_own[...])
        part += dot(beside_terms(west, east, at, count), smooth_beside[...])
        part = part.reshape(24, count, NL)
        if at < 32:
            low[:, 8 + at : 8 + at + count, :] = part
            if at == 0:
                low[:, 56:64, :] = part[:, 0:8]
        else:
            low[:, 0:8, :] = part
            low[:, 40:48, :] = part
            low[:, 48:56, :] = part

    def rows_two(v, _):
        for t in range(3):
            lifted = [
                lift_rows(lambda s: low[v * 8 + p, pl.ds(16 * t + s, 8, stride=2), :], 8) for p in range(8)
            ]
            for bx in range(2):
                smooth, detail = lift_planes([pair[bx] for pair in lifted])
                for bz, part in ((0, smooth), (1, detail)):
                    for z in range(4):
                        second[2 * bz + bx, t, pl.ds(pl.multiple_of((v * 4 + z) * 8, 8), 8), :] = part[z]
        return 0

    lax.fori_loop(0, NV, rows_two, 0)
    for n in range(4):
        for t in range(3):
            terms = jnp.concatenate(two_terms(second[n, t]), 1)
            if t < 2:
                kept2[n, :, 8 + 8 * t : 16 + 8 * t, :] = dot(terms, gain2[t + 1, n]).reshape(NV * 4, 8, NL)
            else:
                kept2[n, :, 0:8, :] = dot(terms, gain2[0, n]).reshape(NV * 4, 8, NL)
                kept2[n, :, 24:32, :] = dot(terms, gain2[3, n]).reshape(NV * 4, 8, NL)

    def back_two(v, _):
        for t in range(3):
            pairs = {}
            for bz in range(2):
                for z in range(4):
                    p = v * 4 + z
                    if t < 2:
                        pairs[bz, z] = unlift_rows(
                            lambda r: kept2[2 * bz, p, pl.ds(r, 8), :],
                            lambda r: kept2[2 * bz + 1, p, pl.ds(r, 8), :],
                            8 + 8 * t,
                        )
                    else:
                        even = kept2[2 * bz, p, 24:32, :] - 0.25 * (
                            kept2[2 * bz + 1, p, 23:31, :] + kept2[2 * bz + 1, p, 24:32, :]
                        )
                        pairs[bz, z] = (even, even)
            for parity in range(2 if t < 2 else 1):
                planes = unlift_planes([pairs[0, z][parity] for z in range(4)], [pairs[1, z][parity] for z in range(4)])
                for z in range(8):
                    low_back[pl.ds((v * 8 + z) * 48 + 16 * t + parity, 8, stride=2), :] = planes[z]
        return 0

    lax.fori_loop(0, NV, back_two, 0)

    forward_f = wide[0:144, :].astype(F32)
    for ib in range(4):
        sides_wide[ib] = jnp.zeros((NL, 4 * NL), F32)
    for ib in range(4):
        for n in range(4):
            b = 8 * ib + 4 * (n // 2) + n % 2 - 1
            smooth_one = lanes[b : b + 1, 0:NL] if n else jnp.zeros((1, NL), F32)
            row = jnp.concatenate([smooth_one, lanes[b + 2 : b + 3, 0:NL]], 1)
            both = dot((forward_f * row).astype(BF16), inverse[...])
            main = both[0:128].astype(BF16)
            gain[ib, n, 0:128, :] = main
            gain[ib, n, 128:256, :] = main
            for i in range(3):
                at = 24 * n + 8 * i
                sides_wide[ib, at : at + 1, n * NL : (n + 1) * NL] = both[128 + i : 129 + i]

    gain_sides = []
    for ib in range(4):
        side = sides_wide[ib].astype(BF16)
        gain_sides.append(jnp.concatenate([side, side], 0))
    def put(n, p, at, rows):
        start = pl.multiple_of((n * 24 + p) * 48 + 8 + at, 8)
        kept[pl.ds(start, rows.shape[0]), :] = rows

    def row_of(ref, first, pitch):
        return ref[pl.ds(first, 24, stride=pitch), :]

    for ib in range(2):
        product = dot(beside_terms(west, east, 16 * ib, 16), gain_sides[ib + 1])
        for n in range(4):
            for p in range(24):
                put(n, p, 16 * ib, product[16 * p : 16 * p + 16, n * NL : (n + 1) * NL])

    def keep(n, _):
        for ib in range(2):
            product = dot(own_terms(parts.at[n], 16 * ib, 16), gain[ib + 1, n])
            for p in range(24):
                start = pl.ds(pl.multiple_of((n * 24 + p) * 48 + 8 + 16 * ib, 8), 16)
                kept[start, :] += product[16 * p : 16 * p + 16]
        return 0

    lax.fori_loop(0, 4, keep, 0)
    for ib in range(2):
        rows = jnp.concatenate([low_back[48 * p + 16 * ib : 48 * p + 16 * ib + 16, :] for p in range(24)], 0)
        product = dot(jnp.concatenate(two_terms(rows), 1), back[...])
        for p in range(24):
            start = 48 * p + 8 + 16 * ib
            kept[start : start + 16, :] += product[16 * p : 16 * p + 16]
    tiles = beside_tiles(west, east, 32, 8)
    for p in range(24):
        turned[8 * p : 8 * p + 8, :] = tiles[p]
    for first, ib, place, row in ((0, 3, 40, 32), (7, 0, 7, 39)):
        beside = dot(jnp.concatenate(two_terms(row_of(turned, first, 8)), 1), gain_sides[ib])
        for n in range(4) if ib else (1, 3):
            own = jnp.concatenate(two_terms(row_of(flat, n * 24 * ROWS + row, ROWS)), 1)
            total = beside[:, n * NL : (n + 1) * NL] + dot(own, gain[ib, n])
            if n == 0:
                total += dot(jnp.concatenate(two_terms(row_of(low_back, row, 48)), 1), back[...])
            kept[pl.ds(n * 24 * 48 + place, 24, stride=48), :] = total


def cells_kernel(kept, out, cells, sems):
    def back_one(step, _):
        v, t = step // 4, step % 4
        pairs = {}
        for bz in range(2):
            for z in range(8):
                p = v * 8 + z
                pairs[bz, z] = unlift_rows(
                    lambda r: kept[2 * bz, p, pl.ds(8 * t + r, 8), :],
                    lambda r: kept[2 * bz + 1, p, pl.ds(8 * t + r, 8), :],
                    8,
                )
        for parity in range(2):
            planes = unlift_planes([pairs[0, z][parity] for z in range(8)], [pairs[1, z][parity] for z in range(8)])
            for z in range(NZ):
                cells[v, z, pl.ds(16 * t + parity, 8, stride=2), :] = planes[z]
        return 0

    def copy(step):
        v, rows = step // 4, pl.ds(pl.multiple_of(16 * (step % 4), 16), 16)
        return pltpu.make_async_copy(cells.at[v, :, rows], out.at[v, :, rows], sems.at[step])

    def one(step, _):
        back_one(step, 0)
        copy(step).start()
        return 0

    lax.fori_loop(0, NV * 4, one, 0)
    for step in range(NV * 4):
        copy(step).wait()


def main_specs():
    vmem = pl.BlockSpec(memory_space=pltpu.VMEM)
    return [
        vmem, vmem, vmem, vmem, vmem,
        pl.BlockSpec((1, 8, NL), lambda i: (12, 0, 0)), pl.BlockSpec((1, 8, NL), lambda i: (18, 0, 0)),
        vmem, vmem,
    ]


def main_step(flat, *operands):
    w = weights()
    return pl.pallas_call(
        main_kernel,
        grid=(1,),
        out_shape=jax.ShapeDtypeStruct((4 * NV * 8 * 48, NL), F32),
        in_specs=main_specs(),
        out_specs=pl.BlockSpec((4 * NV * 8 * 48, NL), lambda i: (0, 0)),
        scratch_shapes=[
            pltpu.VMEM((4, 4, 256, NL), BF16),
            pltpu.VMEM((NV * 8, 64, NL), F32),
            pltpu.VMEM((4, 3, NV * 32, NL), F32),
            pltpu.VMEM((4, NV * 4, 40, NL), F32),
            pltpu.VMEM((NV * 8 * 48, NL), F32),
            pltpu.VMEM((4, 4, 256, NL), BF16),
            pltpu.VMEM((4, NL, 4 * NL), F32),
            pltpu.VMEM((NV * 64, NL), F32),
        ],
        cost_estimate=cost(8),
        compiler_params=pltpu.CompilerParams(vmem_limit_bytes=VMEM_LIMIT),
    )(flat.reshape(4, NV * 8, ROWS, NL), flat, *operands, w["wide"], w["narrow"])


def cells_step(kept):
    shape = (NV, NZ, NR, NL)
    return pl.pallas_call(
        cells_kernel,
        out_shape=jax.ShapeDtypeStruct(shape, F32),
        in_specs=[pl.BlockSpec(memory_space=pltpu.VMEM)],
        out_specs=pl.BlockSpec(memory_space=pltpu.HBM),
        scratch_shapes=[pltpu.VMEM(shape, F32), pltpu.SemaphoreType.DMA((NV * 4,))],
        cost_estimate=cost(4),
        compiler_params=pltpu.CompilerParams(vmem_limit_bytes=VMEM_LIMIT),
    )(kept)


def rows_kernel(count_x, count_z, *refs):
    shares, out = refs[:count_x], refs[count_x + 1]
    me, me_y = lax.axis_index("gx"), lax.axis_index("gy")
    row = lax.broadcasted_iota(jnp.int32, (8, NL), 0)
    piece = lax.broadcasted_iota(jnp.int32, (8, NL), 1) // 21
    turns = []
    for j in range(count_z):
        place = lax.rem(2 * (lax.shift_right_logical(me_y, 1) ^ j) + lax.rem(me_y, 2), 4)
        turns.append(lax.rem(32 * place + NL - 1, NL))
    for r in range(count_x):
        at = pl.multiple_of(16 * (me ^ r), 16)
        for j in range(count_z):
            for z in range(4):
                start = 64 * j + 16 * z
                out[j, z, pl.ds(at, 16), :] = pltpu.roll(shares[r][start : start + 16, :], turns[j], 1)
    for r in range(count_x):
        i = me ^ r
        below = pl.multiple_of(16 * lax.rem(i + 1, count_x), 16)
        above = pl.multiple_of(16 * lax.rem(i + count_x - 1, count_x) + 8, 8)
        for j in range(count_z):
            tiles = [shares[r][64 * j + 8 * g : 64 * j + 8 * g + 8, :] for g in range(8)]
            low, high = jnp.zeros((8, NL), F32), jnp.zeros((8, NL), F32)
            for p in range(5):
                back = (21 * p - 105) % NL
                low = jnp.where(piece == p, pltpu.roll(tiles[p], back, 1), low)
                extra = tiles[5 + p // 2]
                extra = extra if p % 2 else pltpu.roll(extra, 4, 0)
                high = jnp.where(piece == p, pltpu.roll(extra, back, 1), high)
            low, high = pltpu.roll(low, turns[j], 1), pltpu.roll(high, turns[j], 1)
            for z in range(4):
                first = pltpu.roll(low, 8 - 2 * z, 0) if z else low
                last = pltpu.roll(high, z, 0) if z else high
                out[j, z, pl.ds(below, 8), :] += jnp.where(row < 2, first, 0.0)
                out[j, z, pl.ds(above, 8), :] += jnp.where(row == 7, last, 0.0)


def rows_step(pieces, count_z, after):
    vmem = pl.BlockSpec(memory_space=pltpu.VMEM)
    count_x = len(pieces)
    return pl.pallas_call(
        functools.partial(rows_kernel, count_x, count_z),
        out_shape=jax.ShapeDtypeStruct((count_z, 4, 16 * count_x, NL), F32),
        in_specs=[vmem] * count_x + [pl.BlockSpec(memory_space=pl.ANY)],
        out_specs=vmem,
        compiler_params=pltpu.CompilerParams(vmem_limit_bytes=VMEM_LIMIT),
    )(*pieces, after)


def coarse_kernel(count_x, count_y, own, other, out_hbm, out, sems):
    me = lax.axis_index("gy")
    me_z, is_even = lax.shift_right_logical(me, 1), lax.rem(me, 2) == 0
    lane = lax.broadcasted_iota(jnp.int32, (8, NL), 1)
    place = [lax.rem(lane + NL - 35 * v, NL) for v in range(NV)]

    def block(i, _):
        rows = pl.ds(pl.multiple_of(8 * i, 8), 8)
        for z in range(4):
            pieces = []
            for j in range(count_y // 2):
                mine, theirs = own[j ^ me_z, z, rows, :], other[j ^ me_z, z, rows, :]
                pieces += [jnp.where(is_even, mine, theirs), jnp.where(is_even, theirs, mine)]
            for v in range(NV):
                at = place[v]
                for t in range(count_y // 4):
                    total = jnp.where(at < 2, pieces[4 * t - 1], 0.0)
                    total += jnp.where(at == NL - 1, pieces[(4 * t + 4) % count_y], 0.0)
                    for q in range(4):
                        inside = (at >= 32 * q - 1) & (at < 32 * q + 34)
                        total += jnp.where(inside, pieces[4 * t + q], 0.0)
                    out[v, z, rows, NL * t : NL * (t + 1)] = pltpu.roll(total, NL - 35 * v, 1) if v else total
        return 0

    def copy(i):
        rows = pl.ds(pl.multiple_of(16 * i, 16), 16)
        return pltpu.make_async_copy(out.at[:, :, rows], out_hbm.at[:, :, rows], sems.at[i])

    def pair(i, _):
        block(2 * i, 0)
        block(2 * i + 1, 0)
        copy(i).start()
        return 0

    lax.fori_loop(0, count_x, pair, 0)
    for i in range(count_x):
        copy(i).wait()


def coarse_step(own, other, count_x, count_y):
    vmem = pl.BlockSpec(memory_space=pltpu.VMEM)
    shape = (NV, 4, 16 * count_x, 32 * count_y)
    return pl.pallas_call(
        functools.partial(coarse_kernel, count_x, count_y),
        out_shape=jax.ShapeDtypeStruct(shape, F32),
        in_specs=[vmem, vmem],
        out_specs=pl.BlockSpec(memory_space=pltpu.HBM),
        scratch_shapes=[pltpu.VMEM(shape, F32), pltpu.SemaphoreType.DMA((count_x,))],
        compiler_params=pltpu.CompilerParams(vmem_limit_bytes=VMEM_LIMIT),
    )(own, other)


def shifted(x, axis, step):
    count = lax.axis_size(axis)
    return lax.ppermute(x, axis, [(i, (i + step) % count) for i in range(count)])


def swapped(x, axis, distance):
    return lax.ppermute(x, axis, [(i, i ^ distance) for i in range(lax.axis_size(axis))])


def body(field, masks):
    count_x, count_y = lax.axis_size("gx"), lax.axis_size("gy")
    lifted, up, down, own_masks, share = first_step(field, masks)
    south = shifted(up, "gx", -1)
    north = shifted(down, "gx", 1)
    shares = [share] + [swapped(share, "gy", r) for r in range(2, count_y, 2)]
    parts, sides = edge_step(lift_step(lifted), lifted, north, south, own_masks)
    west = shifted(sides, "gy", 1)
    east = shifted(sides, "gy", -1)
    joined = join_step(shares, sides)
    pieces = [joined] + [swapped(joined, "gx", r) for r in range(1, count_x)]
    kept = main_step(parts, west, east, own_masks, north, south)
    own = rows_step(pieces, count_y // 2, kept)
    other = swapped(own, "gy", 1)
    return cells_step(kept.reshape(4, NV * 8, 48, NL)), coarse_step(own, other, count_x, count_y)


def solution(mesh):
    placed = P(None, None, "gx", "gy")
    return jax.shard_map(
        body,
        mesh=mesh,
        in_specs=(placed, placed),
        out_specs=(placed, P()),
        check_vma=False,
    )
```

```python
import functools

import jax
import jax.numpy as jnp
import ml_dtypes
import numpy as np
from jax import lax
from jax.experimental import pallas as pl
from jax.experimental.pallas import tpu as pltpu
from jax.sharding import PartitionSpec as P

F32 = jnp.float32
BF16 = jnp.bfloat16
VMEM_LIMIT = 32 * 1024 * 1024

NV, NZ, NR, NL = 3, 16, 64, 128


def detail_row(k):
    return {2 * k + 1: 1.0, 2 * k: -0.5, 2 * k + 2: -0.5}


def smooth_row(k):
    row = {2 * k: 1.0}
    for j in (k - 1, k):
        for cell, value in detail_row(j).items():
            row[cell] = row.get(cell, 0.0) + 0.25 * value
    return row


def even_row(k):
    return {("s", k): 1.0, ("d", k - 1): -0.25, ("d", k): -0.25}


def odd_row(k):
    row = {("d", k): 1.0}
    for j in (k, k + 1):
        for name, value in even_row(j).items():
            row[name] = row.get(name, 0.0) + 0.5 * value
    return row


def as_bf16(matrix):
    cast = matrix.astype(ml_dtypes.bfloat16)
    assert (cast.astype(np.float64) == matrix).all()
    return cast


def combine(*terms):
    total = {}
    for factor, row in terms:
        for cell, value in row.items():
            total[cell] = total.get(cell, 0.0) + factor * value
    return total


def level_one_columns():
    names = {("s", k): k for k in range(65)}
    names.update({("d", k): 128 + k for k in range(65)})
    names[("d", -1)] = 128 + 65
    return names


def level_two_columns():
    names = {("s", k): k for k in range(33)}
    names.update({("d", k): 64 + k for k in range(33)})
    names[("d", -1)] = 64 + 33
    return names


def smooth_place(k):
    return k + 2


def beyond(n):
    return {"cell": 24 * n, "after": 24 * n + 8, "before": 24 * n + 16}


BEYOND_SMOOTH = {65: 96, 66: 104, -2: 112, -1: 120}


def own_row(kind, k, n):
    place = {name: 128 + lane for name, lane in beyond(n).items()}
    if kind == "d":
        if k == -1:
            return {place["before"]: 1.0, 0: -0.5}
        if k == 64:
            return {place["after"]: 1.0}
        return {(place["cell"] if y == 128 else y): value for y, value in detail_row(k).items()}
    if k in BEYOND_SMOOTH:
        row = {128 + BEYOND_SMOOTH[k]: 1.0}
        return combine((1.0, row), (1.0, {0: -0.125})) if k == -1 else row
    even = place["cell"] if k == 64 else 2 * k
    return combine((1.0, {even: 1.0}), (0.25, own_row("d", k - 1, n)), (0.25, own_row("d", k, n)))


@functools.lru_cache(maxsize=None)
def weights():
    w = {}
    names = level_one_columns()
    forward = np.zeros((4, 256, 256))
    inverse = np.zeros((256, 128))
    for (kind, k), column in names.items():
        for n in range(4):
            for place, value in own_row(kind, k, n).items():
                forward[n, place, column] += value
    for k in range(64):
        for y, row in ((2 * k, even_row(k)), (2 * k + 1, odd_row(k))):
            for name, value in row.items():
                inverse[names[name], y] += value
    short = np.zeros((144, 256))
    short[:128] = forward[0, :128]
    for i, lane in enumerate(beyond(0).values()):
        short[128 + i] = forward[0, 128 + lane]
    smooth = np.zeros((256, 128))
    for k in range(-2, 67):
        for place, value in own_row("s", k, 0).items():
            smooth[place, smooth_place(k)] += value
    names2 = level_two_columns()
    forward2 = np.zeros((128, 128))
    inverse2 = np.zeros((128, 128))
    for (kind, k), column in names2.items():
        for cell, value in (smooth_row(k) if kind == "s" else detail_row(k)).items():
            forward2[smooth_place(cell), column] += value
    for k in range(33):
        rows = [(2 * k, even_row(k))] + ([(2 * k + 1, odd_row(k))] if k < 32 else [])
        for y, row in rows:
            for name, value in row.items():
                inverse2[names2[name], y] += value
    back = np.zeros((256, 128))
    back[:65] = inverse[:65]
    back[128 : 128 + 65] = inverse[:65]
    spread = np.zeros((3, 128, 2, 128))
    for k in range(64):
        spread[0, k, 0, k] = 1
    spread[1, 0, 0, 64] = 1
    spread[2, 63, 0, 65] = 1
    for k in range(32):
        spread[0, 64 + k, 1, k] = 1
        spread[0, 64 + k, 1, 64 + k] = 1
    for base in (0, 64):
        spread[1, 64, 1, base + 32] = 1
        spread[2, 95, 1, base + 33] = 1
    w["wide"] = np.concatenate([short, spread.reshape(384, 256)], 0)
    own, beside = smooth[:128], smooth[128:]
    w["narrow"] = np.concatenate([inverse, own, own, beside, beside, back, forward2, inverse2], 0)
    edge = np.zeros((4, 128, 128))

    def put(n, lane, row):
        for z in range(8):
            for y, value in row.items():
                j = y - 120 if y >= 120 else y + 8
                edge[n, 16 * z + j, lane + z] += value

    part = {127: 1.0, 126: -0.5}
    for n in range(4):
        put(n, beyond(n)["cell"], {0: 1.0})
        put(n, beyond(n)["after"], detail_row(0))
        put(n, beyond(n)["before"], part)
    put(0, BEYOND_SMOOTH[65], smooth_row(1))
    put(0, BEYOND_SMOOTH[66], smooth_row(2))
    put(0, BEYOND_SMOOTH[-2], smooth_row(62))
    put(0, BEYOND_SMOOTH[-1], combine((1.0, {126: 1.0}), (0.25, detail_row(62)), (0.25, part)))
    w["edge"] = edge.reshape(512, 128)
    expand = np.zeros((2, 4, 128))
    for j in range(4):
        expand[0, j, 16 * j : 16 * j + 16] = 1
        expand[1, j, 64 + 8 * j : 64 + 8 * j + 8] = 1
    twice = combine(*[(value, smooth_row(k)) for k, value in smooth_row(0).items()])
    columns = np.zeros((2, 128, 128))
    for m in range(-1, 34):
        for t, value in twice.items():
            if 0 <= 4 * m + t < NL:
                columns[:, 4 * m + t, m + 1] = value
    rows = np.zeros((4, 32, 2, 64))
    for z in range(4):
        places = {m: m for m in range(16)}
        places.update({16: 16 + 2 * z, 17: 17 + 2 * z, -1: 16 + 15 - z})
        for m, place in places.items():
            for t, value in twice.items():
                if 0 <= 4 * m + t < NR:
                    rows[z, place, :, 4 * m + t] = value
    pad = np.zeros((8, 128))
    w["first"] = np.concatenate([columns.reshape(256, 128), rows.reshape(128, 128), expand.reshape(8, 128), pad], 0)
    return {name: as_bf16(matrix) for name, matrix in w.items()}


def two_terms(x):
    high = x.astype(BF16)
    low = (x - high.astype(F32)).astype(BF16)
    return high, low


def cost(gigaflops):
    return pl.CostEstimate(flops=gigaflops * 10**9, bytes_accessed=8 * 10**6, transcendentals=0)


def dot(a, b):
    return jnp.dot(a, b, preferred_element_type=F32)


def lift_planes(cells):
    half = len(cells) // 2
    even, odd = cells[0::2], cells[1::2]
    detail = [odd[k] - 0.5 * (even[k] + even[min(k + 1, half - 1)]) for k in range(half)]
    smooth = [even[k] + 0.25 * (detail[max(k - 1, 0)] + detail[k]) for k in range(half)]
    return smooth, detail


def unlift_planes(smooth, detail):
    half = len(smooth)
    even = [smooth[k] - 0.25 * (detail[max(k - 1, 0)] + detail[k]) for k in range(half)]
    out = []
    for k in range(half):
        out += [even[k], detail[k] + 0.5 * (even[k] + even[min(k + 1, half - 1)])]
    return out


def lift_rows(load, start):
    even, odd, after = load(start), load(start + 1), load(start + 2)
    before, odd_before = load(start - 2), load(start - 1)
    detail = odd - 0.5 * (even + after)
    detail_before = odd_before - 0.5 * (before + even)
    return even + 0.25 * (detail_before + detail), detail


def unlift_rows(smooth, detail, row):
    here, after = detail(row), detail(row + 1)
    even = smooth(row) - 0.25 * (detail(row - 1) + here)
    next_even = smooth(row + 1) - 0.25 * (here + after)
    return even, here + 0.5 * (even + next_even)


PITCH = 80


def lanes_turn(j):
    return lax.rem(32 * lax.rem(j, 4) + NL - 1, NL)


def first_kernel(
    field, masks_hbm, table_hbm, lifted, up, down, own_masks, share, cells, twice, masks, table, sems
):
    small = [
        pltpu.make_async_copy(masks_hbm, masks, sems.at[0]),
        pltpu.make_async_copy(table_hbm, table, sems.at[1]),
    ]
    copies = []
    for v in range(NV):
        for c in range(4):
            part = pl.ds(16 * c, 16)
            copies.append(pltpu.make_async_copy(field.at[v, :, part], cells.at[v, :, part], sems.at[2 + 4 * v + c]))
    for copy in small + copies:
        copy.start()
    for p in range(NV * NZ):
        lifted[p * PITCH : p * PITCH + 8, :] = jnp.zeros((8, NL), F32)
        lifted[p * PITCH + 72 : p * PITCH + 80, :] = jnp.zeros((8, NL), F32)
    for copy in small:
        copy.wait()
    for i, out, tile in ((0, up, 18), (1, down, 12)):
        total = jnp.zeros((7, NL), F32)
        for l in range(2):
            flags = masks[l, i].astype(F32).astype(BF16)
            spread = table[384 + 4 * l : 388 + 4 * l, :]
            total += lax.dot_general(flags, spread, (((0,), (0,)), ((), ())), preferred_element_type=F32)
        own_masks[i] = jnp.concatenate([total, jnp.zeros((1, NL), F32)], 0)
        out[tile] = own_masks[i]

    total = jnp.zeros((80, NL), F32)
    for v in range(NV):
        for t in range(8):
            if t % 2 == 0:
                copies[4 * v + t // 2].wait()
            smooth, detail = lift_planes([cells[v, z, 8 * t : 8 * t + 8, :] for z in range(NZ)])
            for k, tile in enumerate(smooth + detail):
                start = (v * NZ + k) * PITCH + 8 + 8 * t
                lifted[start : start + 8, :] = tile
            for k, tile in enumerate(lift_planes(smooth)[0]):
                twice[v * 4 + k, 8 * t : 8 * t + 8, :] = tile
        for bz in range(2):

            def row(x):
                return lifted[pl.ds((v * NZ + bz * 8) * PITCH + 8 + x, 8, stride=PITCH), :]

            x = [row(j) for j in range(7 if bz == 0 else 3)]
            first = x[1] - 0.5 * (x[0] + x[2])
            up[v * 6 + bz] = x[0]
            up[v * 6 + 2 + bz] = first
            y = {j: row(j) for j in (range(58, 64) if bz == 0 else (62, 63))}
            part = y[63] - 0.5 * y[62]
            down[v * 4 + bz] = part
            if bz == 0:
                second = x[3] - 0.5 * (x[2] + x[4])
                third = x[5] - 0.5 * (x[4] + x[6])
                up[v * 6 + 4] = x[2] + 0.25 * (first + second)
                up[v * 6 + 5] = x[4] + 0.25 * (second + third)
                before = y[59] - 0.5 * (y[58] + y[60])
                last = y[61] - 0.5 * (y[60] + y[62])
                down[v * 4 + 2] = y[60] + 0.25 * (before + last)
                down[v * 4 + 3] = y[62] + 0.25 * (last + part)
        main, extra = [], jnp.zeros((16, NL), F32)
        for z in range(4):
            terms = jnp.concatenate(two_terms(twice[v * 4 + z]), 0)
            part = dot(table[256 + 32 * z : 288 + 32 * z, :], terms)
            main.append(part[:16])
            extra += part[16:]
        terms = jnp.concatenate(two_terms(jnp.concatenate(main + [extra], 0)), 1)
        part = dot(terms, table[0:256, :])
        total += pltpu.roll(part, 35 * v, 1) if v else part

    turn = lanes_turn(lax.axis_index("gy"))
    lane = lax.broadcasted_iota(jnp.int32, (8, NL), 1)
    spare = (lane >= 105) & (lane < 126)
    upper = lax.broadcasted_iota(jnp.int32, (8, NL), 0) < 4
    below, above = total[64:72], total[72:80]
    pieces = [pltpu.roll(above, 105 - 21 * p, 1) for p in range(5)]
    for g in range(8):
        if g < 5:
            extra = pltpu.roll(below, 105 - 21 * g, 1)
        else:
            extra = pltpu.roll(pieces[2 * g - 10], 4, 0)
            extra = jnp.where(upper, extra, pieces[2 * g - 9] if g < 7 else 0.0)
        tile = jnp.where(spare, extra, total[8 * g : 8 * g + 8])
        share[8 * g : 8 * g + 8, :] = pltpu.roll(tile, turn, 1)


def in_hbm(x):
    return pltpu.with_memory_space_constraint(x, pltpu.HBM)


def first_step(field, masks):
    vmem = pl.BlockSpec(memory_space=pltpu.VMEM)
    shapes = [(NV * NZ * PITCH, NL), (19, 8, NL), (13, 8, NL), (2, 8, NL), (64, NL)]
    return pl.pallas_call(
        first_kernel,
        out_shape=[jax.ShapeDtypeStruct(s, F32) for s in shapes],
        in_specs=[pl.BlockSpec(memory_space=pltpu.HBM)] * 3,
        out_specs=[vmem] * 5,
        scratch_shapes=[
            pltpu.VMEM((NV, NZ, NR, NL), F32),
            pltpu.VMEM((NV * 4, NR, NL), F32),
            pltpu.VMEM((2, 2, 4, 7), jnp.int32),
            pltpu.VMEM((400, NL), BF16),
            pltpu.SemaphoreType.DMA((4 * NV + 2,)),
        ],
        compiler_params=pltpu.CompilerParams(vmem_limit_bytes=VMEM_LIMIT),
    )(*[in_hbm(x) for x in (field, masks.transpose(0, 2, 3, 1), jnp.asarray(weights()["first"]))])


ROWS = 40


def lift_kernel(lifted, parts):
    def lift(step, _):
        v, bz = step // 2, lax.rem(step, 2)
        for z in range(8):
            start = pl.multiple_of((step * 8 + z) * PITCH, 8)
            for t in range(4):
                pair = lift_rows(lambda s: lifted[pl.ds(start + 16 * t + s, 8, stride=2), :], 8)
                for bx in range(2):
                    plane = (2 * bz + bx) * 24 + v * 8 + z
                    parts[pl.ds(pl.multiple_of(plane * ROWS + 8 * t, 8), 8), :] = pair[bx]
        return 0

    lax.fori_loop(0, NV * 2, lift, 0)


def lift_step(lifted):
    vmem = pl.BlockSpec(memory_space=pltpu.VMEM)
    return pl.pallas_call(
        lift_kernel,
        out_shape=jax.ShapeDtypeStruct((4 * NV * 8 * ROWS, NL), F32),
        in_specs=[vmem],
        out_specs=vmem,
        compiler_params=pltpu.CompilerParams(vmem_limit_bytes=VMEM_LIMIT),
    )(lifted)


def edge_kernel(parts_in, lifted, north, south, own_masks, table_hbm, parts, sides, packed, table, sem):
    copy = pltpu.make_async_copy(table_hbm, table, sem.at[0])
    copy.start()
    for p in range(4 * NV * 8):
        parts[p * ROWS + 32 : p * ROWS + 40, :] = jnp.zeros((8, NL), F32)
    for v in range(NV):
        for bz in range(2):

            def cell(x):
                return lifted[pl.ds((v * NZ + bz * 8) * PITCH + 8 + x, 8, stride=PITCH), :]

            def at(bx, r):
                return pl.ds(((2 * bz + bx) * 24 + v * 8) * ROWS + r, 8, stride=ROWS)

            before, after, detail = north[v * 4 + bz], south[v * 6 + bz], south[v * 6 + 2 + bz]
            start = cell(0)
            last = cell(63) - 0.5 * (cell(62) + after)
            parts[at(0, 0), :] = parts[at(0, 0), :] + 0.25 * before
            parts[at(0, 31), :] = parts[at(0, 31), :] - 0.125 * after
            parts[at(1, 31), :] = parts[at(1, 31), :] - 0.5 * after
            parts[at(0, 32), :] = after + 0.25 * (last + detail)
            parts[at(1, 32), :] = detail
            parts[at(1, 39), :] = before - 0.5 * start
            if bz == 0:
                parts[at(0, 33), :] = south[v * 6 + 4]
                parts[at(0, 34), :] = south[v * 6 + 5]
                parts[at(0, 38), :] = north[v * 4 + 2]
                parts[at(0, 39), :] = north[v * 4 + 3] - 0.125 * start

    lane = lax.broadcasted_iota(jnp.int32, (8, NL), 1) // 16

    def pack(v, _):
        for n in range(4):
            for t in range(5):
                tile = jnp.zeros((8, NL), F32)
                for z in range(8):
                    start = (n * 24 + v * 8 + z) * ROWS + 8 * t
                    x = parts[pl.ds(pl.multiple_of(start, 8), 8), :]
                    tile = jnp.where(lane == z, pltpu.roll(x, (8 + 16 * z) % NL, 1), tile)
                packed[pl.ds(pl.multiple_of(n * 120 + v * ROWS + 8 * t, 8), 8), :] = tile
        return 0

    lax.fori_loop(0, NV, pack, 0)
    copy.wait()
    terms = [two_terms(packed[n * 120 : (n + 1) * 120, :]) for n in range(4)]
    high, low = [jnp.concatenate(part, 1) for part in zip(*terms)]
    sides[0:120, :] = dot(high, table[...]) + dot(low, table[...])
    sides[120:128, :] = north[12]
    sides[128:136, :] = own_masks[0]
    sides[136:144, :] = own_masks[1]
    sides[144:152, :] = south[18]


def edge_step(parts, lifted, north, south, own_masks):
    vmem = pl.BlockSpec(memory_space=pltpu.VMEM)
    shapes = [(4 * NV * 8 * ROWS, NL), (152, NL)]
    return pl.pallas_call(
        edge_kernel,
        out_shape=[jax.ShapeDtypeStruct(s, F32) for s in shapes],
        in_specs=[vmem] * 5 + [pl.BlockSpec(memory_space=pltpu.HBM)],
        out_specs=[vmem] * 2,
        input_output_aliases={0: 0},
        cost_estimate=cost(20),
        scratch_shapes=[pltpu.VMEM((480, NL), F32), pltpu.VMEM((512, NL), BF16), pltpu.SemaphoreType.DMA((1,))],
        compiler_params=pltpu.CompilerParams(vmem_limit_bytes=VMEM_LIMIT),
    )(parts, lifted, north, south, own_masks, in_hbm(jnp.asarray(weights()["edge"])))


def join_kernel(*refs):
    shares, out = refs[:-2], refs[-1]
    for n, piece in enumerate(shares):
        out[64 * n : 64 * (n + 1), :] = piece[...]


def join_step(shares, after):
    vmem = pl.BlockSpec(memory_space=pltpu.VMEM)
    return pl.pallas_call(
        join_kernel,
        out_shape=jax.ShapeDtypeStruct((64 * len(shares), NL), F32),
        in_specs=[vmem] * len(shares) + [pl.BlockSpec(memory_space=pl.ANY)],
        out_specs=vmem,
        cost_estimate=cost(20),
        compiler_params=pltpu.CompilerParams(vmem_limit_bytes=VMEM_LIMIT),
    )(*shares, after)


def mask_lanes(near, far, own_masks, north_mask, south_mask, wide):
    near_masks, far_masks = [
        jnp.concatenate([ref[120 + 8 * i : 128 + 8 * i, :] for i in range(4)], 0) for ref in (near, far)
    ]
    is_even = lax.rem(lax.axis_index("gy"), 2) == 0
    masks = [jnp.where(is_even, near_masks, far_masks), jnp.where(is_even, far_masks, near_masks)]
    own = jnp.concatenate([north_mask[0], own_masks[0], own_masks[1], south_mask[0]], 0)
    flags = jnp.concatenate([own] + masks, 1).astype(BF16)
    return dot(flags, wide[144:528, :])


def beside_tiles(near, far, at, count):
    lane = lax.broadcasted_iota(jnp.int32, (count, NL), 1)
    from_west = ((lane >= 112) | ((lane < 96) & (lax.rem(lane, 24) >= 16))).astype(jnp.int32)
    from_near = from_west == lax.rem(lax.axis_index("gy"), 2)
    tiles = []
    for v in range(NV):
        rows = slice(v * ROWS + at, v * ROWS + at + count)
        beside = jnp.where(from_near, near[rows, :], far[rows, :])
        tiles += [pltpu.roll(beside, NL - z, 1) if z else beside for z in range(8)]
    return tiles


def beside_terms(near, far, at, count):
    return jnp.concatenate(two_terms(jnp.concatenate(beside_tiles(near, far, at, count), 0)), 1)


def own_terms(planes, at, count):
    return jnp.concatenate(two_terms(planes[:, at : at + count, :].reshape(24 * count, NL)), 1)


def main_kernel(
    parts, flat, near, far, own_masks, north_mask, south_mask, wide, narrow,
    kept,
    gain2, low, second, kept2, low_back, gain, sides_wide, turned,
):
    inverse, smooth_own, smooth_beside = narrow.at[0:256], narrow.at[256:512], narrow.at[512:768]
    back, forward2, inverse2 = narrow.at[768:1024], narrow.at[1024:1152], narrow.at[1152:1280]
    lanes = mask_lanes(near, far, own_masks, north_mask, south_mask, wide)
    lane64 = lax.broadcasted_iota(jnp.int32, (1, NL), 1) < 64
    forward2_f = forward2[...].astype(F32)
    for ib in range(4):
        for n in range(4):
            b = 8 * ib + 4 * (n // 2) + n % 2 - 1
            smooth_two = lanes[b : b + 1, NL:] if n else jnp.ones((1, NL), F32)
            row = jnp.where(lane64, smooth_two, lanes[b + 2 : b + 3, NL:])
            both = dot((forward2_f * row).astype(BF16), inverse2[...]).astype(BF16)
            gain2[ib, n, 0:128, :] = both
            gain2[ib, n, 128:256, :] = both

    for at, count in ((0, 16), (16, 16), (32, 8)):
        part = dot(own_terms(parts.at[0], at, count), smooth_own[...])
        part += dot(beside_terms(near, far, at, count), smooth_beside[...])
        part = part.reshape(24, count, NL)
        if at < 32:
            low[:, 8 + at : 8 + at + count, :] = part
            if at == 0:
                low[:, 56:64, :] = part[:, 0:8]
        else:
            low[:, 0:8, :] = part
            low[:, 40:48, :] = part
            low[:, 48:56, :] = part

    def rows_two(v, _):
        for t in range(3):
            lifted = [
                lift_rows(lambda s: low[v * 8 + p, pl.ds(16 * t + s, 8, stride=2), :], 8) for p in range(8)
            ]
            for bx in range(2):
                smooth, detail = lift_planes([pair[bx] for pair in lifted])
                for bz, part in ((0, smooth), (1, detail)):
                    for z in range(4):
                        second[2 * bz + bx, t, pl.ds(pl.multiple_of((v * 4 + z) * 8, 8), 8), :] = part[z]
        return 0

    lax.fori_loop(0, NV, rows_two, 0)
    for n in range(4):
        for t in range(3):
            terms = jnp.concatenate(two_terms(second[n, t]), 1)
            if t < 2:
                kept2[n, :, 8 + 8 * t : 16 + 8 * t, :] = dot(terms, gain2[t + 1, n]).reshape(NV * 4, 8, NL)
            else:
                kept2[n, :, 0:8, :] = dot(terms, gain2[0, n]).reshape(NV * 4, 8, NL)
                kept2[n, :, 24:32, :] = dot(terms, gain2[3, n]).reshape(NV * 4, 8, NL)

    def back_two(v, _):
        for t in range(3):
            pairs = {}
            for bz in range(2):
                for z in range(4):
                    p = v * 4 + z
                    if t < 2:
                        pairs[bz, z] = unlift_rows(
                            lambda r: kept2[2 * bz, p, pl.ds(r, 8), :],
                            lambda r: kept2[2 * bz + 1, p, pl.ds(r, 8), :],
                            8 + 8 * t,
                        )
                    else:
                        even = kept2[2 * bz, p, 24:32, :] - 0.25 * (
                            kept2[2 * bz + 1, p, 23:31, :] + kept2[2 * bz + 1, p, 24:32, :]
                        )
                        pairs[bz, z] = (even, even)
            for parity in range(2 if t < 2 else 1):
                planes = unlift_planes([pairs[0, z][parity] for z in range(4)], [pairs[1, z][parity] for z in range(4)])
                for z in range(8):
                    low_back[pl.ds((v * 8 + z) * 48 + 16 * t + parity, 8, stride=2), :] = planes[z]
        return 0

    lax.fori_loop(0, NV, back_two, 0)

    forward_f = wide[0:144, :].astype(F32)
    for ib in range(4):
        sides_wide[ib] = jnp.zeros((NL, 4 * NL), F32)
    for ib in range(4):
        for n in range(4):
            b = 8 * ib + 4 * (n // 2) + n % 2 - 1
            smooth_one = lanes[b : b + 1, 0:NL] if n else jnp.zeros((1, NL), F32)
            row = jnp.concatenate([smooth_one, lanes[b + 2 : b + 3, 0:NL]], 1)
            both = dot((forward_f * row).astype(BF16), inverse[...])
            main = both[0:128].astype(BF16)
            gain[ib, n, 0:128, :] = main
            gain[ib, n, 128:256, :] = main
            for i in range(3):
                at = 24 * n + 8 * i
                sides_wide[ib, at : at + 1, n * NL : (n + 1) * NL] = both[128 + i : 129 + i]

    gain_sides = []
    for ib in range(4):
        side = sides_wide[ib].astype(BF16)
        gain_sides.append(jnp.concatenate([side, side], 0))
    def put(n, p, at, rows):
        start = pl.multiple_of((n * 24 + p) * 48 + 8 + at, 8)
        kept[pl.ds(start, rows.shape[0]), :] = rows

    def row_of(ref, first, pitch):
        return ref[pl.ds(first, 24, stride=pitch), :]

    for ib in range(2):
        product = dot(beside_terms(near, far, 16 * ib, 16), gain_sides[ib + 1])
        for n in range(4):
            for p in range(24):
                put(n, p, 16 * ib, product[16 * p : 16 * p + 16, n * NL : (n + 1) * NL])

    def keep(n, _):
        for ib in range(2):
            product = dot(own_terms(parts.at[n], 16 * ib, 16), gain[ib + 1, n])
            for p in range(24):
                start = pl.ds(pl.multiple_of((n * 24 + p) * 48 + 8 + 16 * ib, 8), 16)
                kept[start, :] += product[16 * p : 16 * p + 16]
        return 0

    lax.fori_loop(0, 4, keep, 0)
    for ib in range(2):
        rows = jnp.concatenate([low_back[48 * p + 16 * ib : 48 * p + 16 * ib + 16, :] for p in range(24)], 0)
        product = dot(jnp.concatenate(two_terms(rows), 1), back[...])
        for p in range(24):
            start = 48 * p + 8 + 16 * ib
            kept[start : start + 16, :] += product[16 * p : 16 * p + 16]
    tiles = beside_tiles(near, far, 32, 8)
    for p in range(24):
        turned[8 * p : 8 * p + 8, :] = tiles[p]
    for first, ib, place, row in ((0, 3, 40, 32), (7, 0, 7, 39)):
        beside = dot(jnp.concatenate(two_terms(row_of(turned, first, 8)), 1), gain_sides[ib])
        for n in range(4) if ib else (1, 3):
            own = jnp.concatenate(two_terms(row_of(flat, n * 24 * ROWS + row, ROWS)), 1)
            total = beside[:, n * NL : (n + 1) * NL] + dot(own, gain[ib, n])
            if n == 0:
                total += dot(jnp.concatenate(two_terms(row_of(low_back, row, 48)), 1), back[...])
            kept[pl.ds(n * 24 * 48 + place, 24, stride=48), :] = total


def cells_kernel(kept, out, cells, sems):
    def back_one(step, _):
        v, t = step // 4, step % 4
        pairs = {}
        for bz in range(2):
            for z in range(8):
                p = v * 8 + z
                pairs[bz, z] = unlift_rows(
                    lambda r: kept[2 * bz, p, pl.ds(8 * t + r, 8), :],
                    lambda r: kept[2 * bz + 1, p, pl.ds(8 * t + r, 8), :],
                    8,
                )
        for parity in range(2):
            planes = unlift_planes([pairs[0, z][parity] for z in range(8)], [pairs[1, z][parity] for z in range(8)])
            for z in range(NZ):
                cells[v, z, pl.ds(16 * t + parity, 8, stride=2), :] = planes[z]
        return 0

    def copy(step):
        v, rows = step // 4, pl.ds(pl.multiple_of(16 * (step % 4), 16), 16)
        return pltpu.make_async_copy(cells.at[v, :, rows], out.at[v, :, rows], sems.at[step])

    def one(step, _):
        back_one(step, 0)
        copy(step).start()
        return 0

    lax.fori_loop(0, NV * 4, one, 0)
    for step in range(NV * 4):
        copy(step).wait()


def main_specs():
    vmem = pl.BlockSpec(memory_space=pltpu.VMEM)
    return [
        vmem, vmem, vmem, vmem, vmem,
        pl.BlockSpec((1, 8, NL), lambda i: (12, 0, 0)), pl.BlockSpec((1, 8, NL), lambda i: (18, 0, 0)),
        vmem, vmem,
    ]


def main_step(flat, *operands):
    w = weights()
    return pl.pallas_call(
        main_kernel,
        grid=(1,),
        out_shape=jax.ShapeDtypeStruct((4 * NV * 8 * 48, NL), F32),
        in_specs=main_specs(),
        out_specs=pl.BlockSpec((4 * NV * 8 * 48, NL), lambda i: (0, 0)),
        scratch_shapes=[
            pltpu.VMEM((4, 4, 256, NL), BF16),
            pltpu.VMEM((NV * 8, 64, NL), F32),
            pltpu.VMEM((4, 3, NV * 32, NL), F32),
            pltpu.VMEM((4, NV * 4, 40, NL), F32),
            pltpu.VMEM((NV * 8 * 48, NL), F32),
            pltpu.VMEM((4, 4, 256, NL), BF16),
            pltpu.VMEM((4, NL, 4 * NL), F32),
            pltpu.VMEM((NV * 64, NL), F32),
        ],
        cost_estimate=cost(8),
        compiler_params=pltpu.CompilerParams(vmem_limit_bytes=VMEM_LIMIT),
    )(flat.reshape(4, NV * 8, ROWS, NL), flat, *operands, w["wide"], w["narrow"])


def cells_step(kept):
    shape = (NV, NZ, NR, NL)
    return pl.pallas_call(
        cells_kernel,
        out_shape=jax.ShapeDtypeStruct(shape, F32),
        in_specs=[pl.BlockSpec(memory_space=pltpu.VMEM)],
        out_specs=pl.BlockSpec(memory_space=pltpu.HBM),
        scratch_shapes=[pltpu.VMEM(shape, F32), pltpu.SemaphoreType.DMA((NV * 4,))],
        cost_estimate=cost(4),
        compiler_params=pltpu.CompilerParams(vmem_limit_bytes=VMEM_LIMIT),
    )(kept)


def rows_kernel(count_x, count_z, *refs):
    shares, out = refs[:count_x], refs[count_x + 1]
    me, me_y = lax.axis_index("gx"), lax.axis_index("gy")
    row = lax.broadcasted_iota(jnp.int32, (8, NL), 0)
    lane = lax.broadcasted_iota(jnp.int32, (8, NL), 1)
    for r in range(count_x):
        at = pl.multiple_of(16 * (me ^ r), 16)
        for j in range(count_z):
            for z in range(4):
                start = 64 * j + 16 * z
                out[j, z, pl.ds(at, 16), :] = shares[r][start : start + 16, :]
    for j in range(count_z):
        turn = lanes_turn(me_y ^ (2 * j))
        piece = lax.rem(lane + (NL - turn), NL) // 21
        inside = [piece == p for p in range(5)]
        for r in range(count_x):
            i = me ^ r
            below = pl.multiple_of(16 * lax.rem(i + 1, count_x), 16)
            above = pl.multiple_of(16 * lax.rem(i + count_x - 1, count_x) + 8, 8)
            tiles = [shares[r][64 * j + 8 * g : 64 * j + 8 * g + 8, :] for g in range(8)]
            low, high = jnp.zeros((8, NL), F32), jnp.zeros((8, NL), F32)
            for p in range(5):
                back = (21 * p - 105) % NL
                low = jnp.where(inside[p], pltpu.roll(tiles[p], back, 1), low)
                extra = tiles[5 + p // 2]
                extra = extra if p % 2 else pltpu.roll(extra, 4, 0)
                high = jnp.where(inside[p], pltpu.roll(extra, back, 1), high)
            for z in range(4):
                first = pltpu.roll(low, 8 - 2 * z, 0) if z else low
                last = pltpu.roll(high, z, 0) if z else high
                out[j, z, pl.ds(below, 8), :] += jnp.where(row < 2, first, 0.0)
                out[j, z, pl.ds(above, 8), :] += jnp.where(row == 7, last, 0.0)


def rows_step(pieces, count_z, after):
    vmem = pl.BlockSpec(memory_space=pltpu.VMEM)
    count_x = len(pieces)
    return pl.pallas_call(
        functools.partial(rows_kernel, count_x, count_z),
        out_shape=jax.ShapeDtypeStruct((count_z, 4, 16 * count_x, NL), F32),
        in_specs=[vmem] * count_x + [pl.BlockSpec(memory_space=pl.ANY)],
        out_specs=vmem,
        compiler_params=pltpu.CompilerParams(vmem_limit_bytes=VMEM_LIMIT),
    )(*pieces, after)


def coarse_kernel(count_x, count_y, own, other, out_hbm, out, sems):
    me = lax.axis_index("gy")
    me_z, is_even = lax.shift_right_logical(me, 1), lax.rem(me, 2) == 0
    lane = lax.broadcasted_iota(jnp.int32, (8, NL), 1)
    place = [lax.rem(lane + NL - 35 * v, NL) for v in range(NV)]

    def block(i, _):
        rows = pl.ds(pl.multiple_of(8 * i, 8), 8)
        for z in range(4):
            pieces = []
            for j in range(count_y // 2):
                mine, theirs = own[j ^ me_z, z, rows, :], other[j ^ me_z, z, rows, :]
                pieces += [jnp.where(is_even, mine, theirs), jnp.where(is_even, theirs, mine)]
            for v in range(NV):
                at = place[v]
                for t in range(count_y // 4):
                    total = jnp.where(at < 2, pieces[4 * t - 1], 0.0)
                    total += jnp.where(at == NL - 1, pieces[(4 * t + 4) % count_y], 0.0)
                    for q in range(4):
                        inside = (at >= 32 * q - 1) & (at < 32 * q + 34)
                        total += jnp.where(inside, pieces[4 * t + q], 0.0)
                    out[v, z, rows, NL * t : NL * (t + 1)] = pltpu.roll(total, NL - 35 * v, 1) if v else total
        return 0

    def copy(i):
        rows = pl.ds(pl.multiple_of(16 * i, 16), 16)
        return pltpu.make_async_copy(out.at[:, :, rows], out_hbm.at[:, :, rows], sems.at[i])

    def pair(i, _):
        block(2 * i, 0)
        block(2 * i + 1, 0)
        copy(i).start()
        return 0

    lax.fori_loop(0, count_x, pair, 0)
    for i in range(count_x):
        copy(i).wait()


def coarse_step(own, other, count_x, count_y):
    vmem = pl.BlockSpec(memory_space=pltpu.VMEM)
    shape = (NV, 4, 16 * count_x, 32 * count_y)
    return pl.pallas_call(
        functools.partial(coarse_kernel, count_x, count_y),
        out_shape=jax.ShapeDtypeStruct(shape, F32),
        in_specs=[vmem, vmem],
        out_specs=pl.BlockSpec(memory_space=pltpu.HBM),
        scratch_shapes=[pltpu.VMEM(shape, F32), pltpu.SemaphoreType.DMA((count_x,))],
        compiler_params=pltpu.CompilerParams(vmem_limit_bytes=VMEM_LIMIT),
    )(own, other)


def shifted(x, axis, step):
    count = lax.axis_size(axis)
    return lax.ppermute(x, axis, [(i, (i + step) % count) for i in range(count)])


def swapped(x, axis, distance):
    return lax.ppermute(x, axis, [(i, i ^ distance) for i in range(lax.axis_size(axis))])


def crossed(x, axis):
    count = lax.axis_size(axis)
    return lax.ppermute(x, axis, [(i, (i + (1 if i % 2 else count - 1)) % count) for i in range(count)])


def body(field, masks):
    count_x, count_y = lax.axis_size("gx"), lax.axis_size("gy")
    lifted, up, down, own_masks, share = first_step(field, masks)
    south = shifted(up, "gx", -1)
    north = shifted(down, "gx", 1)
    shares = [share] + [swapped(share, "gy", r) for r in range(2, count_y, 2)]
    parts, sides = edge_step(lift_step(lifted), lifted, north, south, own_masks)
    near, far = swapped(sides, "gy", 1), crossed(sides, "gy")
    joined = join_step(shares, sides)
    pieces = [joined] + [swapped(joined, "gx", r) for r in range(1, count_x)]
    kept = main_step(parts, near, far, own_masks, north, south)
    own = rows_step(pieces, count_y // 2, kept)
    other = swapped(own, "gy", 1)
    return cells_step(kept.reshape(4, NV * 8, 48, NL)), coarse_step(own, other, count_x, count_y)


def solution(mesh):
    placed = P(None, None, "gx", "gy")
    return jax.shard_map(
        body,
        mesh=mesh,
        in_specs=(placed, placed),
        out_specs=(placed, P()),
        check_vma=False,
    )
```

```python
import functools

import jax
import jax.numpy as jnp
import ml_dtypes
import numpy as np
from jax import lax
from jax.experimental import pallas as pl
from jax.experimental.pallas import tpu as pltpu
from jax.sharding import PartitionSpec as P

F32 = jnp.float32
BF16 = jnp.bfloat16
VMEM_LIMIT = 32 * 1024 * 1024

NV, NZ, NR, NL = 3, 16, 64, 128


def detail_row(k):
    return {2 * k + 1: 1.0, 2 * k: -0.5, 2 * k + 2: -0.5}


def smooth_row(k):
    row = {2 * k: 1.0}
    for j in (k - 1, k):
        for cell, value in detail_row(j).items():
            row[cell] = row.get(cell, 0.0) + 0.25 * value
    return row


def even_row(k):
    return {("s", k): 1.0, ("d", k - 1): -0.25, ("d", k): -0.25}


def odd_row(k):
    row = {("d", k): 1.0}
    for j in (k, k + 1):
        for name, value in even_row(j).items():
            row[name] = row.get(name, 0.0) + 0.5 * value
    return row


def as_bf16(matrix):
    cast = matrix.astype(ml_dtypes.bfloat16)
    assert (cast.astype(np.float64) == matrix).all()
    return cast


def combine(*terms):
    total = {}
    for factor, row in terms:
        for cell, value in row.items():
            total[cell] = total.get(cell, 0.0) + factor * value
    return total


def level_one_columns():
    names = {("s", k): k for k in range(65)}
    names.update({("d", k): 128 + k for k in range(65)})
    names[("d", -1)] = 128 + 65
    return names


def level_two_columns():
    names = {("s", k): k for k in range(33)}
    names.update({("d", k): 64 + k for k in range(33)})
    names[("d", -1)] = 64 + 33
    return names


def smooth_place(k):
    return k + 2


def beyond(n):
    return {"cell": 24 * n, "after": 24 * n + 8, "before": 24 * n + 16}


BEYOND_SMOOTH = {65: 96, 66: 104, -2: 112, -1: 120}


def own_row(kind, k, n):
    place = {name: 128 + lane for name, lane in beyond(n).items()}
    if kind == "d":
        if k == -1:
            return {place["before"]: 1.0, 0: -0.5}
        if k == 64:
            return {place["after"]: 1.0}
        return {(place["cell"] if y == 128 else y): value for y, value in detail_row(k).items()}
    if k in BEYOND_SMOOTH:
        row = {128 + BEYOND_SMOOTH[k]: 1.0}
        return combine((1.0, row), (1.0, {0: -0.125})) if k == -1 else row
    even = place["cell"] if k == 64 else 2 * k
    return combine((1.0, {even: 1.0}), (0.25, own_row("d", k - 1, n)), (0.25, own_row("d", k, n)))


@functools.lru_cache(maxsize=None)
def weights():
    w = {}
    names = level_one_columns()
    forward = np.zeros((4, 256, 256))
    inverse = np.zeros((256, 128))
    for (kind, k), column in names.items():
        for n in range(4):
            for place, value in own_row(kind, k, n).items():
                forward[n, place, column] += value
    for k in range(64):
        for y, row in ((2 * k, even_row(k)), (2 * k + 1, odd_row(k))):
            for name, value in row.items():
                inverse[names[name], y] += value
    short = np.zeros((144, 256))
    short[:128] = forward[0, :128]
    for i, lane in enumerate(beyond(0).values()):
        short[128 + i] = forward[0, 128 + lane]
    smooth = np.zeros((256, 128))
    for k in range(-2, 67):
        for place, value in own_row("s", k, 0).items():
            smooth[place, smooth_place(k)] += value
    names2 = level_two_columns()
    forward2 = np.zeros((128, 128))
    inverse2 = np.zeros((128, 128))
    for (kind, k), column in names2.items():
        for cell, value in (smooth_row(k) if kind == "s" else detail_row(k)).items():
            forward2[smooth_place(cell), column] += value
    for k in range(33):
        rows = [(2 * k, even_row(k))] + ([(2 * k + 1, odd_row(k))] if k < 32 else [])
        for y, row in rows:
            for name, value in row.items():
                inverse2[names2[name], y] += value
    back = np.zeros((256, 128))
    back[:65] = inverse[:65]
    back[128 : 128 + 65] = inverse[:65]
    spread = np.zeros((3, 128, 2, 128))
    for k in range(64):
        spread[0, k, 0, k] = 1
    spread[1, 0, 0, 64] = 1
    spread[2, 63, 0, 65] = 1
    for k in range(32):
        spread[0, 64 + k, 1, k] = 1
        spread[0, 64 + k, 1, 64 + k] = 1
    for base in (0, 64):
        spread[1, 64, 1, base + 32] = 1
        spread[2, 95, 1, base + 33] = 1
    w["wide"] = np.concatenate([short, spread.reshape(384, 256)], 0)
    own, beside = smooth[:128], smooth[128:]
    w["narrow"] = np.concatenate([inverse, own, own, beside, beside, back, forward2, inverse2], 0)
    edge = np.zeros((4, 128, 128))

    def put(n, lane, row):
        for z in range(8):
            for y, value in row.items():
                j = y - 120 if y >= 120 else y + 8
                edge[n, 16 * z + j, lane + z] += value

    part = {127: 1.0, 126: -0.5}
    for n in range(4):
        put(n, beyond(n)["cell"], {0: 1.0})
        put(n, beyond(n)["after"], detail_row(0))
        put(n, beyond(n)["before"], part)
    put(0, BEYOND_SMOOTH[65], smooth_row(1))
    put(0, BEYOND_SMOOTH[66], smooth_row(2))
    put(0, BEYOND_SMOOTH[-2], smooth_row(62))
    put(0, BEYOND_SMOOTH[-1], combine((1.0, {126: 1.0}), (0.25, detail_row(62)), (0.25, part)))
    w["edge"] = edge.reshape(512, 128)
    expand = np.zeros((2, 4, 128))
    for j in range(4):
        expand[0, j, 16 * j : 16 * j + 16] = 1
        expand[1, j, 64 + 8 * j : 64 + 8 * j + 8] = 1
    twice = combine(*[(value, smooth_row(k)) for k, value in smooth_row(0).items()])
    columns = np.zeros((2, 128, 128))
    for m in range(-1, 34):
        for t, value in twice.items():
            if 0 <= 4 * m + t < NL:
                columns[:, 4 * m + t, m + 1] = value
    rows = np.zeros((4, 32, 2, 64))
    for z in range(4):
        places = {m: m for m in range(16)}
        places.update({16: 16 + 2 * z, 17: 17 + 2 * z, -1: 16 + 15 - z})
        for m, place in places.items():
            for t, value in twice.items():
                if 0 <= 4 * m + t < NR:
                    rows[z, place, :, 4 * m + t] = value
    pad = np.zeros((8, 128))
    w["first"] = np.concatenate([columns.reshape(256, 128), rows.reshape(128, 128), expand.reshape(8, 128), pad], 0)
    return {name: as_bf16(matrix) for name, matrix in w.items()}


def two_terms(x):
    high = x.astype(BF16)
    low = (x - high.astype(F32)).astype(BF16)
    return high, low


def cost(gigaflops):
    return pl.CostEstimate(flops=gigaflops * 10**9, bytes_accessed=8 * 10**6, transcendentals=0)


def dot(a, b):
    return jnp.dot(a, b, preferred_element_type=F32)


def lift_planes(cells):
    half = len(cells) // 2
    even, odd = cells[0::2], cells[1::2]
    detail = [odd[k] - 0.5 * (even[k] + even[min(k + 1, half - 1)]) for k in range(half)]
    smooth = [even[k] + 0.25 * (detail[max(k - 1, 0)] + detail[k]) for k in range(half)]
    return smooth, detail


def unlift_planes(smooth, detail):
    half = len(smooth)
    even = [smooth[k] - 0.25 * (detail[max(k - 1, 0)] + detail[k]) for k in range(half)]
    out = []
    for k in range(half):
        out += [even[k], detail[k] + 0.5 * (even[k] + even[min(k + 1, half - 1)])]
    return out


def lift_rows(load, start):
    even, odd, after = load(start), load(start + 1), load(start + 2)
    before, odd_before = load(start - 2), load(start - 1)
    detail = odd - 0.5 * (even + after)
    detail_before = odd_before - 0.5 * (before + even)
    return even + 0.25 * (detail_before + detail), detail


def unlift_rows(smooth, detail, row):
    here, after = detail(row), detail(row + 1)
    even = smooth(row) - 0.25 * (detail(row - 1) + here)
    next_even = smooth(row + 1) - 0.25 * (here + after)
    return even, here + 0.5 * (even + next_even)


PITCH = 80


def lanes_turn(j):
    return lax.rem(32 * lax.rem(j, 4) + NL - 1, NL)


def first_kernel(
    field, masks_hbm, table_hbm, lifted, up, down, own_masks, share, cells, twice, masks, table, sems
):
    small = [
        pltpu.make_async_copy(masks_hbm, masks, sems.at[0]),
        pltpu.make_async_copy(table_hbm, table, sems.at[1]),
    ]
    copies = []
    for v in range(NV):
        for c in range(4):
            part = pl.ds(16 * c, 16)
            copies.append(pltpu.make_async_copy(field.at[v, :, part], cells.at[v, :, part], sems.at[2 + 4 * v + c]))
    for copy in small + copies:
        copy.start()
    for p in range(NV * NZ):
        lifted[p * PITCH : p * PITCH + 8, :] = jnp.zeros((8, NL), F32)
        lifted[p * PITCH + 72 : p * PITCH + 80, :] = jnp.zeros((8, NL), F32)
    for copy in small:
        copy.wait()
    for i, out, tile in ((0, up, 18), (1, down, 12)):
        total = jnp.zeros((7, NL), F32)
        for l in range(2):
            flags = masks[l, i].astype(F32).astype(BF16)
            spread = table[384 + 4 * l : 388 + 4 * l, :]
            total += lax.dot_general(flags, spread, (((0,), (0,)), ((), ())), preferred_element_type=F32)
        own_masks[i] = jnp.concatenate([total, jnp.zeros((1, NL), F32)], 0)
        out[tile] = own_masks[i]

    for v in range(NV):
        for t in range(8):
            if t % 2 == 0:
                copies[4 * v + t // 2].wait()
            smooth, detail = lift_planes([cells[v, z, 8 * t : 8 * t + 8, :] for z in range(NZ)])
            for k, tile in enumerate(smooth + detail):
                start = (v * NZ + k) * PITCH + 8 + 8 * t
                lifted[start : start + 8, :] = tile
            for k, tile in enumerate(lift_planes(smooth)[0]):
                twice[v * 4 + k, 8 * t : 8 * t + 8, :] = tile
        for bz in range(2):

            def row(x):
                return lifted[pl.ds((v * NZ + bz * 8) * PITCH + 8 + x, 8, stride=PITCH), :]

            x = [row(j) for j in range(7 if bz == 0 else 3)]
            first = x[1] - 0.5 * (x[0] + x[2])
            up[v * 6 + bz] = x[0]
            up[v * 6 + 2 + bz] = first
            y = {j: row(j) for j in (range(58, 64) if bz == 0 else (62, 63))}
            part = y[63] - 0.5 * y[62]
            down[v * 4 + bz] = part
            if bz == 0:
                second = x[3] - 0.5 * (x[2] + x[4])
                third = x[5] - 0.5 * (x[4] + x[6])
                up[v * 6 + 4] = x[2] + 0.25 * (first + second)
                up[v * 6 + 5] = x[4] + 0.25 * (second + third)
                before = y[59] - 0.5 * (y[58] + y[60])
                last = y[61] - 0.5 * (y[60] + y[62])
                down[v * 4 + 2] = y[60] + 0.25 * (before + last)
                down[v * 4 + 3] = y[62] + 0.25 * (last + part)

    total = jnp.zeros((80, NL), F32)
    for v in range(NV):
        main, extra = [], jnp.zeros((16, NL), F32)
        for z in range(4):
            terms = jnp.concatenate(two_terms(twice[v * 4 + z]), 0)
            part = dot(table[256 + 32 * z : 288 + 32 * z, :], terms)
            main.append(part[:16])
            extra += part[16:]
        terms = jnp.concatenate(two_terms(jnp.concatenate(main + [extra], 0)), 1)
        part = dot(terms, table[0:256, :])
        total += pltpu.roll(part, 35 * v, 1) if v else part
    turn = lanes_turn(lax.axis_index("gy"))
    lane = lax.broadcasted_iota(jnp.int32, (8, NL), 1)
    spare = (lane >= 105) & (lane < 126)
    upper = lax.broadcasted_iota(jnp.int32, (8, NL), 0) < 4
    below, above = total[64:72], total[72:80]
    pieces = [pltpu.roll(above, 105 - 21 * p, 1) for p in range(5)]
    for g in range(8):
        if g < 5:
            extra = pltpu.roll(below, 105 - 21 * g, 1)
        else:
            extra = pltpu.roll(pieces[2 * g - 10], 4, 0)
            extra = jnp.where(upper, extra, pieces[2 * g - 9] if g < 7 else 0.0)
        tile = jnp.where(spare, extra, total[8 * g : 8 * g + 8])
        share[8 * g : 8 * g + 8, :] = pltpu.roll(tile, turn, 1)


def in_hbm(x):
    return pltpu.with_memory_space_constraint(x, pltpu.HBM)


def first_step(field, masks):
    vmem = pl.BlockSpec(memory_space=pltpu.VMEM)
    shapes = [(NV * NZ * PITCH, NL), (19, 8, NL), (13, 8, NL), (2, 8, NL), (64, NL)]
    return pl.pallas_call(
        first_kernel,
        out_shape=[jax.ShapeDtypeStruct(s, F32) for s in shapes],
        in_specs=[pl.BlockSpec(memory_space=pltpu.HBM)] * 3,
        out_specs=[vmem] * 5,
        scratch_shapes=[
            pltpu.VMEM((NV, NZ, NR, NL), F32),
            pltpu.VMEM((NV * 4, NR, NL), F32),
            pltpu.VMEM((2, 2, 4, 7), jnp.int32),
            pltpu.VMEM((400, NL), BF16),
            pltpu.SemaphoreType.DMA((4 * NV + 2,)),
        ],
        compiler_params=pltpu.CompilerParams(vmem_limit_bytes=VMEM_LIMIT),
    )(*[in_hbm(x) for x in (field, masks.transpose(0, 2, 3, 1), jnp.asarray(weights()["first"]))])


ROWS = 40


def lift_kernel(lifted, parts):
    def lift(step, _):
        v, bz = step // 2, lax.rem(step, 2)
        for z in range(8):
            start = pl.multiple_of((step * 8 + z) * PITCH, 8)
            for t in range(4):
                pair = lift_rows(lambda s: lifted[pl.ds(start + 16 * t + s, 8, stride=2), :], 8)
                for bx in range(2):
                    plane = (2 * bz + bx) * 24 + v * 8 + z
                    parts[pl.ds(pl.multiple_of(plane * ROWS + 8 * t, 8), 8), :] = pair[bx]
        return 0

    lax.fori_loop(0, NV * 2, lift, 0)


def lift_step(lifted):
    vmem = pl.BlockSpec(memory_space=pltpu.VMEM)
    return pl.pallas_call(
        lift_kernel,
        out_shape=jax.ShapeDtypeStruct((4 * NV * 8 * ROWS, NL), F32),
        in_specs=[vmem],
        out_specs=vmem,
        compiler_params=pltpu.CompilerParams(vmem_limit_bytes=VMEM_LIMIT),
    )(lifted)


def edge_kernel(parts_in, lifted, north, south, own_masks, table_hbm, parts, sides, packed, table, sem):
    copy = pltpu.make_async_copy(table_hbm, table, sem.at[0])
    copy.start()
    for p in range(4 * NV * 8):
        parts[p * ROWS + 32 : p * ROWS + 40, :] = jnp.zeros((8, NL), F32)
    for v in range(NV):
        for bz in range(2):

            def cell(x):
                return lifted[pl.ds((v * NZ + bz * 8) * PITCH + 8 + x, 8, stride=PITCH), :]

            def at(bx, r):
                return pl.ds(((2 * bz + bx) * 24 + v * 8) * ROWS + r, 8, stride=ROWS)

            before, after, detail = north[v * 4 + bz], south[v * 6 + bz], south[v * 6 + 2 + bz]
            start = cell(0)
            last = cell(63) - 0.5 * (cell(62) + after)
            parts[at(0, 0), :] = parts[at(0, 0), :] + 0.25 * before
            parts[at(0, 31), :] = parts[at(0, 31), :] - 0.125 * after
            parts[at(1, 31), :] = parts[at(1, 31), :] - 0.5 * after
            parts[at(0, 32), :] = after + 0.25 * (last + detail)
            parts[at(1, 32), :] = detail
            parts[at(1, 39), :] = before - 0.5 * start
            if bz == 0:
                parts[at(0, 33), :] = south[v * 6 + 4]
                parts[at(0, 34), :] = south[v * 6 + 5]
                parts[at(0, 38), :] = north[v * 4 + 2]
                parts[at(0, 39), :] = north[v * 4 + 3] - 0.125 * start

    lane = lax.broadcasted_iota(jnp.int32, (8, NL), 1) // 16

    def pack(v, _):
        for n in range(4):
            for t in range(5):
                tile = jnp.zeros((8, NL), F32)
                for z in range(8):
                    start = (n * 24 + v * 8 + z) * ROWS + 8 * t
                    x = parts[pl.ds(pl.multiple_of(start, 8), 8), :]
                    tile = jnp.where(lane == z, pltpu.roll(x, (8 + 16 * z) % NL, 1), tile)
                packed[pl.ds(pl.multiple_of(n * 120 + v * ROWS + 8 * t, 8), 8), :] = tile
        return 0

    lax.fori_loop(0, NV, pack, 0)
    copy.wait()
    terms = [two_terms(packed[n * 120 : (n + 1) * 120, :]) for n in range(4)]
    high, low = [jnp.concatenate(part, 1) for part in zip(*terms)]
    sides[0:120, :] = dot(high, table[...]) + dot(low, table[...])
    sides[120:128, :] = north[12]
    sides[128:136, :] = own_masks[0]
    sides[136:144, :] = own_masks[1]
    sides[144:152, :] = south[18]


def edge_step(parts, lifted, north, south, own_masks):
    vmem = pl.BlockSpec(memory_space=pltpu.VMEM)
    shapes = [(4 * NV * 8 * ROWS, NL), (152, NL)]
    return pl.pallas_call(
        edge_kernel,
        out_shape=[jax.ShapeDtypeStruct(s, F32) for s in shapes],
        in_specs=[vmem] * 5 + [pl.BlockSpec(memory_space=pltpu.HBM)],
        out_specs=[vmem] * 2,
        input_output_aliases={0: 0},
        cost_estimate=cost(20),
        scratch_shapes=[pltpu.VMEM((480, NL), F32), pltpu.VMEM((512, NL), BF16), pltpu.SemaphoreType.DMA((1,))],
        compiler_params=pltpu.CompilerParams(vmem_limit_bytes=VMEM_LIMIT),
    )(parts, lifted, north, south, own_masks, in_hbm(jnp.asarray(weights()["edge"])))


def join_kernel(*refs):
    shares, sides, (out, message) = refs[:-3], refs[-3], refs[-2:]
    for n, piece in enumerate(shares):
        out[64 * n : 64 * (n + 1), :] = piece[...]
    message[...] = sides[...]


def join_step(shares, sides):
    vmem = pl.BlockSpec(memory_space=pltpu.VMEM)
    return pl.pallas_call(
        join_kernel,
        out_shape=[jax.ShapeDtypeStruct((64 * len(shares), NL), F32), jax.ShapeDtypeStruct(sides.shape, F32)],
        in_specs=[vmem] * (len(shares) + 1),
        out_specs=[vmem, vmem],
        cost_estimate=cost(20),
        compiler_params=pltpu.CompilerParams(vmem_limit_bytes=VMEM_LIMIT),
    )(*shares, sides)


def mask_lanes(near, far, own_masks, north_mask, south_mask, wide):
    near_masks, far_masks = [
        jnp.concatenate([ref[120 + 8 * i : 128 + 8 * i, :] for i in range(4)], 0) for ref in (near, far)
    ]
    is_even = lax.rem(lax.axis_index("gy"), 2) == 0
    masks = [jnp.where(is_even, near_masks, far_masks), jnp.where(is_even, far_masks, near_masks)]
    own = jnp.concatenate([north_mask[0], own_masks[0], own_masks[1], south_mask[0]], 0)
    flags = jnp.concatenate([own] + masks, 1).astype(BF16)
    return dot(flags, wide[144:528, :])


def beside_tiles(near, far, at, count):
    lane = lax.broadcasted_iota(jnp.int32, (count, NL), 1)
    from_west = ((lane >= 112) | ((lane < 96) & (lax.rem(lane, 24) >= 16))).astype(jnp.int32)
    from_near = from_west == lax.rem(lax.axis_index("gy"), 2)
    tiles = []
    for v in range(NV):
        rows = slice(v * ROWS + at, v * ROWS + at + count)
        beside = jnp.where(from_near, near[rows, :], far[rows, :])
        tiles += [pltpu.roll(beside, NL - z, 1) if z else beside for z in range(8)]
    return tiles


def beside_terms(near, far, at, count):
    return jnp.concatenate(two_terms(jnp.concatenate(beside_tiles(near, far, at, count), 0)), 1)


def own_terms(planes, at, count):
    return jnp.concatenate(two_terms(planes[:, at : at + count, :].reshape(24 * count, NL)), 1)


def main_kernel(
    parts, flat, near, far, own_masks, north_mask, south_mask, wide, narrow,
    kept,
    gain2, low, second, kept2, low_back, gain, sides_wide, turned,
):
    inverse, smooth_own, smooth_beside = narrow.at[0:256], narrow.at[256:512], narrow.at[512:768]
    back, forward2, inverse2 = narrow.at[768:1024], narrow.at[1024:1152], narrow.at[1152:1280]
    lanes = mask_lanes(near, far, own_masks, north_mask, south_mask, wide)
    lane64 = lax.broadcasted_iota(jnp.int32, (1, NL), 1) < 64
    forward2_f = forward2[...].astype(F32)
    for ib in range(4):
        for n in range(4):
            b = 8 * ib + 4 * (n // 2) + n % 2 - 1
            smooth_two = lanes[b : b + 1, NL:] if n else jnp.ones((1, NL), F32)
            row = jnp.where(lane64, smooth_two, lanes[b + 2 : b + 3, NL:])
            both = dot((forward2_f * row).astype(BF16), inverse2[...]).astype(BF16)
            gain2[ib, n, 0:128, :] = both
            gain2[ib, n, 128:256, :] = both

    for at, count in ((0, 16), (16, 16), (32, 8)):
        part = dot(own_terms(parts.at[0], at, count), smooth_own[...])
        part += dot(beside_terms(near, far, at, count), smooth_beside[...])
        part = part.reshape(24, count, NL)
        if at < 32:
            low[:, 8 + at : 8 + at + count, :] = part
            if at == 0:
                low[:, 56:64, :] = part[:, 0:8]
        else:
            low[:, 0:8, :] = part
            low[:, 40:48, :] = part
            low[:, 48:56, :] = part

    def rows_two(v, _):
        for t in range(3):
            lifted = [
                lift_rows(lambda s: low[v * 8 + p, pl.ds(16 * t + s, 8, stride=2), :], 8) for p in range(8)
            ]
            for bx in range(2):
                smooth, detail = lift_planes([pair[bx] for pair in lifted])
                for bz, part in ((0, smooth), (1, detail)):
                    for z in range(4):
                        second[2 * bz + bx, t, pl.ds(pl.multiple_of((v * 4 + z) * 8, 8), 8), :] = part[z]
        return 0

    lax.fori_loop(0, NV, rows_two, 0)
    for n in range(4):
        for t in range(3):
            terms = jnp.concatenate(two_terms(second[n, t]), 1)
            if t < 2:
                kept2[n, :, 8 + 8 * t : 16 + 8 * t, :] = dot(terms, gain2[t + 1, n]).reshape(NV * 4, 8, NL)
            else:
                kept2[n, :, 0:8, :] = dot(terms, gain2[0, n]).reshape(NV * 4, 8, NL)
                kept2[n, :, 24:32, :] = dot(terms, gain2[3, n]).reshape(NV * 4, 8, NL)

    def back_two(v, _):
        for t in range(3):
            pairs = {}
            for bz in range(2):
                for z in range(4):
                    p = v * 4 + z
                    if t < 2:
                        pairs[bz, z] = unlift_rows(
                            lambda r: kept2[2 * bz, p, pl.ds(r, 8), :],
                            lambda r: kept2[2 * bz + 1, p, pl.ds(r, 8), :],
                            8 + 8 * t,
                        )
                    else:
                        even = kept2[2 * bz, p, 24:32, :] - 0.25 * (
                            kept2[2 * bz + 1, p, 23:31, :] + kept2[2 * bz + 1, p, 24:32, :]
                        )
                        pairs[bz, z] = (even, even)
            for parity in range(2 if t < 2 else 1):
                planes = unlift_planes([pairs[0, z][parity] for z in range(4)], [pairs[1, z][parity] for z in range(4)])
                for z in range(8):
                    low_back[pl.ds((v * 8 + z) * 48 + 16 * t + parity, 8, stride=2), :] = planes[z]
        return 0

    lax.fori_loop(0, NV, back_two, 0)

    forward_f = wide[0:144, :].astype(F32)
    for ib in range(4):
        sides_wide[ib] = jnp.zeros((NL, 4 * NL), F32)
    for ib in range(4):
        for n in range(4):
            b = 8 * ib + 4 * (n // 2) + n % 2 - 1
            smooth_one = lanes[b : b + 1, 0:NL] if n else jnp.zeros((1, NL), F32)
            row = jnp.concatenate([smooth_one, lanes[b + 2 : b + 3, 0:NL]], 1)
            both = dot((forward_f * row).astype(BF16), inverse[...])
            main = both[0:128].astype(BF16)
            gain[ib, n, 0:128, :] = main
            gain[ib, n, 128:256, :] = main
            for i in range(3):
                at = 24 * n + 8 * i
                sides_wide[ib, at : at + 1, n * NL : (n + 1) * NL] = both[128 + i : 129 + i]

    gain_sides = []
    for ib in range(4):
        side = sides_wide[ib].astype(BF16)
        gain_sides.append(jnp.concatenate([side, side], 0))
    def put(n, p, at, rows):
        start = pl.multiple_of((n * 24 + p) * 48 + 8 + at, 8)
        kept[pl.ds(start, rows.shape[0]), :] = rows

    def row_of(ref, first, pitch):
        return ref[pl.ds(first, 24, stride=pitch), :]

    for ib in range(2):
        product = dot(beside_terms(near, far, 16 * ib, 16), gain_sides[ib + 1])
        for n in range(4):
            for p in range(24):
                put(n, p, 16 * ib, product[16 * p : 16 * p + 16, n * NL : (n + 1) * NL])

    def keep(n, _):
        for ib in range(2):
            product = dot(own_terms(parts.at[n], 16 * ib, 16), gain[ib + 1, n])
            for p in range(24):
                start = pl.ds(pl.multiple_of((n * 24 + p) * 48 + 8 + 16 * ib, 8), 16)
                kept[start, :] += product[16 * p : 16 * p + 16]
        return 0

    lax.fori_loop(0, 4, keep, 0)
    for ib in range(2):
        rows = jnp.concatenate([low_back[48 * p + 16 * ib : 48 * p + 16 * ib + 16, :] for p in range(24)], 0)
        product = dot(jnp.concatenate(two_terms(rows), 1), back[...])
        for p in range(24):
            start = 48 * p + 8 + 16 * ib
            kept[start : start + 16, :] += product[16 * p : 16 * p + 16]
    tiles = beside_tiles(near, far, 32, 8)
    for p in range(24):
        turned[8 * p : 8 * p + 8, :] = tiles[p]
    for first, ib, place, row in ((0, 3, 40, 32), (7, 0, 7, 39)):
        beside = dot(jnp.concatenate(two_terms(row_of(turned, first, 8)), 1), gain_sides[ib])
        for n in range(4) if ib else (1, 3):
            own = jnp.concatenate(two_terms(row_of(flat, n * 24 * ROWS + row, ROWS)), 1)
            total = beside[:, n * NL : (n + 1) * NL] + dot(own, gain[ib, n])
            if n == 0:
                total += dot(jnp.concatenate(two_terms(row_of(low_back, row, 48)), 1), back[...])
            kept[pl.ds(n * 24 * 48 + place, 24, stride=48), :] = total


def cells_kernel(kept, out, cells, sems):
    def back_one(step, _):
        v, t = step // 4, step % 4
        pairs = {}
        for bz in range(2):
            for z in range(8):
                p = v * 8 + z
                pairs[bz, z] = unlift_rows(
                    lambda r: kept[2 * bz, p, pl.ds(8 * t + r, 8), :],
                    lambda r: kept[2 * bz + 1, p, pl.ds(8 * t + r, 8), :],
                    8,
                )
        for parity in range(2):
            planes = unlift_planes([pairs[0, z][parity] for z in range(8)], [pairs[1, z][parity] for z in range(8)])
            for z in range(NZ):
                cells[v, z, pl.ds(16 * t + parity, 8, stride=2), :] = planes[z]
        return 0

    def copy(step):
        v, rows = step // 4, pl.ds(pl.multiple_of(16 * (step % 4), 16), 16)
        return pltpu.make_async_copy(cells.at[v, :, rows], out.at[v, :, rows], sems.at[step])

    def one(step, _):
        back_one(step, 0)
        copy(step).start()
        return 0

    lax.fori_loop(0, NV * 4, one, 0)
    for step in range(NV * 4):
        copy(step).wait()


def main_specs():
    vmem = pl.BlockSpec(memory_space=pltpu.VMEM)
    return [
        vmem, vmem, vmem, vmem, vmem,
        pl.BlockSpec((1, 8, NL), lambda i: (12, 0, 0)), pl.BlockSpec((1, 8, NL), lambda i: (18, 0, 0)),
        vmem, vmem,
    ]


def main_step(flat, *operands):
    w = weights()
    return pl.pallas_call(
        main_kernel,
        grid=(1,),
        out_shape=jax.ShapeDtypeStruct((4 * NV * 8 * 48, NL), F32),
        in_specs=main_specs(),
        out_specs=pl.BlockSpec((4 * NV * 8 * 48, NL), lambda i: (0, 0)),
        scratch_shapes=[
            pltpu.VMEM((4, 4, 256, NL), BF16),
            pltpu.VMEM((NV * 8, 64, NL), F32),
            pltpu.VMEM((4, 3, NV * 32, NL), F32),
            pltpu.VMEM((4, NV * 4, 40, NL), F32),
            pltpu.VMEM((NV * 8 * 48, NL), F32),
            pltpu.VMEM((4, 4, 256, NL), BF16),
            pltpu.VMEM((4, NL, 4 * NL), F32),
            pltpu.VMEM((NV * 64, NL), F32),
        ],
        cost_estimate=cost(8),
        compiler_params=pltpu.CompilerParams(vmem_limit_bytes=VMEM_LIMIT),
    )(flat.reshape(4, NV * 8, ROWS, NL), flat, *operands, w["wide"], w["narrow"])


def cells_step(kept):
    shape = (NV, NZ, NR, NL)
    return pl.pallas_call(
        cells_kernel,
        out_shape=jax.ShapeDtypeStruct(shape, F32),
        in_specs=[pl.BlockSpec(memory_space=pltpu.VMEM)],
        out_specs=pl.BlockSpec(memory_space=pltpu.HBM),
        scratch_shapes=[pltpu.VMEM(shape, F32), pltpu.SemaphoreType.DMA((NV * 4,))],
        cost_estimate=cost(4),
        compiler_params=pltpu.CompilerParams(vmem_limit_bytes=VMEM_LIMIT),
    )(kept)


def rows_kernel(count_x, count_z, *refs):
    shares, out = refs[:count_x], refs[count_x + 1]
    me, me_y = lax.axis_index("gx"), lax.axis_index("gy")
    row = lax.broadcasted_iota(jnp.int32, (8, NL), 0)
    lane = lax.broadcasted_iota(jnp.int32, (8, NL), 1)
    for r in range(count_x):
        at = pl.multiple_of(16 * (me ^ r), 16)
        for j in range(count_z):
            for z in range(4):
                start = 64 * j + 16 * z
                out[j, z, pl.ds(at, 16), :] = shares[r][start : start + 16, :]
    for j in range(count_z):
        turn = lanes_turn(me_y ^ (2 * j))
        piece = lax.rem(lane + (NL - turn), NL) // 21
        inside = [piece == p for p in range(5)]
        for r in range(count_x):
            i = me ^ r
            below = pl.multiple_of(16 * lax.rem(i + 1, count_x), 16)
            above = pl.multiple_of(16 * lax.rem(i + count_x - 1, count_x) + 8, 8)
            tiles = [shares[r][64 * j + 8 * g : 64 * j + 8 * g + 8, :] for g in range(8)]
            low, high = jnp.zeros((8, NL), F32), jnp.zeros((8, NL), F32)
            for p in range(5):
                back = (21 * p - 105) % NL
                low = jnp.where(inside[p], pltpu.roll(tiles[p], back, 1), low)
                extra = tiles[5 + p // 2]
                extra = extra if p % 2 else pltpu.roll(extra, 4, 0)
                high = jnp.where(inside[p], pltpu.roll(extra, back, 1), high)
            for z in range(4):
                first = pltpu.roll(low, 8 - 2 * z, 0) if z else low
                last = pltpu.roll(high, z, 0) if z else high
                out[j, z, pl.ds(below, 8), :] += jnp.where(row < 2, first, 0.0)
                out[j, z, pl.ds(above, 8), :] += jnp.where(row == 7, last, 0.0)


def rows_step(pieces, count_z, after):
    vmem = pl.BlockSpec(memory_space=pltpu.VMEM)
    count_x = len(pieces)
    return pl.pallas_call(
        functools.partial(rows_kernel, count_x, count_z),
        out_shape=jax.ShapeDtypeStruct((count_z, 4, 16 * count_x, NL), F32),
        in_specs=[vmem] * count_x + [pl.BlockSpec(memory_space=pl.ANY)],
        out_specs=vmem,
        compiler_params=pltpu.CompilerParams(vmem_limit_bytes=VMEM_LIMIT),
    )(*pieces, after)


def coarse_kernel(count_x, count_y, own, other, out_hbm, out, sems):
    me = lax.axis_index("gy")
    me_z, is_even = lax.shift_right_logical(me, 1), lax.rem(me, 2) == 0
    lane = lax.broadcasted_iota(jnp.int32, (8, NL), 1)
    place = [lax.rem(lane + NL - 35 * v, NL) for v in range(NV)]

    def block(i, _):
        rows = pl.ds(pl.multiple_of(8 * i, 8), 8)
        for z in range(4):
            pieces = []
            for j in range(count_y // 2):
                mine, theirs = own[j ^ me_z, z, rows, :], other[j ^ me_z, z, rows, :]
                pieces += [jnp.where(is_even, mine, theirs), jnp.where(is_even, theirs, mine)]
            for v in range(NV):
                at = place[v]
                for t in range(count_y // 4):
                    total = jnp.where(at < 2, pieces[4 * t - 1], 0.0)
                    total += jnp.where(at == NL - 1, pieces[(4 * t + 4) % count_y], 0.0)
                    for q in range(4):
                        inside = (at >= 32 * q - 1) & (at < 32 * q + 34)
                        total += jnp.where(inside, pieces[4 * t + q], 0.0)
                    out[v, z, rows, NL * t : NL * (t + 1)] = pltpu.roll(total, NL - 35 * v, 1) if v else total
        return 0

    def copy(i):
        rows = pl.ds(pl.multiple_of(16 * i, 16), 16)
        return pltpu.make_async_copy(out.at[:, :, rows], out_hbm.at[:, :, rows], sems.at[i])

    def pair(i, _):
        block(2 * i, 0)
        block(2 * i + 1, 0)
        copy(i).start()
        return 0

    lax.fori_loop(0, count_x, pair, 0)
    for i in range(count_x):
        copy(i).wait()


def coarse_step(own, other, count_x, count_y):
    vmem = pl.BlockSpec(memory_space=pltpu.VMEM)
    shape = (NV, 4, 16 * count_x, 32 * count_y)
    return pl.pallas_call(
        functools.partial(coarse_kernel, count_x, count_y),
        out_shape=jax.ShapeDtypeStruct(shape, F32),
        in_specs=[vmem, vmem],
        out_specs=pl.BlockSpec(memory_space=pltpu.HBM),
        scratch_shapes=[pltpu.VMEM(shape, F32), pltpu.SemaphoreType.DMA((count_x,))],
        compiler_params=pltpu.CompilerParams(vmem_limit_bytes=VMEM_LIMIT),
    )(own, other)


def shifted(x, axis, step):
    count = lax.axis_size(axis)
    return lax.ppermute(x, axis, [(i, (i + step) % count) for i in range(count)])


def swapped(x, axis, distance):
    return lax.ppermute(x, axis, [(i, i ^ distance) for i in range(lax.axis_size(axis))])


def crossed(x, axis):
    count = lax.axis_size(axis)
    return lax.ppermute(x, axis, [(i, (i + (1 if i % 2 else count - 1)) % count) for i in range(count)])


def body(field, masks):
    count_x, count_y = lax.axis_size("gx"), lax.axis_size("gy")
    lifted, up, down, own_masks, share = first_step(field, masks)
    south = shifted(up, "gx", -1)
    north = shifted(down, "gx", 1)
    shares = [share] + [swapped(share, "gy", r) for r in range(2, count_y, 2)]
    parts, sides = edge_step(lift_step(lifted), lifted, north, south, own_masks)
    near = swapped(sides, "gy", 1)
    joined, message = join_step(shares, sides)
    far = crossed(message, "gy")
    pieces = [joined] + [swapped(joined, "gx", r) for r in range(1, count_x)]
    kept = main_step(parts, near, far, own_masks, north, south)
    own = rows_step(pieces, count_y // 2, kept)
    other = swapped(own, "gy", 1)
    return cells_step(kept.reshape(4, NV * 8, 48, NL)), coarse_step(own, other, count_x, count_y)


def solution(mesh):
    placed = P(None, None, "gx", "gy")
    return jax.shard_map(
        body,
        mesh=mesh,
        in_specs=(placed, placed),
        out_specs=(placed, P()),
        check_vma=False,
    )
```

```python
import functools

import jax
import jax.numpy as jnp
import ml_dtypes
import numpy as np
from jax import lax
from jax.experimental import pallas as pl
from jax.experimental.pallas import tpu as pltpu
from jax.sharding import PartitionSpec as P

F32 = jnp.float32
BF16 = jnp.bfloat16
VMEM_LIMIT = 32 * 1024 * 1024

NV, NZ, NR, NL = 3, 16, 64, 128


def detail_row(k):
    return {2 * k + 1: 1.0, 2 * k: -0.5, 2 * k + 2: -0.5}


def smooth_row(k):
    row = {2 * k: 1.0}
    for j in (k - 1, k):
        for cell, value in detail_row(j).items():
            row[cell] = row.get(cell, 0.0) + 0.25 * value
    return row


def even_row(k):
    return {("s", k): 1.0, ("d", k - 1): -0.25, ("d", k): -0.25}


def odd_row(k):
    row = {("d", k): 1.0}
    for j in (k, k + 1):
        for name, value in even_row(j).items():
            row[name] = row.get(name, 0.0) + 0.5 * value
    return row


def as_bf16(matrix):
    cast = matrix.astype(ml_dtypes.bfloat16)
    assert (cast.astype(np.float64) == matrix).all()
    return cast


def combine(*terms):
    total = {}
    for factor, row in terms:
        for cell, value in row.items():
            total[cell] = total.get(cell, 0.0) + factor * value
    return total


def level_one_columns():
    names = {("s", k): k for k in range(65)}
    names.update({("d", k): 128 + k for k in range(65)})
    names[("d", -1)] = 128 + 65
    return names


def level_two_columns():
    names = {("s", k): k for k in range(33)}
    names.update({("d", k): 64 + k for k in range(33)})
    names[("d", -1)] = 64 + 33
    return names


def smooth_place(k):
    return k + 2


def beyond(n):
    return {"cell": 24 * n, "after": 24 * n + 8, "before": 24 * n + 16}


BEYOND_SMOOTH = {65: 96, 66: 104, -2: 112, -1: 120}


def own_row(kind, k, n):
    place = {name: 128 + lane for name, lane in beyond(n).items()}
    if kind == "d":
        if k == -1:
            return {place["before"]: 1.0, 0: -0.5}
        if k == 64:
            return {place["after"]: 1.0}
        return {(place["cell"] if y == 128 else y): value for y, value in detail_row(k).items()}
    if k in BEYOND_SMOOTH:
        row = {128 + BEYOND_SMOOTH[k]: 1.0}
        return combine((1.0, row), (1.0, {0: -0.125})) if k == -1 else row
    even = place["cell"] if k == 64 else 2 * k
    return combine((1.0, {even: 1.0}), (0.25, own_row("d", k - 1, n)), (0.25, own_row("d", k, n)))


@functools.lru_cache(maxsize=None)
def weights():
    w = {}
    names = level_one_columns()
    forward = np.zeros((4, 256, 256))
    inverse = np.zeros((256, 128))
    for (kind, k), column in names.items():
        for n in range(4):
            for place, value in own_row(kind, k, n).items():
                forward[n, place, column] += value
    for k in range(64):
        for y, row in ((2 * k, even_row(k)), (2 * k + 1, odd_row(k))):
            for name, value in row.items():
                inverse[names[name], y] += value
    short = np.zeros((144, 256))
    short[:128] = forward[0, :128]
    for i, lane in enumerate(beyond(0).values()):
        short[128 + i] = forward[0, 128 + lane]
    smooth = np.zeros((256, 128))
    for k in range(-2, 67):
        for place, value in own_row("s", k, 0).items():
            smooth[place, smooth_place(k)] += value
    names2 = level_two_columns()
    forward2 = np.zeros((128, 128))
    inverse2 = np.zeros((128, 128))
    for (kind, k), column in names2.items():
        for cell, value in (smooth_row(k) if kind == "s" else detail_row(k)).items():
            forward2[smooth_place(cell), column] += value
    for k in range(33):
        rows = [(2 * k, even_row(k))] + ([(2 * k + 1, odd_row(k))] if k < 32 else [])
        for y, row in rows:
            for name, value in row.items():
                inverse2[names2[name], y] += value
    back = np.zeros((256, 128))
    back[:65] = inverse[:65]
    back[128 : 128 + 65] = inverse[:65]
    spread = np.zeros((3, 128, 2, 128))
    for k in range(64):
        spread[0, k, 0, k] = 1
    spread[1, 0, 0, 64] = 1
    spread[2, 63, 0, 65] = 1
    for k in range(32):
        spread[0, 64 + k, 1, k] = 1
        spread[0, 64 + k, 1, 64 + k] = 1
    for base in (0, 64):
        spread[1, 64, 1, base + 32] = 1
        spread[2, 95, 1, base + 33] = 1
    w["wide"] = np.concatenate([short, spread.reshape(384, 256)], 0)
    own, beside = smooth[:128], smooth[128:]
    w["narrow"] = np.concatenate([inverse, own, own, beside, beside, back, forward2, inverse2], 0)
    edge = np.zeros((4, 128, 128))

    def put(n, lane, row):
        for z in range(8):
            for y, value in row.items():
                j = y - 120 if y >= 120 else y + 8
                edge[n, 16 * z + j, lane + z] += value

    part = {127: 1.0, 126: -0.5}
    for n in range(4):
        put(n, beyond(n)["cell"], {0: 1.0})
        put(n, beyond(n)["after"], detail_row(0))
        put(n, beyond(n)["before"], part)
    put(0, BEYOND_SMOOTH[65], smooth_row(1))
    put(0, BEYOND_SMOOTH[66], smooth_row(2))
    put(0, BEYOND_SMOOTH[-2], smooth_row(62))
    put(0, BEYOND_SMOOTH[-1], combine((1.0, {126: 1.0}), (0.25, detail_row(62)), (0.25, part)))
    w["edge"] = edge.reshape(512, 128)
    expand = np.zeros((2, 4, 128))
    for j in range(4):
        expand[0, j, 16 * j : 16 * j + 16] = 1
        expand[1, j, 64 + 8 * j : 64 + 8 * j + 8] = 1
    twice = combine(*[(value, smooth_row(k)) for k, value in smooth_row(0).items()])
    columns = np.zeros((2, 128, 128))
    for m in range(-1, 34):
        for t, value in twice.items():
            if 0 <= 4 * m + t < NL:
                columns[:, 4 * m + t, m + 1] = value
    rows = np.zeros((4, 32, 2, 64))
    for z in range(4):
        places = {m: m for m in range(16)}
        places.update({16: 16 + 2 * z, 17: 17 + 2 * z, -1: 16 + 15 - z})
        for m, place in places.items():
            for t, value in twice.items():
                if 0 <= 4 * m + t < NR:
                    rows[z, place, :, 4 * m + t] = value
    pad = np.zeros((8, 128))
    w["first"] = np.concatenate([columns.reshape(256, 128), rows.reshape(128, 128), expand.reshape(8, 128), pad], 0)
    return {name: as_bf16(matrix) for name, matrix in w.items()}


def two_terms(x):
    high = x.astype(BF16)
    low = (x - high.astype(F32)).astype(BF16)
    return high, low


def cost(gigaflops):
    return pl.CostEstimate(flops=gigaflops * 10**9, bytes_accessed=8 * 10**6, transcendentals=0)


def dot(a, b):
    return jnp.dot(a, b, preferred_element_type=F32)


def lift_planes(cells):
    half = len(cells) // 2
    even, odd = cells[0::2], cells[1::2]
    detail = [odd[k] - 0.5 * (even[k] + even[min(k + 1, half - 1)]) for k in range(half)]
    smooth = [even[k] + 0.25 * (detail[max(k - 1, 0)] + detail[k]) for k in range(half)]
    return smooth, detail


def unlift_planes(smooth, detail):
    half = len(smooth)
    even = [smooth[k] - 0.25 * (detail[max(k - 1, 0)] + detail[k]) for k in range(half)]
    out = []
    for k in range(half):
        out += [even[k], detail[k] + 0.5 * (even[k] + even[min(k + 1, half - 1)])]
    return out


def lift_rows(load, start):
    even, odd, after = load(start), load(start + 1), load(start + 2)
    before, odd_before = load(start - 2), load(start - 1)
    detail = odd - 0.5 * (even + after)
    detail_before = odd_before - 0.5 * (before + even)
    return even + 0.25 * (detail_before + detail), detail


def unlift_rows(smooth, detail, row):
    here, after = detail(row), detail(row + 1)
    even = smooth(row) - 0.25 * (detail(row - 1) + here)
    next_even = smooth(row + 1) - 0.25 * (here + after)
    return even, here + 0.5 * (even + next_even)


PITCH = 80


def lanes_turn(j):
    return lax.rem(32 * lax.rem(j, 4) + NL - 1, NL)


def first_kernel(
    field, masks_hbm, table_hbm, lifted, up, down, own_masks, share, cells, twice, masks, table, sems
):
    small = [
        pltpu.make_async_copy(masks_hbm, masks, sems.at[0]),
        pltpu.make_async_copy(table_hbm, table, sems.at[1]),
    ]
    copies = []
    for v in range(NV):
        for c in range(4):
            part = pl.ds(16 * c, 16)
            copies.append(pltpu.make_async_copy(field.at[v, :, part], cells.at[v, :, part], sems.at[2 + 4 * v + c]))
    for copy in small + copies:
        copy.start()
    for p in range(NV * NZ):
        lifted[p * PITCH : p * PITCH + 8, :] = jnp.zeros((8, NL), F32)
        lifted[p * PITCH + 72 : p * PITCH + 80, :] = jnp.zeros((8, NL), F32)
    for copy in small:
        copy.wait()
    for i, out, tile in ((0, up, 18), (1, down, 12)):
        total = jnp.zeros((7, NL), F32)
        for l in range(2):
            flags = masks[l, i].astype(F32).astype(BF16)
            spread = table[384 + 4 * l : 388 + 4 * l, :]
            total += lax.dot_general(flags, spread, (((0,), (0,)), ((), ())), preferred_element_type=F32)
        own_masks[i] = jnp.concatenate([total, jnp.zeros((1, NL), F32)], 0)
        out[tile] = own_masks[i]

    for v in range(NV):
        for t in range(8):
            if t % 2 == 0:
                copies[4 * v + t // 2].wait()
            smooth, detail = lift_planes([cells[v, z, 8 * t : 8 * t + 8, :] for z in range(NZ)])
            for k, tile in enumerate(smooth + detail):
                start = (v * NZ + k) * PITCH + 8 + 8 * t
                lifted[start : start + 8, :] = tile
            for k, tile in enumerate(lift_planes(smooth)[0]):
                twice[v * 4 + k, 8 * t : 8 * t + 8, :] = tile
        for bz in range(2):

            def row(x):
                return lifted[pl.ds((v * NZ + bz * 8) * PITCH + 8 + x, 8, stride=PITCH), :]

            x = [row(j) for j in range(7 if bz == 0 else 3)]
            first = x[1] - 0.5 * (x[0] + x[2])
            up[v * 6 + bz] = x[0]
            up[v * 6 + 2 + bz] = first
            y = {j: row(j) for j in (range(58, 64) if bz == 0 else (62, 63))}
            part = y[63] - 0.5 * y[62]
            down[v * 4 + bz] = part
            if bz == 0:
                second = x[3] - 0.5 * (x[2] + x[4])
                third = x[5] - 0.5 * (x[4] + x[6])
                up[v * 6 + 4] = x[2] + 0.25 * (first + second)
                up[v * 6 + 5] = x[4] + 0.25 * (second + third)
                before = y[59] - 0.5 * (y[58] + y[60])
                last = y[61] - 0.5 * (y[60] + y[62])
                down[v * 4 + 2] = y[60] + 0.25 * (before + last)
                down[v * 4 + 3] = y[62] + 0.25 * (last + part)

    total = jnp.zeros((80, NL), F32)
    for v in range(NV):
        main, extra = [], jnp.zeros((16, NL), F32)
        for z in range(4):
            terms = jnp.concatenate(two_terms(twice[v * 4 + z]), 0)
            part = dot(table[256 + 32 * z : 288 + 32 * z, :], terms)
            main.append(part[:16])
            extra += part[16:]
        terms = jnp.concatenate(two_terms(jnp.concatenate(main + [extra], 0)), 1)
        part = dot(terms, table[0:256, :])
        total += pltpu.roll(part, 35 * v, 1) if v else part
    turn = lanes_turn(lax.axis_index("gy"))
    lane = lax.broadcasted_iota(jnp.int32, (8, NL), 1)
    spare = (lane >= 105) & (lane < 126)
    upper = lax.broadcasted_iota(jnp.int32, (8, NL), 0) < 4
    below, above = total[64:72], total[72:80]
    pieces = [pltpu.roll(above, 105 - 21 * p, 1) for p in range(5)]
    for g in range(8):
        if g < 5:
            extra = pltpu.roll(below, 105 - 21 * g, 1)
        else:
            extra = pltpu.roll(pieces[2 * g - 10], 4, 0)
            extra = jnp.where(upper, extra, pieces[2 * g - 9] if g < 7 else 0.0)
        tile = jnp.where(spare, extra, total[8 * g : 8 * g + 8])
        share[8 * g : 8 * g + 8, :] = pltpu.roll(tile, turn, 1)


def in_hbm(x):
    return pltpu.with_memory_space_constraint(x, pltpu.HBM)


def first_step(field, masks):
    vmem = pl.BlockSpec(memory_space=pltpu.VMEM)
    shapes = [(NV * NZ * PITCH, NL), (19, 8, NL), (13, 8, NL), (2, 8, NL), (64, NL)]
    return pl.pallas_call(
        first_kernel,
        out_shape=[jax.ShapeDtypeStruct(s, F32) for s in shapes],
        in_specs=[pl.BlockSpec(memory_space=pltpu.HBM)] * 3,
        out_specs=[vmem] * 5,
        scratch_shapes=[
            pltpu.VMEM((NV, NZ, NR, NL), F32),
            pltpu.VMEM((NV * 4, NR, NL), F32),
            pltpu.VMEM((2, 2, 4, 7), jnp.int32),
            pltpu.VMEM((400, NL), BF16),
            pltpu.SemaphoreType.DMA((4 * NV + 2,)),
        ],
        compiler_params=pltpu.CompilerParams(vmem_limit_bytes=VMEM_LIMIT),
    )(*[in_hbm(x) for x in (field, masks.transpose(0, 2, 3, 1), jnp.asarray(weights()["first"]))])


ROWS = 40


def lift_kernel(lifted, parts):
    def lift(step, _):
        v, bz = step // 2, lax.rem(step, 2)
        for z in range(8):
            start = pl.multiple_of((step * 8 + z) * PITCH, 8)
            for t in range(4):
                pair = lift_rows(lambda s: lifted[pl.ds(start + 16 * t + s, 8, stride=2), :], 8)
                for bx in range(2):
                    plane = (2 * bz + bx) * 24 + v * 8 + z
                    parts[pl.ds(pl.multiple_of(plane * ROWS + 8 * t, 8), 8), :] = pair[bx]
        return 0

    lax.fori_loop(0, NV * 2, lift, 0)


def lift_step(lifted):
    vmem = pl.BlockSpec(memory_space=pltpu.VMEM)
    return pl.pallas_call(
        lift_kernel,
        out_shape=jax.ShapeDtypeStruct((4 * NV * 8 * ROWS, NL), F32),
        in_specs=[vmem],
        out_specs=vmem,
        compiler_params=pltpu.CompilerParams(vmem_limit_bytes=VMEM_LIMIT),
    )(lifted)


def edge_kernel(parts_in, lifted, north, south, own_masks, table_hbm, parts, sides, packed, table, sem):
    copy = pltpu.make_async_copy(table_hbm, table, sem.at[0])
    copy.start()
    for p in range(4 * NV * 8):
        parts[p * ROWS + 32 : p * ROWS + 40, :] = jnp.zeros((8, NL), F32)
    for v in range(NV):
        for bz in range(2):

            def cell(x):
                return lifted[pl.ds((v * NZ + bz * 8) * PITCH + 8 + x, 8, stride=PITCH), :]

            def at(bx, r):
                return pl.ds(((2 * bz + bx) * 24 + v * 8) * ROWS + r, 8, stride=ROWS)

            before, after, detail = north[v * 4 + bz], south[v * 6 + bz], south[v * 6 + 2 + bz]
            start = cell(0)
            last = cell(63) - 0.5 * (cell(62) + after)
            parts[at(0, 0), :] = parts[at(0, 0), :] + 0.25 * before
            parts[at(0, 31), :] = parts[at(0, 31), :] - 0.125 * after
            parts[at(1, 31), :] = parts[at(1, 31), :] - 0.5 * after
            parts[at(0, 32), :] = after + 0.25 * (last + detail)
            parts[at(1, 32), :] = detail
            parts[at(1, 39), :] = before - 0.5 * start
            if bz == 0:
                parts[at(0, 33), :] = south[v * 6 + 4]
                parts[at(0, 34), :] = south[v * 6 + 5]
                parts[at(0, 38), :] = north[v * 4 + 2]
                parts[at(0, 39), :] = north[v * 4 + 3] - 0.125 * start

    lane = lax.broadcasted_iota(jnp.int32, (8, NL), 1) // 16

    def pack(v, _):
        for n in range(4):
            for t in range(5):
                tile = jnp.zeros((8, NL), F32)
                for z in range(8):
                    start = (n * 24 + v * 8 + z) * ROWS + 8 * t
                    x = parts[pl.ds(pl.multiple_of(start, 8), 8), :]
                    tile = jnp.where(lane == z, pltpu.roll(x, (8 + 16 * z) % NL, 1), tile)
                packed[pl.ds(pl.multiple_of(n * 120 + v * ROWS + 8 * t, 8), 8), :] = tile
        return 0

    lax.fori_loop(0, NV, pack, 0)
    copy.wait()
    terms = [two_terms(packed[n * 120 : (n + 1) * 120, :]) for n in range(4)]
    high, low = [jnp.concatenate(part, 1) for part in zip(*terms)]
    sides[0:120, :] = dot(high, table[...]) + dot(low, table[...])
    sides[120:128, :] = north[12]
    sides[128:136, :] = own_masks[0]
    sides[136:144, :] = own_masks[1]
    sides[144:152, :] = south[18]


def edge_step(parts, lifted, north, south, own_masks):
    vmem = pl.BlockSpec(memory_space=pltpu.VMEM)
    shapes = [(4 * NV * 8 * ROWS, NL), (152, NL)]
    return pl.pallas_call(
        edge_kernel,
        out_shape=[jax.ShapeDtypeStruct(s, F32) for s in shapes],
        in_specs=[vmem] * 5 + [pl.BlockSpec(memory_space=pltpu.HBM)],
        out_specs=[vmem] * 2,
        input_output_aliases={0: 0},
        cost_estimate=cost(20),
        scratch_shapes=[pltpu.VMEM((480, NL), F32), pltpu.VMEM((512, NL), BF16), pltpu.SemaphoreType.DMA((1,))],
        compiler_params=pltpu.CompilerParams(vmem_limit_bytes=VMEM_LIMIT),
    )(parts, lifted, north, south, own_masks, in_hbm(jnp.asarray(weights()["edge"])))


def mask_lanes(near, far, own_masks, north_mask, south_mask, wide):
    near_masks, far_masks = [
        jnp.concatenate([ref[120 + 8 * i : 128 + 8 * i, :] for i in range(4)], 0) for ref in (near, far)
    ]
    is_even = lax.rem(lax.axis_index("gy"), 2) == 0
    masks = [jnp.where(is_even, near_masks, far_masks), jnp.where(is_even, far_masks, near_masks)]
    own = jnp.concatenate([north_mask[0], own_masks[0], own_masks[1], south_mask[0]], 0)
    flags = jnp.concatenate([own] + masks, 1).astype(BF16)
    return dot(flags, wide[144:528, :])


def beside_tiles(near, far, at, count):
    lane = lax.broadcasted_iota(jnp.int32, (count, NL), 1)
    from_west = ((lane >= 112) | ((lane < 96) & (lax.rem(lane, 24) >= 16))).astype(jnp.int32)
    from_near = from_west == lax.rem(lax.axis_index("gy"), 2)
    tiles = []
    for v in range(NV):
        rows = slice(v * ROWS + at, v * ROWS + at + count)
        beside = jnp.where(from_near, near[rows, :], far[rows, :])
        tiles += [pltpu.roll(beside, NL - z, 1) if z else beside for z in range(8)]
    return tiles


def beside_terms(near, far, at, count):
    return jnp.concatenate(two_terms(jnp.concatenate(beside_tiles(near, far, at, count), 0)), 1)


def own_terms(planes, at, count):
    return jnp.concatenate(two_terms(planes[:, at : at + count, :].reshape(24 * count, NL)), 1)


def main_kernel(
    parts, flat, near, far, own_masks, north_mask, south_mask, wide, narrow,
    kept,
    gain2, low, second, kept2, low_back, gain, sides_wide, turned,
):
    inverse, smooth_own, smooth_beside = narrow.at[0:256], narrow.at[256:512], narrow.at[512:768]
    back, forward2, inverse2 = narrow.at[768:1024], narrow.at[1024:1152], narrow.at[1152:1280]
    lanes = mask_lanes(near, far, own_masks, north_mask, south_mask, wide)
    lane64 = lax.broadcasted_iota(jnp.int32, (1, NL), 1) < 64
    forward2_f = forward2[...].astype(F32)
    for ib in range(4):
        for n in range(4):
            b = 8 * ib + 4 * (n // 2) + n % 2 - 1
            smooth_two = lanes[b : b + 1, NL:] if n else jnp.ones((1, NL), F32)
            row = jnp.where(lane64, smooth_two, lanes[b + 2 : b + 3, NL:])
            both = dot((forward2_f * row).astype(BF16), inverse2[...]).astype(BF16)
            gain2[ib, n, 0:128, :] = both
            gain2[ib, n, 128:256, :] = both

    for at, count in ((0, 16), (16, 16), (32, 8)):
        part = dot(own_terms(parts.at[0], at, count), smooth_own[...])
        part += dot(beside_terms(near, far, at, count), smooth_beside[...])
        part = part.reshape(24, count, NL)
        if at < 32:
            low[:, 8 + at : 8 + at + count, :] = part
            if at == 0:
                low[:, 56:64, :] = part[:, 0:8]
        else:
            low[:, 0:8, :] = part
            low[:, 40:48, :] = part
            low[:, 48:56, :] = part

    def rows_two(v, _):
        for t in range(3):
            lifted = [
                lift_rows(lambda s: low[v * 8 + p, pl.ds(16 * t + s, 8, stride=2), :], 8) for p in range(8)
            ]
            for bx in range(2):
                smooth, detail = lift_planes([pair[bx] for pair in lifted])
                for bz, part in ((0, smooth), (1, detail)):
                    for z in range(4):
                        second[2 * bz + bx, t, pl.ds(pl.multiple_of((v * 4 + z) * 8, 8), 8), :] = part[z]
        return 0

    lax.fori_loop(0, NV, rows_two, 0)
    for n in range(4):
        for t in range(3):
            terms = jnp.concatenate(two_terms(second[n, t]), 1)
            if t < 2:
                kept2[n, :, 8 + 8 * t : 16 + 8 * t, :] = dot(terms, gain2[t + 1, n]).reshape(NV * 4, 8, NL)
            else:
                kept2[n, :, 0:8, :] = dot(terms, gain2[0, n]).reshape(NV * 4, 8, NL)
                kept2[n, :, 24:32, :] = dot(terms, gain2[3, n]).reshape(NV * 4, 8, NL)

    def back_two(v, _):
        for t in range(3):
            pairs = {}
            for bz in range(2):
                for z in range(4):
                    p = v * 4 + z
                    if t < 2:
                        pairs[bz, z] = unlift_rows(
                            lambda r: kept2[2 * bz, p, pl.ds(r, 8), :],
                            lambda r: kept2[2 * bz + 1, p, pl.ds(r, 8), :],
                            8 + 8 * t,
                        )
                    else:
                        even = kept2[2 * bz, p, 24:32, :] - 0.25 * (
                            kept2[2 * bz + 1, p, 23:31, :] + kept2[2 * bz + 1, p, 24:32, :]
                        )
                        pairs[bz, z] = (even, even)
            for parity in range(2 if t < 2 else 1):
                planes = unlift_planes([pairs[0, z][parity] for z in range(4)], [pairs[1, z][parity] for z in range(4)])
                for z in range(8):
                    low_back[pl.ds((v * 8 + z) * 48 + 16 * t + parity, 8, stride=2), :] = planes[z]
        return 0

    lax.fori_loop(0, NV, back_two, 0)

    forward_f = wide[0:144, :].astype(F32)
    for ib in range(4):
        sides_wide[ib] = jnp.zeros((NL, 4 * NL), F32)
    for ib in range(4):
        for n in range(4):
            b = 8 * ib + 4 * (n // 2) + n % 2 - 1
            smooth_one = lanes[b : b + 1, 0:NL] if n else jnp.zeros((1, NL), F32)
            row = jnp.concatenate([smooth_one, lanes[b + 2 : b + 3, 0:NL]], 1)
            both = dot((forward_f * row).astype(BF16), inverse[...])
            main = both[0:128].astype(BF16)
            gain[ib, n, 0:128, :] = main
            gain[ib, n, 128:256, :] = main
            for i in range(3):
                at = 24 * n + 8 * i
                sides_wide[ib, at : at + 1, n * NL : (n + 1) * NL] = both[128 + i : 129 + i]

    gain_sides = []
    for ib in range(4):
        side = sides_wide[ib].astype(BF16)
        gain_sides.append(jnp.concatenate([side, side], 0))
    def put(n, p, at, rows):
        start = pl.multiple_of((n * 24 + p) * 48 + 8 + at, 8)
        kept[pl.ds(start, rows.shape[0]), :] = rows

    def row_of(ref, first, pitch):
        return ref[pl.ds(first, 24, stride=pitch), :]

    for ib in range(2):
        product = dot(beside_terms(near, far, 16 * ib, 16), gain_sides[ib + 1])
        for n in range(4):
            for p in range(24):
                put(n, p, 16 * ib, product[16 * p : 16 * p + 16, n * NL : (n + 1) * NL])

    def keep(n, _):
        for ib in range(2):
            product = dot(own_terms(parts.at[n], 16 * ib, 16), gain[ib + 1, n])
            for p in range(24):
                start = pl.ds(pl.multiple_of((n * 24 + p) * 48 + 8 + 16 * ib, 8), 16)
                kept[start, :] += product[16 * p : 16 * p + 16]
        return 0

    lax.fori_loop(0, 4, keep, 0)
    for ib in range(2):
        rows = jnp.concatenate([low_back[48 * p + 16 * ib : 48 * p + 16 * ib + 16, :] for p in range(24)], 0)
        product = dot(jnp.concatenate(two_terms(rows), 1), back[...])
        for p in range(24):
            start = 48 * p + 8 + 16 * ib
            kept[start : start + 16, :] += product[16 * p : 16 * p + 16]
    tiles = beside_tiles(near, far, 32, 8)
    for p in range(24):
        turned[8 * p : 8 * p + 8, :] = tiles[p]
    for first, ib, place, row in ((0, 3, 40, 32), (7, 0, 7, 39)):
        beside = dot(jnp.concatenate(two_terms(row_of(turned, first, 8)), 1), gain_sides[ib])
        for n in range(4) if ib else (1, 3):
            own = jnp.concatenate(two_terms(row_of(flat, n * 24 * ROWS + row, ROWS)), 1)
            total = beside[:, n * NL : (n + 1) * NL] + dot(own, gain[ib, n])
            if n == 0:
                total += dot(jnp.concatenate(two_terms(row_of(low_back, row, 48)), 1), back[...])
            kept[pl.ds(n * 24 * 48 + place, 24, stride=48), :] = total


def cells_kernel(kept, out, cells, sems):
    def back_one(step, _):
        v, t = step // 4, step % 4
        pairs = {}
        for bz in range(2):
            for z in range(8):
                p = v * 8 + z
                pairs[bz, z] = unlift_rows(
                    lambda r: kept[2 * bz, p, pl.ds(8 * t + r, 8), :],
                    lambda r: kept[2 * bz + 1, p, pl.ds(8 * t + r, 8), :],
                    8,
                )
        for parity in range(2):
            planes = unlift_planes([pairs[0, z][parity] for z in range(8)], [pairs[1, z][parity] for z in range(8)])
            for z in range(NZ):
                cells[v, z, pl.ds(16 * t + parity, 8, stride=2), :] = planes[z]
        return 0

    def copy(step):
        v, rows = step // 4, pl.ds(pl.multiple_of(16 * (step % 4), 16), 16)
        return pltpu.make_async_copy(cells.at[v, :, rows], out.at[v, :, rows], sems.at[step])

    def one(step, _):
        back_one(step, 0)
        copy(step).start()
        return 0

    lax.fori_loop(0, NV * 4, one, 0)
    for step in range(NV * 4):
        copy(step).wait()


def main_specs():
    vmem = pl.BlockSpec(memory_space=pltpu.VMEM)
    return [
        vmem, vmem, vmem, vmem, vmem,
        pl.BlockSpec((1, 8, NL), lambda i: (12, 0, 0)), pl.BlockSpec((1, 8, NL), lambda i: (18, 0, 0)),
        vmem, vmem,
    ]


def main_step(flat, *operands):
    w = weights()
    return pl.pallas_call(
        main_kernel,
        grid=(1,),
        out_shape=jax.ShapeDtypeStruct((4 * NV * 8 * 48, NL), F32),
        in_specs=main_specs(),
        out_specs=pl.BlockSpec((4 * NV * 8 * 48, NL), lambda i: (0, 0)),
        scratch_shapes=[
            pltpu.VMEM((4, 4, 256, NL), BF16),
            pltpu.VMEM((NV * 8, 64, NL), F32),
            pltpu.VMEM((4, 3, NV * 32, NL), F32),
            pltpu.VMEM((4, NV * 4, 40, NL), F32),
            pltpu.VMEM((NV * 8 * 48, NL), F32),
            pltpu.VMEM((4, 4, 256, NL), BF16),
            pltpu.VMEM((4, NL, 4 * NL), F32),
            pltpu.VMEM((NV * 64, NL), F32),
        ],
        cost_estimate=cost(8),
        compiler_params=pltpu.CompilerParams(vmem_limit_bytes=VMEM_LIMIT),
    )(flat.reshape(4, NV * 8, ROWS, NL), flat, *operands, w["wide"], w["narrow"])


def cells_step(kept):
    shape = (NV, NZ, NR, NL)
    return pl.pallas_call(
        cells_kernel,
        out_shape=jax.ShapeDtypeStruct(shape, F32),
        in_specs=[pl.BlockSpec(memory_space=pltpu.VMEM)],
        out_specs=pl.BlockSpec(memory_space=pltpu.HBM),
        scratch_shapes=[pltpu.VMEM(shape, F32), pltpu.SemaphoreType.DMA((NV * 4,))],
        cost_estimate=cost(4),
        compiler_params=pltpu.CompilerParams(vmem_limit_bytes=VMEM_LIMIT),
    )(kept)


def rows_kernel(count_x, count_z, *refs):
    shares, out = refs[:count_x], refs[count_x + 1]
    me, me_y = lax.axis_index("gx"), lax.axis_index("gy")
    row = lax.broadcasted_iota(jnp.int32, (8, NL), 0)
    lane = lax.broadcasted_iota(jnp.int32, (8, NL), 1)
    for r in range(count_x):
        at = pl.multiple_of(16 * (me ^ r), 16)
        for j in range(count_z):
            for z in range(4):
                start = 64 * j + 16 * z
                out[j, z, pl.ds(at, 16), :] = shares[r][start : start + 16, :]
    for j in range(count_z):
        turn = lanes_turn(2 * j + lax.rem(me_y, 2))
        piece = lax.rem(lane + (NL - turn), NL) // 21
        inside = [piece == p for p in range(5)]
        for r in range(count_x):
            i = me ^ r
            below = pl.multiple_of(16 * lax.rem(i + 1, count_x), 16)
            above = pl.multiple_of(16 * lax.rem(i + count_x - 1, count_x) + 8, 8)
            tiles = [shares[r][64 * j + 8 * g : 64 * j + 8 * g + 8, :] for g in range(8)]
            low, high = jnp.zeros((8, NL), F32), jnp.zeros((8, NL), F32)
            for p in range(5):
                back = (21 * p - 105) % NL
                low = jnp.where(inside[p], pltpu.roll(tiles[p], back, 1), low)
                extra = tiles[5 + p // 2]
                extra = extra if p % 2 else pltpu.roll(extra, 4, 0)
                high = jnp.where(inside[p], pltpu.roll(extra, back, 1), high)
            for z in range(4):
                first = pltpu.roll(low, 8 - 2 * z, 0) if z else low
                last = pltpu.roll(high, z, 0) if z else high
                out[j, z, pl.ds(below, 8), :] += jnp.where(row < 2, first, 0.0)
                out[j, z, pl.ds(above, 8), :] += jnp.where(row == 7, last, 0.0)


def rows_step(pieces, count_z, after):
    vmem = pl.BlockSpec(memory_space=pltpu.VMEM)
    count_x = len(pieces)
    return pl.pallas_call(
        functools.partial(rows_kernel, count_x, count_z),
        out_shape=jax.ShapeDtypeStruct((count_z, 4, 16 * count_x, NL), F32),
        in_specs=[vmem] * count_x + [pl.BlockSpec(memory_space=pl.ANY)],
        out_specs=vmem,
        compiler_params=pltpu.CompilerParams(vmem_limit_bytes=VMEM_LIMIT),
    )(*pieces, after)


def coarse_kernel(count_x, count_y, own, other, out_hbm, out, sems):
    me = lax.axis_index("gy")
    is_even = lax.rem(me, 2) == 0
    lane = lax.broadcasted_iota(jnp.int32, (8, NL), 1)
    place = [lax.rem(lane + NL - 35 * v, NL) for v in range(NV)]

    def block(i, _):
        rows = pl.ds(pl.multiple_of(8 * i, 8), 8)
        for z in range(4):
            pieces = []
            for j in range(count_y // 2):
                mine, theirs = own[j, z, rows, :], other[j, z, rows, :]
                pieces += [jnp.where(is_even, mine, theirs), jnp.where(is_even, theirs, mine)]
            for v in range(NV):
                at = place[v]
                for t in range(count_y // 4):
                    total = jnp.where(at < 2, pieces[4 * t - 1], 0.0)
                    total += jnp.where(at == NL - 1, pieces[(4 * t + 4) % count_y], 0.0)
                    for q in range(4):
                        inside = (at >= 32 * q - 1) & (at < 32 * q + 34)
                        total += jnp.where(inside, pieces[4 * t + q], 0.0)
                    out[v, z, rows, NL * t : NL * (t + 1)] = pltpu.roll(total, NL - 35 * v, 1) if v else total
        return 0

    def copy(i):
        rows = pl.ds(pl.multiple_of(16 * i, 16), 16)
        return pltpu.make_async_copy(out.at[:, :, rows], out_hbm.at[:, :, rows], sems.at[i])

    def pair(i, _):
        block(2 * i, 0)
        block(2 * i + 1, 0)
        copy(i).start()
        return 0

    lax.fori_loop(0, count_x, pair, 0)
    for i in range(count_x):
        copy(i).wait()


def coarse_step(own, other, count_x, count_y):
    vmem = pl.BlockSpec(memory_space=pltpu.VMEM)
    shape = (NV, 4, 16 * count_x, 32 * count_y)
    return pl.pallas_call(
        functools.partial(coarse_kernel, count_x, count_y),
        out_shape=jax.ShapeDtypeStruct(shape, F32),
        in_specs=[vmem, vmem],
        out_specs=pl.BlockSpec(memory_space=pltpu.HBM),
        scratch_shapes=[pltpu.VMEM(shape, F32), pltpu.SemaphoreType.DMA((count_x,))],
        compiler_params=pltpu.CompilerParams(vmem_limit_bytes=VMEM_LIMIT),
    )(own, other)


def shifted(x, axis, step):
    count = lax.axis_size(axis)
    return lax.ppermute(x, axis, [(i, (i + step) % count) for i in range(count)])


def swapped(x, axis, distance):
    return lax.ppermute(x, axis, [(i, i ^ distance) for i in range(lax.axis_size(axis))])


def crossed(x, axis):
    count = lax.axis_size(axis)
    return lax.ppermute(x, axis, [(i, (i + (1 if i % 2 else count - 1)) % count) for i in range(count)])


def body(field, masks):
    count_x, count_y = lax.axis_size("gx"), lax.axis_size("gy")
    lifted, up, down, own_masks, share = first_step(field, masks)
    south = shifted(up, "gx", -1)
    north = shifted(down, "gx", 1)
    same_core = [list(range(c, count_y, 2)) for c in range(2)]
    joined = lax.all_gather(share, "gy", axis=0, tiled=True, axis_index_groups=same_core)
    parts, sides = edge_step(lift_step(lifted), lifted, north, south, own_masks)
    near, far = swapped(sides, "gy", 1), crossed(sides, "gy")
    pieces = [joined] + [swapped(joined, "gx", r) for r in range(1, count_x)]
    kept = main_step(parts, near, far, own_masks, north, south)
    own = rows_step(pieces, count_y // 2, kept)
    other = swapped(own, "gy", 1)
    return cells_step(kept.reshape(4, NV * 8, 48, NL)), coarse_step(own, other, count_x, count_y)


def solution(mesh):
    placed = P(None, None, "gx", "gy")
    return jax.shard_map(
        body,
        mesh=mesh,
        in_specs=(placed, placed),
        out_specs=(placed, P()),
        check_vma=False,
    )
```

```python
import functools

import jax
import jax.numpy as jnp
import ml_dtypes
import numpy as np
from jax import lax
from jax.experimental import pallas as pl
from jax.experimental.pallas import tpu as pltpu
from jax.sharding import PartitionSpec as P

F32 = jnp.float32
BF16 = jnp.bfloat16
VMEM_LIMIT = 32 * 1024 * 1024

NV, NZ, NR, NL = 3, 16, 64, 128


def detail_row(k):
    return {2 * k + 1: 1.0, 2 * k: -0.5, 2 * k + 2: -0.5}


def smooth_row(k):
    row = {2 * k: 1.0}
    for j in (k - 1, k):
        for cell, value in detail_row(j).items():
            row[cell] = row.get(cell, 0.0) + 0.25 * value
    return row


def even_row(k):
    return {("s", k): 1.0, ("d", k - 1): -0.25, ("d", k): -0.25}


def odd_row(k):
    row = {("d", k): 1.0}
    for j in (k, k + 1):
        for name, value in even_row(j).items():
            row[name] = row.get(name, 0.0) + 0.5 * value
    return row


def as_bf16(matrix):
    cast = matrix.astype(ml_dtypes.bfloat16)
    assert (cast.astype(np.float64) == matrix).all()
    return cast


def combine(*terms):
    total = {}
    for factor, row in terms:
        for cell, value in row.items():
            total[cell] = total.get(cell, 0.0) + factor * value
    return total


def level_one_columns():
    names = {("s", k): k for k in range(65)}
    names.update({("d", k): 128 + k for k in range(65)})
    names[("d", -1)] = 128 + 65
    return names


def level_two_columns():
    names = {("s", k): k for k in range(33)}
    names.update({("d", k): 64 + k for k in range(33)})
    names[("d", -1)] = 64 + 33
    return names


def smooth_place(k):
    return k + 2


def beyond(n):
    return {"cell": 24 * n, "after": 24 * n + 8, "before": 24 * n + 16}


BEYOND_SMOOTH = {65: 96, 66: 104, -2: 112, -1: 120}


def own_row(kind, k, n):
    place = {name: 128 + lane for name, lane in beyond(n).items()}
    if kind == "d":
        if k == -1:
            return {place["before"]: 1.0, 0: -0.5}
        if k == 64:
            return {place["after"]: 1.0}
        return {(place["cell"] if y == 128 else y): value for y, value in detail_row(k).items()}
    if k in BEYOND_SMOOTH:
        row = {128 + BEYOND_SMOOTH[k]: 1.0}
        return combine((1.0, row), (1.0, {0: -0.125})) if k == -1 else row
    even = place["cell"] if k == 64 else 2 * k
    return combine((1.0, {even: 1.0}), (0.25, own_row("d", k - 1, n)), (0.25, own_row("d", k, n)))


@functools.lru_cache(maxsize=None)
def weights():
    w = {}
    names = level_one_columns()
    forward = np.zeros((4, 256, 256))
    inverse = np.zeros((256, 128))
    for (kind, k), column in names.items():
        for n in range(4):
            for place, value in own_row(kind, k, n).items():
                forward[n, place, column] += value
    for k in range(64):
        for y, row in ((2 * k, even_row(k)), (2 * k + 1, odd_row(k))):
            for name, value in row.items():
                inverse[names[name], y] += value
    short = np.zeros((144, 256))
    short[:128] = forward[0, :128]
    for i, lane in enumerate(beyond(0).values()):
        short[128 + i] = forward[0, 128 + lane]
    smooth = np.zeros((256, 128))
    for k in range(-2, 67):
        for place, value in own_row("s", k, 0).items():
            smooth[place, smooth_place(k)] += value
    names2 = level_two_columns()
    forward2 = np.zeros((128, 128))
    inverse2 = np.zeros((128, 128))
    for (kind, k), column in names2.items():
        for cell, value in (smooth_row(k) if kind == "s" else detail_row(k)).items():
            forward2[smooth_place(cell), column] += value
    for k in range(33):
        rows = [(2 * k, even_row(k))] + ([(2 * k + 1, odd_row(k))] if k < 32 else [])
        for y, row in rows:
            for name, value in row.items():
                inverse2[names2[name], y] += value
    back = np.zeros((256, 128))
    back[:65] = inverse[:65]
    back[128 : 128 + 65] = inverse[:65]
    spread = np.zeros((3, 128, 2, 128))
    for k in range(64):
        spread[0, k, 0, k] = 1
    spread[1, 0, 0, 64] = 1
    spread[2, 63, 0, 65] = 1
    for k in range(32):
        spread[0, 64 + k, 1, k] = 1
        spread[0, 64 + k, 1, 64 + k] = 1
    for base in (0, 64):
        spread[1, 64, 1, base + 32] = 1
        spread[2, 95, 1, base + 33] = 1
    w["wide"] = np.concatenate([short, spread.reshape(384, 256)], 0)
    own, beside = smooth[:128], smooth[128:]
    w["narrow"] = np.concatenate([inverse, own, own, beside, beside, back, forward2, inverse2], 0)
    edge = np.zeros((4, 128, 128))

    def put(n, lane, row):
        for z in range(8):
            for y, value in row.items():
                j = y - 120 if y >= 120 else y + 8
                edge[n, 16 * z + j, lane + z] += value

    part = {127: 1.0, 126: -0.5}
    for n in range(4):
        put(n, beyond(n)["cell"], {0: 1.0})
        put(n, beyond(n)["after"], detail_row(0))
        put(n, beyond(n)["before"], part)
    put(0, BEYOND_SMOOTH[65], smooth_row(1))
    put(0, BEYOND_SMOOTH[66], smooth_row(2))
    put(0, BEYOND_SMOOTH[-2], smooth_row(62))
    put(0, BEYOND_SMOOTH[-1], combine((1.0, {126: 1.0}), (0.25, detail_row(62)), (0.25, part)))
    w["edge"] = edge.reshape(512, 128)
    expand = np.zeros((2, 4, 128))
    for j in range(4):
        expand[0, j, 16 * j : 16 * j + 16] = 1
        expand[1, j, 64 + 8 * j : 64 + 8 * j + 8] = 1
    twice = combine(*[(value, smooth_row(k)) for k, value in smooth_row(0).items()])
    columns = np.zeros((2, 128, 128))
    for m in range(-1, 34):
        for t, value in twice.items():
            if 0 <= 4 * m + t < NL:
                columns[:, 4 * m + t, m + 1] = value
    rows = np.zeros((4, 32, 2, 64))
    for z in range(4):
        places = {m: m for m in range(16)}
        places.update({16: 16 + 2 * z, 17: 17 + 2 * z, -1: 16 + 15 - z})
        for m, place in places.items():
            for t, value in twice.items():
                if 0 <= 4 * m + t < NR:
                    rows[z, place, :, 4 * m + t] = value
    pad = np.zeros((8, 128))
    w["first"] = np.concatenate([columns.reshape(256, 128), rows.reshape(128, 128), expand.reshape(8, 128), pad], 0)
    return {name: as_bf16(matrix) for name, matrix in w.items()}


def two_terms(x):
    high = x.astype(BF16)
    low = (x - high.astype(F32)).astype(BF16)
    return high, low


def cost(gigaflops):
    return pl.CostEstimate(flops=gigaflops * 10**9, bytes_accessed=8 * 10**6, transcendentals=0)


def dot(a, b):
    return jnp.dot(a, b, preferred_element_type=F32)


def lift_planes(cells):
    half = len(cells) // 2
    even, odd = cells[0::2], cells[1::2]
    detail = [odd[k] - 0.5 * (even[k] + even[min(k + 1, half - 1)]) for k in range(half)]
    smooth = [even[k] + 0.25 * (detail[max(k - 1, 0)] + detail[k]) for k in range(half)]
    return smooth, detail


def unlift_planes(smooth, detail):
    half = len(smooth)
    even = [smooth[k] - 0.25 * (detail[max(k - 1, 0)] + detail[k]) for k in range(half)]
    out = []
    for k in range(half):
        out += [even[k], detail[k] + 0.5 * (even[k] + even[min(k + 1, half - 1)])]
    return out


def lift_rows(load, start):
    even, odd, after = load(start), load(start + 1), load(start + 2)
    before, odd_before = load(start - 2), load(start - 1)
    detail = odd - 0.5 * (even + after)
    detail_before = odd_before - 0.5 * (before + even)
    return even + 0.25 * (detail_before + detail), detail


def unlift_rows(smooth, detail, row):
    here, after = detail(row), detail(row + 1)
    even = smooth(row) - 0.25 * (detail(row - 1) + here)
    next_even = smooth(row + 1) - 0.25 * (here + after)
    return even, here + 0.5 * (even + next_even)


PITCH = 80


def lanes_turn(j):
    return lax.rem(32 * lax.rem(j, 4) + NL - 1, NL)


def first_kernel(
    field, masks_hbm, table_hbm, lifted, up, down, own_masks, share, cells, twice, masks, table, sems
):
    small = [
        pltpu.make_async_copy(masks_hbm, masks, sems.at[0]),
        pltpu.make_async_copy(table_hbm, table, sems.at[1]),
    ]
    copies = []
    for v in range(NV):
        for c in range(4):
            part = pl.ds(16 * c, 16)
            copies.append(pltpu.make_async_copy(field.at[v, :, part], cells.at[v, :, part], sems.at[2 + 4 * v + c]))
    for copy in small + copies:
        copy.start()
    for p in range(NV * NZ):
        lifted[p * PITCH : p * PITCH + 8, :] = jnp.zeros((8, NL), F32)
        lifted[p * PITCH + 72 : p * PITCH + 80, :] = jnp.zeros((8, NL), F32)
    for copy in small:
        copy.wait()
    for i, out, tile in ((0, up, 18), (1, down, 12)):
        total = jnp.zeros((7, NL), F32)
        for l in range(2):
            flags = masks[l, i].astype(F32).astype(BF16)
            spread = table[384 + 4 * l : 388 + 4 * l, :]
            total += lax.dot_general(flags, spread, (((0,), (0,)), ((), ())), preferred_element_type=F32)
        own_masks[i] = jnp.concatenate([total, jnp.zeros((1, NL), F32)], 0)
        out[tile] = own_masks[i]

    for v in range(NV):
        for t in range(8):
            if t % 2 == 0:
                copies[4 * v + t // 2].wait()
            smooth, detail = lift_planes([cells[v, z, 8 * t : 8 * t + 8, :] for z in range(NZ)])
            for k, tile in enumerate(smooth + detail):
                start = (v * NZ + k) * PITCH + 8 + 8 * t
                lifted[start : start + 8, :] = tile
            for k, tile in enumerate(lift_planes(smooth)[0]):
                twice[v * 4 + k, 8 * t : 8 * t + 8, :] = tile
        for bz in range(2):

            def row(x):
                return lifted[pl.ds((v * NZ + bz * 8) * PITCH + 8 + x, 8, stride=PITCH), :]

            x = [row(j) for j in range(7 if bz == 0 else 3)]
            first = x[1] - 0.5 * (x[0] + x[2])
            up[v * 6 + bz] = x[0]
            up[v * 6 + 2 + bz] = first
            y = {j: row(j) for j in (range(58, 64) if bz == 0 else (62, 63))}
            part = y[63] - 0.5 * y[62]
            down[v * 4 + bz] = part
            if bz == 0:
                second = x[3] - 0.5 * (x[2] + x[4])
                third = x[5] - 0.5 * (x[4] + x[6])
                up[v * 6 + 4] = x[2] + 0.25 * (first + second)
                up[v * 6 + 5] = x[4] + 0.25 * (second + third)
                before = y[59] - 0.5 * (y[58] + y[60])
                last = y[61] - 0.5 * (y[60] + y[62])
                down[v * 4 + 2] = y[60] + 0.25 * (before + last)
                down[v * 4 + 3] = y[62] + 0.25 * (last + part)

    total = jnp.zeros((80, NL), F32)
    for v in range(NV):
        main, extra = [], jnp.zeros((16, NL), F32)
        for z in range(4):
            terms = jnp.concatenate(two_terms(twice[v * 4 + z]), 0)
            part = dot(table[256 + 32 * z : 288 + 32 * z, :], terms)
            main.append(part[:16])
            extra += part[16:]
        terms = jnp.concatenate(two_terms(jnp.concatenate(main + [extra], 0)), 1)
        part = dot(terms, table[0:256, :])
        total += pltpu.roll(part, 35 * v, 1) if v else part
    turn = lanes_turn(lax.axis_index("gy"))
    lane = lax.broadcasted_iota(jnp.int32, (8, NL), 1)
    spare = (lane >= 105) & (lane < 126)
    upper = lax.broadcasted_iota(jnp.int32, (8, NL), 0) < 4
    below, above = total[64:72], total[72:80]
    pieces = [pltpu.roll(above, 105 - 21 * p, 1) for p in range(5)]
    for g in range(8):
        if g < 5:
            extra = pltpu.roll(below, 105 - 21 * g, 1)
        else:
            extra = pltpu.roll(pieces[2 * g - 10], 4, 0)
            extra = jnp.where(upper, extra, pieces[2 * g - 9] if g < 7 else 0.0)
        tile = jnp.where(spare, extra, total[8 * g : 8 * g + 8])
        share[8 * g : 8 * g + 8, :] = pltpu.roll(tile, turn, 1)


def in_hbm(x):
    return pltpu.with_memory_space_constraint(x, pltpu.HBM)


def first_step(field, masks):
    vmem = pl.BlockSpec(memory_space=pltpu.VMEM)
    shapes = [(NV * NZ * PITCH, NL), (19, 8, NL), (13, 8, NL), (2, 8, NL), (64, NL)]
    return pl.pallas_call(
        first_kernel,
        out_shape=[jax.ShapeDtypeStruct(s, F32) for s in shapes],
        in_specs=[pl.BlockSpec(memory_space=pltpu.HBM)] * 3,
        out_specs=[vmem] * 5,
        scratch_shapes=[
            pltpu.VMEM((NV, NZ, NR, NL), F32),
            pltpu.VMEM((NV * 4, NR, NL), F32),
            pltpu.VMEM((2, 2, 4, 7), jnp.int32),
            pltpu.VMEM((400, NL), BF16),
            pltpu.SemaphoreType.DMA((4 * NV + 2,)),
        ],
        compiler_params=pltpu.CompilerParams(vmem_limit_bytes=VMEM_LIMIT),
    )(*[in_hbm(x) for x in (field, masks.transpose(0, 2, 3, 1), jnp.asarray(weights()["first"]))])


ROWS = 40


def lift_kernel(lifted, parts):
    def lift(step, _):
        v, bz = step // 2, lax.rem(step, 2)
        for z in range(8):
            start = pl.multiple_of((step * 8 + z) * PITCH, 8)
            for t in range(4):
                pair = lift_rows(lambda s: lifted[pl.ds(start + 16 * t + s, 8, stride=2), :], 8)
                for bx in range(2):
                    plane = (2 * bz + bx) * 24 + v * 8 + z
                    parts[pl.ds(pl.multiple_of(plane * ROWS + 8 * t, 8), 8), :] = pair[bx]
        return 0

    lax.fori_loop(0, NV * 2, lift, 0)


def lift_step(lifted):
    vmem = pl.BlockSpec(memory_space=pltpu.VMEM)
    return pl.pallas_call(
        lift_kernel,
        out_shape=jax.ShapeDtypeStruct((4 * NV * 8 * ROWS, NL), F32),
        in_specs=[vmem],
        out_specs=vmem,
        compiler_params=pltpu.CompilerParams(vmem_limit_bytes=VMEM_LIMIT),
    )(lifted)


def edge_kernel(parts_in, lifted, north, south, own_masks, table_hbm, parts, sides, packed, table, sem):
    copy = pltpu.make_async_copy(table_hbm, table, sem.at[0])
    copy.start()
    for p in range(4 * NV * 8):
        parts[p * ROWS + 32 : p * ROWS + 40, :] = jnp.zeros((8, NL), F32)
    for v in range(NV):
        for bz in range(2):

            def cell(x):
                return lifted[pl.ds((v * NZ + bz * 8) * PITCH + 8 + x, 8, stride=PITCH), :]

            def at(bx, r):
                return pl.ds(((2 * bz + bx) * 24 + v * 8) * ROWS + r, 8, stride=ROWS)

            before, after, detail = north[v * 4 + bz], south[v * 6 + bz], south[v * 6 + 2 + bz]
            start = cell(0)
            last = cell(63) - 0.5 * (cell(62) + after)
            parts[at(0, 0), :] = parts[at(0, 0), :] + 0.25 * before
            parts[at(0, 31), :] = parts[at(0, 31), :] - 0.125 * after
            parts[at(1, 31), :] = parts[at(1, 31), :] - 0.5 * after
            parts[at(0, 32), :] = after + 0.25 * (last + detail)
            parts[at(1, 32), :] = detail
            parts[at(1, 39), :] = before - 0.5 * start
            if bz == 0:
                parts[at(0, 33), :] = south[v * 6 + 4]
                parts[at(0, 34), :] = south[v * 6 + 5]
                parts[at(0, 38), :] = north[v * 4 + 2]
                parts[at(0, 39), :] = north[v * 4 + 3] - 0.125 * start

    lane = lax.broadcasted_iota(jnp.int32, (8, NL), 1) // 16

    def pack(v, _):
        for n in range(4):
            for t in range(5):
                tile = jnp.zeros((8, NL), F32)
                for z in range(8):
                    start = (n * 24 + v * 8 + z) * ROWS + 8 * t
                    x = parts[pl.ds(pl.multiple_of(start, 8), 8), :]
                    tile = jnp.where(lane == z, pltpu.roll(x, (8 + 16 * z) % NL, 1), tile)
                packed[pl.ds(pl.multiple_of(n * 120 + v * ROWS + 8 * t, 8), 8), :] = tile
        return 0

    lax.fori_loop(0, NV, pack, 0)
    copy.wait()
    terms = [two_terms(packed[n * 120 : (n + 1) * 120, :]) for n in range(4)]
    high, low = [jnp.concatenate(part, 1) for part in zip(*terms)]
    sides[0:120, :] = dot(high, table[...]) + dot(low, table[...])
    sides[120:128, :] = north[12]
    sides[128:136, :] = own_masks[0]
    sides[136:144, :] = own_masks[1]
    sides[144:152, :] = south[18]


def edge_step(parts, lifted, north, south, own_masks):
    vmem = pl.BlockSpec(memory_space=pltpu.VMEM)
    shapes = [(4 * NV * 8 * ROWS, NL), (152, NL)]
    return pl.pallas_call(
        edge_kernel,
        out_shape=[jax.ShapeDtypeStruct(s, F32) for s in shapes],
        in_specs=[vmem] * 5 + [pl.BlockSpec(memory_space=pltpu.HBM)],
        out_specs=[vmem] * 2,
        input_output_aliases={0: 0},
        cost_estimate=cost(20),
        scratch_shapes=[pltpu.VMEM((480, NL), F32), pltpu.VMEM((512, NL), BF16), pltpu.SemaphoreType.DMA((1,))],
        compiler_params=pltpu.CompilerParams(vmem_limit_bytes=VMEM_LIMIT),
    )(parts, lifted, north, south, own_masks, in_hbm(jnp.asarray(weights()["edge"])))


def join_kernel(*refs):
    shares, out = refs[:-2], refs[-1]
    for n, piece in enumerate(shares):
        out[64 * n : 64 * (n + 1), :] = piece[...]


def join_step(shares, after):
    vmem = pl.BlockSpec(memory_space=pltpu.VMEM)
    return pl.pallas_call(
        join_kernel,
        out_shape=jax.ShapeDtypeStruct((64 * len(shares), NL), F32),
        in_specs=[vmem] * len(shares) + [pl.BlockSpec(memory_space=pl.ANY)],
        out_specs=vmem,
        cost_estimate=cost(20),
        compiler_params=pltpu.CompilerParams(vmem_limit_bytes=VMEM_LIMIT),
    )(*shares, after)


def mask_lanes(west, east, own_masks, north_mask, south_mask, wide):
    masks = [jnp.concatenate([ref[120 + 8 * i : 128 + 8 * i, :] for i in range(4)], 0) for ref in (east, west)]
    own = jnp.concatenate([north_mask[0], own_masks[0], own_masks[1], south_mask[0]], 0)
    flags = jnp.concatenate([own] + masks, 1).astype(BF16)
    return dot(flags, wide[144:528, :])


def beside_tiles(west, east, at, count):
    lane = lax.broadcasted_iota(jnp.int32, (count, NL), 1)
    from_west = (lane >= 112) | ((lane < 96) & (lax.rem(lane, 24) >= 16))
    tiles = []
    for v in range(NV):
        rows = slice(v * ROWS + at, v * ROWS + at + count)
        beside = jnp.where(from_west, west[rows, :], east[rows, :])
        tiles += [pltpu.roll(beside, NL - z, 1) if z else beside for z in range(8)]
    return tiles


def beside_terms(west, east, at, count):
    return jnp.concatenate(two_terms(jnp.concatenate(beside_tiles(west, east, at, count), 0)), 1)


def own_terms(planes, at, count):
    return jnp.concatenate(two_terms(planes[:, at : at + count, :].reshape(24 * count, NL)), 1)


def main_kernel(
    parts, flat, east, west, own_masks, north_mask, south_mask, wide, narrow,
    kept,
    gain2, low, second, kept2, low_back, gain, sides_wide, turned,
):
    inverse, smooth_own, smooth_beside = narrow.at[0:256], narrow.at[256:512], narrow.at[512:768]
    back, forward2, inverse2 = narrow.at[768:1024], narrow.at[1024:1152], narrow.at[1152:1280]
    lanes = mask_lanes(west, east, own_masks, north_mask, south_mask, wide)
    lane64 = lax.broadcasted_iota(jnp.int32, (1, NL), 1) < 64
    forward2_f = forward2[...].astype(F32)
    for ib in range(4):
        for n in range(4):
            b = 8 * ib + 4 * (n // 2) + n % 2 - 1
            smooth_two = lanes[b : b + 1, NL:] if n else jnp.ones((1, NL), F32)
            row = jnp.where(lane64, smooth_two, lanes[b + 2 : b + 3, NL:])
            both = dot((forward2_f * row).astype(BF16), inverse2[...]).astype(BF16)
            gain2[ib, n, 0:128, :] = both
            gain2[ib, n, 128:256, :] = both

    for at, count in ((0, 16), (16, 16), (32, 8)):
        part = dot(own_terms(parts.at[0], at, count), smooth_own[...])
        part += dot(beside_terms(west, east, at, count), smooth_beside[...])
        part = part.reshape(24, count, NL)
        if at < 32:
            low[:, 8 + at : 8 + at + count, :] = part
            if at == 0:
                low[:, 56:64, :] = part[:, 0:8]
        else:
            low[:, 0:8, :] = part
            low[:, 40:48, :] = part
            low[:, 48:56, :] = part

    def rows_two(v, _):
        for t in range(3):
            lifted = [
                lift_rows(lambda s: low[v * 8 + p, pl.ds(16 * t + s, 8, stride=2), :], 8) for p in range(8)
            ]
            for bx in range(2):
                smooth, detail = lift_planes([pair[bx] for pair in lifted])
                for bz, part in ((0, smooth), (1, detail)):
                    for z in range(4):
                        second[2 * bz + bx, t, pl.ds(pl.multiple_of((v * 4 + z) * 8, 8), 8), :] = part[z]
        return 0

    lax.fori_loop(0, NV, rows_two, 0)
    for n in range(4):
        for t in range(3):
            terms = jnp.concatenate(two_terms(second[n, t]), 1)
            if t < 2:
                kept2[n, :, 8 + 8 * t : 16 + 8 * t, :] = dot(terms, gain2[t + 1, n]).reshape(NV * 4, 8, NL)
            else:
                kept2[n, :, 0:8, :] = dot(terms, gain2[0, n]).reshape(NV * 4, 8, NL)
                kept2[n, :, 24:32, :] = dot(terms, gain2[3, n]).reshape(NV * 4, 8, NL)

    def back_two(v, _):
        for t in range(3):
            pairs = {}
            for bz in range(2):
                for z in range(4):
                    p = v * 4 + z
                    if t < 2:
                        pairs[bz, z] = unlift_rows(
                            lambda r: kept2[2 * bz, p, pl.ds(r, 8), :],
                            lambda r: kept2[2 * bz + 1, p, pl.ds(r, 8), :],
                            8 + 8 * t,
                        )
                    else:
                        even = kept2[2 * bz, p, 24:32, :] - 0.25 * (
                            kept2[2 * bz + 1, p, 23:31, :] + kept2[2 * bz + 1, p, 24:32, :]
                        )
                        pairs[bz, z] = (even, even)
            for parity in range(2 if t < 2 else 1):
                planes = unlift_planes([pairs[0, z][parity] for z in range(4)], [pairs[1, z][parity] for z in range(4)])
                for z in range(8):
                    low_back[pl.ds((v * 8 + z) * 48 + 16 * t + parity, 8, stride=2), :] = planes[z]
        return 0

    lax.fori_loop(0, NV, back_two, 0)

    forward_f = wide[0:144, :].astype(F32)
    for ib in range(4):
        sides_wide[ib] = jnp.zeros((NL, 4 * NL), F32)
    for ib in range(4):
        for n in range(4):
            b = 8 * ib + 4 * (n // 2) + n % 2 - 1
            smooth_one = lanes[b : b + 1, 0:NL] if n else jnp.zeros((1, NL), F32)
            row = jnp.concatenate([smooth_one, lanes[b + 2 : b + 3, 0:NL]], 1)
            both = dot((forward_f * row).astype(BF16), inverse[...])
            main = both[0:128].astype(BF16)
            gain[ib, n, 0:128, :] = main
            gain[ib, n, 128:256, :] = main
            for i in range(3):
                at = 24 * n + 8 * i
                sides_wide[ib, at : at + 1, n * NL : (n + 1) * NL] = both[128 + i : 129 + i]

    gain_sides = []
    for ib in range(4):
        side = sides_wide[ib].astype(BF16)
        gain_sides.append(jnp.concatenate([side, side], 0))
    def put(n, p, at, rows):
        start = pl.multiple_of((n * 24 + p) * 48 + 8 + at, 8)
        kept[pl.ds(start, rows.shape[0]), :] = rows

    def row_of(ref, first, pitch):
        return ref[pl.ds(first, 24, stride=pitch), :]

    for ib in range(2):
        product = dot(beside_terms(west, east, 16 * ib, 16), gain_sides[ib + 1])
        for n in range(4):
            for p in range(24):
                put(n, p, 16 * ib, product[16 * p : 16 * p + 16, n * NL : (n + 1) * NL])

    def keep(n, _):
        for ib in range(2):
            product = dot(own_terms(parts.at[n], 16 * ib, 16), gain[ib + 1, n])
            for p in range(24):
                start = pl.ds(pl.multiple_of((n * 24 + p) * 48 + 8 + 16 * ib, 8), 16)
                kept[start, :] += product[16 * p : 16 * p + 16]
        return 0

    lax.fori_loop(0, 4, keep, 0)
    for ib in range(2):
        rows = jnp.concatenate([low_back[48 * p + 16 * ib : 48 * p + 16 * ib + 16, :] for p in range(24)], 0)
        product = dot(jnp.concatenate(two_terms(rows), 1), back[...])
        for p in range(24):
            start = 48 * p + 8 + 16 * ib
            kept[start : start + 16, :] += product[16 * p : 16 * p + 16]
    tiles = beside_tiles(west, east, 32, 8)
    for p in range(24):
        turned[8 * p : 8 * p + 8, :] = tiles[p]
    for first, ib, place, row in ((0, 3, 40, 32), (7, 0, 7, 39)):
        beside = dot(jnp.concatenate(two_terms(row_of(turned, first, 8)), 1), gain_sides[ib])
        for n in range(4) if ib else (1, 3):
            own = jnp.concatenate(two_terms(row_of(flat, n * 24 * ROWS + row, ROWS)), 1)
            total = beside[:, n * NL : (n + 1) * NL] + dot(own, gain[ib, n])
            if n == 0:
                total += dot(jnp.concatenate(two_terms(row_of(low_back, row, 48)), 1), back[...])
            kept[pl.ds(n * 24 * 48 + place, 24, stride=48), :] = total


def cells_kernel(kept, out, cells, sems):
    def back_one(step, _):
        v, t = step // 4, step % 4
        pairs = {}
        for bz in range(2):
            for z in range(8):
                p = v * 8 + z
                pairs[bz, z] = unlift_rows(
                    lambda r: kept[2 * bz, p, pl.ds(8 * t + r, 8), :],
                    lambda r: kept[2 * bz + 1, p, pl.ds(8 * t + r, 8), :],
                    8,
                )
        for parity in range(2):
            planes = unlift_planes([pairs[0, z][parity] for z in range(8)], [pairs[1, z][parity] for z in range(8)])
            for z in range(NZ):
                cells[v, z, pl.ds(16 * t + parity, 8, stride=2), :] = planes[z]
        return 0

    def copy(step):
        v, rows = step // 4, pl.ds(pl.multiple_of(16 * (step % 4), 16), 16)
        return pltpu.make_async_copy(cells.at[v, :, rows], out.at[v, :, rows], sems.at[step])

    def one(step, _):
        back_one(step, 0)
        copy(step).start()
        return 0

    lax.fori_loop(0, NV * 4, one, 0)
    for step in range(NV * 4):
        copy(step).wait()


def main_specs():
    vmem = pl.BlockSpec(memory_space=pltpu.VMEM)
    return [
        vmem, vmem, vmem, vmem, vmem,
        pl.BlockSpec((1, 8, NL), lambda i: (12, 0, 0)), pl.BlockSpec((1, 8, NL), lambda i: (18, 0, 0)),
        vmem, vmem,
    ]


def main_step(flat, *operands):
    w = weights()
    return pl.pallas_call(
        main_kernel,
        grid=(1,),
        out_shape=jax.ShapeDtypeStruct((4 * NV * 8 * 48, NL), F32),
        in_specs=main_specs(),
        out_specs=pl.BlockSpec((4 * NV * 8 * 48, NL), lambda i: (0, 0)),
        scratch_shapes=[
            pltpu.VMEM((4, 4, 256, NL), BF16),
            pltpu.VMEM((NV * 8, 64, NL), F32),
            pltpu.VMEM((4, 3, NV * 32, NL), F32),
            pltpu.VMEM((4, NV * 4, 40, NL), F32),
            pltpu.VMEM((NV * 8 * 48, NL), F32),
            pltpu.VMEM((4, 4, 256, NL), BF16),
            pltpu.VMEM((4, NL, 4 * NL), F32),
            pltpu.VMEM((NV * 64, NL), F32),
        ],
        cost_estimate=cost(8),
        compiler_params=pltpu.CompilerParams(vmem_limit_bytes=VMEM_LIMIT),
    )(flat.reshape(4, NV * 8, ROWS, NL), flat, *operands, w["wide"], w["narrow"])


def cells_step(kept):
    shape = (NV, NZ, NR, NL)
    return pl.pallas_call(
        cells_kernel,
        out_shape=jax.ShapeDtypeStruct(shape, F32),
        in_specs=[pl.BlockSpec(memory_space=pltpu.VMEM)],
        out_specs=pl.BlockSpec(memory_space=pltpu.HBM),
        scratch_shapes=[pltpu.VMEM(shape, F32), pltpu.SemaphoreType.DMA((NV * 4,))],
        cost_estimate=cost(4),
        compiler_params=pltpu.CompilerParams(vmem_limit_bytes=VMEM_LIMIT),
    )(kept)


def rows_kernel(count_x, count_z, *refs):
    shares, out = refs[:count_x], refs[count_x + 1]
    me, me_y = lax.axis_index("gx"), lax.axis_index("gy")
    row = lax.broadcasted_iota(jnp.int32, (8, NL), 0)
    lane = lax.broadcasted_iota(jnp.int32, (8, NL), 1)
    for r in range(count_x):
        at = pl.multiple_of(16 * (me ^ r), 16)
        for j in range(count_z):
            for z in range(4):
                start = 64 * j + 16 * z
                out[j, z, pl.ds(at, 16), :] = shares[r][start : start + 16, :]
    for j in range(count_z):
        turn = lanes_turn(me_y ^ (2 * j))
        piece = lax.rem(lane + (NL - turn), NL) // 21
        inside = [piece == p for p in range(5)]
        for r in range(count_x):
            i = me ^ r
            below = pl.multiple_of(16 * lax.rem(i + 1, count_x), 16)
            above = pl.multiple_of(16 * lax.rem(i + count_x - 1, count_x) + 8, 8)
            tiles = [shares[r][64 * j + 8 * g : 64 * j + 8 * g + 8, :] for g in range(8)]
            low, high = jnp.zeros((8, NL), F32), jnp.zeros((8, NL), F32)
            for p in range(5):
                back = (21 * p - 105) % NL
                low = jnp.where(inside[p], pltpu.roll(tiles[p], back, 1), low)
                extra = tiles[5 + p // 2]
                extra = extra if p % 2 else pltpu.roll(extra, 4, 0)
                high = jnp.where(inside[p], pltpu.roll(extra, back, 1), high)
            for z in range(4):
                first = pltpu.roll(low, 8 - 2 * z, 0) if z else low
                last = pltpu.roll(high, z, 0) if z else high
                out[j, z, pl.ds(below, 8), :] += jnp.where(row < 2, first, 0.0)
                out[j, z, pl.ds(above, 8), :] += jnp.where(row == 7, last, 0.0)


def rows_step(pieces, count_z, after):
    vmem = pl.BlockSpec(memory_space=pltpu.VMEM)
    count_x = len(pieces)
    return pl.pallas_call(
        functools.partial(rows_kernel, count_x, count_z),
        out_shape=jax.ShapeDtypeStruct((count_z, 4, 16 * count_x, NL), F32),
        in_specs=[vmem] * count_x + [pl.BlockSpec(memory_space=pl.ANY)],
        out_specs=vmem,
        compiler_params=pltpu.CompilerParams(vmem_limit_bytes=VMEM_LIMIT),
    )(*pieces, after)


def coarse_kernel(count_x, count_y, own, other, out_hbm, out, sems):
    me = lax.axis_index("gy")
    me_z, is_even = lax.shift_right_logical(me, 1), lax.rem(me, 2) == 0
    lane = lax.broadcasted_iota(jnp.int32, (8, NL), 1)
    place = [lax.rem(lane + NL - 35 * v, NL) for v in range(NV)]

    def block(i, _):
        rows = pl.ds(pl.multiple_of(8 * i, 8), 8)
        for z in range(4):
            pieces = []
            for j in range(count_y // 2):
                mine, theirs = own[j ^ me_z, z, rows, :], other[j ^ me_z, z, rows, :]
                pieces += [jnp.where(is_even, mine, theirs), jnp.where(is_even, theirs, mine)]
            for v in range(NV):
                at = place[v]
                for t in range(count_y // 4):
                    total = jnp.where(at < 2, pieces[4 * t - 1], 0.0)
                    total += jnp.where(at == NL - 1, pieces[(4 * t + 4) % count_y], 0.0)
                    for q in range(4):
                        inside = (at >= 32 * q - 1) & (at < 32 * q + 34)
                        total += jnp.where(inside, pieces[4 * t + q], 0.0)
                    out[v, z, rows, NL * t : NL * (t + 1)] = pltpu.roll(total, NL - 35 * v, 1) if v else total
        return 0

    def copy(i):
        rows = pl.ds(pl.multiple_of(16 * i, 16), 16)
        return pltpu.make_async_copy(out.at[:, :, rows], out_hbm.at[:, :, rows], sems.at[i])

    def pair(i, _):
        block(2 * i, 0)
        block(2 * i + 1, 0)
        copy(i).start()
        return 0

    lax.fori_loop(0, count_x, pair, 0)
    for i in range(count_x):
        copy(i).wait()


def coarse_step(own, other, count_x, count_y):
    vmem = pl.BlockSpec(memory_space=pltpu.VMEM)
    shape = (NV, 4, 16 * count_x, 32 * count_y)
    return pl.pallas_call(
        functools.partial(coarse_kernel, count_x, count_y),
        out_shape=jax.ShapeDtypeStruct(shape, F32),
        in_specs=[vmem, vmem],
        out_specs=pl.BlockSpec(memory_space=pltpu.HBM),
        scratch_shapes=[pltpu.VMEM(shape, F32), pltpu.SemaphoreType.DMA((count_x,))],
        compiler_params=pltpu.CompilerParams(vmem_limit_bytes=VMEM_LIMIT),
    )(own, other)


def shifted(x, axis, step):
    count = lax.axis_size(axis)
    return lax.ppermute(x, axis, [(i, (i + step) % count) for i in range(count)])


def swapped(x, axis, distance):
    return lax.ppermute(x, axis, [(i, i ^ distance) for i in range(lax.axis_size(axis))])


def body(field, masks):
    count_x, count_y = lax.axis_size("gx"), lax.axis_size("gy")
    lifted, up, down, own_masks, share = first_step(field, masks)
    south = shifted(up, "gx", -1)
    north = shifted(down, "gx", 1)
    shares = [share] + [swapped(share, "gy", r) for r in range(2, count_y, 2)]
    parts, sides = edge_step(lift_step(lifted), lifted, north, south, own_masks)
    east = shifted(sides, "gy", -1)
    west = shifted(sides, "gy", 1)
    joined = join_step(shares, sides)
    pieces = [joined] + [swapped(joined, "gx", r) for r in range(1, count_x)]
    kept = main_step(parts, east, west, own_masks, north, south)
    own = rows_step(pieces, count_y // 2, kept)
    other = swapped(own, "gy", 1)
    return cells_step(kept.reshape(4, NV * 8, 48, NL)), coarse_step(own, other, count_x, count_y)


def solution(mesh):
    placed = P(None, None, "gx", "gy")
    return jax.shard_map(
        body,
        mesh=mesh,
        in_specs=(placed, placed),
        out_specs=(placed, P()),
        check_vma=False,
    )
```

```python
import functools

import jax
import jax.numpy as jnp
import ml_dtypes
import numpy as np
from jax import lax
from jax.experimental import pallas as pl
from jax.experimental.pallas import tpu as pltpu
from jax.sharding import PartitionSpec as P

F32 = jnp.float32
BF16 = jnp.bfloat16
VMEM_LIMIT = 32 * 1024 * 1024

NV, NZ, NR, NL = 3, 16, 64, 128


def detail_row(k):
    return {2 * k + 1: 1.0, 2 * k: -0.5, 2 * k + 2: -0.5}


def smooth_row(k):
    row = {2 * k: 1.0}
    for j in (k - 1, k):
        for cell, value in detail_row(j).items():
            row[cell] = row.get(cell, 0.0) + 0.25 * value
    return row


def even_row(k):
    return {("s", k): 1.0, ("d", k - 1): -0.25, ("d", k): -0.25}


def odd_row(k):
    row = {("d", k): 1.0}
    for j in (k, k + 1):
        for name, value in even_row(j).items():
            row[name] = row.get(name, 0.0) + 0.5 * value
    return row


def as_bf16(matrix):
    cast = matrix.astype(ml_dtypes.bfloat16)
    assert (cast.astype(np.float64) == matrix).all()
    return cast


def combine(*terms):
    total = {}
    for factor, row in terms:
        for cell, value in row.items():
            total[cell] = total.get(cell, 0.0) + factor * value
    return total


def level_one_columns():
    names = {("s", k): k for k in range(65)}
    names.update({("d", k): 128 + k for k in range(65)})
    names[("d", -1)] = 128 + 65
    return names


def level_two_columns():
    names = {("s", k): k for k in range(33)}
    names.update({("d", k): 64 + k for k in range(33)})
    names[("d", -1)] = 64 + 33
    return names


def smooth_place(k):
    return k + 2


def beyond(n):
    return {"cell": 24 * n, "after": 24 * n + 8, "before": 24 * n + 16}


BEYOND_SMOOTH = {65: 96, 66: 104, -2: 112, -1: 120}


def own_row(kind, k, n):
    place = {name: 128 + lane for name, lane in beyond(n).items()}
    if kind == "d":
        if k == -1:
            return {place["before"]: 1.0, 0: -0.5}
        if k == 64:
            return {place["after"]: 1.0}
        return {(place["cell"] if y == 128 else y): value for y, value in detail_row(k).items()}
    if k in BEYOND_SMOOTH:
        row = {128 + BEYOND_SMOOTH[k]: 1.0}
        return combine((1.0, row), (1.0, {0: -0.125})) if k == -1 else row
    even = place["cell"] if k == 64 else 2 * k
    return combine((1.0, {even: 1.0}), (0.25, own_row("d", k - 1, n)), (0.25, own_row("d", k, n)))


@functools.lru_cache(maxsize=None)
def weights():
    w = {}
    names = level_one_columns()
    forward = np.zeros((4, 256, 256))
    inverse = np.zeros((256, 128))
    for (kind, k), column in names.items():
        for n in range(4):
            for place, value in own_row(kind, k, n).items():
                forward[n, place, column] += value
    for k in range(64):
        for y, row in ((2 * k, even_row(k)), (2 * k + 1, odd_row(k))):
            for name, value in row.items():
                inverse[names[name], y] += value
    short = np.zeros((144, 256))
    short[:128] = forward[0, :128]
    for i, lane in enumerate(beyond(0).values()):
        short[128 + i] = forward[0, 128 + lane]
    smooth = np.zeros((256, 128))
    for k in range(-2, 67):
        for place, value in own_row("s", k, 0).items():
            smooth[place, smooth_place(k)] += value
    names2 = level_two_columns()
    forward2 = np.zeros((128, 128))
    inverse2 = np.zeros((128, 128))
    for (kind, k), column in names2.items():
        for cell, value in (smooth_row(k) if kind == "s" else detail_row(k)).items():
            forward2[smooth_place(cell), column] += value
    for k in range(33):
        rows = [(2 * k, even_row(k))] + ([(2 * k + 1, odd_row(k))] if k < 32 else [])
        for y, row in rows:
            for name, value in row.items():
                inverse2[names2[name], y] += value
    back = np.zeros((256, 128))
    back[:65] = inverse[:65]
    back[128 : 128 + 65] = inverse[:65]
    spread = np.zeros((3, 128, 2, 128))
    for k in range(64):
        spread[0, k, 0, k] = 1
    spread[1, 0, 0, 64] = 1
    spread[2, 63, 0, 65] = 1
    for k in range(32):
        spread[0, 64 + k, 1, k] = 1
        spread[0, 64 + k, 1, 64 + k] = 1
    for base in (0, 64):
        spread[1, 64, 1, base + 32] = 1
        spread[2, 95, 1, base + 33] = 1
    w["wide"] = np.concatenate([short, spread.reshape(384, 256)], 0)
    own, beside = smooth[:128], smooth[128:]
    w["narrow"] = np.concatenate([inverse, own, own, beside, beside, back, forward2, inverse2], 0)
    edge = np.zeros((4, 128, 128))

    def put(n, lane, row):
        for z in range(8):
            for y, value in row.items():
                j = y - 120 if y >= 120 else y + 8
                edge[n, 16 * z + j, lane + z] += value

    part = {127: 1.0, 126: -0.5}
    for n in range(4):
        put(n, beyond(n)["cell"], {0: 1.0})
        put(n, beyond(n)["after"], detail_row(0))
        put(n, beyond(n)["before"], part)
    put(0, BEYOND_SMOOTH[65], smooth_row(1))
    put(0, BEYOND_SMOOTH[66], smooth_row(2))
    put(0, BEYOND_SMOOTH[-2], smooth_row(62))
    put(0, BEYOND_SMOOTH[-1], combine((1.0, {126: 1.0}), (0.25, detail_row(62)), (0.25, part)))
    w["edge"] = edge.reshape(512, 128)
    expand = np.zeros((2, 4, 128))
    for j in range(4):
        expand[0, j, 16 * j : 16 * j + 16] = 1
        expand[1, j, 64 + 8 * j : 64 + 8 * j + 8] = 1
    twice = combine(*[(value, smooth_row(k)) for k, value in smooth_row(0).items()])
    columns = np.zeros((2, 128, 128))
    for m in range(-1, 34):
        for t, value in twice.items():
            if 0 <= 4 * m + t < NL:
                columns[:, 4 * m + t, m + 1] = value
    rows = np.zeros((4, 32, 2, 64))
    for z in range(4):
        places = {m: m for m in range(16)}
        places.update({16: 16 + 2 * z, 17: 17 + 2 * z, -1: 16 + 15 - z})
        for m, place in places.items():
            for t, value in twice.items():
                if 0 <= 4 * m + t < NR:
                    rows[z, place, :, 4 * m + t] = value
    pad = np.zeros((8, 128))
    w["first"] = np.concatenate([columns.reshape(256, 128), rows.reshape(128, 128), expand.reshape(8, 128), pad], 0)
    return {name: as_bf16(matrix) for name, matrix in w.items()}


def two_terms(x):
    high = x.astype(BF16)
    low = (x - high.astype(F32)).astype(BF16)
    return high, low


def cost(gigaflops):
    return pl.CostEstimate(flops=gigaflops * 10**9, bytes_accessed=8 * 10**6, transcendentals=0)


def dot(a, b):
    return jnp.dot(a, b, preferred_element_type=F32)


def lift_planes(cells):
    half = len(cells) // 2
    even, odd = cells[0::2], cells[1::2]
    detail = [odd[k] - 0.5 * (even[k] + even[min(k + 1, half - 1)]) for k in range(half)]
    smooth = [even[k] + 0.25 * (detail[max(k - 1, 0)] + detail[k]) for k in range(half)]
    return smooth, detail


def unlift_planes(smooth, detail):
    half = len(smooth)
    even = [smooth[k] - 0.25 * (detail[max(k - 1, 0)] + detail[k]) for k in range(half)]
    out = []
    for k in range(half):
        out += [even[k], detail[k] + 0.5 * (even[k] + even[min(k + 1, half - 1)])]
    return out


def lift_rows(load, start):
    even, odd, after = load(start), load(start + 1), load(start + 2)
    before, odd_before = load(start - 2), load(start - 1)
    detail = odd - 0.5 * (even + after)
    detail_before = odd_before - 0.5 * (before + even)
    return even + 0.25 * (detail_before + detail), detail


def unlift_rows(smooth, detail, row):
    here, after = detail(row), detail(row + 1)
    even = smooth(row) - 0.25 * (detail(row - 1) + here)
    next_even = smooth(row + 1) - 0.25 * (here + after)
    return even, here + 0.5 * (even + next_even)


PITCH = 80


def lanes_turn(j):
    return lax.rem(32 * lax.rem(j, 4) + NL - 1, NL)


def first_kernel(
    field, masks_hbm, table_hbm, lifted, up, down, own_masks, share, cells, twice, masks, table, sems
):
    small = [
        pltpu.make_async_copy(masks_hbm, masks, sems.at[0]),
        pltpu.make_async_copy(table_hbm, table, sems.at[1]),
    ]
    copies = []
    for v in range(NV):
        for c in range(4):
            part = pl.ds(16 * c, 16)
            copies.append(pltpu.make_async_copy(field.at[v, :, part], cells.at[v, :, part], sems.at[2 + 4 * v + c]))
    for copy in small + copies:
        copy.start()
    for p in range(NV * NZ):
        lifted[p * PITCH : p * PITCH + 8, :] = jnp.zeros((8, NL), F32)
        lifted[p * PITCH + 72 : p * PITCH + 80, :] = jnp.zeros((8, NL), F32)
    for copy in small:
        copy.wait()
    for i, out, tile in ((0, up, 18), (1, down, 12)):
        total = jnp.zeros((7, NL), F32)
        for l in range(2):
            flags = masks[l, i].astype(F32).astype(BF16)
            spread = table[384 + 4 * l : 388 + 4 * l, :]
            total += lax.dot_general(flags, spread, (((0,), (0,)), ((), ())), preferred_element_type=F32)
        own_masks[i] = jnp.concatenate([total, jnp.zeros((1, NL), F32)], 0)
        out[tile] = own_masks[i]

    for v in range(NV):
        for t in range(8):
            if t % 2 == 0:
                copies[4 * v + t // 2].wait()
            smooth, detail = lift_planes([cells[v, z, 8 * t : 8 * t + 8, :] for z in range(NZ)])
            for k, tile in enumerate(smooth + detail):
                start = (v * NZ + k) * PITCH + 8 + 8 * t
                lifted[start : start + 8, :] = tile
            for k, tile in enumerate(lift_planes(smooth)[0]):
                twice[v * 4 + k, 8 * t : 8 * t + 8, :] = tile
        for bz in range(2):

            def row(x):
                return lifted[pl.ds((v * NZ + bz * 8) * PITCH + 8 + x, 8, stride=PITCH), :]

            x = [row(j) for j in range(7 if bz == 0 else 3)]
            first = x[1] - 0.5 * (x[0] + x[2])
            up[v * 6 + bz] = x[0]
            up[v * 6 + 2 + bz] = first
            y = {j: row(j) for j in (range(58, 64) if bz == 0 else (62, 63))}
            part = y[63] - 0.5 * y[62]
            down[v * 4 + bz] = part
            if bz == 0:
                second = x[3] - 0.5 * (x[2] + x[4])
                third = x[5] - 0.5 * (x[4] + x[6])
                up[v * 6 + 4] = x[2] + 0.25 * (first + second)
                up[v * 6 + 5] = x[4] + 0.25 * (second + third)
                before = y[59] - 0.5 * (y[58] + y[60])
                last = y[61] - 0.5 * (y[60] + y[62])
                down[v * 4 + 2] = y[60] + 0.25 * (before + last)
                down[v * 4 + 3] = y[62] + 0.25 * (last + part)

    total = jnp.zeros((80, NL), F32)
    for v in range(NV):
        main, extra = [], jnp.zeros((16, NL), F32)
        for z in range(4):
            terms = jnp.concatenate(two_terms(twice[v * 4 + z]), 0)
            part = dot(table[256 + 32 * z : 288 + 32 * z, :], terms)
            main.append(part[:16])
            extra += part[16:]
        terms = jnp.concatenate(two_terms(jnp.concatenate(main + [extra], 0)), 1)
        part = dot(terms, table[0:256, :])
        total += pltpu.roll(part, 35 * v, 1) if v else part
    turn = lanes_turn(lax.axis_index("gy"))
    lane = lax.broadcasted_iota(jnp.int32, (8, NL), 1)
    spare = (lane >= 105) & (lane < 126)
    upper = lax.broadcasted_iota(jnp.int32, (8, NL), 0) < 4
    below, above = total[64:72], total[72:80]
    pieces = [pltpu.roll(above, 105 - 21 * p, 1) for p in range(5)]
    for g in range(8):
        if g < 5:
            extra = pltpu.roll(below, 105 - 21 * g, 1)
        else:
            extra = pltpu.roll(pieces[2 * g - 10], 4, 0)
            extra = jnp.where(upper, extra, pieces[2 * g - 9] if g < 7 else 0.0)
        tile = jnp.where(spare, extra, total[8 * g : 8 * g + 8])
        share[8 * g : 8 * g + 8, :] = pltpu.roll(tile, turn, 1)


def in_hbm(x):
    return pltpu.with_memory_space_constraint(x, pltpu.HBM)


def first_step(field, masks):
    vmem = pl.BlockSpec(memory_space=pltpu.VMEM)
    shapes = [(NV * NZ * PITCH, NL), (19, 8, NL), (13, 8, NL), (2, 8, NL), (64, NL)]
    return pl.pallas_call(
        first_kernel,
        out_shape=[jax.ShapeDtypeStruct(s, F32) for s in shapes],
        in_specs=[pl.BlockSpec(memory_space=pltpu.HBM)] * 3,
        out_specs=[vmem] * 5,
        scratch_shapes=[
            pltpu.VMEM((NV, NZ, NR, NL), F32),
            pltpu.VMEM((NV * 4, NR, NL), F32),
            pltpu.VMEM((2, 2, 4, 7), jnp.int32),
            pltpu.VMEM((400, NL), BF16),
            pltpu.SemaphoreType.DMA((4 * NV + 2,)),
        ],
        compiler_params=pltpu.CompilerParams(vmem_limit_bytes=VMEM_LIMIT),
    )(*[in_hbm(x) for x in (field, masks.transpose(0, 2, 3, 1), jnp.asarray(weights()["first"]))])


ROWS = 40


def lift_kernel(lifted, parts):
    def lift(step, _):
        v, bz = step // 2, lax.rem(step, 2)
        for z in range(8):
            start = pl.multiple_of((step * 8 + z) * PITCH, 8)
            for t in range(4):
                pair = lift_rows(lambda s: lifted[pl.ds(start + 16 * t + s, 8, stride=2), :], 8)
                for bx in range(2):
                    plane = (2 * bz + bx) * 24 + v * 8 + z
                    parts[pl.ds(pl.multiple_of(plane * ROWS + 8 * t, 8), 8), :] = pair[bx]
        return 0

    lax.fori_loop(0, NV * 2, lift, 0)


def lift_step(lifted):
    vmem = pl.BlockSpec(memory_space=pltpu.VMEM)
    return pl.pallas_call(
        lift_kernel,
        out_shape=jax.ShapeDtypeStruct((4 * NV * 8 * ROWS, NL), F32),
        in_specs=[vmem],
        out_specs=vmem,
        compiler_params=pltpu.CompilerParams(vmem_limit_bytes=VMEM_LIMIT),
    )(lifted)


def edge_kernel(parts_in, lifted, north, south, own_masks, table_hbm, parts, sides, packed, table, sem):
    copy = pltpu.make_async_copy(table_hbm, table, sem.at[0])
    copy.start()
    for p in range(4 * NV * 8):
        parts[p * ROWS + 32 : p * ROWS + 40, :] = jnp.zeros((8, NL), F32)
    for v in range(NV):
        for bz in range(2):

            def cell(x):
                return lifted[pl.ds((v * NZ + bz * 8) * PITCH + 8 + x, 8, stride=PITCH), :]

            def at(bx, r):
                return pl.ds(((2 * bz + bx) * 24 + v * 8) * ROWS + r, 8, stride=ROWS)

            before, after, detail = north[v * 4 + bz], south[v * 6 + bz], south[v * 6 + 2 + bz]
            start = cell(0)
            last = cell(63) - 0.5 * (cell(62) + after)
            parts[at(0, 0), :] = parts[at(0, 0), :] + 0.25 * before
            parts[at(0, 31), :] = parts[at(0, 31), :] - 0.125 * after
            parts[at(1, 31), :] = parts[at(1, 31), :] - 0.5 * after
            parts[at(0, 32), :] = after + 0.25 * (last + detail)
            parts[at(1, 32), :] = detail
            parts[at(1, 39), :] = before - 0.5 * start
            if bz == 0:
                parts[at(0, 33), :] = south[v * 6 + 4]
                parts[at(0, 34), :] = south[v * 6 + 5]
                parts[at(0, 38), :] = north[v * 4 + 2]
                parts[at(0, 39), :] = north[v * 4 + 3] - 0.125 * start

    lane = lax.broadcasted_iota(jnp.int32, (8, NL), 1) // 16

    def pack(v, _):
        for n in range(4):
            for t in range(5):
                tile = jnp.zeros((8, NL), F32)
                for z in range(8):
                    start = (n * 24 + v * 8 + z) * ROWS + 8 * t
                    x = parts[pl.ds(pl.multiple_of(start, 8), 8), :]
                    tile = jnp.where(lane == z, pltpu.roll(x, (8 + 16 * z) % NL, 1), tile)
                packed[pl.ds(pl.multiple_of(n * 120 + v * ROWS + 8 * t, 8), 8), :] = tile
        return 0

    lax.fori_loop(0, NV, pack, 0)
    copy.wait()
    terms = [two_terms(packed[n * 120 : (n + 1) * 120, :]) for n in range(4)]
    high, low = [jnp.concatenate(part, 1) for part in zip(*terms)]
    sides[0:120, :] = dot(high, table[...]) + dot(low, table[...])
    sides[120:128, :] = north[12]
    sides[128:136, :] = own_masks[0]
    sides[136:144, :] = own_masks[1]
    sides[144:152, :] = south[18]


def edge_step(parts, lifted, north, south, own_masks):
    vmem = pl.BlockSpec(memory_space=pltpu.VMEM)
    shapes = [(4 * NV * 8 * ROWS, NL), (152, NL)]
    return pl.pallas_call(
        edge_kernel,
        out_shape=[jax.ShapeDtypeStruct(s, F32) for s in shapes],
        in_specs=[vmem] * 5 + [pl.BlockSpec(memory_space=pltpu.HBM)],
        out_specs=[vmem] * 2,
        input_output_aliases={0: 0},
        cost_estimate=cost(20),
        scratch_shapes=[pltpu.VMEM((480, NL), F32), pltpu.VMEM((512, NL), BF16), pltpu.SemaphoreType.DMA((1,))],
        compiler_params=pltpu.CompilerParams(vmem_limit_bytes=VMEM_LIMIT),
    )(parts, lifted, north, south, own_masks, in_hbm(jnp.asarray(weights()["edge"])))


def join_kernel(*refs):
    shares, out = refs[-3::-1], refs[-1]
    for n, piece in enumerate(shares):
        out[64 * n : 64 * (n + 1), :] = piece[...]


def join_step(shares, after):
    vmem = pl.BlockSpec(memory_space=pltpu.VMEM)
    return pl.pallas_call(
        join_kernel,
        out_shape=jax.ShapeDtypeStruct((64 * len(shares), NL), F32),
        in_specs=[vmem] * len(shares) + [pl.BlockSpec(memory_space=pl.ANY)],
        out_specs=vmem,
        cost_estimate=cost(20),
        compiler_params=pltpu.CompilerParams(vmem_limit_bytes=VMEM_LIMIT),
    )(*shares[::-1], after)


def mask_lanes(west, east, own_masks, north_mask, south_mask, wide):
    masks = [jnp.concatenate([ref[120 + 8 * i : 128 + 8 * i, :] for i in range(4)], 0) for ref in (east, west)]
    own = jnp.concatenate([north_mask[0], own_masks[0], own_masks[1], south_mask[0]], 0)
    flags = jnp.concatenate([own] + masks, 1).astype(BF16)
    return dot(flags, wide[144:528, :])


def beside_tiles(west, east, at, count):
    lane = lax.broadcasted_iota(jnp.int32, (count, NL), 1)
    from_west = (lane >= 112) | ((lane < 96) & (lax.rem(lane, 24) >= 16))
    tiles = []
    for v in range(NV):
        rows = slice(v * ROWS + at, v * ROWS + at + count)
        beside = jnp.where(from_west, west[rows, :], east[rows, :])
        tiles += [pltpu.roll(beside, NL - z, 1) if z else beside for z in range(8)]
    return tiles


def beside_terms(west, east, at, count):
    return jnp.concatenate(two_terms(jnp.concatenate(beside_tiles(west, east, at, count), 0)), 1)


def own_terms(planes, at, count):
    return jnp.concatenate(two_terms(planes[:, at : at + count, :].reshape(24 * count, NL)), 1)


def main_kernel(
    parts, flat, east, west, own_masks, north_mask, south_mask, wide, narrow,
    kept,
    gain2, low, second, kept2, low_back, gain, sides_wide, turned,
):
    inverse, smooth_own, smooth_beside = narrow.at[0:256], narrow.at[256:512], narrow.at[512:768]
    back, forward2, inverse2 = narrow.at[768:1024], narrow.at[1024:1152], narrow.at[1152:1280]
    lanes = mask_lanes(west, east, own_masks, north_mask, south_mask, wide)
    lane64 = lax.broadcasted_iota(jnp.int32, (1, NL), 1) < 64
    needed = [(ib, n) for ib in range(4) for n in range(4) if ib or n % 2]
    forward2_f = forward2[0:80, :].astype(F32)
    masked = []
    for ib, n in needed:
        b = 8 * ib + 4 * (n // 2) + n % 2 - 1
        smooth_two = lanes[b : b + 1, NL:] if n else jnp.ones((1, NL), F32)
        row = jnp.where(lane64, smooth_two, lanes[b + 2 : b + 3, NL:])
        masked.append((forward2_f * row).astype(BF16))
    both = dot(jnp.concatenate(masked, 0), inverse2[...]).astype(BF16)
    for i, (ib, n) in enumerate(needed):
        for half in (0, 128):
            gain2[ib, n, half : half + 80, :] = both[80 * i : 80 * i + 80]
            gain2[ib, n, half + 80 : half + 128, :] = jnp.zeros((48, NL), BF16)

    for at, count in ((0, 16), (16, 16), (32, 8)):
        part = dot(own_terms(parts.at[0], at, count), smooth_own[...])
        part += dot(beside_terms(west, east, at, count), smooth_beside[...])
        part = part.reshape(24, count, NL)
        if at < 32:
            low[:, 8 + at : 8 + at + count, :] = part
            if at == 0:
                low[:, 56:64, :] = part[:, 0:8]
        else:
            low[:, 0:8, :] = part
            low[:, 40:48, :] = part
            low[:, 48:56, :] = part

    def rows_two(v, _):
        for t in range(3):
            lifted = [
                lift_rows(lambda s: low[v * 8 + p, pl.ds(16 * t + s, 8, stride=2), :], 8) for p in range(8)
            ]
            for bx in range(2):
                smooth, detail = lift_planes([pair[bx] for pair in lifted])
                for bz, part in ((0, smooth), (1, detail)):
                    for z in range(4):
                        second[2 * bz + bx, t, pl.ds(pl.multiple_of((v * 4 + z) * 8, 8), 8), :] = part[z]
        return 0

    lax.fori_loop(0, NV, rows_two, 0)
    for n in range(4):
        for t in range(3):
            terms = jnp.concatenate(two_terms(second[n, t]), 1)
            if t < 2:
                kept2[n, :, 8 + 8 * t : 16 + 8 * t, :] = dot(terms, gain2[t + 1, n]).reshape(NV * 4, 8, NL)
            else:
                if n % 2:
                    kept2[n, :, 0:8, :] = dot(terms, gain2[0, n]).reshape(NV * 4, 8, NL)
                kept2[n, :, 24:32, :] = dot(terms, gain2[3, n]).reshape(NV * 4, 8, NL)

    def back_two(v, _):
        for t in range(3):
            pairs = {}
            for bz in range(2):
                for z in range(4):
                    p = v * 4 + z
                    if t < 2:
                        pairs[bz, z] = unlift_rows(
                            lambda r: kept2[2 * bz, p, pl.ds(r, 8), :],
                            lambda r: kept2[2 * bz + 1, p, pl.ds(r, 8), :],
                            8 + 8 * t,
                        )
                    else:
                        even = kept2[2 * bz, p, 24:32, :] - 0.25 * (
                            kept2[2 * bz + 1, p, 23:31, :] + kept2[2 * bz + 1, p, 24:32, :]
                        )
                        pairs[bz, z] = (even, even)
            for parity in range(2 if t < 2 else 1):
                planes = unlift_planes([pairs[0, z][parity] for z in range(4)], [pairs[1, z][parity] for z in range(4)])
                for z in range(8):
                    low_back[pl.ds((v * 8 + z) * 48 + 16 * t + parity, 8, stride=2), :] = planes[z]
        return 0

    lax.fori_loop(0, NV, back_two, 0)

    forward_f = wide[0:144, :].astype(F32)
    for ib in range(4):
        sides_wide[ib] = jnp.zeros((NL, 4 * NL), F32)
    masked = []
    for ib, n in needed:
        b = 8 * ib + 4 * (n // 2) + n % 2 - 1
        smooth_one = lanes[b : b + 1, 0:NL] if n else jnp.zeros((1, NL), F32)
        row = jnp.concatenate([smooth_one, lanes[b + 2 : b + 3, 0:NL]], 1)
        masked.append((forward_f * row).astype(BF16))
    both = dot(jnp.concatenate(masked, 0), inverse[...])
    for i, (ib, n) in enumerate(needed):
        main = both[144 * i : 144 * i + 128].astype(BF16)
        gain[ib, n, 0:128, :] = main
        gain[ib, n, 128:256, :] = main
        for j in range(3):
            at = 24 * n + 8 * j
            sides_wide[ib, at : at + 1, n * NL : (n + 1) * NL] = both[144 * i + 128 + j : 144 * i + 129 + j]

    gain_sides = []
    for ib in range(4):
        side = sides_wide[ib].astype(BF16)
        gain_sides.append(jnp.concatenate([side, side], 0))
    def put(n, p, at, rows):
        start = pl.multiple_of((n * 24 + p) * 48 + 8 + at, 8)
        kept[pl.ds(start, rows.shape[0]), :] = rows

    def row_of(ref, first, pitch):
        return ref[pl.ds(first, 24, stride=pitch), :]

    for ib in range(2):
        product = dot(beside_terms(west, east, 16 * ib, 16), gain_sides[ib + 1])
        for n in range(4):
            for p in range(24):
                put(n, p, 16 * ib, product[16 * p : 16 * p + 16, n * NL : (n + 1) * NL])

    def keep(n, _):
        for ib in range(2):
            product = dot(own_terms(parts.at[n], 16 * ib, 16), gain[ib + 1, n])
            for p in range(24):
                start = pl.ds(pl.multiple_of((n * 24 + p) * 48 + 8 + 16 * ib, 8), 16)
                kept[start, :] += product[16 * p : 16 * p + 16]
        return 0

    lax.fori_loop(0, 4, keep, 0)
    for ib in range(2):
        rows = jnp.concatenate([low_back[48 * p + 16 * ib : 48 * p + 16 * ib + 16, :] for p in range(24)], 0)
        product = dot(jnp.concatenate(two_terms(rows), 1), back[...])
        for p in range(24):
            start = 48 * p + 8 + 16 * ib
            kept[start : start + 16, :] += product[16 * p : 16 * p + 16]
    tiles = beside_tiles(west, east, 32, 8)
    for p in range(24):
        turned[8 * p : 8 * p + 8, :] = tiles[p]
    for first, ib, place, row in ((0, 3, 40, 32), (7, 0, 7, 39)):
        beside = dot(jnp.concatenate(two_terms(row_of(turned, first, 8)), 1), gain_sides[ib])
        for n in range(4) if ib else (1, 3):
            own = jnp.concatenate(two_terms(row_of(flat, n * 24 * ROWS + row, ROWS)), 1)
            total = beside[:, n * NL : (n + 1) * NL] + dot(own, gain[ib, n])
            if n == 0:
                total += dot(jnp.concatenate(two_terms(row_of(low_back, row, 48)), 1), back[...])
            kept[pl.ds(n * 24 * 48 + place, 24, stride=48), :] = total


def cells_kernel(kept, out, cells, sems):
    def back_one(step, _):
        v, t = step // 4, step % 4
        pairs = {}
        for bz in range(2):
            for z in range(8):
                p = v * 8 + z
                pairs[bz, z] = unlift_rows(
                    lambda r: kept[2 * bz, p, pl.ds(8 * t + r, 8), :],
                    lambda r: kept[2 * bz + 1, p, pl.ds(8 * t + r, 8), :],
                    8,
                )
        for parity in range(2):
            planes = unlift_planes([pairs[0, z][parity] for z in range(8)], [pairs[1, z][parity] for z in range(8)])
            for z in range(NZ):
                cells[v, z, pl.ds(16 * t + parity, 8, stride=2), :] = planes[z]
        return 0

    def copy(step):
        v, rows = step // 4, pl.ds(pl.multiple_of(16 * (step % 4), 16), 16)
        return pltpu.make_async_copy(cells.at[v, :, rows], out.at[v, :, rows], sems.at[step])

    def one(step, _):
        back_one(step, 0)
        copy(step).start()
        return 0

    lax.fori_loop(0, NV * 4, one, 0)
    for step in range(NV * 4):
        copy(step).wait()


def main_specs():
    vmem = pl.BlockSpec(memory_space=pltpu.VMEM)
    return [
        vmem, vmem, vmem, vmem, vmem,
        pl.BlockSpec((1, 8, NL), lambda i: (12, 0, 0)), pl.BlockSpec((1, 8, NL), lambda i: (18, 0, 0)),
        vmem, vmem,
    ]


def main_step(flat, *operands):
    w = weights()
    return pl.pallas_call(
        main_kernel,
        grid=(1,),
        out_shape=jax.ShapeDtypeStruct((4 * NV * 8 * 48, NL), F32),
        in_specs=main_specs(),
        out_specs=pl.BlockSpec((4 * NV * 8 * 48, NL), lambda i: (0, 0)),
        scratch_shapes=[
            pltpu.VMEM((4, 4, 256, NL), BF16),
            pltpu.VMEM((NV * 8, 64, NL), F32),
            pltpu.VMEM((4, 3, NV * 32, NL), F32),
            pltpu.VMEM((4, NV * 4, 40, NL), F32),
            pltpu.VMEM((NV * 8 * 48, NL), F32),
            pltpu.VMEM((4, 4, 256, NL), BF16),
            pltpu.VMEM((4, NL, 4 * NL), F32),
            pltpu.VMEM((NV * 64, NL), F32),
        ],
        cost_estimate=cost(8),
        compiler_params=pltpu.CompilerParams(vmem_limit_bytes=VMEM_LIMIT),
    )(flat.reshape(4, NV * 8, ROWS, NL), flat, *operands, w["wide"], w["narrow"])


def cells_step(kept):
    shape = (NV, NZ, NR, NL)
    return pl.pallas_call(
        cells_kernel,
        out_shape=jax.ShapeDtypeStruct(shape, F32),
        in_specs=[pl.BlockSpec(memory_space=pltpu.VMEM)],
        out_specs=pl.BlockSpec(memory_space=pltpu.HBM),
        scratch_shapes=[pltpu.VMEM(shape, F32), pltpu.SemaphoreType.DMA((NV * 4,))],
        cost_estimate=cost(4),
        compiler_params=pltpu.CompilerParams(vmem_limit_bytes=VMEM_LIMIT),
    )(kept)


def rows_kernel(count_x, count_z, *refs):
    shares, out = refs[count_x - 1 :: -1], refs[count_x + 1]
    me, me_y = lax.axis_index("gx"), lax.axis_index("gy")
    row = lax.broadcasted_iota(jnp.int32, (8, NL), 0)
    lane = lax.broadcasted_iota(jnp.int32, (8, NL), 1)
    for r in range(count_x):
        at = pl.multiple_of(16 * (me ^ r), 16)
        for j in range(count_z):
            for z in range(4):
                start = 64 * j + 16 * z
                out[j, z, pl.ds(at, 16), :] = shares[r][start : start + 16, :]
    for j in range(count_z):
        turn = lanes_turn(me_y ^ (2 * j))
        piece = lax.rem(lane + (NL - turn), NL) // 21
        inside = [piece == p for p in range(5)]
        for r in range(count_x):
            i = me ^ r
            below = pl.multiple_of(16 * lax.rem(i + 1, count_x), 16)
            above = pl.multiple_of(16 * lax.rem(i + count_x - 1, count_x) + 8, 8)
            tiles = [shares[r][64 * j + 8 * g : 64 * j + 8 * g + 8, :] for g in range(8)]
            low, high = jnp.zeros((8, NL), F32), jnp.zeros((8, NL), F32)
            for p in range(5):
                back = (21 * p - 105) % NL
                low = jnp.where(inside[p], pltpu.roll(tiles[p], back, 1), low)
                extra = tiles[5 + p // 2]
                extra = extra if p % 2 else pltpu.roll(extra, 4, 0)
                high = jnp.where(inside[p], pltpu.roll(extra, back, 1), high)
            for z in range(4):
                first = pltpu.roll(low, 8 - 2 * z, 0) if z else low
                last = pltpu.roll(high, z, 0) if z else high
                out[j, z, pl.ds(below, 8), :] += jnp.where(row < 2, first, 0.0)
                out[j, z, pl.ds(above, 8), :] += jnp.where(row == 7, last, 0.0)


def rows_step(pieces, count_z, after):
    vmem = pl.BlockSpec(memory_space=pltpu.VMEM)
    count_x = len(pieces)
    return pl.pallas_call(
        functools.partial(rows_kernel, count_x, count_z),
        out_shape=jax.ShapeDtypeStruct((count_z, 4, 16 * count_x, NL), F32),
        in_specs=[vmem] * count_x + [pl.BlockSpec(memory_space=pl.ANY)],
        out_specs=vmem,
        compiler_params=pltpu.CompilerParams(vmem_limit_bytes=VMEM_LIMIT),
    )(*pieces[::-1], after)


def coarse_kernel(count_x, count_y, own, other, out_hbm, out, sems):
    me = lax.axis_index("gy")
    me_z, is_even = lax.shift_right_logical(me, 1), lax.rem(me, 2) == 0
    lane = lax.broadcasted_iota(jnp.int32, (8, NL), 1)
    place = [lax.rem(lane + NL - 35 * v, NL) for v in range(NV)]

    def block(i, _):
        rows = pl.ds(pl.multiple_of(8 * i, 8), 8)
        for z in range(4):
            pieces = []
            for j in range(count_y // 2):
                mine, theirs = own[j ^ me_z, z, rows, :], other[j ^ me_z, z, rows, :]
                pieces += [jnp.where(is_even, mine, theirs), jnp.where(is_even, theirs, mine)]
            for v in range(NV):
                at = place[v]
                for t in range(count_y // 4):
                    total = jnp.where(at < 2, pieces[4 * t - 1], 0.0)
                    total += jnp.where(at == NL - 1, pieces[(4 * t + 4) % count_y], 0.0)
                    for q in range(4):
                        inside = (at >= 32 * q - 1) & (at < 32 * q + 34)
                        total += jnp.where(inside, pieces[4 * t + q], 0.0)
                    out[v, z, rows, NL * t : NL * (t + 1)] = pltpu.roll(total, NL - 35 * v, 1) if v else total
        return 0

    def copy(i):
        rows = pl.ds(pl.multiple_of(16 * i, 16), 16)
        return pltpu.make_async_copy(out.at[:, :, rows], out_hbm.at[:, :, rows], sems.at[i])

    def pair(i, _):
        block(2 * i, 0)
        block(2 * i + 1, 0)
        copy(i).start()
        return 0

    lax.fori_loop(0, count_x, pair, 0)
    for i in range(count_x):
        copy(i).wait()


def coarse_step(own, other, count_x, count_y):
    vmem = pl.BlockSpec(memory_space=pltpu.VMEM)
    shape = (NV, 4, 16 * count_x, 32 * count_y)
    return pl.pallas_call(
        functools.partial(coarse_kernel, count_x, count_y),
        out_shape=jax.ShapeDtypeStruct(shape, F32),
        in_specs=[vmem, vmem],
        out_specs=pl.BlockSpec(memory_space=pltpu.HBM),
        scratch_shapes=[pltpu.VMEM(shape, F32), pltpu.SemaphoreType.DMA((count_x,))],
        compiler_params=pltpu.CompilerParams(vmem_limit_bytes=VMEM_LIMIT),
    )(own, other)


def shifted(x, axis, step):
    count = lax.axis_size(axis)
    return lax.ppermute(x, axis, [(i, (i + step) % count) for i in range(count)])


def swapped(x, axis, distance):
    return lax.ppermute(x, axis, [(i, i ^ distance) for i in range(lax.axis_size(axis))])


def body(field, masks):
    count_x, count_y = lax.axis_size("gx"), lax.axis_size("gy")
    lifted, up, down, own_masks, share = first_step(field, masks)
    south = shifted(up, "gx", -1)
    north = shifted(down, "gx", 1)
    shares = [share] + [swapped(share, "gy", r) for r in range(2, count_y, 2)]
    parts, sides = edge_step(lift_step(lifted), lifted, north, south, own_masks)
    east = shifted(sides, "gy", -1)
    west = shifted(sides, "gy", 1)
    joined = join_step(shares, sides)
    pieces = [joined] + [swapped(joined, "gx", r) for r in range(1, count_x)]
    kept = main_step(parts, east, west, own_masks, north, south)
    own = rows_step(pieces, count_y // 2, kept)
    other = swapped(own, "gy", 1)
    return cells_step(kept.reshape(4, NV * 8, 48, NL)), coarse_step(own, other, count_x, count_y)


def solution(mesh):
    placed = P(None, None, "gx", "gy")
    return jax.shard_map(
        body,
        mesh=mesh,
        in_specs=(placed, placed),
        out_specs=(placed, P()),
        check_vma=False,
    )
```

```python
import functools

import jax
import jax.numpy as jnp
import ml_dtypes
import numpy as np
from jax import lax
from jax.experimental import pallas as pl
from jax.experimental.pallas import tpu as pltpu
from jax.sharding import PartitionSpec as P

F32 = jnp.float32
BF16 = jnp.bfloat16
VMEM_LIMIT = 32 * 1024 * 1024

NV, NZ, NR, NL = 3, 16, 64, 128


def detail_row(k):
    return {2 * k + 1: 1.0, 2 * k: -0.5, 2 * k + 2: -0.5}


def smooth_row(k):
    row = {2 * k: 1.0}
    for j in (k - 1, k):
        for cell, value in detail_row(j).items():
            row[cell] = row.get(cell, 0.0) + 0.25 * value
    return row


def even_row(k):
    return {("s", k): 1.0, ("d", k - 1): -0.25, ("d", k): -0.25}


def odd_row(k):
    row = {("d", k): 1.0}
    for j in (k, k + 1):
        for name, value in even_row(j).items():
            row[name] = row.get(name, 0.0) + 0.5 * value
    return row


def as_bf16(matrix):
    cast = matrix.astype(ml_dtypes.bfloat16)
    assert (cast.astype(np.float64) == matrix).all()
    return cast


def combine(*terms):
    total = {}
    for factor, row in terms:
        for cell, value in row.items():
            total[cell] = total.get(cell, 0.0) + factor * value
    return total


def level_one_columns():
    names = {("s", k): k for k in range(65)}
    names.update({("d", k): 128 + k for k in range(65)})
    names[("d", -1)] = 128 + 65
    return names


def level_two_columns():
    names = {("s", k): k for k in range(33)}
    names.update({("d", k): 64 + k for k in range(33)})
    names[("d", -1)] = 64 + 33
    return names


def smooth_place(k):
    return k + 2


def beyond(n):
    return {"cell": 24 * n, "after": 24 * n + 8, "before": 24 * n + 16}


BEYOND_SMOOTH = {65: 96, 66: 104, -2: 112, -1: 120}


def own_row(kind, k, n):
    place = {name: 128 + lane for name, lane in beyond(n).items()}
    if kind == "d":
        if k == -1:
            return {place["before"]: 1.0, 0: -0.5}
        if k == 64:
            return {place["after"]: 1.0}
        return {(place["cell"] if y == 128 else y): value for y, value in detail_row(k).items()}
    if k in BEYOND_SMOOTH:
        row = {128 + BEYOND_SMOOTH[k]: 1.0}
        return combine((1.0, row), (1.0, {0: -0.125})) if k == -1 else row
    even = place["cell"] if k == 64 else 2 * k
    return combine((1.0, {even: 1.0}), (0.25, own_row("d", k - 1, n)), (0.25, own_row("d", k, n)))


@functools.lru_cache(maxsize=None)
def weights():
    w = {}
    names = level_one_columns()
    forward = np.zeros((4, 256, 256))
    inverse = np.zeros((256, 128))
    for (kind, k), column in names.items():
        for n in range(4):
            for place, value in own_row(kind, k, n).items():
                forward[n, place, column] += value
    for k in range(64):
        for y, row in ((2 * k, even_row(k)), (2 * k + 1, odd_row(k))):
            for name, value in row.items():
                inverse[names[name], y] += value
    short = np.zeros((144, 256))
    short[:128] = forward[0, :128]
    for i, lane in enumerate(beyond(0).values()):
        short[128 + i] = forward[0, 128 + lane]
    smooth = np.zeros((256, 128))
    for k in range(-2, 67):
        for place, value in own_row("s", k, 0).items():
            smooth[place, smooth_place(k)] += value
    names2 = level_two_columns()
    forward2 = np.zeros((128, 128))
    inverse2 = np.zeros((128, 128))
    for (kind, k), column in names2.items():
        for cell, value in (smooth_row(k) if kind == "s" else detail_row(k)).items():
            forward2[smooth_place(cell), column] += value
    for k in range(33):
        rows = [(2 * k, even_row(k))] + ([(2 * k + 1, odd_row(k))] if k < 32 else [])
        for y, row in rows:
            for name, value in row.items():
                inverse2[names2[name], y] += value
    back = np.zeros((256, 128))
    back[:65] = inverse[:65]
    back[128 : 128 + 65] = inverse[:65]
    spread = np.zeros((3, 128, 2, 128))
    for k in range(64):
        spread[0, k, 0, k] = 1
    spread[1, 0, 0, 64] = 1
    spread[2, 63, 0, 65] = 1
    for k in range(32):
        spread[0, 64 + k, 1, k] = 1
        spread[0, 64 + k, 1, 64 + k] = 1
    for base in (0, 64):
        spread[1, 64, 1, base + 32] = 1
        spread[2, 95, 1, base + 33] = 1
    w["wide"] = np.concatenate([short, spread.reshape(384, 256)], 0)
    own, beside = smooth[:128], smooth[128:]
    w["narrow"] = np.concatenate([inverse, own, own, beside, beside, back, forward2, inverse2], 0)
    edge = np.zeros((4, 128, 128))

    def put(n, lane, row):
        for z in range(8):
            for y, value in row.items():
                j = y - 120 if y >= 120 else y + 8
                edge[n, 16 * z + j, lane + z] += value

    part = {127: 1.0, 126: -0.5}
    for n in range(4):
        put(n, beyond(n)["cell"], {0: 1.0})
        put(n, beyond(n)["after"], detail_row(0))
        put(n, beyond(n)["before"], part)
    put(0, BEYOND_SMOOTH[65], smooth_row(1))
    put(0, BEYOND_SMOOTH[66], smooth_row(2))
    put(0, BEYOND_SMOOTH[-2], smooth_row(62))
    put(0, BEYOND_SMOOTH[-1], combine((1.0, {126: 1.0}), (0.25, detail_row(62)), (0.25, part)))
    w["edge"] = edge.reshape(512, 128)
    expand = np.zeros((2, 4, 128))
    for j in range(4):
        expand[0, j, 16 * j : 16 * j + 16] = 1
        expand[1, j, 64 + 8 * j : 64 + 8 * j + 8] = 1
    twice = combine(*[(value, smooth_row(k)) for k, value in smooth_row(0).items()])
    columns = np.zeros((2, 128, 128))
    for m in range(-1, 34):
        for t, value in twice.items():
            if 0 <= 4 * m + t < NL:
                columns[:, 4 * m + t, m + 1] = value
    rows = np.zeros((4, 32, 2, 64))
    for z in range(4):
        places = {m: m for m in range(16)}
        places.update({16: 16 + 2 * z, 17: 17 + 2 * z, -1: 16 + 15 - z})
        for m, place in places.items():
            for t, value in twice.items():
                if 0 <= 4 * m + t < NR:
                    rows[z, place, :, 4 * m + t] = value
    pad = np.zeros((8, 128))
    w["first"] = np.concatenate([columns.reshape(256, 128), rows.reshape(128, 128), expand.reshape(8, 128), pad], 0)
    return {name: as_bf16(matrix) for name, matrix in w.items()}


def two_terms(x):
    high = x.astype(BF16)
    low = (x - high.astype(F32)).astype(BF16)
    return high, low


def cost(gigaflops):
    return pl.CostEstimate(flops=gigaflops * 10**9, bytes_accessed=8 * 10**6, transcendentals=0)


def dot(a, b):
    return jnp.dot(a, b, preferred_element_type=F32)


def lift_planes(cells):
    half = len(cells) // 2
    even, odd = cells[0::2], cells[1::2]
    detail = [odd[k] - 0.5 * (even[k] + even[min(k + 1, half - 1)]) for k in range(half)]
    smooth = [even[k] + 0.25 * (detail[max(k - 1, 0)] + detail[k]) for k in range(half)]
    return smooth, detail


def unlift_planes(smooth, detail):
    half = len(smooth)
    even = [smooth[k] - 0.25 * (detail[max(k - 1, 0)] + detail[k]) for k in range(half)]
    out = []
    for k in range(half):
        out += [even[k], detail[k] + 0.5 * (even[k] + even[min(k + 1, half - 1)])]
    return out


def lift_rows(load, start):
    even, odd, after = load(start), load(start + 1), load(start + 2)
    before, odd_before = load(start - 2), load(start - 1)
    detail = odd - 0.5 * (even + after)
    detail_before = odd_before - 0.5 * (before + even)
    return even + 0.25 * (detail_before + detail), detail


def unlift_rows(smooth, detail, row):
    here, after = detail(row), detail(row + 1)
    even = smooth(row) - 0.25 * (detail(row - 1) + here)
    next_even = smooth(row + 1) - 0.25 * (here + after)
    return even, here + 0.5 * (even + next_even)


PITCH = 80


def lanes_turn(j):
    return lax.rem(32 * lax.rem(j, 4) + NL - 1, NL)


def first_kernel(
    field, masks_hbm, table_hbm, lifted, up, down, own_masks, share, cells, twice, masks, table, sems
):
    small = [
        pltpu.make_async_copy(masks_hbm, masks, sems.at[0]),
        pltpu.make_async_copy(table_hbm, table, sems.at[1]),
    ]
    copies = []
    for v in range(NV):
        for c in range(4):
            part = pl.ds(16 * c, 16)
            copies.append(pltpu.make_async_copy(field.at[v, :, part], cells.at[v, :, part], sems.at[2 + 4 * v + c]))
    for copy in small + copies:
        copy.start()
    for p in range(NV * NZ):
        lifted[p * PITCH : p * PITCH + 8, :] = jnp.zeros((8, NL), F32)
        lifted[p * PITCH + 72 : p * PITCH + 80, :] = jnp.zeros((8, NL), F32)
    for copy in small:
        copy.wait()
    for i, out, tile in ((0, up, 15), (1, down, 9)):
        total = jnp.zeros((7, NL), F32)
        for l in range(2):
            flags = masks[l, i].astype(F32).astype(BF16)
            spread = table[384 + 4 * l : 388 + 4 * l, :]
            total += lax.dot_general(flags, spread, (((0,), (0,)), ((), ())), preferred_element_type=F32)
        own_masks[i] = jnp.concatenate([total, jnp.zeros((1, NL), F32)], 0)
        out[tile] = own_masks[i]

    for v in range(NV):
        for t in range(8):
            if t % 2 == 0:
                copies[4 * v + t // 2].wait()
            smooth, detail = lift_planes([cells[v, z, 8 * t : 8 * t + 8, :] for z in range(NZ)])
            for k, tile in enumerate(smooth + detail):
                start = (v * NZ + k) * PITCH + 8 + 8 * t
                lifted[start : start + 8, :] = tile
            for k, tile in enumerate(lift_planes(smooth)[0]):
                twice[v * 4 + k, 8 * t : 8 * t + 8, :] = tile
        for bz in range(2):

            def row(x):
                return lifted[pl.ds((v * NZ + bz * 8) * PITCH + 8 + x, 8, stride=PITCH), :]

            x = [row(j) for j in range(7 if bz == 0 else 3)]
            first = x[1] - 0.5 * (x[0] + x[2])
            up[v * 5 + bz] = x[0]
            up[v * 5 + 2 + bz] = first
            y = {j: row(j) for j in (range(58, 64) if bz == 0 else (62, 63))}
            part = y[63] - 0.5 * y[62]
            down[v * 3 + bz] = part
            if bz == 0:
                second = x[3] - 0.5 * (x[2] + x[4])
                third = x[5] - 0.5 * (x[4] + x[6])
                up[v * 5 + 4] = x[2] + 0.25 * (first + second) - 0.5 * (x[4] + 0.25 * (second + third))
                before = y[59] - 0.5 * (y[58] + y[60])
                last = y[61] - 0.5 * (y[60] + y[62])
                down[v * 3 + 2] = y[62] + 0.25 * (last + part) - 0.5 * (y[60] + 0.25 * (before + last))

    total = jnp.zeros((80, NL), F32)
    for v in range(NV):
        main, extra = [], jnp.zeros((16, NL), F32)
        for z in range(4):
            terms = jnp.concatenate(two_terms(twice[v * 4 + z]), 0)
            part = dot(table[256 + 32 * z : 288 + 32 * z, :], terms)
            main.append(part[:16])
            extra += part[16:]
        terms = jnp.concatenate(two_terms(jnp.concatenate(main + [extra], 0)), 1)
        part = dot(terms, table[0:256, :])
        total += pltpu.roll(part, 35 * v, 1) if v else part
    turn = lanes_turn(lax.axis_index("gy"))
    lane = lax.broadcasted_iota(jnp.int32, (8, NL), 1)
    spare = (lane >= 105) & (lane < 126)
    upper = lax.broadcasted_iota(jnp.int32, (8, NL), 0) < 4
    below, above = total[64:72], total[72:80]
    pieces = [pltpu.roll(above, 105 - 21 * p, 1) for p in range(5)]
    for g in range(8):
        if g < 5:
            extra = pltpu.roll(below, 105 - 21 * g, 1)
        else:
            extra = pltpu.roll(pieces[2 * g - 10], 4, 0)
            extra = jnp.where(upper, extra, pieces[2 * g - 9] if g < 7 else 0.0)
        tile = jnp.where(spare, extra, total[8 * g : 8 * g + 8])
        share[8 * g : 8 * g + 8, :] = pltpu.roll(tile, turn, 1)


def in_hbm(x):
    return pltpu.with_memory_space_constraint(x, pltpu.HBM)


def first_step(field, masks):
    vmem = pl.BlockSpec(memory_space=pltpu.VMEM)
    shapes = [(NV * NZ * PITCH, NL), (16, 8, NL), (10, 8, NL), (2, 8, NL), (64, NL)]
    return pl.pallas_call(
        first_kernel,
        out_shape=[jax.ShapeDtypeStruct(s, F32) for s in shapes],
        in_specs=[pl.BlockSpec(memory_space=pltpu.HBM)] * 3,
        out_specs=[vmem] * 5,
        scratch_shapes=[
            pltpu.VMEM((NV, NZ, NR, NL), F32),
            pltpu.VMEM((NV * 4, NR, NL), F32),
            pltpu.VMEM((2, 2, 4, 7), jnp.int32),
            pltpu.VMEM((400, NL), BF16),
            pltpu.SemaphoreType.DMA((4 * NV + 2,)),
        ],
        compiler_params=pltpu.CompilerParams(vmem_limit_bytes=VMEM_LIMIT),
    )(*[in_hbm(x) for x in (field, masks.transpose(0, 2, 3, 1), jnp.asarray(weights()["first"]))])


ROWS = 40


def lift_kernel(lifted, parts):
    def lift(step, _):
        v, bz = step // 2, lax.rem(step, 2)
        for z in range(8):
            start = pl.multiple_of((step * 8 + z) * PITCH, 8)
            for t in range(4):
                pair = lift_rows(lambda s: lifted[pl.ds(start + 16 * t + s, 8, stride=2), :], 8)
                for bx in range(2):
                    plane = (2 * bz + bx) * 24 + v * 8 + z
                    parts[pl.ds(pl.multiple_of(plane * ROWS + 8 * t, 8), 8), :] = pair[bx]
        return 0

    lax.fori_loop(0, NV * 2, lift, 0)


def lift_step(lifted):
    vmem = pl.BlockSpec(memory_space=pltpu.VMEM)
    return pl.pallas_call(
        lift_kernel,
        out_shape=jax.ShapeDtypeStruct((4 * NV * 8 * ROWS, NL), F32),
        in_specs=[vmem],
        out_specs=vmem,
        compiler_params=pltpu.CompilerParams(vmem_limit_bytes=VMEM_LIMIT),
    )(lifted)


def edge_kernel(parts_in, lifted, north, south, own_masks, table_hbm, parts, sides, packed, table, sem):
    copy = pltpu.make_async_copy(table_hbm, table, sem.at[0])
    copy.start()
    for p in range(4 * NV * 8):
        parts[p * ROWS + 32 : p * ROWS + 40, :] = jnp.zeros((8, NL), F32)
    for v in range(NV):
        for bz in range(2):

            def cell(x):
                return lifted[pl.ds((v * NZ + bz * 8) * PITCH + 8 + x, 8, stride=PITCH), :]

            def at(bx, r):
                return pl.ds(((2 * bz + bx) * 24 + v * 8) * ROWS + r, 8, stride=ROWS)

            before, after, detail = north[v * 3 + bz], south[v * 5 + bz], south[v * 5 + 2 + bz]
            start = cell(0)
            last = cell(63) - 0.5 * (cell(62) + after)
            parts[at(0, 0), :] = parts[at(0, 0), :] + 0.25 * before
            parts[at(0, 31), :] = parts[at(0, 31), :] - 0.125 * after
            parts[at(1, 31), :] = parts[at(1, 31), :] - 0.5 * after
            parts[at(0, 32), :] = after + 0.25 * (last + detail)
            parts[at(1, 32), :] = detail
            parts[at(1, 39), :] = before - 0.5 * start
            if bz == 0:
                parts[at(0, 33), :] = south[v * 5 + 4]
                parts[at(0, 39), :] = north[v * 3 + 2] - 0.125 * start

    lane = lax.broadcasted_iota(jnp.int32, (8, NL), 1) // 16

    def pack(v, _):
        for n in range(4):
            for t in range(5):
                tile = jnp.zeros((8, NL), F32)
                for z in range(8):
                    start = (n * 24 + v * 8 + z) * ROWS + 8 * t
                    x = parts[pl.ds(pl.multiple_of(start, 8), 8), :]
                    tile = jnp.where(lane == z, pltpu.roll(x, (8 + 16 * z) % NL, 1), tile)
                packed[pl.ds(pl.multiple_of(n * 120 + v * ROWS + 8 * t, 8), 8), :] = tile
        return 0

    lax.fori_loop(0, NV, pack, 0)
    copy.wait()
    terms = [two_terms(packed[n * 120 : (n + 1) * 120, :]) for n in range(4)]
    high, low = [jnp.concatenate(part, 1) for part in zip(*terms)]
    sides[0:120, :] = dot(high, table[...]) + dot(low, table[...])
    sides[120:128, :] = north[9]
    sides[128:136, :] = own_masks[0]
    sides[136:144, :] = own_masks[1]
    sides[144:152, :] = south[15]


def edge_step(parts, lifted, north, south, own_masks):
    vmem = pl.BlockSpec(memory_space=pltpu.VMEM)
    shapes = [(4 * NV * 8 * ROWS, NL), (152, NL)]
    return pl.pallas_call(
        edge_kernel,
        out_shape=[jax.ShapeDtypeStruct(s, F32) for s in shapes],
        in_specs=[vmem] * 5 + [pl.BlockSpec(memory_space=pltpu.HBM)],
        out_specs=[vmem] * 2,
        input_output_aliases={0: 0},
        cost_estimate=cost(20),
        scratch_shapes=[pltpu.VMEM((480, NL), F32), pltpu.VMEM((512, NL), BF16), pltpu.SemaphoreType.DMA((1,))],
        compiler_params=pltpu.CompilerParams(vmem_limit_bytes=VMEM_LIMIT),
    )(parts, lifted, north, south, own_masks, in_hbm(jnp.asarray(weights()["edge"])))


def join_kernel(*refs):
    shares, out = refs[-3::-1], refs[-1]
    for n, piece in enumerate(shares):
        out[64 * n : 64 * (n + 1), :] = piece[...]


def join_step(shares, after):
    vmem = pl.BlockSpec(memory_space=pltpu.VMEM)
    return pl.pallas_call(
        join_kernel,
        out_shape=jax.ShapeDtypeStruct((64 * len(shares), NL), F32),
        in_specs=[vmem] * len(shares) + [pl.BlockSpec(memory_space=pl.ANY)],
        out_specs=vmem,
        cost_estimate=cost(20),
        compiler_params=pltpu.CompilerParams(vmem_limit_bytes=VMEM_LIMIT),
    )(*shares[::-1], after)


def mask_lanes(west, east, own_masks, north_mask, south_mask, wide):
    masks = [jnp.concatenate([ref[120 + 8 * i : 128 + 8 * i, :] for i in range(4)], 0) for ref in (east, west)]
    own = jnp.concatenate([north_mask[0], own_masks[0], own_masks[1], south_mask[0]], 0)
    flags = jnp.concatenate([own] + masks, 1).astype(BF16)
    return dot(flags, wide[144:528, :])


def beside_tiles(west, east, at, count):
    lane = lax.broadcasted_iota(jnp.int32, (count, NL), 1)
    from_west = (lane >= 112) | ((lane < 96) & (lax.rem(lane, 24) >= 16))
    tiles = []
    for v in range(NV):
        rows = slice(v * ROWS + at, v * ROWS + at + count)
        beside = jnp.where(from_west, west[rows, :], east[rows, :])
        tiles += [pltpu.roll(beside, NL - z, 1) if z else beside for z in range(8)]
    return tiles


def beside_terms(west, east, at, count):
    return jnp.concatenate(two_terms(jnp.concatenate(beside_tiles(west, east, at, count), 0)), 1)


def own_terms(planes, at, count):
    return jnp.concatenate(two_terms(planes[:, at : at + count, :].reshape(24 * count, NL)), 1)


def main_kernel(
    parts, flat, east, west, own_masks, north_mask, south_mask, wide, narrow,
    kept,
    gain2, low, second, kept2, low_back, gain, sides_wide, turned,
):
    inverse, smooth_own, smooth_beside = narrow.at[0:256], narrow.at[256:512], narrow.at[512:768]
    back, forward2, inverse2 = narrow.at[768:1024], narrow.at[1024:1152], narrow.at[1152:1280]
    lanes = mask_lanes(west, east, own_masks, north_mask, south_mask, wide)
    lane64 = lax.broadcasted_iota(jnp.int32, (1, NL), 1) < 64
    forward2_f = forward2[...].astype(F32)
    for ib in range(4):
        for n in range(4) if ib else (1, 3):
            b = 8 * ib + 4 * (n // 2) + n % 2 - 1
            smooth_two = lanes[b : b + 1, NL:] if n else jnp.ones((1, NL), F32)
            row = jnp.where(lane64, smooth_two, lanes[b + 2 : b + 3, NL:])
            both = dot((forward2_f * row).astype(BF16), inverse2[...]).astype(BF16)
            gain2[ib, n, 0:128, :] = both
            gain2[ib, n, 128:256, :] = both

    for at, count in ((0, 16), (16, 16), (32, 8)):
        part = dot(own_terms(parts.at[0], at, count), smooth_own[...])
        part += dot(beside_terms(west, east, at, count), smooth_beside[...])
        part = part.reshape(24, count, NL)
        if at < 32:
            low[:, 8 + at : 8 + at + count, :] = part
            if at == 0:
                low[:, 56:64, :] = part[:, 0:8]
        else:
            low[:, 0:8, :] = part
            low[:, 40:48, :] = part
            low[:, 48:56, :] = part

    def rows_two(v, _):
        for t in range(3):
            lifted = [
                lift_rows(lambda s: low[v * 8 + p, pl.ds(16 * t + s, 8, stride=2), :], 8) for p in range(8)
            ]
            for bx in range(2):
                smooth, detail = lift_planes([pair[bx] for pair in lifted])
                for bz, part in ((0, smooth), (1, detail)):
                    for z in range(4):
                        second[2 * bz + bx, t, pl.ds(pl.multiple_of((v * 4 + z) * 8, 8), 8), :] = part[z]
        return 0

    lax.fori_loop(0, NV, rows_two, 0)
    for n in range(4):
        for t in range(3):
            terms = jnp.concatenate(two_terms(second[n, t]), 1)
            if t < 2:
                kept2[n, :, 8 + 8 * t : 16 + 8 * t, :] = dot(terms, gain2[t + 1, n]).reshape(NV * 4, 8, NL)
            else:
                if n % 2:
                    kept2[n, :, 0:8, :] = dot(terms, gain2[0, n]).reshape(NV * 4, 8, NL)
                kept2[n, :, 24:32, :] = dot(terms, gain2[3, n]).reshape(NV * 4, 8, NL)

    def back_two(v, _):
        for t in range(3):
            pairs = {}
            for bz in range(2):
                for z in range(4):
                    p = v * 4 + z
                    if t < 2:
                        pairs[bz, z] = unlift_rows(
                            lambda r: kept2[2 * bz, p, pl.ds(r, 8), :],
                            lambda r: kept2[2 * bz + 1, p, pl.ds(r, 8), :],
                            8 + 8 * t,
                        )
                    else:
                        even = kept2[2 * bz, p, 24:32, :] - 0.25 * (
                            kept2[2 * bz + 1, p, 23:31, :] + kept2[2 * bz + 1, p, 24:32, :]
                        )
                        pairs[bz, z] = (even, even)
            for parity in range(2 if t < 2 else 1):
                planes = unlift_planes([pairs[0, z][parity] for z in range(4)], [pairs[1, z][parity] for z in range(4)])
                for z in range(8):
                    low_back[pl.ds((v * 8 + z) * 48 + 16 * t + parity, 8, stride=2), :] = planes[z]
        return 0

    lax.fori_loop(0, NV, back_two, 0)

    forward_f = wide[0:144, :].astype(F32)
    for ib in range(4):
        sides_wide[ib] = jnp.zeros((NL, 4 * NL), F32)
    for ib in range(4):
        for n in range(4) if ib else (1, 3):
            b = 8 * ib + 4 * (n // 2) + n % 2 - 1
            smooth_one = lanes[b : b + 1, 0:NL] if n else jnp.zeros((1, NL), F32)
            row = jnp.concatenate([smooth_one, lanes[b + 2 : b + 3, 0:NL]], 1)
            both = dot((forward_f * row).astype(BF16), inverse[...])
            main = both[0:128].astype(BF16)
            gain[ib, n, 0:128, :] = main
            gain[ib, n, 128:256, :] = main
            for i in range(3):
                at = 24 * n + 8 * i
                sides_wide[ib, at : at + 1, n * NL : (n + 1) * NL] = both[128 + i : 129 + i]

    gain_sides = []
    for ib in range(4):
        side = sides_wide[ib].astype(BF16)
        gain_sides.append(jnp.concatenate([side, side], 0))
    def put(n, p, at, rows):
        start = pl.multiple_of((n * 24 + p) * 48 + 8 + at, 8)
        kept[pl.ds(start, rows.shape[0]), :] = rows

    def row_of(ref, first, pitch):
        return ref[pl.ds(first, 24, stride=pitch), :]

    for ib in range(2):
        product = dot(beside_terms(west, east, 16 * ib, 16), gain_sides[ib + 1])
        for n in range(4):
            for p in range(24):
                put(n, p, 16 * ib, product[16 * p : 16 * p + 16, n * NL : (n + 1) * NL])

    def keep(n, _):
        for ib in range(2):
            product = dot(own_terms(parts.at[n], 16 * ib, 16), gain[ib + 1, n])
            for p in range(24):
                start = pl.ds(pl.multiple_of((n * 24 + p) * 48 + 8 + 16 * ib, 8), 16)
                kept[start, :] += product[16 * p : 16 * p + 16]
        return 0

    lax.fori_loop(0, 4, keep, 0)
    for ib in range(2):
        rows = jnp.concatenate([low_back[48 * p + 16 * ib : 48 * p + 16 * ib + 16, :] for p in range(24)], 0)
        product = dot(jnp.concatenate(two_terms(rows), 1), back[...])
        for p in range(24):
            start = 48 * p + 8 + 16 * ib
            kept[start : start + 16, :] += product[16 * p : 16 * p + 16]
    tiles = beside_tiles(west, east, 32, 8)
    for p in range(24):
        turned[8 * p : 8 * p + 8, :] = tiles[p]
    for first, ib, place, row in ((0, 3, 40, 32), (7, 0, 7, 39)):
        beside = dot(jnp.concatenate(two_terms(row_of(turned, first, 8)), 1), gain_sides[ib])
        for n in range(4) if ib else (1, 3):
            own = jnp.concatenate(two_terms(row_of(flat, n * 24 * ROWS + row, ROWS)), 1)
            total = beside[:, n * NL : (n + 1) * NL] + dot(own, gain[ib, n])
            if n == 0:
                total += dot(jnp.concatenate(two_terms(row_of(low_back, row, 48)), 1), back[...])
            kept[pl.ds(n * 24 * 48 + place, 24, stride=48), :] = total


def cells_kernel(kept, out, cells, sems):
    def back_one(step, _):
        v, t = step // 4, step % 4
        pairs = {}
        for bz in range(2):
            for z in range(8):
                p = v * 8 + z
                pairs[bz, z] = unlift_rows(
                    lambda r: kept[2 * bz, p, pl.ds(8 * t + r, 8), :],
                    lambda r: kept[2 * bz + 1, p, pl.ds(8 * t + r, 8), :],
                    8,
                )
        for parity in range(2):
            planes = unlift_planes([pairs[0, z][parity] for z in range(8)], [pairs[1, z][parity] for z in range(8)])
            for z in range(NZ):
                cells[v, z, pl.ds(16 * t + parity, 8, stride=2), :] = planes[z]
        return 0

    def copy(step):
        v, rows = step // 4, pl.ds(pl.multiple_of(16 * (step % 4), 16), 16)
        return pltpu.make_async_copy(cells.at[v, :, rows], out.at[v, :, rows], sems.at[step])

    def one(step, _):
        back_one(step, 0)
        copy(step).start()
        return 0

    lax.fori_loop(0, NV * 4, one, 0)
    for step in range(NV * 4):
        copy(step).wait()


def main_specs():
    vmem = pl.BlockSpec(memory_space=pltpu.VMEM)
    return [
        vmem, vmem, vmem, vmem, vmem,
        pl.BlockSpec((1, 8, NL), lambda i: (9, 0, 0)), pl.BlockSpec((1, 8, NL), lambda i: (15, 0, 0)),
        vmem, vmem,
    ]


def main_step(flat, *operands):
    w = weights()
    return pl.pallas_call(
        main_kernel,
        grid=(1,),
        out_shape=jax.ShapeDtypeStruct((4 * NV * 8 * 48, NL), F32),
        in_specs=main_specs(),
        out_specs=pl.BlockSpec((4 * NV * 8 * 48, NL), lambda i: (0, 0)),
        scratch_shapes=[
            pltpu.VMEM((4, 4, 256, NL), BF16),
            pltpu.VMEM((NV * 8, 64, NL), F32),
            pltpu.VMEM((4, 3, NV * 32, NL), F32),
            pltpu.VMEM((4, NV * 4, 40, NL), F32),
            pltpu.VMEM((NV * 8 * 48, NL), F32),
            pltpu.VMEM((4, 4, 256, NL), BF16),
            pltpu.VMEM((4, NL, 4 * NL), F32),
            pltpu.VMEM((NV * 64, NL), F32),
        ],
        cost_estimate=cost(8),
        compiler_params=pltpu.CompilerParams(vmem_limit_bytes=VMEM_LIMIT),
    )(flat.reshape(4, NV * 8, ROWS, NL), flat, *operands, w["wide"], w["narrow"])


def cells_step(kept):
    shape = (NV, NZ, NR, NL)
    return pl.pallas_call(
        cells_kernel,
        out_shape=jax.ShapeDtypeStruct(shape, F32),
        in_specs=[pl.BlockSpec(memory_space=pltpu.VMEM)],
        out_specs=pl.BlockSpec(memory_space=pltpu.HBM),
        scratch_shapes=[pltpu.VMEM(shape, F32), pltpu.SemaphoreType.DMA((NV * 4,))],
        cost_estimate=cost(4),
        compiler_params=pltpu.CompilerParams(vmem_limit_bytes=VMEM_LIMIT),
    )(kept)


def rows_kernel(count_x, count_z, *refs):
    shares, out = refs[count_x - 1 :: -1], refs[count_x + 1]
    me, me_y = lax.axis_index("gx"), lax.axis_index("gy")
    row = lax.broadcasted_iota(jnp.int32, (8, NL), 0)
    lane = lax.broadcasted_iota(jnp.int32, (8, NL), 1)
    for r in range(count_x):
        at = pl.multiple_of(16 * (me ^ r), 16)
        for j in range(count_z):
            for z in range(4):
                start = 64 * j + 16 * z
                out[j, z, pl.ds(at, 16), :] = shares[r][start : start + 16, :]
    for j in range(count_z):
        turn = lanes_turn(me_y ^ (2 * j))
        piece = lax.rem(lane + (NL - turn), NL) // 21
        inside = [piece == p for p in range(5)]
        for r in range(count_x):
            i = me ^ r
            below = pl.multiple_of(16 * lax.rem(i + 1, count_x), 16)
            above = pl.multiple_of(16 * lax.rem(i + count_x - 1, count_x) + 8, 8)
            tiles = [shares[r][64 * j + 8 * g : 64 * j + 8 * g + 8, :] for g in range(8)]
            low, high = jnp.zeros((8, NL), F32), jnp.zeros((8, NL), F32)
            for p in range(5):
                back = (21 * p - 105) % NL
                low = jnp.where(inside[p], pltpu.roll(tiles[p], back, 1), low)
                extra = tiles[5 + p // 2]
                extra = extra if p % 2 else pltpu.roll(extra, 4, 0)
                high = jnp.where(inside[p], pltpu.roll(extra, back, 1), high)
            for z in range(4):
                first = pltpu.roll(low, 8 - 2 * z, 0) if z else low
                last = pltpu.roll(high, z, 0) if z else high
                out[j, z, pl.ds(below, 8), :] += jnp.where(row < 2, first, 0.0)
                out[j, z, pl.ds(above, 8), :] += jnp.where(row == 7, last, 0.0)


def rows_step(pieces, count_z, after):
    vmem = pl.BlockSpec(memory_space=pltpu.VMEM)
    count_x = len(pieces)
    return pl.pallas_call(
        functools.partial(rows_kernel, count_x, count_z),
        out_shape=jax.ShapeDtypeStruct((count_z, 4, 16 * count_x, NL), F32),
        in_specs=[vmem] * count_x + [pl.BlockSpec(memory_space=pl.ANY)],
        out_specs=vmem,
        compiler_params=pltpu.CompilerParams(vmem_limit_bytes=VMEM_LIMIT),
    )(*pieces[::-1], after)


def coarse_kernel(count_x, count_y, own, other, out_hbm, out, sems):
    me = lax.axis_index("gy")
    me_z, is_even = lax.shift_right_logical(me, 1), lax.rem(me, 2) == 0
    lane = lax.broadcasted_iota(jnp.int32, (8, NL), 1)
    place = [lax.rem(lane + NL - 35 * v, NL) for v in range(NV)]

    def block(i, _):
        rows = pl.ds(pl.multiple_of(8 * i, 8), 8)
        for z in range(4):
            pieces = []
            for j in range(count_y // 2):
                mine, theirs = own[j ^ me_z, z, rows, :], other[j ^ me_z, z, rows, :]
                pieces += [jnp.where(is_even, mine, theirs), jnp.where(is_even, theirs, mine)]
            for v in range(NV):
                at = place[v]
                for t in range(count_y // 4):
                    total = jnp.where(at < 2, pieces[4 * t - 1], 0.0)
                    total += jnp.where(at == NL - 1, pieces[(4 * t + 4) % count_y], 0.0)
                    for q in range(4):
                        inside = (at >= 32 * q - 1) & (at < 32 * q + 34)
                        total += jnp.where(inside, pieces[4 * t + q], 0.0)
                    out[v, z, rows, NL * t : NL * (t + 1)] = pltpu.roll(total, NL - 35 * v, 1) if v else total
        return 0

    def copy(i):
        rows = pl.ds(pl.multiple_of(16 * i, 16), 16)
        return pltpu.make_async_copy(out.at[:, :, rows], out_hbm.at[:, :, rows], sems.at[i])

    def pair(i, _):
        block(2 * i, 0)
        block(2 * i + 1, 0)
        copy(i).start()
        return 0

    lax.fori_loop(0, count_x, pair, 0)
    for i in range(count_x):
        copy(i).wait()


def coarse_step(own, other, count_x, count_y):
    vmem = pl.BlockSpec(memory_space=pltpu.VMEM)
    shape = (NV, 4, 16 * count_x, 32 * count_y)
    return pl.pallas_call(
        functools.partial(coarse_kernel, count_x, count_y),
        out_shape=jax.ShapeDtypeStruct(shape, F32),
        in_specs=[vmem, vmem],
        out_specs=pl.BlockSpec(memory_space=pltpu.HBM),
        scratch_shapes=[pltpu.VMEM(shape, F32), pltpu.SemaphoreType.DMA((count_x,))],
        compiler_params=pltpu.CompilerParams(vmem_limit_bytes=VMEM_LIMIT),
    )(own, other)


def shifted(x, axis, step):
    count = lax.axis_size(axis)
    return lax.ppermute(x, axis, [(i, (i + step) % count) for i in range(count)])


def swapped(x, axis, distance):
    return lax.ppermute(x, axis, [(i, i ^ distance) for i in range(lax.axis_size(axis))])


def body(field, masks):
    count_x, count_y = lax.axis_size("gx"), lax.axis_size("gy")
    lifted, up, down, own_masks, share = first_step(field, masks)
    south = shifted(up, "gx", -1)
    north = shifted(down, "gx", 1)
    shares = [share] + [swapped(share, "gy", r) for r in range(2, count_y, 2)]
    parts, sides = edge_step(lift_step(lifted), lifted, north, south, own_masks)
    east = shifted(sides, "gy", -1)
    west = shifted(sides, "gy", 1)
    joined = join_step(shares, sides)
    pieces = [joined] + [swapped(joined, "gx", r) for r in range(1, count_x)]
    kept = main_step(parts, east, west, own_masks, north, south)
    own = rows_step(pieces, count_y // 2, kept)
    other = swapped(own, "gy", 1)
    return cells_step(kept.reshape(4, NV * 8, 48, NL)), coarse_step(own, other, count_x, count_y)


def solution(mesh):
    placed = P(None, None, "gx", "gy")
    return jax.shard_map(
        body,
        mesh=mesh,
        in_specs=(placed, placed),
        out_specs=(placed, P()),
        check_vma=False,
    )
```

```python
import functools

import jax
import jax.numpy as jnp
import ml_dtypes
import numpy as np
from jax import lax
from jax.experimental import pallas as pl
from jax.experimental.pallas import tpu as pltpu
from jax.sharding import PartitionSpec as P

F32 = jnp.float32
BF16 = jnp.bfloat16
VMEM_LIMIT = 32 * 1024 * 1024

NV, NZ, NR, NL = 3, 16, 64, 128


def detail_row(k):
    return {2 * k + 1: 1.0, 2 * k: -0.5, 2 * k + 2: -0.5}


def smooth_row(k):
    row = {2 * k: 1.0}
    for j in (k - 1, k):
        for cell, value in detail_row(j).items():
            row[cell] = row.get(cell, 0.0) + 0.25 * value
    return row


def even_row(k):
    return {("s", k): 1.0, ("d", k - 1): -0.25, ("d", k): -0.25}


def odd_row(k):
    row = {("d", k): 1.0}
    for j in (k, k + 1):
        for name, value in even_row(j).items():
            row[name] = row.get(name, 0.0) + 0.5 * value
    return row


def as_bf16(matrix):
    cast = matrix.astype(ml_dtypes.bfloat16)
    assert (cast.astype(np.float64) == matrix).all()
    return cast


def combine(*terms):
    total = {}
    for factor, row in terms:
        for cell, value in row.items():
            total[cell] = total.get(cell, 0.0) + factor * value
    return total


def level_one_columns():
    names = {("s", k): k for k in range(65)}
    names.update({("d", k): 128 + k for k in range(65)})
    names[("d", -1)] = 128 + 65
    return names


def level_two_columns():
    names = {("s", k): k for k in range(33)}
    names.update({("d", k): 64 + k for k in range(33)})
    names[("d", -1)] = 64 + 33
    return names


def smooth_place(k):
    return k + 2


def beyond(n):
    return {"cell": 40 + 16 * n, "after": 48 + 16 * n, "before": 8 * n}


BEYOND_SMOOTH = {65: 104, -1: 32}
FROM_WEST = 40


def own_row(kind, k, n):
    place = {name: 128 + lane for name, lane in beyond(n).items()}
    if kind == "d":
        if k == -1:
            return {place["before"]: 1.0, 0: -0.5}
        if k == 64:
            return {place["after"]: 1.0}
        return {(place["cell"] if y == 128 else y): value for y, value in detail_row(k).items()}
    if k in (-2, 66):
        return {}
    if k in BEYOND_SMOOTH:
        row = {128 + BEYOND_SMOOTH[k]: 1.0}
        return combine((1.0, row), (1.0, {0: -0.125})) if k == -1 else row
    even = place["cell"] if k == 64 else 2 * k
    return combine((1.0, {even: 1.0}), (0.25, own_row("d", k - 1, n)), (0.25, own_row("d", k, n)))


@functools.lru_cache(maxsize=None)
def weights():
    w = {}
    names = level_one_columns()
    forward = np.zeros((4, 256, 256))
    inverse = np.zeros((256, 128))
    for (kind, k), column in names.items():
        for n in range(4):
            for place, value in own_row(kind, k, n).items():
                forward[n, place, column] += value
    for k in range(64):
        for y, row in ((2 * k, even_row(k)), (2 * k + 1, odd_row(k))):
            for name, value in row.items():
                inverse[names[name], y] += value
    short = np.zeros((144, 256))
    short[:128] = forward[0, :128]
    for i, lane in enumerate(beyond(0).values()):
        short[128 + i] = forward[0, 128 + lane]
    smooth = np.zeros((256, 128))
    for k in range(-2, 67):
        for place, value in own_row("s", k, 0).items():
            smooth[place, smooth_place(k)] += value
    names2 = level_two_columns()
    forward2 = np.zeros((128, 128))
    inverse2 = np.zeros((128, 128))
    for (kind, k), column in names2.items():
        for cell, value in (smooth_row(k) if kind == "s" else detail_row(k)).items():
            forward2[smooth_place(cell), column] += value
    for k in range(33):
        rows = [(2 * k, even_row(k))] + ([(2 * k + 1, odd_row(k))] if k < 32 else [])
        for y, row in rows:
            for name, value in row.items():
                inverse2[names2[name], y] += value
    back = np.zeros((256, 128))
    back[:65] = inverse[:65]
    back[128 : 128 + 65] = inverse[:65]
    spread = np.zeros((3, 128, 2, 128))
    for k in range(64):
        spread[0, k, 0, k] = 1
    for k in range(32):
        spread[0, 64 + k, 1, k] = 1
        spread[0, 64 + k, 1, 64 + k] = 1
    for at in range(0, 16, 4):
        spread[1, at, 0, 64] = 1
        spread[2, at + 1, 0, 65] = 1
        for base in (0, 64):
            spread[1, at + 2, 1, base + 32] = 1
            spread[2, at + 3, 1, base + 33] = 1
    w["wide"] = np.concatenate([short, spread.reshape(384, 256)], 0)
    own, beside = smooth[:128], smooth[128:]
    w["narrow"] = np.concatenate([inverse, own, own, beside, beside, back, forward2, inverse2], 0)
    edge = np.zeros((4, 128, 128))

    def put(n, lane, row):
        for z in range(8):
            for y, value in row.items():
                j = y - 120 if y >= 120 else y + 8
                edge[n, 16 * z + j, lane + z] += value

    part = {127: 1.0, 126: -0.5}
    for n in range(4):
        put(n, beyond(n)["cell"], {0: 1.0})
        put(n, beyond(n)["after"], detail_row(0))
        put(n, beyond(n)["before"], part)
    put(0, BEYOND_SMOOTH[65], combine((1.0, smooth_row(1)), (-0.5, smooth_row(2))))
    share = combine((1.0, {126: 1.0}), (0.25, detail_row(62)), (0.25, part))
    put(0, BEYOND_SMOOTH[-1], combine((1.0, share), (-0.5, smooth_row(62))))
    w["edge"] = edge.reshape(512, 128)
    expand = np.zeros((2, 4, 128))
    for j in range(4):
        expand[0, j, 16 * j : 16 * j + 16] = 1
        expand[1, j, 64 + 8 * j : 64 + 8 * j + 8] = 1
    twice = combine(*[(value, smooth_row(k)) for k, value in smooth_row(0).items()])
    columns = np.zeros((2, 128, 128))
    for m in range(-1, 34):
        for t, value in twice.items():
            if 0 <= 4 * m + t < NL:
                columns[:, 4 * m + t, m + 1] = value
    rows = np.zeros((4, 32, 2, 64))
    for z in range(4):
        places = {m: m for m in range(16)}
        places.update({16: 16 + 2 * z, 17: 17 + 2 * z, -1: 16 + 15 - z})
        for m, place in places.items():
            for t, value in twice.items():
                if 0 <= 4 * m + t < NR:
                    rows[z, place, :, 4 * m + t] = value
    pad = np.zeros((8, 128))
    w["first"] = np.concatenate([columns.reshape(256, 128), rows.reshape(128, 128), expand.reshape(8, 128), pad], 0)
    return {name: as_bf16(matrix) for name, matrix in w.items()}


def two_terms(x):
    high = x.astype(BF16)
    low = (x - high.astype(F32)).astype(BF16)
    return high, low


def cost(gigaflops):
    return pl.CostEstimate(flops=gigaflops * 10**9, bytes_accessed=8 * 10**6, transcendentals=0)


def dot(a, b):
    return jnp.dot(a, b, preferred_element_type=F32)


def lift_planes(cells):
    half = len(cells) // 2
    even, odd = cells[0::2], cells[1::2]
    detail = [odd[k] - 0.5 * (even[k] + even[min(k + 1, half - 1)]) for k in range(half)]
    smooth = [even[k] + 0.25 * (detail[max(k - 1, 0)] + detail[k]) for k in range(half)]
    return smooth, detail


def unlift_planes(smooth, detail):
    half = len(smooth)
    even = [smooth[k] - 0.25 * (detail[max(k - 1, 0)] + detail[k]) for k in range(half)]
    out = []
    for k in range(half):
        out += [even[k], detail[k] + 0.5 * (even[k] + even[min(k + 1, half - 1)])]
    return out


def lift_rows(load, start):
    even, odd, after = load(start), load(start + 1), load(start + 2)
    before, odd_before = load(start - 2), load(start - 1)
    detail = odd - 0.5 * (even + after)
    detail_before = odd_before - 0.5 * (before + even)
    return even + 0.25 * (detail_before + detail), detail


def unlift_rows(smooth, detail, row):
    here, after = detail(row), detail(row + 1)
    even = smooth(row) - 0.25 * (detail(row - 1) + here)
    next_even = smooth(row + 1) - 0.25 * (here + after)
    return even, here + 0.5 * (even + next_even)


PITCH = 80


def lanes_turn(j):
    return lax.rem(32 * lax.rem(j, 4) + NL - 1, NL)


def first_kernel(
    field, masks_hbm, table_hbm, lifted, up, down, own_masks, share, cells, twice, masks, table, sems
):
    small = [
        pltpu.make_async_copy(masks_hbm, masks, sems.at[0]),
        pltpu.make_async_copy(table_hbm, table, sems.at[1]),
    ]
    copies = []
    for v in range(NV):
        for c in range(4):
            part = pl.ds(16 * c, 16)
            copies.append(pltpu.make_async_copy(field.at[v, :, part], cells.at[v, :, part], sems.at[2 + 4 * v + c]))
    for copy in small + copies:
        copy.start()
    for p in range(NV * NZ):
        lifted[p * PITCH : p * PITCH + 8, :] = jnp.zeros((8, NL), F32)
        lifted[p * PITCH + 72 : p * PITCH + 80, :] = jnp.zeros((8, NL), F32)
    for copy in small:
        copy.wait()
    for i, out, tile in ((0, up, 15), (1, down, 9)):
        total = jnp.zeros((7, NL), F32)
        for l in range(2):
            flags = masks[l, i].astype(F32).astype(BF16)
            spread = table[384 + 4 * l : 388 + 4 * l, :]
            total += lax.dot_general(flags, spread, (((0,), (0,)), ((), ())), preferred_element_type=F32)
        own_masks[i] = jnp.concatenate([total, jnp.zeros((1, NL), F32)], 0)
        out[tile] = own_masks[i]

    for v in range(NV):
        for t in range(8):
            if t % 2 == 0:
                copies[4 * v + t // 2].wait()
            smooth, detail = lift_planes([cells[v, z, 8 * t : 8 * t + 8, :] for z in range(NZ)])
            for k, tile in enumerate(smooth + detail):
                start = (v * NZ + k) * PITCH + 8 + 8 * t
                lifted[start : start + 8, :] = tile
            for k, tile in enumerate(lift_planes(smooth)[0]):
                twice[v * 4 + k, 8 * t : 8 * t + 8, :] = tile
        for bz in range(2):

            def row(x):
                return lifted[pl.ds((v * NZ + bz * 8) * PITCH + 8 + x, 8, stride=PITCH), :]

            x = [row(j) for j in range(7 if bz == 0 else 3)]
            first = x[1] - 0.5 * (x[0] + x[2])
            up[v * 5 + bz] = x[0]
            up[v * 5 + 2 + bz] = first
            y = {j: row(j) for j in (range(58, 64) if bz == 0 else (62, 63))}
            part = y[63] - 0.5 * y[62]
            down[v * 3 + bz] = part
            if bz == 0:
                second = x[3] - 0.5 * (x[2] + x[4])
                third = x[5] - 0.5 * (x[4] + x[6])
                up[v * 5 + 4] = x[2] + 0.25 * (first + second) - 0.5 * (x[4] + 0.25 * (second + third))
                before = y[59] - 0.5 * (y[58] + y[60])
                last = y[61] - 0.5 * (y[60] + y[62])
                down[v * 3 + 2] = y[62] + 0.25 * (last + part) - 0.5 * (y[60] + 0.25 * (before + last))

    total = jnp.zeros((80, NL), F32)
    for v in range(NV):
        main, extra = [], jnp.zeros((16, NL), F32)
        for z in range(4):
            terms = jnp.concatenate(two_terms(twice[v * 4 + z]), 0)
            part = dot(table[256 + 32 * z : 288 + 32 * z, :], terms)
            main.append(part[:16])
            extra += part[16:]
        terms = jnp.concatenate(two_terms(jnp.concatenate(main + [extra], 0)), 1)
        part = dot(terms, table[0:256, :])
        total += pltpu.roll(part, 35 * v, 1) if v else part
    turn = lanes_turn(lax.axis_index("gy"))
    lane = lax.broadcasted_iota(jnp.int32, (8, NL), 1)
    spare = (lane >= 105) & (lane < 126)
    upper = lax.broadcasted_iota(jnp.int32, (8, NL), 0) < 4
    below, above = total[64:72], total[72:80]
    pieces = [pltpu.roll(above, 105 - 21 * p, 1) for p in range(5)]
    for g in range(8):
        if g < 5:
            extra = pltpu.roll(below, 105 - 21 * g, 1)
        else:
            extra = pltpu.roll(pieces[2 * g - 10], 4, 0)
            extra = jnp.where(upper, extra, pieces[2 * g - 9] if g < 7 else 0.0)
        tile = jnp.where(spare, extra, total[8 * g : 8 * g + 8])
        share[8 * g : 8 * g + 8, :] = pltpu.roll(tile, turn, 1)


def in_hbm(x):
    return pltpu.with_memory_space_constraint(x, pltpu.HBM)


def first_step(field, masks):
    vmem = pl.BlockSpec(memory_space=pltpu.VMEM)
    shapes = [(NV * NZ * PITCH, NL), (16, 8, NL), (10, 8, NL), (2, 8, NL), (64, NL)]
    return pl.pallas_call(
        first_kernel,
        out_shape=[jax.ShapeDtypeStruct(s, F32) for s in shapes],
        in_specs=[pl.BlockSpec(memory_space=pltpu.HBM)] * 3,
        out_specs=[vmem] * 5,
        scratch_shapes=[
            pltpu.VMEM((NV, NZ, NR, NL), F32),
            pltpu.VMEM((NV * 4, NR, NL), F32),
            pltpu.VMEM((2, 2, 4, 7), jnp.int32),
            pltpu.VMEM((400, NL), BF16),
            pltpu.SemaphoreType.DMA((4 * NV + 2,)),
        ],
        compiler_params=pltpu.CompilerParams(vmem_limit_bytes=VMEM_LIMIT),
    )(*[in_hbm(x) for x in (field, masks.transpose(0, 2, 3, 1), jnp.asarray(weights()["first"]))])


ROWS = 40


def lift_kernel(lifted, parts):
    def lift(step, _):
        v, bz = step // 2, lax.rem(step, 2)
        for z in range(8):
            start = pl.multiple_of((step * 8 + z) * PITCH, 8)
            for t in range(4):
                pair = lift_rows(lambda s: lifted[pl.ds(start + 16 * t + s, 8, stride=2), :], 8)
                for bx in range(2):
                    plane = (2 * bz + bx) * 24 + v * 8 + z
                    parts[pl.ds(pl.multiple_of(plane * ROWS + 8 * t, 8), 8), :] = pair[bx]
        return 0

    lax.fori_loop(0, NV * 2, lift, 0)


def lift_step(lifted):
    vmem = pl.BlockSpec(memory_space=pltpu.VMEM)
    return pl.pallas_call(
        lift_kernel,
        out_shape=jax.ShapeDtypeStruct((4 * NV * 8 * ROWS, NL), F32),
        in_specs=[vmem],
        out_specs=vmem,
        compiler_params=pltpu.CompilerParams(vmem_limit_bytes=VMEM_LIMIT),
    )(lifted)


def edge_kernel(parts_in, lifted, north, south, own_masks, table_hbm, parts, to_left, to_right, packed, table, sem):
    copy = pltpu.make_async_copy(table_hbm, table, sem.at[0])
    copy.start()
    for p in range(4 * NV * 8):
        parts[p * ROWS + 32 : p * ROWS + 40, :] = jnp.zeros((8, NL), F32)
    for v in range(NV):
        for bz in range(2):

            def cell(x):
                return lifted[pl.ds((v * NZ + bz * 8) * PITCH + 8 + x, 8, stride=PITCH), :]

            def at(bx, r):
                return pl.ds(((2 * bz + bx) * 24 + v * 8) * ROWS + r, 8, stride=ROWS)

            before, after, detail = north[v * 3 + bz], south[v * 5 + bz], south[v * 5 + 2 + bz]
            start = cell(0)
            last = cell(63) - 0.5 * (cell(62) + after)
            parts[at(0, 0), :] = parts[at(0, 0), :] + 0.25 * before
            parts[at(0, 31), :] = parts[at(0, 31), :] - 0.125 * after
            parts[at(1, 31), :] = parts[at(1, 31), :] - 0.5 * after
            parts[at(0, 32), :] = after + 0.25 * (last + detail)
            parts[at(1, 32), :] = detail
            parts[at(1, 39), :] = before - 0.5 * start
            if bz == 0:
                parts[at(0, 33), :] = south[v * 5 + 4]
                parts[at(0, 39), :] = north[v * 3 + 2] - 0.125 * start

    lane = lax.broadcasted_iota(jnp.int32, (8, NL), 1) // 16

    def pack(v, _):
        for n in range(4):
            for t in range(5):
                tile = jnp.zeros((8, NL), F32)
                for z in range(8):
                    start = (n * 24 + v * 8 + z) * ROWS + 8 * t
                    x = parts[pl.ds(pl.multiple_of(start, 8), 8), :]
                    tile = jnp.where(lane == z, pltpu.roll(x, (8 + 16 * z) % NL, 1), tile)
                packed[pl.ds(pl.multiple_of(n * 120 + v * ROWS + 8 * t, 8), 8), :] = tile
        return 0

    lax.fori_loop(0, NV, pack, 0)
    copy.wait()
    terms = [two_terms(packed[n * 120 : (n + 1) * 120, :]) for n in range(4)]
    high, low = [jnp.concatenate(part, 1) for part in zip(*terms)]
    sides = dot(high, table[...]) + dot(low, table[...])
    lane = lax.broadcasted_iota(jnp.int32, (ROWS, NL), 1)
    each = [sides[v * ROWS : (v + 1) * ROWS] for v in range(NV)]
    right = jnp.where(lane < 40, each[0], pltpu.roll(each[1], 40, 1))
    to_right[0:ROWS, :] = jnp.where(lane < 80, right, pltpu.roll(each[2], 80, 1))
    last = jnp.where(lane < 32, pltpu.roll(each[2], NL - 40, 1), pltpu.roll(each[2], NL - 72, 1))
    to_left[0:ROWS, :] = jnp.where(lane < 40, last, each[0])
    to_left[ROWS : 2 * ROWS, :] = jnp.where(lane < 32, pltpu.roll(each[2], NL - 72, 1), each[1])
    lane = lax.broadcasted_iota(jnp.int32, (8, NL), 1)
    ends = jnp.zeros((8, NL), F32)
    for ib, tile in enumerate((north[9], own_masks[0], own_masks[1], south[15])):
        for j, source in enumerate((0, 63, 64, 95)):
            target = 4 * ib + j
            ends = jnp.where(lane == target, pltpu.roll(tile, (target - source) % NL, 1), ends)
    to_left[2 * ROWS : 2 * ROWS + 8, :] = ends
    to_right[ROWS : ROWS + 8, :] = ends


def edge_step(parts, lifted, north, south, own_masks):
    vmem = pl.BlockSpec(memory_space=pltpu.VMEM)
    shapes = [(4 * NV * 8 * ROWS, NL), (2 * ROWS + 8, NL), (ROWS + 8, NL)]
    return pl.pallas_call(
        edge_kernel,
        out_shape=[jax.ShapeDtypeStruct(s, F32) for s in shapes],
        in_specs=[vmem] * 5 + [pl.BlockSpec(memory_space=pltpu.HBM)],
        out_specs=[vmem] * 3,
        input_output_aliases={0: 0},
        cost_estimate=cost(20),
        scratch_shapes=[pltpu.VMEM((480, NL), F32), pltpu.VMEM((512, NL), BF16), pltpu.SemaphoreType.DMA((1,))],
        compiler_params=pltpu.CompilerParams(vmem_limit_bytes=VMEM_LIMIT),
    )(parts, lifted, north, south, own_masks, in_hbm(jnp.asarray(weights()["edge"])))


def join_kernel(*refs):
    shares, out = refs[-3::-1], refs[-1]
    for n, piece in enumerate(shares):
        out[64 * n : 64 * (n + 1), :] = piece[...]


def join_step(shares, after):
    vmem = pl.BlockSpec(memory_space=pltpu.VMEM)
    return pl.pallas_call(
        join_kernel,
        out_shape=jax.ShapeDtypeStruct((64 * len(shares), NL), F32),
        in_specs=[vmem] * len(shares) + [pl.BlockSpec(memory_space=pl.ANY)],
        out_specs=vmem,
        cost_estimate=cost(20),
        compiler_params=pltpu.CompilerParams(vmem_limit_bytes=VMEM_LIMIT),
    )(*shares[::-1], after)


def mask_lanes(west, east, own_masks, north_mask, south_mask, wide):
    group = lax.broadcasted_iota(jnp.int32, (8, NL), 1) // 4
    masks = [
        jnp.concatenate([jnp.where(group == ib, tile, 0.0) for ib in range(4)], 0)
        for tile in (east[2 * ROWS : 2 * ROWS + 8, :], west[ROWS : ROWS + 8, :])
    ]
    own = jnp.concatenate([north_mask[0], own_masks[0], own_masks[1], south_mask[0]], 0)
    flags = jnp.concatenate([own] + masks, 1).astype(BF16)
    return dot(flags, wide[144:528, :])


def beside_tiles(west, east, at, count):
    lane = lax.broadcasted_iota(jnp.int32, (count, NL), 1)
    left = west[at : at + count, :]
    first, second = east[at : at + count, :], east[ROWS + at : ROWS + at + count, :]
    third = jnp.where(lane < 104, pltpu.roll(second, 72, 1), pltpu.roll(first, 72, 1))
    third = jnp.where(lane < 72, pltpu.roll(first, 40, 1), third)
    tiles = []
    for v, right in enumerate((first, second, third)):
        beside = jnp.where(lane < FROM_WEST, pltpu.roll(left, NL - 40 * v, 1) if v else left, right)
        tiles += [pltpu.roll(beside, NL - z, 1) if z else beside for z in range(8)]
    return tiles


def beside_terms(west, east, at, count):
    return jnp.concatenate(two_terms(jnp.concatenate(beside_tiles(west, east, at, count), 0)), 1)


def own_terms(planes, at, count):
    return jnp.concatenate(two_terms(planes[:, at : at + count, :].reshape(24 * count, NL)), 1)


def main_kernel(
    parts, flat, east, west, own_masks, north_mask, south_mask, wide, narrow,
    kept,
    gain2, low, second, kept2, low_back, gain, sides_wide, turned,
):
    inverse, smooth_own, smooth_beside = narrow.at[0:256], narrow.at[256:512], narrow.at[512:768]
    back, forward2, inverse2 = narrow.at[768:1024], narrow.at[1024:1152], narrow.at[1152:1280]
    lanes = mask_lanes(west, east, own_masks, north_mask, south_mask, wide)
    lane64 = lax.broadcasted_iota(jnp.int32, (1, NL), 1) < 64
    forward2_f = forward2[...].astype(F32)
    for ib in range(4):
        for n in range(4) if ib else (1, 3):
            b = 8 * ib + 4 * (n // 2) + n % 2 - 1
            smooth_two = lanes[b : b + 1, NL:] if n else jnp.ones((1, NL), F32)
            row = jnp.where(lane64, smooth_two, lanes[b + 2 : b + 3, NL:])
            both = dot((forward2_f * row).astype(BF16), inverse2[...]).astype(BF16)
            gain2[ib, n, 0:128, :] = both
            gain2[ib, n, 128:256, :] = both

    for at, count in ((0, 16), (16, 16), (32, 8)):
        part = dot(own_terms(parts.at[0], at, count), smooth_own[...])
        part += dot(beside_terms(west, east, at, count), smooth_beside[...])
        part = part.reshape(24, count, NL)
        if at < 32:
            low[:, 8 + at : 8 + at + count, :] = part
            if at == 0:
                low[:, 56:64, :] = part[:, 0:8]
        else:
            low[:, 0:8, :] = part
            low[:, 40:48, :] = part
            low[:, 48:56, :] = part

    def rows_two(v, _):
        for t in range(3):
            lifted = [
                lift_rows(lambda s: low[v * 8 + p, pl.ds(16 * t + s, 8, stride=2), :], 8) for p in range(8)
            ]
            for bx in range(2):
                smooth, detail = lift_planes([pair[bx] for pair in lifted])
                for bz, part in ((0, smooth), (1, detail)):
                    for z in range(4):
                        second[2 * bz + bx, t, pl.ds(pl.multiple_of((v * 4 + z) * 8, 8), 8), :] = part[z]
        return 0

    lax.fori_loop(0, NV, rows_two, 0)
    for n in range(4):
        for t in range(3):
            terms = jnp.concatenate(two_terms(second[n, t]), 1)
            if t < 2:
                kept2[n, :, 8 + 8 * t : 16 + 8 * t, :] = dot(terms, gain2[t + 1, n]).reshape(NV * 4, 8, NL)
            else:
                if n % 2:
                    kept2[n, :, 0:8, :] = dot(terms, gain2[0, n]).reshape(NV * 4, 8, NL)
                kept2[n, :, 24:32, :] = dot(terms, gain2[3, n]).reshape(NV * 4, 8, NL)

    def back_two(v, _):
        for t in range(3):
            pairs = {}
            for bz in range(2):
                for z in range(4):
                    p = v * 4 + z
                    if t < 2:
                        pairs[bz, z] = unlift_rows(
                            lambda r: kept2[2 * bz, p, pl.ds(r, 8), :],
                            lambda r: kept2[2 * bz + 1, p, pl.ds(r, 8), :],
                            8 + 8 * t,
                        )
                    else:
                        even = kept2[2 * bz, p, 24:32, :] - 0.25 * (
                            kept2[2 * bz + 1, p, 23:31, :] + kept2[2 * bz + 1, p, 24:32, :]
                        )
                        pairs[bz, z] = (even, even)
            for parity in range(2 if t < 2 else 1):
                planes = unlift_planes([pairs[0, z][parity] for z in range(4)], [pairs[1, z][parity] for z in range(4)])
                for z in range(8):
                    low_back[pl.ds((v * 8 + z) * 48 + 16 * t + parity, 8, stride=2), :] = planes[z]
        return 0

    lax.fori_loop(0, NV, back_two, 0)

    forward_f = wide[0:144, :].astype(F32)
    for ib in range(4):
        sides_wide[ib] = jnp.zeros((NL, 4 * NL), F32)
    for ib in range(4):
        for n in range(4) if ib else (1, 3):
            b = 8 * ib + 4 * (n // 2) + n % 2 - 1
            smooth_one = lanes[b : b + 1, 0:NL] if n else jnp.zeros((1, NL), F32)
            row = jnp.concatenate([smooth_one, lanes[b + 2 : b + 3, 0:NL]], 1)
            both = dot((forward_f * row).astype(BF16), inverse[...])
            main = both[0:128].astype(BF16)
            gain[ib, n, 0:128, :] = main
            gain[ib, n, 128:256, :] = main
            for i in range(3):
                at = list(beyond(n).values())[i]
                sides_wide[ib, at : at + 1, n * NL : (n + 1) * NL] = both[128 + i : 129 + i]

    gain_sides = []
    for ib in range(4):
        side = sides_wide[ib].astype(BF16)
        gain_sides.append(jnp.concatenate([side, side], 0))
    def put(n, p, at, rows):
        start = pl.multiple_of((n * 24 + p) * 48 + 8 + at, 8)
        kept[pl.ds(start, rows.shape[0]), :] = rows

    def row_of(ref, first, pitch):
        return ref[pl.ds(first, 24, stride=pitch), :]

    for ib in range(2):
        product = dot(beside_terms(west, east, 16 * ib, 16), gain_sides[ib + 1])
        for n in range(4):
            for p in range(24):
                put(n, p, 16 * ib, product[16 * p : 16 * p + 16, n * NL : (n + 1) * NL])

    def keep(n, _):
        for ib in range(2):
            product = dot(own_terms(parts.at[n], 16 * ib, 16), gain[ib + 1, n])
            for p in range(24):
                start = pl.ds(pl.multiple_of((n * 24 + p) * 48 + 8 + 16 * ib, 8), 16)
                kept[start, :] += product[16 * p : 16 * p + 16]
        return 0

    lax.fori_loop(0, 4, keep, 0)
    for ib in range(2):
        rows = jnp.concatenate([low_back[48 * p + 16 * ib : 48 * p + 16 * ib + 16, :] for p in range(24)], 0)
        product = dot(jnp.concatenate(two_terms(rows), 1), back[...])
        for p in range(24):
            start = 48 * p + 8 + 16 * ib
            kept[start : start + 16, :] += product[16 * p : 16 * p + 16]
    tiles = beside_tiles(west, east, 32, 8)
    for p in range(24):
        turned[8 * p : 8 * p + 8, :] = tiles[p]
    for first, ib, place, row in ((0, 3, 40, 32), (7, 0, 7, 39)):
        beside = dot(jnp.concatenate(two_terms(row_of(turned, first, 8)), 1), gain_sides[ib])
        for n in range(4) if ib else (1, 3):
            own = jnp.concatenate(two_terms(row_of(flat, n * 24 * ROWS + row, ROWS)), 1)
            total = beside[:, n * NL : (n + 1) * NL] + dot(own, gain[ib, n])
            if n == 0:
                total += dot(jnp.concatenate(two_terms(row_of(low_back, row, 48)), 1), back[...])
            kept[pl.ds(n * 24 * 48 + place, 24, stride=48), :] = total


def cells_kernel(kept, out, cells, sems):
    def back_one(step, _):
        v, t = step // 4, step % 4
        pairs = {}
        for bz in range(2):
            for z in range(8):
                p = v * 8 + z
                pairs[bz, z] = unlift_rows(
                    lambda r: kept[2 * bz, p, pl.ds(8 * t + r, 8), :],
                    lambda r: kept[2 * bz + 1, p, pl.ds(8 * t + r, 8), :],
                    8,
                )
        for parity in range(2):
            planes = unlift_planes([pairs[0, z][parity] for z in range(8)], [pairs[1, z][parity] for z in range(8)])
            for z in range(NZ):
                cells[v, z, pl.ds(16 * t + parity, 8, stride=2), :] = planes[z]
        return 0

    def copy(step):
        v, rows = step // 4, pl.ds(pl.multiple_of(16 * (step % 4), 16), 16)
        return pltpu.make_async_copy(cells.at[v, :, rows], out.at[v, :, rows], sems.at[step])

    def one(step, _):
        back_one(step, 0)
        copy(step).start()
        return 0

    lax.fori_loop(0, NV * 4, one, 0)
    for step in range(NV * 4):
        copy(step).wait()


def main_specs():
    vmem = pl.BlockSpec(memory_space=pltpu.VMEM)
    return [
        vmem, vmem, vmem, vmem, vmem,
        pl.BlockSpec((1, 8, NL), lambda i: (9, 0, 0)), pl.BlockSpec((1, 8, NL), lambda i: (15, 0, 0)),
        vmem, vmem,
    ]


def main_step(flat, *operands):
    w = weights()
    return pl.pallas_call(
        main_kernel,
        grid=(1,),
        out_shape=jax.ShapeDtypeStruct((4 * NV * 8 * 48, NL), F32),
        in_specs=main_specs(),
        out_specs=pl.BlockSpec((4 * NV * 8 * 48, NL), lambda i: (0, 0)),
        scratch_shapes=[
            pltpu.VMEM((4, 4, 256, NL), BF16),
            pltpu.VMEM((NV * 8, 64, NL), F32),
            pltpu.VMEM((4, 3, NV * 32, NL), F32),
            pltpu.VMEM((4, NV * 4, 40, NL), F32),
            pltpu.VMEM((NV * 8 * 48, NL), F32),
            pltpu.VMEM((4, 4, 256, NL), BF16),
            pltpu.VMEM((4, NL, 4 * NL), F32),
            pltpu.VMEM((NV * 64, NL), F32),
        ],
        cost_estimate=cost(8),
        compiler_params=pltpu.CompilerParams(vmem_limit_bytes=VMEM_LIMIT),
    )(flat.reshape(4, NV * 8, ROWS, NL), flat, *operands, w["wide"], w["narrow"])


def cells_step(kept):
    shape = (NV, NZ, NR, NL)
    return pl.pallas_call(
        cells_kernel,
        out_shape=jax.ShapeDtypeStruct(shape, F32),
        in_specs=[pl.BlockSpec(memory_space=pltpu.VMEM)],
        out_specs=pl.BlockSpec(memory_space=pltpu.HBM),
        scratch_shapes=[pltpu.VMEM(shape, F32), pltpu.SemaphoreType.DMA((NV * 4,))],
        cost_estimate=cost(4),
        compiler_params=pltpu.CompilerParams(vmem_limit_bytes=VMEM_LIMIT),
    )(kept)


def rows_kernel(count_x, count_z, *refs):
    shares, out = refs[count_x - 1 :: -1], refs[count_x + 1]
    me, me_y = lax.axis_index("gx"), lax.axis_index("gy")
    row = lax.broadcasted_iota(jnp.int32, (8, NL), 0)
    lane = lax.broadcasted_iota(jnp.int32, (8, NL), 1)
    for r in range(count_x):
        at = pl.multiple_of(16 * (me ^ r), 16)
        for j in range(count_z):
            for z in range(4):
                start = 64 * j + 16 * z
                out[j, z, pl.ds(at, 16), :] = shares[r][start : start + 16, :]
    for j in range(count_z):
        turn = lanes_turn(me_y ^ (2 * j))
        piece = lax.rem(lane + (NL - turn), NL) // 21
        inside = [piece == p for p in range(5)]
        for r in range(count_x):
            i = me ^ r
            below = pl.multiple_of(16 * lax.rem(i + 1, count_x), 16)
            above = pl.multiple_of(16 * lax.rem(i + count_x - 1, count_x) + 8, 8)
            tiles = [shares[r][64 * j + 8 * g : 64 * j + 8 * g + 8, :] for g in range(8)]
            low, high = jnp.zeros((8, NL), F32), jnp.zeros((8, NL), F32)
            for p in range(5):
                back = (21 * p - 105) % NL
                low = jnp.where(inside[p], pltpu.roll(tiles[p], back, 1), low)
                extra = tiles[5 + p // 2]
                extra = extra if p % 2 else pltpu.roll(extra, 4, 0)
                high = jnp.where(inside[p], pltpu.roll(extra, back, 1), high)
            for z in range(4):
                first = pltpu.roll(low, 8 - 2 * z, 0) if z else low
                last = pltpu.roll(high, z, 0) if z else high
                out[j, z, pl.ds(below, 8), :] += jnp.where(row < 2, first, 0.0)
                out[j, z, pl.ds(above, 8), :] += jnp.where(row == 7, last, 0.0)


def rows_step(pieces, count_z, after):
    vmem = pl.BlockSpec(memory_space=pltpu.VMEM)
    count_x = len(pieces)
    return pl.pallas_call(
        functools.partial(rows_kernel, count_x, count_z),
        out_shape=jax.ShapeDtypeStruct((count_z, 4, 16 * count_x, NL), F32),
        in_specs=[vmem] * count_x + [pl.BlockSpec(memory_space=pl.ANY)],
        out_specs=vmem,
        compiler_params=pltpu.CompilerParams(vmem_limit_bytes=VMEM_LIMIT),
    )(*pieces[::-1], after)


def coarse_kernel(count_x, count_y, own, other, out_hbm, out, sems):
    me = lax.axis_index("gy")
    me_z, is_even = lax.shift_right_logical(me, 1), lax.rem(me, 2) == 0
    lane = lax.broadcasted_iota(jnp.int32, (8, NL), 1)
    place = [lax.rem(lane + NL - 35 * v, NL) for v in range(NV)]

    def block(i, _):
        rows = pl.ds(pl.multiple_of(8 * i, 8), 8)
        for z in range(4):
            pieces = []
            for j in range(count_y // 2):
                mine, theirs = own[j ^ me_z, z, rows, :], other[j ^ me_z, z, rows, :]
                pieces += [jnp.where(is_even, mine, theirs), jnp.where(is_even, theirs, mine)]
            for v in range(NV):
                at = place[v]
                for t in range(count_y // 4):
                    total = jnp.where(at < 2, pieces[4 * t - 1], 0.0)
                    total += jnp.where(at == NL - 1, pieces[(4 * t + 4) % count_y], 0.0)
                    for q in range(4):
                        inside = (at >= 32 * q - 1) & (at < 32 * q + 34)
                        total += jnp.where(inside, pieces[4 * t + q], 0.0)
                    out[v, z, rows, NL * t : NL * (t + 1)] = pltpu.roll(total, NL - 35 * v, 1) if v else total
        return 0

    def copy(i):
        rows = pl.ds(pl.multiple_of(16 * i, 16), 16)
        return pltpu.make_async_copy(out.at[:, :, rows], out_hbm.at[:, :, rows], sems.at[i])

    def pair(i, _):
        block(2 * i, 0)
        block(2 * i + 1, 0)
        copy(i).start()
        return 0

    lax.fori_loop(0, count_x, pair, 0)
    for i in range(count_x):
        copy(i).wait()


def coarse_step(own, other, count_x, count_y):
    vmem = pl.BlockSpec(memory_space=pltpu.VMEM)
    shape = (NV, 4, 16 * count_x, 32 * count_y)
    return pl.pallas_call(
        functools.partial(coarse_kernel, count_x, count_y),
        out_shape=jax.ShapeDtypeStruct(shape, F32),
        in_specs=[vmem, vmem],
        out_specs=pl.BlockSpec(memory_space=pltpu.HBM),
        scratch_shapes=[pltpu.VMEM(shape, F32), pltpu.SemaphoreType.DMA((count_x,))],
        compiler_params=pltpu.CompilerParams(vmem_limit_bytes=VMEM_LIMIT),
    )(own, other)


def shifted(x, axis, step):
    count = lax.axis_size(axis)
    return lax.ppermute(x, axis, [(i, (i + step) % count) for i in range(count)])


def swapped(x, axis, distance):
    return lax.ppermute(x, axis, [(i, i ^ distance) for i in range(lax.axis_size(axis))])


def body(field, masks):
    count_x, count_y = lax.axis_size("gx"), lax.axis_size("gy")
    lifted, up, down, own_masks, share = first_step(field, masks)
    south = shifted(up, "gx", -1)
    north = shifted(down, "gx", 1)
    shares = [share] + [swapped(share, "gy", r) for r in range(2, count_y, 2)]
    parts, to_left, to_right = edge_step(lift_step(lifted), lifted, north, south, own_masks)
    east = shifted(to_left, "gy", -1)
    west = shifted(to_right, "gy", 1)
    joined = join_step(shares, to_left)
    pieces = [joined] + [swapped(joined, "gx", r) for r in range(1, count_x)]
    kept = main_step(parts, east, west, own_masks, north, south)
    own = rows_step(pieces, count_y // 2, kept)
    other = swapped(own, "gy", 1)
    return cells_step(kept.reshape(4, NV * 8, 48, NL)), coarse_step(own, other, count_x, count_y)


def solution(mesh):
    placed = P(None, None, "gx", "gy")
    return jax.shard_map(
        body,
        mesh=mesh,
        in_specs=(placed, placed),
        out_specs=(placed, P()),
        check_vma=False,
    )
```

```python
import functools

import jax
import jax.numpy as jnp
import ml_dtypes
import numpy as np
from jax import lax
from jax.experimental import pallas as pl
from jax.experimental.pallas import tpu as pltpu
from jax.sharding import PartitionSpec as P

F32 = jnp.float32
BF16 = jnp.bfloat16
VMEM_LIMIT = 32 * 1024 * 1024

NV, NZ, NR, NL = 3, 16, 64, 128


def detail_row(k):
    return {2 * k + 1: 1.0, 2 * k: -0.5, 2 * k + 2: -0.5}


def smooth_row(k):
    row = {2 * k: 1.0}
    for j in (k - 1, k):
        for cell, value in detail_row(j).items():
            row[cell] = row.get(cell, 0.0) + 0.25 * value
    return row


def even_row(k):
    return {("s", k): 1.0, ("d", k - 1): -0.25, ("d", k): -0.25}


def odd_row(k):
    row = {("d", k): 1.0}
    for j in (k, k + 1):
        for name, value in even_row(j).items():
            row[name] = row.get(name, 0.0) + 0.5 * value
    return row


def as_bf16(matrix):
    cast = matrix.astype(ml_dtypes.bfloat16)
    assert (cast.astype(np.float64) == matrix).all()
    return cast


def combine(*terms):
    total = {}
    for factor, row in terms:
        for cell, value in row.items():
            total[cell] = total.get(cell, 0.0) + factor * value
    return total


def level_one_columns():
    names = {("s", k): k for k in range(65)}
    names.update({("d", k): 128 + k for k in range(65)})
    names[("d", -1)] = 128 + 65
    return names


def level_two_columns():
    names = {("s", k): k for k in range(33)}
    names.update({("d", k): 64 + k for k in range(33)})
    names[("d", -1)] = 64 + 33
    return names


def smooth_place(k):
    return k + 2


def beyond(n):
    return {"cell": 40 + 16 * n, "after": 48 + 16 * n, "before": 8 * n}


BEYOND_SMOOTH = {65: 104, -1: 32}
FROM_WEST = 40


def own_row(kind, k, n):
    place = {name: 128 + lane for name, lane in beyond(n).items()}
    if kind == "d":
        if k == -1:
            return {place["before"]: 1.0, 0: -0.5}
        if k == 64:
            return {place["after"]: 1.0}
        return {(place["cell"] if y == 128 else y): value for y, value in detail_row(k).items()}
    if k in (-2, 66):
        return {}
    if k in BEYOND_SMOOTH:
        row = {128 + BEYOND_SMOOTH[k]: 1.0}
        return combine((1.0, row), (1.0, {0: -0.125})) if k == -1 else row
    even = place["cell"] if k == 64 else 2 * k
    return combine((1.0, {even: 1.0}), (0.25, own_row("d", k - 1, n)), (0.25, own_row("d", k, n)))


@functools.lru_cache(maxsize=None)
def weights():
    w = {}
    names = level_one_columns()
    forward = np.zeros((4, 256, 256))
    inverse = np.zeros((256, 128))
    for (kind, k), column in names.items():
        for n in range(4):
            for place, value in own_row(kind, k, n).items():
                forward[n, place, column] += value
    for k in range(64):
        for y, row in ((2 * k, even_row(k)), (2 * k + 1, odd_row(k))):
            for name, value in row.items():
                inverse[names[name], y] += value
    short = np.zeros((144, 256))
    short[:128] = forward[0, :128]
    for i, lane in enumerate(beyond(0).values()):
        short[128 + i] = forward[0, 128 + lane]
    smooth = np.zeros((256, 128))
    for k in range(-2, 67):
        for place, value in own_row("s", k, 0).items():
            smooth[place, smooth_place(k)] += value
    names2 = level_two_columns()
    forward2 = np.zeros((128, 128))
    inverse2 = np.zeros((128, 128))
    for (kind, k), column in names2.items():
        for cell, value in (smooth_row(k) if kind == "s" else detail_row(k)).items():
            forward2[smooth_place(cell), column] += value
    for k in range(33):
        rows = [(2 * k, even_row(k))] + ([(2 * k + 1, odd_row(k))] if k < 32 else [])
        for y, row in rows:
            for name, value in row.items():
                inverse2[names2[name], y] += value
    back = np.zeros((256, 128))
    back[:65] = inverse[:65]
    back[128 : 128 + 65] = inverse[:65]
    spread = np.zeros((3, 128, 2, 128))
    for k in range(64):
        spread[0, k, 0, k] = 1
    for k in range(32):
        spread[0, 64 + k, 1, k] = 1
        spread[0, 64 + k, 1, 64 + k] = 1
    for at in range(0, 16, 4):
        spread[1, at, 0, 64] = 1
        spread[2, at + 1, 0, 65] = 1
        for base in (0, 64):
            spread[1, at + 2, 1, base + 32] = 1
            spread[2, at + 3, 1, base + 33] = 1
    w["wide"] = np.concatenate([short, spread.reshape(384, 256)], 0)
    own, beside = smooth[:128], smooth[128:]
    w["narrow"] = np.concatenate([inverse, own, own, beside, beside, back, forward2, inverse2], 0)
    edge = np.zeros((4, 128, 128))

    def put(n, lane, row):
        for z in range(8):
            for y, value in row.items():
                j = y - 120 if y >= 120 else y + 8
                edge[n, 16 * z + j, lane + z] += value

    part = {127: 1.0, 126: -0.5}
    for n in range(4):
        put(n, beyond(n)["cell"], {0: 1.0})
        put(n, beyond(n)["after"], detail_row(0))
        put(n, beyond(n)["before"], part)
    put(0, BEYOND_SMOOTH[65], combine((1.0, smooth_row(1)), (-0.5, smooth_row(2))))
    share = combine((1.0, {126: 1.0}), (0.25, detail_row(62)), (0.25, part))
    put(0, BEYOND_SMOOTH[-1], combine((1.0, share), (-0.5, smooth_row(62))))
    w["edge"] = edge.reshape(512, 128)
    expand = np.zeros((2, 4, 128))
    for j in range(4):
        expand[0, j, 16 * j : 16 * j + 16] = 1
        expand[1, j, 64 + 8 * j : 64 + 8 * j + 8] = 1
    twice = combine(*[(value, smooth_row(k)) for k, value in smooth_row(0).items()])
    columns = np.zeros((2, 128, 128))
    for m in range(-1, 34):
        for t, value in twice.items():
            if 0 <= 4 * m + t < NL:
                columns[:, 4 * m + t, m + 1] = value
    rows = np.zeros((4, 32, 2, 64))
    for z in range(4):
        places = {m: m for m in range(16)}
        places.update({16: 16 + 2 * z, 17: 17 + 2 * z, -1: 16 + 15 - z})
        for m, place in places.items():
            for t, value in twice.items():
                if 0 <= 4 * m + t < NR:
                    rows[z, place, :, 4 * m + t] = value
    pad = np.zeros((8, 128))
    w["first"] = np.concatenate([columns.reshape(256, 128), rows.reshape(128, 128), expand.reshape(8, 128), pad], 0)
    return {name: as_bf16(matrix) for name, matrix in w.items()}


def two_terms(x):
    high = x.astype(BF16)
    low = (x - high.astype(F32)).astype(BF16)
    return high, low


def cost(gigaflops):
    return pl.CostEstimate(flops=gigaflops * 10**9, bytes_accessed=8 * 10**6, transcendentals=0)


def dot(a, b):
    return jnp.dot(a, b, preferred_element_type=F32)


def lift_planes(cells):
    half = len(cells) // 2
    even, odd = cells[0::2], cells[1::2]
    detail = [odd[k] - 0.5 * (even[k] + even[min(k + 1, half - 1)]) for k in range(half)]
    smooth = [even[k] + 0.25 * (detail[max(k - 1, 0)] + detail[k]) for k in range(half)]
    return smooth, detail


def unlift_planes(smooth, detail):
    half = len(smooth)
    even = [smooth[k] - 0.25 * (detail[max(k - 1, 0)] + detail[k]) for k in range(half)]
    out = []
    for k in range(half):
        out += [even[k], detail[k] + 0.5 * (even[k] + even[min(k + 1, half - 1)])]
    return out


def lift_rows(load, start):
    even, odd, after = load(start), load(start + 1), load(start + 2)
    before, odd_before = load(start - 2), load(start - 1)
    detail = odd - 0.5 * (even + after)
    detail_before = odd_before - 0.5 * (before + even)
    return even + 0.25 * (detail_before + detail), detail


def unlift_rows(smooth, detail, row):
    here, after = detail(row), detail(row + 1)
    even = smooth(row) - 0.25 * (detail(row - 1) + here)
    next_even = smooth(row + 1) - 0.25 * (here + after)
    return even, here + 0.5 * (even + next_even)


PITCH = 80


def lanes_turn(j):
    return lax.rem(32 * lax.rem(j, 4) + NL - 1, NL)


def first_kernel(
    field, masks_hbm, table_hbm, lifted, up, down, own_masks, share, cells, twice, masks, table, sems
):
    small = [
        pltpu.make_async_copy(masks_hbm, masks, sems.at[0]),
        pltpu.make_async_copy(table_hbm, table, sems.at[1]),
    ]
    copies = []
    for v in range(NV):
        for c in range(4):
            part = pl.ds(16 * c, 16)
            copies.append(pltpu.make_async_copy(field.at[v, :, part], cells.at[v, :, part], sems.at[2 + 4 * v + c]))
    for copy in small + copies:
        copy.start()
    for p in range(NV * NZ):
        lifted[p * PITCH : p * PITCH + 8, :] = jnp.zeros((8, NL), F32)
        lifted[p * PITCH + 72 : p * PITCH + 80, :] = jnp.zeros((8, NL), F32)
    for copy in small:
        copy.wait()
    for i, out, tile in ((0, up, 15), (1, down, 9)):
        total = jnp.zeros((7, NL), F32)
        for l in range(2):
            flags = masks[l, i].astype(F32).astype(BF16)
            spread = table[384 + 4 * l : 388 + 4 * l, :]
            total += lax.dot_general(flags, spread, (((0,), (0,)), ((), ())), preferred_element_type=F32)
        own_masks[i] = jnp.concatenate([total, jnp.zeros((1, NL), F32)], 0)
        out[tile] = own_masks[i]

    for v in range(NV):
        for t in range(8):
            if t % 2 == 0:
                copies[4 * v + t // 2].wait()
            smooth, detail = lift_planes([cells[v, z, 8 * t : 8 * t + 8, :] for z in range(NZ)])
            for k, tile in enumerate(smooth + detail):
                start = (v * NZ + k) * PITCH + 8 + 8 * t
                lifted[start : start + 8, :] = tile
            for k, tile in enumerate(lift_planes(smooth)[0]):
                twice[v * 4 + k, 8 * t : 8 * t + 8, :] = tile
        for bz in range(2):

            def row(x):
                return lifted[pl.ds((v * NZ + bz * 8) * PITCH + 8 + x, 8, stride=PITCH), :]

            x = [row(j) for j in range(7 if bz == 0 else 3)]
            first = x[1] - 0.5 * (x[0] + x[2])
            up[v * 5 + bz] = x[0]
            up[v * 5 + 2 + bz] = first
            y = {j: row(j) for j in (range(58, 64) if bz == 0 else (62, 63))}
            part = y[63] - 0.5 * y[62]
            down[v * 3 + bz] = part
            if bz == 0:
                second = x[3] - 0.5 * (x[2] + x[4])
                third = x[5] - 0.5 * (x[4] + x[6])
                up[v * 5 + 4] = x[2] + 0.25 * (first + second) - 0.5 * (x[4] + 0.25 * (second + third))
                before = y[59] - 0.5 * (y[58] + y[60])
                last = y[61] - 0.5 * (y[60] + y[62])
                down[v * 3 + 2] = y[62] + 0.25 * (last + part) - 0.5 * (y[60] + 0.25 * (before + last))

    total = jnp.zeros((80, NL), F32)
    for v in range(NV):
        main, extra = [], jnp.zeros((16, NL), F32)
        for z in range(4):
            terms = jnp.concatenate(two_terms(twice[v * 4 + z]), 0)
            part = dot(table[256 + 32 * z : 288 + 32 * z, :], terms)
            main.append(part[:16])
            extra += part[16:]
        terms = jnp.concatenate(two_terms(jnp.concatenate(main + [extra], 0)), 1)
        part = dot(terms, table[0:256, :])
        total += pltpu.roll(part, 35 * v, 1) if v else part
    turn = lanes_turn(lax.axis_index("gy"))
    lane = lax.broadcasted_iota(jnp.int32, (8, NL), 1)
    spare = (lane >= 105) & (lane < 126)
    upper = lax.broadcasted_iota(jnp.int32, (8, NL), 0) < 4
    below, above = total[64:72], total[72:80]
    pieces = [pltpu.roll(above, 105 - 21 * p, 1) for p in range(5)]
    for g in range(8):
        if g < 5:
            extra = pltpu.roll(below, 105 - 21 * g, 1)
        else:
            extra = pltpu.roll(pieces[2 * g - 10], 4, 0)
            extra = jnp.where(upper, extra, pieces[2 * g - 9] if g < 7 else 0.0)
        tile = jnp.where(spare, extra, total[8 * g : 8 * g + 8])
        share[8 * g : 8 * g + 8, :] = pltpu.roll(tile, turn, 1)


def in_hbm(x):
    return pltpu.with_memory_space_constraint(x, pltpu.HBM)


def first_step(field, masks):
    vmem = pl.BlockSpec(memory_space=pltpu.VMEM)
    shapes = [(NV * NZ * PITCH, NL), (16, 8, NL), (10, 8, NL), (2, 8, NL), (64, NL)]
    return pl.pallas_call(
        first_kernel,
        out_shape=[jax.ShapeDtypeStruct(s, F32) for s in shapes],
        in_specs=[pl.BlockSpec(memory_space=pltpu.HBM)] * 3,
        out_specs=[vmem] * 5,
        scratch_shapes=[
            pltpu.VMEM((NV, NZ, NR, NL), F32),
            pltpu.VMEM((NV * 4, NR, NL), F32),
            pltpu.VMEM((2, 2, 4, 7), jnp.int32),
            pltpu.VMEM((400, NL), BF16),
            pltpu.SemaphoreType.DMA((4 * NV + 2,)),
        ],
        compiler_params=pltpu.CompilerParams(vmem_limit_bytes=VMEM_LIMIT),
    )(*[in_hbm(x) for x in (field, masks.transpose(0, 2, 3, 1), jnp.asarray(weights()["first"]))])


ROWS = 40


def lift_kernel(lifted, parts):
    def lift(step, _):
        v, bz = step // 2, lax.rem(step, 2)
        for z in range(8):
            start = pl.multiple_of((step * 8 + z) * PITCH, 8)
            for t in range(4):
                pair = lift_rows(lambda s: lifted[pl.ds(start + 16 * t + s, 8, stride=2), :], 8)
                for bx in range(2):
                    plane = (2 * bz + bx) * 24 + v * 8 + z
                    parts[pl.ds(pl.multiple_of(plane * ROWS + 8 * t, 8), 8), :] = pair[bx]
        return 0

    lax.fori_loop(0, NV * 2, lift, 0)


def lift_step(lifted):
    vmem = pl.BlockSpec(memory_space=pltpu.VMEM)
    return pl.pallas_call(
        lift_kernel,
        out_shape=jax.ShapeDtypeStruct((4 * NV * 8 * ROWS, NL), F32),
        in_specs=[vmem],
        out_specs=vmem,
        compiler_params=pltpu.CompilerParams(vmem_limit_bytes=VMEM_LIMIT),
    )(lifted)


def edge_kernel(parts_in, lifted, north, south, own_masks, table_hbm, parts, to_left, to_right, packed, table, sem):
    copy = pltpu.make_async_copy(table_hbm, table, sem.at[0])
    copy.start()
    for p in range(4 * NV * 8):
        parts[p * ROWS + 32 : p * ROWS + 40, :] = jnp.zeros((8, NL), F32)
    for v in range(NV):
        for bz in range(2):

            def cell(x):
                return lifted[pl.ds((v * NZ + bz * 8) * PITCH + 8 + x, 8, stride=PITCH), :]

            def at(bx, r):
                return pl.ds(((2 * bz + bx) * 24 + v * 8) * ROWS + r, 8, stride=ROWS)

            before, after, detail = north[v * 3 + bz], south[v * 5 + bz], south[v * 5 + 2 + bz]
            start = cell(0)
            last = cell(63) - 0.5 * (cell(62) + after)
            parts[at(0, 0), :] = parts[at(0, 0), :] + 0.25 * before
            parts[at(0, 31), :] = parts[at(0, 31), :] - 0.125 * after
            parts[at(1, 31), :] = parts[at(1, 31), :] - 0.5 * after
            parts[at(0, 32), :] = after + 0.25 * (last + detail)
            parts[at(1, 32), :] = detail
            parts[at(1, 39), :] = before - 0.5 * start
            if bz == 0:
                parts[at(0, 33), :] = south[v * 5 + 4]
                parts[at(0, 39), :] = north[v * 3 + 2] - 0.125 * start

    lane = lax.broadcasted_iota(jnp.int32, (8, NL), 1) // 16

    def pack(v, _):
        for n in range(4):
            for t in range(5):
                tile = jnp.zeros((8, NL), F32)
                for z in range(8):
                    start = (n * 24 + v * 8 + z) * ROWS + 8 * t
                    x = parts[pl.ds(pl.multiple_of(start, 8), 8), :]
                    tile = jnp.where(lane == z, pltpu.roll(x, (8 + 16 * z) % NL, 1), tile)
                packed[pl.ds(pl.multiple_of(n * 120 + v * ROWS + 8 * t, 8), 8), :] = tile
        return 0

    lax.fori_loop(0, NV, pack, 0)
    copy.wait()
    terms = [two_terms(packed[n * 120 : (n + 1) * 120, :]) for n in range(4)]
    high, low = [jnp.concatenate(part, 1) for part in zip(*terms)]
    sides = dot(high, table[...]) + dot(low, table[...])
    lane = lax.broadcasted_iota(jnp.int32, (ROWS, NL), 1)
    each = [sides[v * ROWS : (v + 1) * ROWS] for v in range(NV)]
    right = jnp.where(lane < 40, each[0], pltpu.roll(each[1], 40, 1))
    to_right[0:ROWS, :] = jnp.where(lane < 80, right, pltpu.roll(each[2], 80, 1))
    last = jnp.where(lane < 32, pltpu.roll(each[2], NL - 40, 1), pltpu.roll(each[2], NL - 72, 1))
    to_left[0:ROWS, :] = jnp.where(lane < 40, last, each[0])
    to_left[ROWS : 2 * ROWS, :] = jnp.where(lane < 32, pltpu.roll(each[2], NL - 72, 1), each[1])
    lane = lax.broadcasted_iota(jnp.int32, (8, NL), 1)
    ends = jnp.zeros((8, NL), F32)
    for ib, tile in enumerate((north[9], own_masks[0], own_masks[1], south[15])):
        for j, source in enumerate((0, 63, 64, 95)):
            target = 4 * ib + j
            ends = jnp.where(lane == target, pltpu.roll(tile, (target - source) % NL, 1), ends)
    to_left[2 * ROWS : 2 * ROWS + 8, :] = ends
    to_right[ROWS : ROWS + 8, :] = ends


def edge_step(parts, lifted, north, south, own_masks):
    vmem = pl.BlockSpec(memory_space=pltpu.VMEM)
    shapes = [(4 * NV * 8 * ROWS, NL), (2 * ROWS + 8, NL), (ROWS + 8, NL)]
    return pl.pallas_call(
        edge_kernel,
        out_shape=[jax.ShapeDtypeStruct(s, F32) for s in shapes],
        in_specs=[vmem] * 5 + [pl.BlockSpec(memory_space=pltpu.HBM)],
        out_specs=[vmem] * 3,
        input_output_aliases={0: 0},
        cost_estimate=cost(20),
        scratch_shapes=[pltpu.VMEM((480, NL), F32), pltpu.VMEM((512, NL), BF16), pltpu.SemaphoreType.DMA((1,))],
        compiler_params=pltpu.CompilerParams(vmem_limit_bytes=VMEM_LIMIT),
    )(parts, lifted, north, south, own_masks, in_hbm(jnp.asarray(weights()["edge"])))


def join_kernel(*refs):
    shares, out = refs[-3::-1], refs[-1]
    for n, piece in enumerate(shares):
        out[64 * n : 64 * (n + 1), :] = piece[...]


def join_step(shares, after):
    vmem = pl.BlockSpec(memory_space=pltpu.VMEM)
    return pl.pallas_call(
        join_kernel,
        out_shape=jax.ShapeDtypeStruct((64 * len(shares), NL), F32),
        in_specs=[vmem] * len(shares) + [pl.BlockSpec(memory_space=pl.ANY)],
        out_specs=vmem,
        cost_estimate=cost(20),
        compiler_params=pltpu.CompilerParams(vmem_limit_bytes=VMEM_LIMIT),
    )(*shares[::-1], after)


def mask_lanes(west, east, own_masks, north_mask, south_mask, wide):
    group = lax.broadcasted_iota(jnp.int32, (8, NL), 1) // 4
    masks = [
        jnp.concatenate([jnp.where(group == ib, tile, 0.0) for ib in range(4)], 0)
        for tile in (east[2 * ROWS : 2 * ROWS + 8, :], west[ROWS : ROWS + 8, :])
    ]
    own = jnp.concatenate([north_mask[0], own_masks[0], own_masks[1], south_mask[0]], 0)
    flags = jnp.concatenate([own] + masks, 1).astype(BF16)
    return dot(flags, wide[144:528, :])


def beside_tiles(west, east, at, count):
    lane = lax.broadcasted_iota(jnp.int32, (count, NL), 1)
    left = west[at : at + count, :]
    first, second = east[at : at + count, :], east[ROWS + at : ROWS + at + count, :]
    third = jnp.where(lane < 104, pltpu.roll(second, 72, 1), pltpu.roll(first, 72, 1))
    third = jnp.where(lane < 72, pltpu.roll(first, 40, 1), third)
    tiles = []
    for v, right in enumerate((first, second, third)):
        beside = jnp.where(lane < FROM_WEST, pltpu.roll(left, NL - 40 * v, 1) if v else left, right)
        tiles += [pltpu.roll(beside, NL - z, 1) if z else beside for z in range(8)]
    return tiles


def beside_terms(west, east, at, count):
    return jnp.concatenate(two_terms(jnp.concatenate(beside_tiles(west, east, at, count), 0)), 1)


def own_terms(planes, at, count):
    return jnp.concatenate(two_terms(planes[:, at : at + count, :].reshape(24 * count, NL)), 1)


def main_kernel(
    parts, flat, east, west, own_masks, north_mask, south_mask, wide, narrow,
    kept,
    gain2, low, second, kept2, low_back, gain, sides_wide, turned,
):
    inverse, smooth_own, smooth_beside = narrow.at[0:256], narrow.at[256:512], narrow.at[512:768]
    back, forward2, inverse2 = narrow.at[768:1024], narrow.at[1024:1152], narrow.at[1152:1280]
    lanes = mask_lanes(west, east, own_masks, north_mask, south_mask, wide)
    lane64 = lax.broadcasted_iota(jnp.int32, (1, NL), 1) < 64
    forward2_f = forward2[...].astype(F32)
    for ib in range(4):
        for n in range(4) if ib else (1, 3):
            b = 8 * ib + 4 * (n // 2) + n % 2 - 1
            smooth_two = lanes[b : b + 1, NL:] if n else jnp.ones((1, NL), F32)
            row = jnp.where(lane64, smooth_two, lanes[b + 2 : b + 3, NL:])
            both = dot((forward2_f * row).astype(BF16), inverse2[...]).astype(BF16)
            gain2[ib, n, 0:128, :] = both
            gain2[ib, n, 128:256, :] = both

    for at, count in ((0, 16), (16, 16), (32, 8)):
        part = dot(own_terms(parts.at[0], at, count), smooth_own[...])
        part += dot(beside_terms(west, east, at, count), smooth_beside[...])
        part = part.reshape(24, count, NL)
        if at < 32:
            low[:, 8 + at : 8 + at + count, :] = part
            if at == 0:
                low[:, 56:64, :] = part[:, 0:8]
        else:
            low[:, 0:8, :] = part
            low[:, 40:48, :] = part
            low[:, 48:56, :] = part

    def rows_two(v, _):
        for t in range(3):
            lifted = [
                lift_rows(lambda s: low[v * 8 + p, pl.ds(16 * t + s, 8, stride=2), :], 8) for p in range(8)
            ]
            for bx in range(2):
                smooth, detail = lift_planes([pair[bx] for pair in lifted])
                for bz, part in ((0, smooth), (1, detail)):
                    for z in range(4):
                        second[2 * bz + bx, t, pl.ds(pl.multiple_of((v * 4 + z) * 8, 8), 8), :] = part[z]
        return 0

    lax.fori_loop(0, NV, rows_two, 0)
    for n in range(4):
        for t in range(3):
            terms = jnp.concatenate(two_terms(second[n, t]), 1)
            if t < 2:
                kept2[n, :, 8 + 8 * t : 16 + 8 * t, :] = dot(terms, gain2[t + 1, n]).reshape(NV * 4, 8, NL)
            else:
                if n % 2:
                    kept2[n, :, 0:8, :] = dot(terms, gain2[0, n]).reshape(NV * 4, 8, NL)
                kept2[n, :, 24:32, :] = dot(terms, gain2[3, n]).reshape(NV * 4, 8, NL)

    def back_two(v, _):
        for t in range(3):
            pairs = {}
            for bz in range(2):
                for z in range(4):
                    p = v * 4 + z
                    if t < 2:
                        pairs[bz, z] = unlift_rows(
                            lambda r: kept2[2 * bz, p, pl.ds(r, 8), :],
                            lambda r: kept2[2 * bz + 1, p, pl.ds(r, 8), :],
                            8 + 8 * t,
                        )
                    else:
                        even = kept2[2 * bz, p, 24:32, :] - 0.25 * (
                            kept2[2 * bz + 1, p, 23:31, :] + kept2[2 * bz + 1, p, 24:32, :]
                        )
                        pairs[bz, z] = (even, even)
            for parity in range(2 if t < 2 else 1):
                planes = unlift_planes([pairs[0, z][parity] for z in range(4)], [pairs[1, z][parity] for z in range(4)])
                for z in range(8):
                    low_back[pl.ds((v * 8 + z) * 48 + 16 * t + parity, 8, stride=2), :] = planes[z]
        return 0

    lax.fori_loop(0, NV, back_two, 0)

    forward_f = wide[0:144, :].astype(F32)
    for ib in range(4):
        sides_wide[ib] = jnp.zeros((NL, 4 * NL), F32)
    for ib in range(4):
        for n in range(4) if ib else (1, 3):
            b = 8 * ib + 4 * (n // 2) + n % 2 - 1
            smooth_one = lanes[b : b + 1, 0:NL] if n else jnp.zeros((1, NL), F32)
            row = jnp.concatenate([smooth_one, lanes[b + 2 : b + 3, 0:NL]], 1)
            both = dot((forward_f * row).astype(BF16), inverse[...])
            main = both[0:128].astype(BF16)
            gain[ib, n, 0:128, :] = main
            gain[ib, n, 128:256, :] = main
            for i in range(3):
                at = list(beyond(n).values())[i]
                sides_wide[ib, at : at + 1, n * NL : (n + 1) * NL] = both[128 + i : 129 + i]

    gain_sides = []
    for ib in range(4):
        side = sides_wide[ib].astype(BF16)
        gain_sides.append(jnp.concatenate([side, side], 0))
    def put(n, p, at, rows):
        start = pl.multiple_of((n * 24 + p) * 48 + 8 + at, 8)
        kept[pl.ds(start, rows.shape[0]), :] = rows

    def row_of(ref, first, pitch):
        return ref[pl.ds(first, 24, stride=pitch), :]

    for ib in range(2):
        product = dot(beside_terms(west, east, 16 * ib, 16), gain_sides[ib + 1])
        for n in range(4):
            for p in range(24):
                put(n, p, 16 * ib, product[16 * p : 16 * p + 16, n * NL : (n + 1) * NL])

    def keep(n, _):
        for ib in range(2):
            product = dot(own_terms(parts.at[n], 16 * ib, 16), gain[ib + 1, n])
            for p in range(24):
                start = pl.ds(pl.multiple_of((n * 24 + p) * 48 + 8 + 16 * ib, 8), 16)
                kept[start, :] += product[16 * p : 16 * p + 16]
        return 0

    lax.fori_loop(0, 4, keep, 0)
    for ib in range(2):
        rows = jnp.concatenate([low_back[48 * p + 16 * ib : 48 * p + 16 * ib + 16, :] for p in range(24)], 0)
        product = dot(jnp.concatenate(two_terms(rows), 1), back[...])
        for p in range(24):
            start = 48 * p + 8 + 16 * ib
            kept[start : start + 16, :] += product[16 * p : 16 * p + 16]
    tiles = beside_tiles(west, east, 32, 8)
    for p in range(24):
        turned[8 * p : 8 * p + 8, :] = tiles[p]
    for first, ib, place, row in ((0, 3, 40, 32), (7, 0, 7, 39)):
        beside = dot(jnp.concatenate(two_terms(row_of(turned, first, 8)), 1), gain_sides[ib])
        for n in range(4) if ib else (1, 3):
            own = jnp.concatenate(two_terms(row_of(flat, n * 24 * ROWS + row, ROWS)), 1)
            total = beside[:, n * NL : (n + 1) * NL] + dot(own, gain[ib, n])
            if n == 0:
                total += dot(jnp.concatenate(two_terms(row_of(low_back, row, 48)), 1), back[...])
            kept[pl.ds(n * 24 * 48 + place, 24, stride=48), :] = total


def cells_kernel(kept, out, cells, sems):
    def back_one(step, _):
        v, t = step // 4, step % 4
        pairs = {}
        for bz in range(2):
            for z in range(8):
                p = v * 8 + z
                pairs[bz, z] = unlift_rows(
                    lambda r: kept[2 * bz, p, pl.ds(8 * t + r, 8), :],
                    lambda r: kept[2 * bz + 1, p, pl.ds(8 * t + r, 8), :],
                    8,
                )
        for parity in range(2):
            planes = unlift_planes([pairs[0, z][parity] for z in range(8)], [pairs[1, z][parity] for z in range(8)])
            for z in range(NZ):
                cells[v, z, pl.ds(16 * t + parity, 8, stride=2), :] = planes[z]
        return 0

    def copy(step):
        v, rows = step // 4, pl.ds(pl.multiple_of(16 * (step % 4), 16), 16)
        return pltpu.make_async_copy(cells.at[v, :, rows], out.at[v, :, rows], sems.at[step])

    def one(step, _):
        back_one(step, 0)
        copy(step).start()
        return 0

    lax.fori_loop(0, NV * 4, one, 0)
    for step in range(NV * 4):
        copy(step).wait()


def main_specs():
    vmem = pl.BlockSpec(memory_space=pltpu.VMEM)
    return [
        vmem, vmem, vmem, vmem, vmem,
        pl.BlockSpec((1, 8, NL), lambda i: (9, 0, 0)), pl.BlockSpec((1, 8, NL), lambda i: (15, 0, 0)),
        vmem, vmem,
    ]


def main_step(flat, *operands):
    w = weights()
    return pl.pallas_call(
        main_kernel,
        grid=(1,),
        out_shape=jax.ShapeDtypeStruct((4 * NV * 8 * 48, NL), F32),
        in_specs=main_specs(),
        out_specs=pl.BlockSpec((4 * NV * 8 * 48, NL), lambda i: (0, 0)),
        scratch_shapes=[
            pltpu.VMEM((4, 4, 256, NL), BF16),
            pltpu.VMEM((NV * 8, 64, NL), F32),
            pltpu.VMEM((4, 3, NV * 32, NL), F32),
            pltpu.VMEM((4, NV * 4, 40, NL), F32),
            pltpu.VMEM((NV * 8 * 48, NL), F32),
            pltpu.VMEM((4, 4, 256, NL), BF16),
            pltpu.VMEM((4, NL, 4 * NL), F32),
            pltpu.VMEM((NV * 64, NL), F32),
        ],
        cost_estimate=cost(8),
        compiler_params=pltpu.CompilerParams(vmem_limit_bytes=VMEM_LIMIT),
    )(flat.reshape(4, NV * 8, ROWS, NL), flat, *operands, w["wide"], w["narrow"])


def cells_step(kept):
    shape = (NV, NZ, NR, NL)
    return pl.pallas_call(
        cells_kernel,
        out_shape=jax.ShapeDtypeStruct(shape, F32),
        in_specs=[pl.BlockSpec(memory_space=pltpu.VMEM)],
        out_specs=pl.BlockSpec(memory_space=pltpu.HBM),
        scratch_shapes=[pltpu.VMEM(shape, F32), pltpu.SemaphoreType.DMA((NV * 4,))],
        cost_estimate=cost(4),
        compiler_params=pltpu.CompilerParams(vmem_limit_bytes=VMEM_LIMIT),
    )(kept)


def sent_order(count):
    return sorted(range(count), key=lambda r: (r == 0, r < 2, r))


def rows_kernel(count_x, count_z, *refs):
    shares, out = [refs[sent_order(count_x).index(r)] for r in range(count_x)], refs[count_x + 1]
    me, me_y = lax.axis_index("gx"), lax.axis_index("gy")
    row = lax.broadcasted_iota(jnp.int32, (8, NL), 0)
    lane = lax.broadcasted_iota(jnp.int32, (8, NL), 1)
    for r in range(count_x):
        at = pl.multiple_of(16 * (me ^ r), 16)
        for j in range(count_z):
            for z in range(4):
                start = 64 * j + 16 * z
                out[j, z, pl.ds(at, 16), :] = shares[r][start : start + 16, :]
    for j in range(count_z):
        turn = lanes_turn(me_y ^ (2 * j))
        piece = lax.rem(lane + (NL - turn), NL) // 21
        inside = [piece == p for p in range(5)]
        for r in range(count_x):
            i = me ^ r
            below = pl.multiple_of(16 * lax.rem(i + 1, count_x), 16)
            above = pl.multiple_of(16 * lax.rem(i + count_x - 1, count_x) + 8, 8)
            tiles = [shares[r][64 * j + 8 * g : 64 * j + 8 * g + 8, :] for g in range(8)]
            low, high = jnp.zeros((8, NL), F32), jnp.zeros((8, NL), F32)
            for p in range(5):
                back = (21 * p - 105) % NL
                low = jnp.where(inside[p], pltpu.roll(tiles[p], back, 1), low)
                extra = tiles[5 + p // 2]
                extra = extra if p % 2 else pltpu.roll(extra, 4, 0)
                high = jnp.where(inside[p], pltpu.roll(extra, back, 1), high)
            for z in range(4):
                first = pltpu.roll(low, 8 - 2 * z, 0) if z else low
                last = pltpu.roll(high, z, 0) if z else high
                out[j, z, pl.ds(below, 8), :] += jnp.where(row < 2, first, 0.0)
                out[j, z, pl.ds(above, 8), :] += jnp.where(row == 7, last, 0.0)


def rows_step(pieces, count_z, after):
    vmem = pl.BlockSpec(memory_space=pltpu.VMEM)
    count_x = len(pieces)
    return pl.pallas_call(
        functools.partial(rows_kernel, count_x, count_z),
        out_shape=jax.ShapeDtypeStruct((count_z, 4, 16 * count_x, NL), F32),
        in_specs=[vmem] * count_x + [pl.BlockSpec(memory_space=pl.ANY)],
        out_specs=vmem,
        compiler_params=pltpu.CompilerParams(vmem_limit_bytes=VMEM_LIMIT),
    )(*[pieces[r] for r in sent_order(count_x)], after)


def coarse_kernel(count_x, count_y, own, other, out_hbm, out, sems):
    me = lax.axis_index("gy")
    me_z, is_even = lax.shift_right_logical(me, 1), lax.rem(me, 2) == 0
    lane = lax.broadcasted_iota(jnp.int32, (8, NL), 1)
    place = [lax.rem(lane + NL - 35 * v, NL) for v in range(NV)]

    def block(i, _):
        rows = pl.ds(pl.multiple_of(8 * i, 8), 8)
        for z in range(4):
            pieces = []
            for j in range(count_y // 2):
                mine, theirs = own[j ^ me_z, z, rows, :], other[j ^ me_z, z, rows, :]
                pieces += [jnp.where(is_even, mine, theirs), jnp.where(is_even, theirs, mine)]
            for v in range(NV):
                at = place[v]
                for t in range(count_y // 4):
                    total = jnp.where(at < 2, pieces[4 * t - 1], 0.0)
                    total += jnp.where(at == NL - 1, pieces[(4 * t + 4) % count_y], 0.0)
                    for q in range(4):
                        inside = (at >= 32 * q - 1) & (at < 32 * q + 34)
                        total += jnp.where(inside, pieces[4 * t + q], 0.0)
                    out[v, z, rows, NL * t : NL * (t + 1)] = pltpu.roll(total, NL - 35 * v, 1) if v else total
        return 0

    def copy(i):
        rows = pl.ds(pl.multiple_of(16 * i, 16), 16)
        return pltpu.make_async_copy(out.at[:, :, rows], out_hbm.at[:, :, rows], sems.at[i])

    def pair(i, _):
        block(2 * i, 0)
        block(2 * i + 1, 0)
        copy(i).start()
        return 0

    lax.fori_loop(0, count_x, pair, 0)
    for i in range(count_x):
        copy(i).wait()


def coarse_step(own, other, count_x, count_y):
    vmem = pl.BlockSpec(memory_space=pltpu.VMEM)
    shape = (NV, 4, 16 * count_x, 32 * count_y)
    return pl.pallas_call(
        functools.partial(coarse_kernel, count_x, count_y),
        out_shape=jax.ShapeDtypeStruct(shape, F32),
        in_specs=[vmem, vmem],
        out_specs=pl.BlockSpec(memory_space=pltpu.HBM),
        scratch_shapes=[pltpu.VMEM(shape, F32), pltpu.SemaphoreType.DMA((count_x,))],
        compiler_params=pltpu.CompilerParams(vmem_limit_bytes=VMEM_LIMIT),
    )(own, other)


def shifted(x, axis, step):
    count = lax.axis_size(axis)
    return lax.ppermute(x, axis, [(i, (i + step) % count) for i in range(count)])


def swapped(x, axis, distance):
    return lax.ppermute(x, axis, [(i, i ^ distance) for i in range(lax.axis_size(axis))])


def body(field, masks):
    count_x, count_y = lax.axis_size("gx"), lax.axis_size("gy")
    lifted, up, down, own_masks, share = first_step(field, masks)
    north = shifted(down, "gx", 1)
    south = shifted(up, "gx", -1)
    shares = [share] + [swapped(share, "gy", r) for r in range(2, count_y, 2)]
    parts, to_left, to_right = edge_step(lift_step(lifted), lifted, north, south, own_masks)
    east = shifted(to_left, "gy", -1)
    west = shifted(to_right, "gy", 1)
    joined = join_step(shares, to_left)
    pieces = [joined] + [swapped(joined, "gx", r) for r in range(1, count_x)]
    kept = main_step(parts, east, west, own_masks, north, south)
    own = rows_step(pieces, count_y // 2, kept)
    other = swapped(own, "gy", 1)
    return cells_step(kept.reshape(4, NV * 8, 48, NL)), coarse_step(own, other, count_x, count_y)


def solution(mesh):
    placed = P(None, None, "gx", "gy")
    return jax.shard_map(
        body,
        mesh=mesh,
        in_specs=(placed, placed),
        out_specs=(placed, P()),
        check_vma=False,
    )
```

```python
import functools

import jax
import jax.numpy as jnp
import ml_dtypes
import numpy as np
from jax import lax
from jax.experimental import pallas as pl
from jax.experimental.pallas import tpu as pltpu
from jax.sharding import PartitionSpec as P

F32 = jnp.float32
BF16 = jnp.bfloat16
VMEM_LIMIT = 32 * 1024 * 1024

NV, NZ, NR, NL = 3, 16, 64, 128


def detail_row(k):
    return {2 * k + 1: 1.0, 2 * k: -0.5, 2 * k + 2: -0.5}


def smooth_row(k):
    row = {2 * k: 1.0}
    for j in (k - 1, k):
        for cell, value in detail_row(j).items():
            row[cell] = row.get(cell, 0.0) + 0.25 * value
    return row


def even_row(k):
    return {("s", k): 1.0, ("d", k - 1): -0.25, ("d", k): -0.25}


def odd_row(k):
    row = {("d", k): 1.0}
    for j in (k, k + 1):
        for name, value in even_row(j).items():
            row[name] = row.get(name, 0.0) + 0.5 * value
    return row


def as_bf16(matrix):
    cast = matrix.astype(ml_dtypes.bfloat16)
    assert (cast.astype(np.float64) == matrix).all()
    return cast


def combine(*terms):
    total = {}
    for factor, row in terms:
        for cell, value in row.items():
            total[cell] = total.get(cell, 0.0) + factor * value
    return total


def level_one_columns():
    names = {("s", k): k for k in range(65)}
    names.update({("d", k): 128 + k for k in range(65)})
    names[("d", -1)] = 128 + 65
    return names


def level_two_columns():
    names = {("s", k): k for k in range(33)}
    names.update({("d", k): 64 + k for k in range(33)})
    names[("d", -1)] = 64 + 33
    return names


def smooth_place(k):
    return k + 2


def beyond(n):
    return {"cell": 40 + 16 * n, "after": 48 + 16 * n, "before": 8 * n}


BEYOND_SMOOTH = {65: 104, -1: 32}
FROM_WEST = 40


def own_row(kind, k, n):
    place = {name: 128 + lane for name, lane in beyond(n).items()}
    if kind == "d":
        if k == -1:
            return {place["before"]: 1.0, 0: -0.5}
        if k == 64:
            return {place["after"]: 1.0}
        return {(place["cell"] if y == 128 else y): value for y, value in detail_row(k).items()}
    if k in (-2, 66):
        return {}
    if k in BEYOND_SMOOTH:
        row = {128 + BEYOND_SMOOTH[k]: 1.0}
        return combine((1.0, row), (1.0, {0: -0.125})) if k == -1 else row
    even = place["cell"] if k == 64 else 2 * k
    return combine((1.0, {even: 1.0}), (0.25, own_row("d", k - 1, n)), (0.25, own_row("d", k, n)))


@functools.lru_cache(maxsize=None)
def weights():
    w = {}
    names = level_one_columns()
    forward = np.zeros((4, 256, 256))
    inverse = np.zeros((256, 128))
    for (kind, k), column in names.items():
        for n in range(4):
            for place, value in own_row(kind, k, n).items():
                forward[n, place, column] += value
    for k in range(64):
        for y, row in ((2 * k, even_row(k)), (2 * k + 1, odd_row(k))):
            for name, value in row.items():
                inverse[names[name], y] += value
    short = np.zeros((144, 256))
    short[:128] = forward[0, :128]
    for i, lane in enumerate(beyond(0).values()):
        short[128 + i] = forward[0, 128 + lane]
    smooth = np.zeros((256, 128))
    for k in range(-2, 67):
        for place, value in own_row("s", k, 0).items():
            smooth[place, smooth_place(k)] += value
    names2 = level_two_columns()
    forward2 = np.zeros((128, 128))
    inverse2 = np.zeros((128, 128))
    for (kind, k), column in names2.items():
        for cell, value in (smooth_row(k) if kind == "s" else detail_row(k)).items():
            forward2[smooth_place(cell), column] += value
    for k in range(33):
        rows = [(2 * k, even_row(k))] + ([(2 * k + 1, odd_row(k))] if k < 32 else [])
        for y, row in rows:
            for name, value in row.items():
                inverse2[names2[name], y] += value
    back = np.zeros((256, 128))
    back[:65] = inverse[:65]
    back[128 : 128 + 65] = inverse[:65]
    spread = np.zeros((3, 128, 2, 128))
    for k in range(64):
        spread[0, k, 0, k] = 1
    for k in range(32):
        spread[0, 64 + k, 1, k] = 1
        spread[0, 64 + k, 1, 64 + k] = 1
    for at in range(0, 16, 4):
        spread[1, at, 0, 64] = 1
        spread[2, at + 1, 0, 65] = 1
        for base in (0, 64):
            spread[1, at + 2, 1, base + 32] = 1
            spread[2, at + 3, 1, base + 33] = 1
    w["wide"] = np.concatenate([short, spread.reshape(384, 256)], 0)
    own, beside = smooth[:128], smooth[128:]
    w["narrow"] = np.concatenate([inverse, own, own, beside, beside, back, forward2, inverse2], 0)
    edge = np.zeros((4, 128, 128))

    def put(n, lane, row):
        for z in range(8):
            for y, value in row.items():
                j = y - 120 if y >= 120 else y + 8
                edge[n, 16 * z + j, lane + z] += value

    part = {127: 1.0, 126: -0.5}
    for n in range(4):
        put(n, beyond(n)["cell"], {0: 1.0})
        put(n, beyond(n)["after"], detail_row(0))
        put(n, beyond(n)["before"], part)
    put(0, BEYOND_SMOOTH[65], combine((1.0, smooth_row(1)), (-0.5, smooth_row(2))))
    share = combine((1.0, {126: 1.0}), (0.25, detail_row(62)), (0.25, part))
    put(0, BEYOND_SMOOTH[-1], combine((1.0, share), (-0.5, smooth_row(62))))
    w["edge"] = edge.reshape(512, 128)
    expand = np.zeros((2, 4, 128))
    for j in range(4):
        expand[0, j, 16 * j : 16 * j + 16] = 1
        expand[1, j, 64 + 8 * j : 64 + 8 * j + 8] = 1
    twice = combine(*[(value, smooth_row(k)) for k, value in smooth_row(0).items()])
    columns = np.zeros((2, 128, 128))
    for m in range(-1, 34):
        for t, value in twice.items():
            if 0 <= 4 * m + t < NL:
                columns[:, 4 * m + t, m + 1] = value
    rows = np.zeros((4, 32, 2, 64))
    for z in range(4):
        places = {m: m for m in range(16)}
        places.update({16: 16 + 2 * z, 17: 17 + 2 * z, -1: 16 + 15 - z})
        for m, place in places.items():
            for t, value in twice.items():
                if 0 <= 4 * m + t < NR:
                    rows[z, place, :, 4 * m + t] = value
    pad = np.zeros((8, 128))
    w["first"] = np.concatenate([columns.reshape(256, 128), rows.reshape(128, 128), expand.reshape(8, 128), pad], 0)
    return {name: as_bf16(matrix) for name, matrix in w.items()}


def two_terms(x):
    high = x.astype(BF16)
    low = (x - high.astype(F32)).astype(BF16)
    return high, low


def cost(gigaflops):
    return pl.CostEstimate(flops=gigaflops * 10**9, bytes_accessed=8 * 10**6, transcendentals=0)


def dot(a, b):
    return jnp.dot(a, b, preferred_element_type=F32)


def lift_planes(cells):
    half = len(cells) // 2
    even, odd = cells[0::2], cells[1::2]
    detail = [odd[k] - 0.5 * (even[k] + even[min(k + 1, half - 1)]) for k in range(half)]
    smooth = [even[k] + 0.25 * (detail[max(k - 1, 0)] + detail[k]) for k in range(half)]
    return smooth, detail


def unlift_planes(smooth, detail):
    half = len(smooth)
    even = [smooth[k] - 0.25 * (detail[max(k - 1, 0)] + detail[k]) for k in range(half)]
    out = []
    for k in range(half):
        out += [even[k], detail[k] + 0.5 * (even[k] + even[min(k + 1, half - 1)])]
    return out


def lift_rows(load, start):
    even, odd, after = load(start), load(start + 1), load(start + 2)
    before, odd_before = load(start - 2), load(start - 1)
    detail = odd - 0.5 * (even + after)
    detail_before = odd_before - 0.5 * (before + even)
    return even + 0.25 * (detail_before + detail), detail


def unlift_rows(smooth, detail, row):
    here, after = detail(row), detail(row + 1)
    even = smooth(row) - 0.25 * (detail(row - 1) + here)
    next_even = smooth(row + 1) - 0.25 * (here + after)
    return even, here + 0.5 * (even + next_even)


PITCH = 80


def lanes_turn(j):
    return lax.rem(32 * lax.rem(j, 4) + NL - 1, NL)


def first_kernel(
    field, masks_hbm, table_hbm, lifted, up, down, own_masks, share, cells, twice, masks, table, sems
):
    small = [
        pltpu.make_async_copy(masks_hbm, masks, sems.at[0]),
        pltpu.make_async_copy(table_hbm, table, sems.at[1]),
    ]
    copies = []
    for v in range(NV):
        for c in range(4):
            part = pl.ds(16 * c, 16)
            copies.append(pltpu.make_async_copy(field.at[v, :, part], cells.at[v, :, part], sems.at[2 + 4 * v + c]))
    for copy in small + copies:
        copy.start()
    for p in range(NV * NZ):
        lifted[p * PITCH : p * PITCH + 8, :] = jnp.zeros((8, NL), F32)
        lifted[p * PITCH + 72 : p * PITCH + 80, :] = jnp.zeros((8, NL), F32)
    for copy in small:
        copy.wait()
    for i, out, tile in ((0, up, 15), (1, down, 9)):
        total = jnp.zeros((7, NL), F32)
        for l in range(2):
            flags = masks[l, i].astype(F32).astype(BF16)
            spread = table[384 + 4 * l : 388 + 4 * l, :]
            total += lax.dot_general(flags, spread, (((0,), (0,)), ((), ())), preferred_element_type=F32)
        own_masks[i] = jnp.concatenate([total, jnp.zeros((1, NL), F32)], 0)
        out[tile] = own_masks[i]

    for v in range(NV):
        for t in range(8):
            if t % 2 == 0:
                copies[4 * v + t // 2].wait()
            smooth, detail = lift_planes([cells[v, z, 8 * t : 8 * t + 8, :] for z in range(NZ)])
            for k, tile in enumerate(smooth + detail):
                start = (v * NZ + k) * PITCH + 8 + 8 * t
                lifted[start : start + 8, :] = tile
            for k, tile in enumerate(lift_planes(smooth)[0]):
                twice[v * 4 + k, 8 * t : 8 * t + 8, :] = tile
        for bz in range(2):

            def row(x):
                return lifted[pl.ds((v * NZ + bz * 8) * PITCH + 8 + x, 8, stride=PITCH), :]

            x = [row(j) for j in range(7 if bz == 0 else 3)]
            first = x[1] - 0.5 * (x[0] + x[2])
            up[v * 5 + bz] = x[0]
            up[v * 5 + 2 + bz] = first
            y = {j: row(j) for j in (range(58, 64) if bz == 0 else (62, 63))}
            part = y[63] - 0.5 * y[62]
            down[v * 3 + bz] = part
            if bz == 0:
                second = x[3] - 0.5 * (x[2] + x[4])
                third = x[5] - 0.5 * (x[4] + x[6])
                up[v * 5 + 4] = x[2] + 0.25 * (first + second) - 0.5 * (x[4] + 0.25 * (second + third))
                before = y[59] - 0.5 * (y[58] + y[60])
                last = y[61] - 0.5 * (y[60] + y[62])
                down[v * 3 + 2] = y[62] + 0.25 * (last + part) - 0.5 * (y[60] + 0.25 * (before + last))

    total = jnp.zeros((80, NL), F32)
    for v in range(NV):
        main, extra = [], jnp.zeros((16, NL), F32)
        for z in range(4):
            terms = jnp.concatenate(two_terms(twice[v * 4 + z]), 0)
            part = dot(table[256 + 32 * z : 288 + 32 * z, :], terms)
            main.append(part[:16])
            extra += part[16:]
        terms = jnp.concatenate(two_terms(jnp.concatenate(main + [extra], 0)), 1)
        part = dot(terms, table[0:256, :])
        total += pltpu.roll(part, 35 * v, 1) if v else part
    turn = lanes_turn(lax.axis_index("gy"))
    lane = lax.broadcasted_iota(jnp.int32, (8, NL), 1)
    spare = (lane >= 105) & (lane < 126)
    upper = lax.broadcasted_iota(jnp.int32, (8, NL), 0) < 4
    below, above = total[64:72], total[72:80]
    pieces = [pltpu.roll(above, 105 - 21 * p, 1) for p in range(5)]
    for g in range(8):
        if g < 5:
            extra = pltpu.roll(below, 105 - 21 * g, 1)
        else:
            extra = pltpu.roll(pieces[2 * g - 10], 4, 0)
            extra = jnp.where(upper, extra, pieces[2 * g - 9] if g < 7 else 0.0)
        tile = jnp.where(spare, extra, total[8 * g : 8 * g + 8])
        share[8 * g : 8 * g + 8, :] = pltpu.roll(tile, turn, 1)


def in_hbm(x):
    return pltpu.with_memory_space_constraint(x, pltpu.HBM)


def first_step(field, masks):
    vmem = pl.BlockSpec(memory_space=pltpu.VMEM)
    shapes = [(NV * NZ * PITCH, NL), (16, 8, NL), (10, 8, NL), (2, 8, NL), (64, NL)]
    return pl.pallas_call(
        first_kernel,
        out_shape=[jax.ShapeDtypeStruct(s, F32) for s in shapes],
        in_specs=[pl.BlockSpec(memory_space=pltpu.HBM)] * 3,
        out_specs=[vmem] * 5,
        scratch_shapes=[
            pltpu.VMEM((NV, NZ, NR, NL), F32),
            pltpu.VMEM((NV * 4, NR, NL), F32),
            pltpu.VMEM((2, 2, 4, 7), jnp.int32),
            pltpu.VMEM((400, NL), BF16),
            pltpu.SemaphoreType.DMA((4 * NV + 2,)),
        ],
        compiler_params=pltpu.CompilerParams(vmem_limit_bytes=VMEM_LIMIT),
    )(*[in_hbm(x) for x in (field, masks.transpose(0, 2, 3, 1), jnp.asarray(weights()["first"]))])


ROWS = 40


def lift_kernel(lifted, parts):
    def lift(step, _):
        v, bz = step // 2, lax.rem(step, 2)
        for z in range(8):
            start = pl.multiple_of((step * 8 + z) * PITCH, 8)
            for t in range(4):
                pair = lift_rows(lambda s: lifted[pl.ds(start + 16 * t + s, 8, stride=2), :], 8)
                for bx in range(2):
                    plane = (2 * bz + bx) * 24 + v * 8 + z
                    parts[pl.ds(pl.multiple_of(plane * ROWS + 8 * t, 8), 8), :] = pair[bx]
        return 0

    lax.fori_loop(0, NV * 2, lift, 0)


def lift_step(lifted):
    vmem = pl.BlockSpec(memory_space=pltpu.VMEM)
    return pl.pallas_call(
        lift_kernel,
        out_shape=jax.ShapeDtypeStruct((4 * NV * 8 * ROWS, NL), F32),
        in_specs=[vmem],
        out_specs=vmem,
        compiler_params=pltpu.CompilerParams(vmem_limit_bytes=VMEM_LIMIT),
    )(lifted)


def edge_kernel(parts_in, lifted, north, south, own_masks, table_hbm, parts, to_left, to_right, packed, table, sem):
    copy = pltpu.make_async_copy(table_hbm, table, sem.at[0])
    copy.start()
    for p in range(4 * NV * 8):
        parts[p * ROWS + 32 : p * ROWS + 40, :] = jnp.zeros((8, NL), F32)
    for v in range(NV):
        for bz in range(2):

            def cell(x):
                return lifted[pl.ds((v * NZ + bz * 8) * PITCH + 8 + x, 8, stride=PITCH), :]

            def at(bx, r):
                return pl.ds(((2 * bz + bx) * 24 + v * 8) * ROWS + r, 8, stride=ROWS)

            before, after, detail = north[v * 3 + bz], south[v * 5 + bz], south[v * 5 + 2 + bz]
            start = cell(0)
            last = cell(63) - 0.5 * (cell(62) + after)
            parts[at(0, 0), :] = parts[at(0, 0), :] + 0.25 * before
            parts[at(0, 31), :] = parts[at(0, 31), :] - 0.125 * after
            parts[at(1, 31), :] = parts[at(1, 31), :] - 0.5 * after
            parts[at(0, 32), :] = after + 0.25 * (last + detail)
            parts[at(1, 32), :] = detail
            parts[at(1, 39), :] = before - 0.5 * start
            if bz == 0:
                parts[at(0, 33), :] = south[v * 5 + 4]
                parts[at(0, 39), :] = north[v * 3 + 2] - 0.125 * start

    lane = lax.broadcasted_iota(jnp.int32, (8, NL), 1) // 16

    def pack(v, _):
        for n in range(4):
            for t in range(5):
                tile = jnp.zeros((8, NL), F32)
                for z in range(8):
                    start = (n * 24 + v * 8 + z) * ROWS + 8 * t
                    x = parts[pl.ds(pl.multiple_of(start, 8), 8), :]
                    tile = jnp.where(lane == z, pltpu.roll(x, (8 + 16 * z) % NL, 1), tile)
                packed[pl.ds(pl.multiple_of(n * 120 + v * ROWS + 8 * t, 8), 8), :] = tile
        return 0

    lax.fori_loop(0, NV, pack, 0)
    copy.wait()
    terms = [two_terms(packed[n * 120 : (n + 1) * 120, :]) for n in range(4)]
    high, low = [jnp.concatenate(part, 1) for part in zip(*terms)]
    sides = dot(high, table[...]) + dot(low, table[...])
    lane = lax.broadcasted_iota(jnp.int32, (ROWS, NL), 1)
    each = [sides[v * ROWS : (v + 1) * ROWS] for v in range(NV)]
    right = jnp.where(lane < 40, each[0], pltpu.roll(each[1], 40, 1))
    to_right[0:ROWS, :] = jnp.where(lane < 80, right, pltpu.roll(each[2], 80, 1))
    last = jnp.where(lane < 32, pltpu.roll(each[2], NL - 40, 1), pltpu.roll(each[2], NL - 72, 1))
    to_left[0:ROWS, :] = jnp.where(lane < 40, last, each[0])
    to_left[ROWS : 2 * ROWS, :] = jnp.where(lane < 32, pltpu.roll(each[2], NL - 72, 1), each[1])
    lane = lax.broadcasted_iota(jnp.int32, (8, NL), 1)
    ends = jnp.zeros((8, NL), F32)
    for ib, tile in enumerate((north[9], own_masks[0], own_masks[1], south[15])):
        for j, source in enumerate((0, 63, 64, 95)):
            target = 4 * ib + j
            ends = jnp.where(lane == target, pltpu.roll(tile, (target - source) % NL, 1), ends)
    to_left[2 * ROWS : 2 * ROWS + 8, :] = ends
    to_right[ROWS : ROWS + 8, :] = ends


def edge_step(parts, lifted, north, south, own_masks):
    vmem = pl.BlockSpec(memory_space=pltpu.VMEM)
    shapes = [(4 * NV * 8 * ROWS, NL), (2 * ROWS + 8, NL), (ROWS + 8, NL)]
    return pl.pallas_call(
        edge_kernel,
        out_shape=[jax.ShapeDtypeStruct(s, F32) for s in shapes],
        in_specs=[vmem] * 5 + [pl.BlockSpec(memory_space=pltpu.HBM)],
        out_specs=[vmem] * 3,
        input_output_aliases={0: 0},
        cost_estimate=cost(20),
        scratch_shapes=[pltpu.VMEM((480, NL), F32), pltpu.VMEM((512, NL), BF16), pltpu.SemaphoreType.DMA((1,))],
        compiler_params=pltpu.CompilerParams(vmem_limit_bytes=VMEM_LIMIT),
    )(parts, lifted, north, south, own_masks, in_hbm(jnp.asarray(weights()["edge"])))


def join_kernel(*refs):
    shares, out = refs[-3::-1], refs[-1]
    for n, piece in enumerate(shares):
        out[64 * n : 64 * (n + 1), :] = piece[...]


def join_step(shares, after):
    vmem = pl.BlockSpec(memory_space=pltpu.VMEM)
    return pl.pallas_call(
        join_kernel,
        out_shape=jax.ShapeDtypeStruct((64 * len(shares), NL), F32),
        in_specs=[vmem] * len(shares) + [pl.BlockSpec(memory_space=pl.ANY)],
        out_specs=vmem,
        cost_estimate=cost(20),
        compiler_params=pltpu.CompilerParams(vmem_limit_bytes=VMEM_LIMIT),
    )(*shares[::-1], after)


def mask_lanes(west, east, own_masks, north_mask, south_mask, wide):
    group = lax.broadcasted_iota(jnp.int32, (8, NL), 1) // 4
    masks = [
        jnp.concatenate([jnp.where(group == ib, tile, 0.0) for ib in range(4)], 0)
        for tile in (east[2 * ROWS : 2 * ROWS + 8, :], west[ROWS : ROWS + 8, :])
    ]
    own = jnp.concatenate([north_mask[0], own_masks[0], own_masks[1], south_mask[0]], 0)
    flags = jnp.concatenate([own] + masks, 1).astype(BF16)
    return dot(flags, wide[144:528, :])


def beside_tiles(west, east, at, count):
    lane = lax.broadcasted_iota(jnp.int32, (count, NL), 1)
    left = west[at : at + count, :]
    first, second = east[at : at + count, :], east[ROWS + at : ROWS + at + count, :]
    third = jnp.where(lane < 104, pltpu.roll(second, 72, 1), pltpu.roll(first, 72, 1))
    third = jnp.where(lane < 72, pltpu.roll(first, 40, 1), third)
    tiles = []
    for v, right in enumerate((first, second, third)):
        beside = jnp.where(lane < FROM_WEST, pltpu.roll(left, NL - 40 * v, 1) if v else left, right)
        tiles += [pltpu.roll(beside, NL - z, 1) if z else beside for z in range(8)]
    return tiles


def beside_terms(west, east, at, count):
    return jnp.concatenate(two_terms(jnp.concatenate(beside_tiles(west, east, at, count), 0)), 1)


def own_terms(planes, at, count):
    return jnp.concatenate(two_terms(planes[:, at : at + count, :].reshape(24 * count, NL)), 1)


def main_kernel(
    parts, flat, east, west, own_masks, north_mask, south_mask, wide, narrow,
    kept,
    gain2, low, second, kept2, low_back, gain, sides_wide, turned,
):
    inverse, smooth_own, smooth_beside = narrow.at[0:256], narrow.at[256:512], narrow.at[512:768]
    back, forward2, inverse2 = narrow.at[768:1024], narrow.at[1024:1152], narrow.at[1152:1280]
    lanes = mask_lanes(west, east, own_masks, north_mask, south_mask, wide)
    lane64 = lax.broadcasted_iota(jnp.int32, (1, NL), 1) < 64
    forward2_f = forward2[...].astype(F32)
    for ib in range(4):
        for n in range(4) if ib else (1, 3):
            b = 8 * ib + 4 * (n // 2) + n % 2 - 1
            smooth_two = lanes[b : b + 1, NL:] if n else jnp.ones((1, NL), F32)
            row = jnp.where(lane64, smooth_two, lanes[b + 2 : b + 3, NL:])
            both = dot((forward2_f * row).astype(BF16), inverse2[...]).astype(BF16)
            gain2[ib, n, 0:128, :] = both
            gain2[ib, n, 128:256, :] = both

    for at, count in ((0, 16), (16, 16), (32, 8)):
        part = dot(own_terms(parts.at[0], at, count), smooth_own[...])
        part += dot(beside_terms(west, east, at, count), smooth_beside[...])
        part = part.reshape(24, count, NL)
        if at < 32:
            low[:, 8 + at : 8 + at + count, :] = part
            if at == 0:
                low[:, 56:64, :] = part[:, 0:8]
        else:
            low[:, 0:8, :] = part
            low[:, 40:48, :] = part
            low[:, 48:56, :] = part

    def rows_two(v, _):
        for t in range(3):
            lifted = [
                lift_rows(lambda s: low[v * 8 + p, pl.ds(16 * t + s, 8, stride=2), :], 8) for p in range(8)
            ]
            for bx in range(2):
                smooth, detail = lift_planes([pair[bx] for pair in lifted])
                for bz, part in ((0, smooth), (1, detail)):
                    for z in range(4):
                        second[2 * bz + bx, t, pl.ds(pl.multiple_of((v * 4 + z) * 8, 8), 8), :] = part[z]
        return 0

    lax.fori_loop(0, NV, rows_two, 0)
    for n in range(4):
        for t in range(3):
            terms = jnp.concatenate(two_terms(second[n, t]), 1)
            if t < 2:
                kept2[n, :, 8 + 8 * t : 16 + 8 * t, :] = dot(terms, gain2[t + 1, n]).reshape(NV * 4, 8, NL)
            else:
                if n % 2:
                    kept2[n, :, 0:8, :] = dot(terms, gain2[0, n]).reshape(NV * 4, 8, NL)
                kept2[n, :, 24:32, :] = dot(terms, gain2[3, n]).reshape(NV * 4, 8, NL)

    def back_two(v, _):
        for t in range(3):
            pairs = {}
            for bz in range(2):
                for z in range(4):
                    p = v * 4 + z
                    if t < 2:
                        pairs[bz, z] = unlift_rows(
                            lambda r: kept2[2 * bz, p, pl.ds(r, 8), :],
                            lambda r: kept2[2 * bz + 1, p, pl.ds(r, 8), :],
                            8 + 8 * t,
                        )
                    else:
                        even = kept2[2 * bz, p, 24:32, :] - 0.25 * (
                            kept2[2 * bz + 1, p, 23:31, :] + kept2[2 * bz + 1, p, 24:32, :]
                        )
                        pairs[bz, z] = (even, even)
            for parity in range(2 if t < 2 else 1):
                planes = unlift_planes([pairs[0, z][parity] for z in range(4)], [pairs[1, z][parity] for z in range(4)])
                for z in range(8):
                    low_back[pl.ds((v * 8 + z) * 48 + 16 * t + parity, 8, stride=2), :] = planes[z]
        return 0

    lax.fori_loop(0, NV, back_two, 0)

    forward_f = wide[0:144, :].astype(F32)
    for ib in range(4):
        sides_wide[ib] = jnp.zeros((NL, 4 * NL), F32)
    for ib in range(4):
        for n in range(4) if ib else (1, 3):
            b = 8 * ib + 4 * (n // 2) + n % 2 - 1
            smooth_one = lanes[b : b + 1, 0:NL] if n else jnp.zeros((1, NL), F32)
            row = jnp.concatenate([smooth_one, lanes[b + 2 : b + 3, 0:NL]], 1)
            both = dot((forward_f * row).astype(BF16), inverse[...])
            main = both[0:128].astype(BF16)
            gain[ib, n, 0:128, :] = main
            gain[ib, n, 128:256, :] = main
            for i in range(3):
                at = list(beyond(n).values())[i]
                sides_wide[ib, at : at + 1, n * NL : (n + 1) * NL] = both[128 + i : 129 + i]

    gain_sides = []
    for ib in range(4):
        side = sides_wide[ib].astype(BF16)
        gain_sides.append(jnp.concatenate([side, side], 0))
    def put(n, p, at, rows):
        start = pl.multiple_of((n * 24 + p) * 48 + 8 + at, 8)
        kept[pl.ds(start, rows.shape[0]), :] = rows

    def row_of(ref, first, pitch):
        return ref[pl.ds(first, 24, stride=pitch), :]

    for ib in range(2):
        product = dot(beside_terms(west, east, 16 * ib, 16), gain_sides[ib + 1])
        for n in range(4):
            for p in range(24):
                put(n, p, 16 * ib, product[16 * p : 16 * p + 16, n * NL : (n + 1) * NL])

    def keep(n, _):
        for ib in range(2):
            product = dot(own_terms(parts.at[n], 16 * ib, 16), gain[ib + 1, n])
            for p in range(24):
                start = pl.ds(pl.multiple_of((n * 24 + p) * 48 + 8 + 16 * ib, 8), 16)
                kept[start, :] += product[16 * p : 16 * p + 16]
        return 0

    lax.fori_loop(0, 4, keep, 0)
    for ib in range(2):
        rows = jnp.concatenate([low_back[48 * p + 16 * ib : 48 * p + 16 * ib + 16, :] for p in range(24)], 0)
        product = dot(jnp.concatenate(two_terms(rows), 1), back[...])
        for p in range(24):
            start = 48 * p + 8 + 16 * ib
            kept[start : start + 16, :] += product[16 * p : 16 * p + 16]
    tiles = beside_tiles(west, east, 32, 8)
    for p in range(24):
        turned[8 * p : 8 * p + 8, :] = tiles[p]
    for first, ib, place, row in ((0, 3, 40, 32), (7, 0, 7, 39)):
        beside = dot(jnp.concatenate(two_terms(row_of(turned, first, 8)), 1), gain_sides[ib])
        for n in range(4) if ib else (1, 3):
            own = jnp.concatenate(two_terms(row_of(flat, n * 24 * ROWS + row, ROWS)), 1)
            total = beside[:, n * NL : (n + 1) * NL] + dot(own, gain[ib, n])
            if n == 0:
                total += dot(jnp.concatenate(two_terms(row_of(low_back, row, 48)), 1), back[...])
            kept[pl.ds(n * 24 * 48 + place, 24, stride=48), :] = total


def cells_kernel(kept, out, cells, sems):
    def back_one(step, _):
        v, t = step // 4, step % 4
        pairs = {}
        for bz in range(2):
            for z in range(8):
                p = v * 8 + z
                pairs[bz, z] = unlift_rows(
                    lambda r: kept[2 * bz, p, pl.ds(8 * t + r, 8), :],
                    lambda r: kept[2 * bz + 1, p, pl.ds(8 * t + r, 8), :],
                    8,
                )
        for parity in range(2):
            planes = unlift_planes([pairs[0, z][parity] for z in range(8)], [pairs[1, z][parity] for z in range(8)])
            for z in range(NZ):
                cells[v, z, pl.ds(16 * t + parity, 8, stride=2), :] = planes[z]
        return 0

    def copy(step):
        v, rows = step // 4, pl.ds(pl.multiple_of(16 * (step % 4), 16), 16)
        return pltpu.make_async_copy(cells.at[v, :, rows], out.at[v, :, rows], sems.at[step])

    def one(step, _):
        back_one(step, 0)
        copy(step).start()
        return 0

    lax.fori_loop(0, NV * 4, one, 0)
    for step in range(NV * 4):
        copy(step).wait()


def main_specs():
    vmem = pl.BlockSpec(memory_space=pltpu.VMEM)
    return [
        vmem, vmem, vmem, vmem, vmem,
        pl.BlockSpec((1, 8, NL), lambda i: (9, 0, 0)), pl.BlockSpec((1, 8, NL), lambda i: (15, 0, 0)),
        vmem, vmem,
    ]


def main_step(flat, *operands):
    w = weights()
    return pl.pallas_call(
        main_kernel,
        grid=(1,),
        out_shape=jax.ShapeDtypeStruct((4 * NV * 8 * 48, NL), F32),
        in_specs=main_specs(),
        out_specs=pl.BlockSpec((4 * NV * 8 * 48, NL), lambda i: (0, 0)),
        scratch_shapes=[
            pltpu.VMEM((4, 4, 256, NL), BF16),
            pltpu.VMEM((NV * 8, 64, NL), F32),
            pltpu.VMEM((4, 3, NV * 32, NL), F32),
            pltpu.VMEM((4, NV * 4, 40, NL), F32),
            pltpu.VMEM((NV * 8 * 48, NL), F32),
            pltpu.VMEM((4, 4, 256, NL), BF16),
            pltpu.VMEM((4, NL, 4 * NL), F32),
            pltpu.VMEM((NV * 64, NL), F32),
        ],
        cost_estimate=cost(8),
        compiler_params=pltpu.CompilerParams(vmem_limit_bytes=VMEM_LIMIT),
    )(flat.reshape(4, NV * 8, ROWS, NL), flat, *operands, w["wide"], w["narrow"])


def cells_step(kept):
    shape = (NV, NZ, NR, NL)
    return pl.pallas_call(
        cells_kernel,
        out_shape=jax.ShapeDtypeStruct(shape, F32),
        in_specs=[pl.BlockSpec(memory_space=pltpu.VMEM)],
        out_specs=pl.BlockSpec(memory_space=pltpu.HBM),
        scratch_shapes=[pltpu.VMEM(shape, F32), pltpu.SemaphoreType.DMA((NV * 4,))],
        cost_estimate=cost(4),
        compiler_params=pltpu.CompilerParams(vmem_limit_bytes=VMEM_LIMIT),
    )(kept)


def rows_kernel(count_x, count_z, *refs):
    shares, out = refs[count_x - 1 :: -1], refs[count_x + 1]
    me, me_y = lax.axis_index("gx"), lax.axis_index("gy")
    row = lax.broadcasted_iota(jnp.int32, (8, NL), 0)
    lane = lax.broadcasted_iota(jnp.int32, (8, NL), 1)
    for r in range(count_x):
        at = pl.multiple_of(16 * (me ^ r), 16)
        for j in range(count_z):
            for z in range(4):
                start = 64 * j + 16 * z
                out[j, z, pl.ds(at, 16), :] = shares[r][start : start + 16, :]
    for j in range(count_z):
        turn = lanes_turn(me_y ^ (2 * j))
        piece = lax.rem(lane + (NL - turn), NL) // 21
        inside = [piece == p for p in range(5)]
        for r in range(count_x):
            i = me ^ r
            below = pl.multiple_of(16 * lax.rem(i + 1, count_x), 16)
            above = pl.multiple_of(16 * lax.rem(i + count_x - 1, count_x) + 8, 8)
            tiles = [shares[r][64 * j + 8 * g : 64 * j + 8 * g + 8, :] for g in range(8)]
            low, high = jnp.zeros((8, NL), F32), jnp.zeros((8, NL), F32)
            for p in range(5):
                back = (21 * p - 105) % NL
                low = jnp.where(inside[p], pltpu.roll(tiles[p], back, 1), low)
                extra = tiles[5 + p // 2]
                extra = extra if p % 2 else pltpu.roll(extra, 4, 0)
                high = jnp.where(inside[p], pltpu.roll(extra, back, 1), high)
            for z in range(4):
                first = pltpu.roll(low, 8 - 2 * z, 0) if z else low
                last = pltpu.roll(high, z, 0) if z else high
                out[j, z, pl.ds(below, 8), :] += jnp.where(row < 2, first, 0.0)
                out[j, z, pl.ds(above, 8), :] += jnp.where(row == 7, last, 0.0)


def rows_step(pieces, count_z, after):
    vmem = pl.BlockSpec(memory_space=pltpu.VMEM)
    count_x = len(pieces)
    return pl.pallas_call(
        functools.partial(rows_kernel, count_x, count_z),
        out_shape=jax.ShapeDtypeStruct((count_z, 4, 16 * count_x, NL), F32),
        in_specs=[vmem] * count_x + [pl.BlockSpec(memory_space=pl.ANY)],
        out_specs=vmem,
        compiler_params=pltpu.CompilerParams(vmem_limit_bytes=VMEM_LIMIT),
    )(*pieces[::-1], after)


def coarse_kernel(count_x, count_y, own, other, out_hbm, out, sems):
    me = lax.axis_index("gy")
    me_z, is_even = lax.shift_right_logical(me, 1), lax.rem(me, 2) == 0
    lane = lax.broadcasted_iota(jnp.int32, (8, NL), 1)
    place = [lax.rem(lane + NL - 35 * v, NL) for v in range(NV)]

    def block(i, _):
        rows = pl.ds(pl.multiple_of(8 * i, 8), 8)
        for z in range(4):
            pieces = []
            for j in range(count_y // 2):
                mine, theirs = own[j ^ me_z, z, rows, :], other[j ^ me_z, z, rows, :]
                pieces += [jnp.where(is_even, mine, theirs), jnp.where(is_even, theirs, mine)]
            for v in range(NV):
                at = place[v]
                for t in range(count_y // 4):
                    total = jnp.where(at < 2, pieces[4 * t - 1], 0.0)
                    total += jnp.where(at == NL - 1, pieces[(4 * t + 4) % count_y], 0.0)
                    for q in range(4):
                        inside = (at >= 32 * q - 1) & (at < 32 * q + 34)
                        total += jnp.where(inside, pieces[4 * t + q], 0.0)
                    out[v, z, rows, NL * t : NL * (t + 1)] = pltpu.roll(total, NL - 35 * v, 1) if v else total
        return 0

    def copy(i):
        rows = pl.ds(pl.multiple_of(8 * i, 8), 8)
        return pltpu.make_async_copy(out.at[:, :, rows], out_hbm.at[:, :, rows], sems.at[i])

    def one(i, _):
        block(i, 0)
        copy(i).start()
        return 0

    lax.fori_loop(0, 2 * count_x, one, 0)
    for i in range(2 * count_x):
        copy(i).wait()


def coarse_step(own, other, count_x, count_y):
    vmem = pl.BlockSpec(memory_space=pltpu.VMEM)
    shape = (NV, 4, 16 * count_x, 32 * count_y)
    return pl.pallas_call(
        functools.partial(coarse_kernel, count_x, count_y),
        out_shape=jax.ShapeDtypeStruct(shape, F32),
        in_specs=[vmem, vmem],
        out_specs=pl.BlockSpec(memory_space=pltpu.HBM),
        scratch_shapes=[pltpu.VMEM(shape, F32), pltpu.SemaphoreType.DMA((2 * count_x,))],
        compiler_params=pltpu.CompilerParams(vmem_limit_bytes=VMEM_LIMIT),
    )(own, other)


def shifted(x, axis, step):
    count = lax.axis_size(axis)
    return lax.ppermute(x, axis, [(i, (i + step) % count) for i in range(count)])


def swapped(x, axis, distance):
    return lax.ppermute(x, axis, [(i, i ^ distance) for i in range(lax.axis_size(axis))])


def body(field, masks):
    count_x, count_y = lax.axis_size("gx"), lax.axis_size("gy")
    lifted, up, down, own_masks, share = first_step(field, masks)
    south = shifted(up, "gx", -1)
    north = shifted(down, "gx", 1)
    shares = [share] + [swapped(share, "gy", r) for r in range(2, count_y, 2)]
    parts, to_left, to_right = edge_step(lift_step(lifted), lifted, north, south, own_masks)
    east = shifted(to_left, "gy", -1)
    west = shifted(to_right, "gy", 1)
    joined = join_step(shares, to_left)
    pieces = [joined] + [swapped(joined, "gx", r) for r in range(1, count_x)]
    kept = main_step(parts, east, west, own_masks, north, south)
    own = rows_step(pieces, count_y // 2, kept)
    other = swapped(own, "gy", 1)
    return cells_step(kept.reshape(4, NV * 8, 48, NL)), coarse_step(own, other, count_x, count_y)


def solution(mesh):
    placed = P(None, None, "gx", "gy")
    return jax.shard_map(
        body,
        mesh=mesh,
        in_specs=(placed, placed),
        out_specs=(placed, P()),
        check_vma=False,
    )
```

```python
import functools

import jax
import jax.numpy as jnp
import ml_dtypes
import numpy as np
from jax import lax
from jax.experimental import pallas as pl
from jax.experimental.pallas import tpu as pltpu
from jax.sharding import PartitionSpec as P

F32 = jnp.float32
BF16 = jnp.bfloat16
VMEM_LIMIT = 32 * 1024 * 1024

NV, NZ, NR, NL = 3, 16, 64, 128


def detail_row(k):
    return {2 * k + 1: 1.0, 2 * k: -0.5, 2 * k + 2: -0.5}


def smooth_row(k):
    row = {2 * k: 1.0}
    for j in (k - 1, k):
        for cell, value in detail_row(j).items():
            row[cell] = row.get(cell, 0.0) + 0.25 * value
    return row


def even_row(k):
    return {("s", k): 1.0, ("d", k - 1): -0.25, ("d", k): -0.25}


def odd_row(k):
    row = {("d", k): 1.0}
    for j in (k, k + 1):
        for name, value in even_row(j).items():
            row[name] = row.get(name, 0.0) + 0.5 * value
    return row


def as_bf16(matrix):
    cast = matrix.astype(ml_dtypes.bfloat16)
    assert (cast.astype(np.float64) == matrix).all()
    return cast


def combine(*terms):
    total = {}
    for factor, row in terms:
        for cell, value in row.items():
            total[cell] = total.get(cell, 0.0) + factor * value
    return total


def level_one_columns():
    names = {("s", k): k for k in range(65)}
    names.update({("d", k): 128 + k for k in range(65)})
    names[("d", -1)] = 128 + 65
    return names


def level_two_columns():
    names = {("s", k): k for k in range(33)}
    names.update({("d", k): 64 + k for k in range(33)})
    names[("d", -1)] = 64 + 33
    return names


def smooth_place(k):
    return k + 2


def beyond(n):
    return {"cell": 40 + 16 * n, "after": 48 + 16 * n, "before": 8 * n}


BEYOND_SMOOTH = {65: 104, -1: 32}
FROM_WEST = 40


def own_row(kind, k, n):
    place = {name: 128 + lane for name, lane in beyond(n).items()}
    if kind == "d":
        if k == -1:
            return {place["before"]: 1.0, 0: -0.5}
        if k == 64:
            return {place["after"]: 1.0}
        return {(place["cell"] if y == 128 else y): value for y, value in detail_row(k).items()}
    if k in (-2, 66):
        return {}
    if k in BEYOND_SMOOTH:
        row = {128 + BEYOND_SMOOTH[k]: 1.0}
        return combine((1.0, row), (1.0, {0: -0.125})) if k == -1 else row
    even = place["cell"] if k == 64 else 2 * k
    return combine((1.0, {even: 1.0}), (0.25, own_row("d", k - 1, n)), (0.25, own_row("d", k, n)))


@functools.lru_cache(maxsize=None)
def weights():
    w = {}
    names = level_one_columns()
    forward = np.zeros((4, 256, 256))
    inverse = np.zeros((256, 128))
    for (kind, k), column in names.items():
        for n in range(4):
            for place, value in own_row(kind, k, n).items():
                forward[n, place, column] += value
    for k in range(64):
        for y, row in ((2 * k, even_row(k)), (2 * k + 1, odd_row(k))):
            for name, value in row.items():
                inverse[names[name], y] += value
    short = np.zeros((144, 256))
    short[:128] = forward[0, :128]
    for i, lane in enumerate(beyond(0).values()):
        short[128 + i] = forward[0, 128 + lane]
    smooth = np.zeros((256, 128))
    for k in range(-2, 67):
        for place, value in own_row("s", k, 0).items():
            smooth[place, smooth_place(k)] += value
    names2 = level_two_columns()
    forward2 = np.zeros((128, 128))
    inverse2 = np.zeros((128, 128))
    for (kind, k), column in names2.items():
        for cell, value in (smooth_row(k) if kind == "s" else detail_row(k)).items():
            forward2[smooth_place(cell), column] += value
    for k in range(33):
        rows = [(2 * k, even_row(k))] + ([(2 * k + 1, odd_row(k))] if k < 32 else [])
        for y, row in rows:
            for name, value in row.items():
                inverse2[names2[name], y] += value
    back = np.zeros((256, 128))
    back[:65] = inverse[:65]
    back[128 : 128 + 65] = inverse[:65]
    spread = np.zeros((3, 128, 2, 128))
    for k in range(64):
        spread[0, k, 0, k] = 1
    for k in range(32):
        spread[0, 64 + k, 1, k] = 1
        spread[0, 64 + k, 1, 64 + k] = 1
    for at in range(0, 16, 4):
        spread[1, at, 0, 64] = 1
        spread[2, at + 1, 0, 65] = 1
        for base in (0, 64):
            spread[1, at + 2, 1, base + 32] = 1
            spread[2, at + 3, 1, base + 33] = 1
    w["wide"] = np.concatenate([short, spread.reshape(384, 256)], 0)
    own, beside = smooth[:128], smooth[128:]
    w["narrow"] = np.concatenate([inverse, own, own, beside, beside, back, forward2, inverse2], 0)
    edge = np.zeros((4, 128, 128))

    def put(n, lane, row):
        for z in range(8):
            for y, value in row.items():
                j = y - 120 if y >= 120 else y + 8
                edge[n, 16 * z + j, lane + z] += value

    part = {127: 1.0, 126: -0.5}
    for n in range(4):
        put(n, beyond(n)["cell"], {0: 1.0})
        put(n, beyond(n)["after"], detail_row(0))
        put(n, beyond(n)["before"], part)
    put(0, BEYOND_SMOOTH[65], combine((1.0, smooth_row(1)), (-0.5, smooth_row(2))))
    share = combine((1.0, {126: 1.0}), (0.25, detail_row(62)), (0.25, part))
    put(0, BEYOND_SMOOTH[-1], combine((1.0, share), (-0.5, smooth_row(62))))
    w["edge"] = edge.reshape(512, 128)
    expand = np.zeros((2, 4, 128))
    for j in range(4):
        expand[0, j, 16 * j : 16 * j + 16] = 1
        expand[1, j, 64 + 8 * j : 64 + 8 * j + 8] = 1
    twice = combine(*[(value, smooth_row(k)) for k, value in smooth_row(0).items()])
    columns = np.zeros((2, 128, 128))
    for m in range(-1, 34):
        for t, value in twice.items():
            if 0 <= 4 * m + t < NL:
                columns[:, 4 * m + t, m + 1] = value
    rows = np.zeros((4, 32, 2, 64))
    for z in range(4):
        places = {m: m for m in range(16)}
        places.update({16: 16 + 2 * z, 17: 17 + 2 * z, -1: 16 + 15 - z})
        for m, place in places.items():
            for t, value in twice.items():
                if 0 <= 4 * m + t < NR:
                    rows[z, place, :, 4 * m + t] = value
    pad = np.zeros((8, 128))
    w["first"] = np.concatenate([columns.reshape(256, 128), rows.reshape(128, 128), expand.reshape(8, 128), pad], 0)
    return {name: as_bf16(matrix) for name, matrix in w.items()}


def two_terms(x):
    high = x.astype(BF16)
    low = (x - high.astype(F32)).astype(BF16)
    return high, low


def cost(gigaflops):
    return pl.CostEstimate(flops=gigaflops * 10**9, bytes_accessed=8 * 10**6, transcendentals=0)


def dot(a, b):
    return jnp.dot(a, b, preferred_element_type=F32)


def lift_planes(cells):
    half = len(cells) // 2
    even, odd = cells[0::2], cells[1::2]
    detail = [odd[k] - 0.5 * (even[k] + even[min(k + 1, half - 1)]) for k in range(half)]
    smooth = [even[k] + 0.25 * (detail[max(k - 1, 0)] + detail[k]) for k in range(half)]
    return smooth, detail


def unlift_planes(smooth, detail):
    half = len(smooth)
    even = [smooth[k] - 0.25 * (detail[max(k - 1, 0)] + detail[k]) for k in range(half)]
    out = []
    for k in range(half):
        out += [even[k], detail[k] + 0.5 * (even[k] + even[min(k + 1, half - 1)])]
    return out


def lift_rows(load, start):
    even, odd, after = load(start), load(start + 1), load(start + 2)
    before, odd_before = load(start - 2), load(start - 1)
    detail = odd - 0.5 * (even + after)
    detail_before = odd_before - 0.5 * (before + even)
    return even + 0.25 * (detail_before + detail), detail


def unlift_rows(smooth, detail, row):
    here, after = detail(row), detail(row + 1)
    even = smooth(row) - 0.25 * (detail(row - 1) + here)
    next_even = smooth(row + 1) - 0.25 * (here + after)
    return even, here + 0.5 * (even + next_even)


PITCH = 80


def lanes_turn(j):
    return lax.rem(32 * lax.rem(j, 4) + NL - 1, NL)


def first_kernel(
    field, masks_hbm, table_hbm, lifted, up, down, own_masks, share, cells, twice, masks, table, sems
):
    small = [
        pltpu.make_async_copy(masks_hbm, masks, sems.at[0]),
        pltpu.make_async_copy(table_hbm, table, sems.at[1]),
    ]
    copies = []
    for v in range(NV):
        for c in range(4):
            part = pl.ds(16 * c, 16)
            copies.append(pltpu.make_async_copy(field.at[v, :, part], cells.at[v, :, part], sems.at[2 + 4 * v + c]))
    for copy in small + copies:
        copy.start()
    for p in range(NV * NZ):
        lifted[p * PITCH : p * PITCH + 8, :] = jnp.zeros((8, NL), F32)
        lifted[p * PITCH + 72 : p * PITCH + 80, :] = jnp.zeros((8, NL), F32)
    for copy in small:
        copy.wait()
    for i, out, tile in ((0, up, 15), (1, down, 9)):
        total = jnp.zeros((7, NL), F32)
        for l in range(2):
            flags = masks[l, i].astype(F32).astype(BF16)
            spread = table[384 + 4 * l : 388 + 4 * l, :]
            total += lax.dot_general(flags, spread, (((0,), (0,)), ((), ())), preferred_element_type=F32)
        own_masks[i] = jnp.concatenate([total, jnp.zeros((1, NL), F32)], 0)
        out[tile] = own_masks[i]

    for v in range(NV):
        for t in range(8):
            if t % 2 == 0:
                copies[4 * v + t // 2].wait()
            smooth, detail = lift_planes([cells[v, z, 8 * t : 8 * t + 8, :] for z in range(NZ)])
            for k, tile in enumerate(smooth + detail):
                start = (v * NZ + k) * PITCH + 8 + 8 * t
                lifted[start : start + 8, :] = tile
            for k, tile in enumerate(lift_planes(smooth)[0]):
                twice[v * 4 + k, 8 * t : 8 * t + 8, :] = tile
        for bz in range(2):

            def row(x):
                return lifted[pl.ds((v * NZ + bz * 8) * PITCH + 8 + x, 8, stride=PITCH), :]

            x = [row(j) for j in range(7 if bz == 0 else 3)]
            first = x[1] - 0.5 * (x[0] + x[2])
            up[v * 5 + bz] = x[0]
            up[v * 5 + 2 + bz] = first
            y = {j: row(j) for j in (range(58, 64) if bz == 0 else (62, 63))}
            part = y[63] - 0.5 * y[62]
            down[v * 3 + bz] = part
            if bz == 0:
                second = x[3] - 0.5 * (x[2] + x[4])
                third = x[5] - 0.5 * (x[4] + x[6])
                up[v * 5 + 4] = x[2] + 0.25 * (first + second) - 0.5 * (x[4] + 0.25 * (second + third))
                before = y[59] - 0.5 * (y[58] + y[60])
                last = y[61] - 0.5 * (y[60] + y[62])
                down[v * 3 + 2] = y[62] + 0.25 * (last + part) - 0.5 * (y[60] + 0.25 * (before + last))

    total = jnp.zeros((80, NL), F32)
    for v in range(NV):
        main, extra = [], jnp.zeros((16, NL), F32)
        for z in range(4):
            terms = jnp.concatenate(two_terms(twice[v * 4 + z]), 0)
            part = dot(table[256 + 32 * z : 288 + 32 * z, :], terms)
            main.append(part[:16])
            extra += part[16:]
        terms = jnp.concatenate(two_terms(jnp.concatenate(main + [extra], 0)), 1)
        part = dot(terms, table[0:256, :])
        total += pltpu.roll(part, 35 * v, 1) if v else part
    turn = lanes_turn(lax.axis_index("gy"))
    lane = lax.broadcasted_iota(jnp.int32, (8, NL), 1)
    spare = (lane >= 105) & (lane < 126)
    upper = lax.broadcasted_iota(jnp.int32, (8, NL), 0) < 4
    below, above = total[64:72], total[72:80]
    pieces = [pltpu.roll(above, 105 - 21 * p, 1) for p in range(5)]
    for g in range(8):
        if g < 5:
            extra = pltpu.roll(below, 105 - 21 * g, 1)
        else:
            extra = pltpu.roll(pieces[2 * g - 10], 4, 0)
            extra = jnp.where(upper, extra, pieces[2 * g - 9] if g < 7 else 0.0)
        tile = jnp.where(spare, extra, total[8 * g : 8 * g + 8])
        share[8 * g : 8 * g + 8, :] = pltpu.roll(tile, turn, 1)


def in_hbm(x):
    return pltpu.with_memory_space_constraint(x, pltpu.HBM)


def first_step(field, masks):
    vmem = pl.BlockSpec(memory_space=pltpu.VMEM)
    shapes = [(NV * NZ * PITCH, NL), (16, 8, NL), (10, 8, NL), (2, 8, NL), (64, NL)]
    return pl.pallas_call(
        first_kernel,
        out_shape=[jax.ShapeDtypeStruct(s, F32) for s in shapes],
        in_specs=[pl.BlockSpec(memory_space=pltpu.HBM)] * 3,
        out_specs=[vmem] * 5,
        scratch_shapes=[
            pltpu.VMEM((NV, NZ, NR, NL), F32),
            pltpu.VMEM((NV * 4, NR, NL), F32),
            pltpu.VMEM((2, 2, 4, 7), jnp.int32),
            pltpu.VMEM((400, NL), BF16),
            pltpu.SemaphoreType.DMA((4 * NV + 2,)),
        ],
        compiler_params=pltpu.CompilerParams(vmem_limit_bytes=VMEM_LIMIT),
    )(*[in_hbm(x) for x in (field, masks.transpose(0, 2, 3, 1), jnp.asarray(weights()["first"]))])


ROWS = 40


def lift_kernel(lifted, parts):
    def lift(step, _):
        v, bz = step // 2, lax.rem(step, 2)
        for z in range(8):
            start = pl.multiple_of((step * 8 + z) * PITCH, 8)
            for t in range(4):
                pair = lift_rows(lambda s: lifted[pl.ds(start + 16 * t + s, 8, stride=2), :], 8)
                for bx in range(2):
                    plane = (2 * bz + bx) * 24 + v * 8 + z
                    parts[pl.ds(pl.multiple_of(plane * ROWS + 8 * t, 8), 8), :] = pair[bx]
        return 0

    lax.fori_loop(0, NV * 2, lift, 0)


def lift_step(lifted):
    vmem = pl.BlockSpec(memory_space=pltpu.VMEM)
    return pl.pallas_call(
        lift_kernel,
        out_shape=jax.ShapeDtypeStruct((4 * NV * 8 * ROWS, NL), F32),
        in_specs=[vmem],
        out_specs=vmem,
        compiler_params=pltpu.CompilerParams(vmem_limit_bytes=VMEM_LIMIT),
    )(lifted)


def edge_kernel(parts_in, lifted, north, south, own_masks, table_hbm, parts, to_left, to_right, packed, table, sem):
    copy = pltpu.make_async_copy(table_hbm, table, sem.at[0])
    copy.start()
    for p in range(4 * NV * 8):
        parts[p * ROWS + 32 : p * ROWS + 40, :] = jnp.zeros((8, NL), F32)
    for v in range(NV):
        for bz in range(2):

            def cell(x):
                return lifted[pl.ds((v * NZ + bz * 8) * PITCH + 8 + x, 8, stride=PITCH), :]

            def at(bx, r):
                return pl.ds(((2 * bz + bx) * 24 + v * 8) * ROWS + r, 8, stride=ROWS)

            before, after, detail = north[v * 3 + bz], south[v * 5 + bz], south[v * 5 + 2 + bz]
            start = cell(0)
            last = cell(63) - 0.5 * (cell(62) + after)
            parts[at(0, 0), :] = parts[at(0, 0), :] + 0.25 * before
            parts[at(0, 31), :] = parts[at(0, 31), :] - 0.125 * after
            parts[at(1, 31), :] = parts[at(1, 31), :] - 0.5 * after
            parts[at(0, 32), :] = after + 0.25 * (last + detail)
            parts[at(1, 32), :] = detail
            parts[at(1, 39), :] = before - 0.5 * start
            if bz == 0:
                parts[at(0, 33), :] = south[v * 5 + 4]
                parts[at(0, 39), :] = north[v * 3 + 2] - 0.125 * start

    lane = lax.broadcasted_iota(jnp.int32, (8, NL), 1) // 16

    def pack(v, _):
        for n in range(4):
            for t in range(5):
                tile = jnp.zeros((8, NL), F32)
                for z in range(8):
                    start = (n * 24 + v * 8 + z) * ROWS + 8 * t
                    x = parts[pl.ds(pl.multiple_of(start, 8), 8), :]
                    tile = jnp.where(lane == z, pltpu.roll(x, (8 + 16 * z) % NL, 1), tile)
                packed[pl.ds(pl.multiple_of(n * 120 + v * ROWS + 8 * t, 8), 8), :] = tile
        return 0

    lax.fori_loop(0, NV, pack, 0)
    copy.wait()
    terms = [two_terms(packed[n * 120 : (n + 1) * 120, :]) for n in range(4)]
    high, low = [jnp.concatenate(part, 1) for part in zip(*terms)]
    sides = dot(high, table[...]) + dot(low, table[...])
    lane = lax.broadcasted_iota(jnp.int32, (ROWS, NL), 1)
    each = [sides[v * ROWS : (v + 1) * ROWS] for v in range(NV)]
    right = jnp.where(lane < 40, each[0], pltpu.roll(each[1], 40, 1))
    to_right[0:ROWS, :] = jnp.where(lane < 80, right, pltpu.roll(each[2], 80, 1))
    last = jnp.where(lane < 32, pltpu.roll(each[2], NL - 40, 1), pltpu.roll(each[2], NL - 72, 1))
    to_left[0:ROWS, :] = jnp.where(lane < 40, last, each[0])
    to_left[ROWS : 2 * ROWS, :] = jnp.where(lane < 32, pltpu.roll(each[2], NL - 72, 1), each[1])
    lane = lax.broadcasted_iota(jnp.int32, (8, NL), 1)
    ends = jnp.zeros((8, NL), F32)
    for ib, tile in enumerate((north[9], own_masks[0], own_masks[1], south[15])):
        for j, source in enumerate((0, 63, 64, 95)):
            target = 4 * ib + j
            ends = jnp.where(lane == target, pltpu.roll(tile, (target - source) % NL, 1), ends)
    to_left[2 * ROWS : 2 * ROWS + 8, :] = ends
    to_right[ROWS : ROWS + 8, :] = ends


def edge_step(parts, lifted, north, south, own_masks):
    vmem = pl.BlockSpec(memory_space=pltpu.VMEM)
    shapes = [(4 * NV * 8 * ROWS, NL), (2 * ROWS + 8, NL), (ROWS + 8, NL)]
    return pl.pallas_call(
        edge_kernel,
        out_shape=[jax.ShapeDtypeStruct(s, F32) for s in shapes],
        in_specs=[vmem] * 5 + [pl.BlockSpec(memory_space=pltpu.HBM)],
        out_specs=[vmem] * 3,
        input_output_aliases={0: 0},
        cost_estimate=cost(20),
        scratch_shapes=[pltpu.VMEM((480, NL), F32), pltpu.VMEM((512, NL), BF16), pltpu.SemaphoreType.DMA((1,))],
        compiler_params=pltpu.CompilerParams(vmem_limit_bytes=VMEM_LIMIT),
    )(parts, lifted, north, south, own_masks, in_hbm(jnp.asarray(weights()["edge"])))


def join_kernel(*refs):
    shares, out = refs[-3::-1], refs[-1]
    for n, piece in enumerate(shares):
        out[64 * n : 64 * (n + 1), :] = piece[...]


def join_step(shares, after):
    vmem = pl.BlockSpec(memory_space=pltpu.VMEM)
    return pl.pallas_call(
        join_kernel,
        out_shape=jax.ShapeDtypeStruct((64 * len(shares), NL), F32),
        in_specs=[vmem] * len(shares) + [pl.BlockSpec(memory_space=pl.ANY)],
        out_specs=vmem,
        cost_estimate=cost(20),
        compiler_params=pltpu.CompilerParams(vmem_limit_bytes=VMEM_LIMIT),
    )(*shares[::-1], after)


def mask_lanes(west, east, own_masks, north_mask, south_mask, wide):
    group = lax.broadcasted_iota(jnp.int32, (8, NL), 1) // 4
    masks = [
        jnp.concatenate([jnp.where(group == ib, tile, 0.0) for ib in range(4)], 0)
        for tile in (east[2 * ROWS : 2 * ROWS + 8, :], west[ROWS : ROWS + 8, :])
    ]
    own = jnp.concatenate([north_mask[0], own_masks[0], own_masks[1], south_mask[0]], 0)
    flags = jnp.concatenate([own] + masks, 1).astype(BF16)
    return dot(flags, wide[144:528, :])


def beside_tiles(west, east, at, count):
    lane = lax.broadcasted_iota(jnp.int32, (count, NL), 1)
    left = west[at : at + count, :]
    first, second = east[at : at + count, :], east[ROWS + at : ROWS + at + count, :]
    third = jnp.where(lane < 104, pltpu.roll(second, 72, 1), pltpu.roll(first, 72, 1))
    third = jnp.where(lane < 72, pltpu.roll(first, 40, 1), third)
    tiles = []
    for v, right in enumerate((first, second, third)):
        beside = jnp.where(lane < FROM_WEST, pltpu.roll(left, NL - 40 * v, 1) if v else left, right)
        tiles += [pltpu.roll(beside, NL - z, 1) if z else beside for z in range(8)]
    return tiles


def beside_terms(west, east, at, count):
    return jnp.concatenate(two_terms(jnp.concatenate(beside_tiles(west, east, at, count), 0)), 1)


def own_terms(planes, at, count):
    return jnp.concatenate(two_terms(planes[:, at : at + count, :].reshape(24 * count, NL)), 1)


def main_kernel(
    parts, flat, east, west, own_masks, north_mask, south_mask, wide, narrow,
    kept,
    gain2, low, second, kept2, low_back, gain, sides_wide, turned,
):
    inverse, smooth_own, smooth_beside = narrow.at[0:256], narrow.at[256:512], narrow.at[512:768]
    back, forward2, inverse2 = narrow.at[768:1024], narrow.at[1024:1152], narrow.at[1152:1280]
    lanes = mask_lanes(west, east, own_masks, north_mask, south_mask, wide)
    lane64 = lax.broadcasted_iota(jnp.int32, (1, NL), 1) < 64
    forward2_f = forward2[...].astype(F32)
    for ib in range(4):
        for n in range(4) if ib else (1, 3):
            b = 8 * ib + 4 * (n // 2) + n % 2 - 1
            smooth_two = lanes[b : b + 1, NL:] if n else jnp.ones((1, NL), F32)
            row = jnp.where(lane64, smooth_two, lanes[b + 2 : b + 3, NL:])
            both = dot((forward2_f * row).astype(BF16), inverse2[...]).astype(BF16)
            gain2[ib, n, 0:128, :] = both
            gain2[ib, n, 128:256, :] = both

    for at, count in ((0, 16), (16, 16), (32, 8)):
        part = dot(own_terms(parts.at[0], at, count), smooth_own[...])
        part += dot(beside_terms(west, east, at, count), smooth_beside[...])
        part = part.reshape(24, count, NL)
        if at < 32:
            low[:, 8 + at : 8 + at + count, :] = part
            if at == 0:
                low[:, 56:64, :] = part[:, 0:8]
        else:
            low[:, 0:8, :] = part
            low[:, 40:48, :] = part
            low[:, 48:56, :] = part

    def rows_two(v, _):
        for t in range(3):
            lifted = [
                lift_rows(lambda s: low[v * 8 + p, pl.ds(16 * t + s, 8, stride=2), :], 8) for p in range(8)
            ]
            for bx in range(2):
                smooth, detail = lift_planes([pair[bx] for pair in lifted])
                for bz, part in ((0, smooth), (1, detail)):
                    for z in range(4):
                        second[2 * bz + bx, t, pl.ds(pl.multiple_of((v * 4 + z) * 8, 8), 8), :] = part[z]
        return 0

    lax.fori_loop(0, NV, rows_two, 0)
    for n in range(4):
        for t in range(3):
            terms = jnp.concatenate(two_terms(second[n, t]), 1)
            if t < 2:
                kept2[n, :, 8 + 8 * t : 16 + 8 * t, :] = dot(terms, gain2[t + 1, n]).reshape(NV * 4, 8, NL)
            else:
                if n % 2:
                    kept2[n, :, 0:8, :] = dot(terms, gain2[0, n]).reshape(NV * 4, 8, NL)
                kept2[n, :, 24:32, :] = dot(terms, gain2[3, n]).reshape(NV * 4, 8, NL)

    def back_two(v, _):
        for t in range(3):
            pairs = {}
            for bz in range(2):
                for z in range(4):
                    p = v * 4 + z
                    if t < 2:
                        pairs[bz, z] = unlift_rows(
                            lambda r: kept2[2 * bz, p, pl.ds(r, 8), :],
                            lambda r: kept2[2 * bz + 1, p, pl.ds(r, 8), :],
                            8 + 8 * t,
                        )
                    else:
                        even = kept2[2 * bz, p, 24:32, :] - 0.25 * (
                            kept2[2 * bz + 1, p, 23:31, :] + kept2[2 * bz + 1, p, 24:32, :]
                        )
                        pairs[bz, z] = (even, even)
            for parity in range(2 if t < 2 else 1):
                planes = unlift_planes([pairs[0, z][parity] for z in range(4)], [pairs[1, z][parity] for z in range(4)])
                for z in range(8):
                    low_back[pl.ds((v * 8 + z) * 48 + 16 * t + parity, 8, stride=2), :] = planes[z]
        return 0

    lax.fori_loop(0, NV, back_two, 0)

    forward_f = wide[0:144, :].astype(F32)
    for ib in range(4):
        sides_wide[ib] = jnp.zeros((NL, 4 * NL), F32)
    for ib in range(4):
        for n in range(4) if ib else (1, 3):
            b = 8 * ib + 4 * (n // 2) + n % 2 - 1
            smooth_one = lanes[b : b + 1, 0:NL] if n else jnp.zeros((1, NL), F32)
            row = jnp.concatenate([smooth_one, lanes[b + 2 : b + 3, 0:NL]], 1)
            both = dot((forward_f * row).astype(BF16), inverse[...])
            main = both[0:128].astype(BF16)
            gain[ib, n, 0:128, :] = main
            gain[ib, n, 128:256, :] = main
            for i in range(3):
                at = list(beyond(n).values())[i]
                sides_wide[ib, at : at + 1, n * NL : (n + 1) * NL] = both[128 + i : 129 + i]

    gain_sides = []
    for ib in range(4):
        side = sides_wide[ib].astype(BF16)
        gain_sides.append(jnp.concatenate([side, side], 0))
    def put(n, p, at, rows):
        start = pl.multiple_of((n * 24 + p) * 48 + 8 + at, 8)
        kept[pl.ds(start, rows.shape[0]), :] = rows

    def row_of(ref, first, pitch):
        return ref[pl.ds(first, 24, stride=pitch), :]

    for ib in range(2):
        product = dot(beside_terms(west, east, 16 * ib, 16), gain_sides[ib + 1])
        for n in range(4):
            for p in range(24):
                put(n, p, 16 * ib, product[16 * p : 16 * p + 16, n * NL : (n + 1) * NL])

    def keep(n, _):
        for ib in range(2):
            product = dot(own_terms(parts.at[n], 16 * ib, 16), gain[ib + 1, n])
            for p in range(24):
                start = pl.ds(pl.multiple_of((n * 24 + p) * 48 + 8 + 16 * ib, 8), 16)
                kept[start, :] += product[16 * p : 16 * p + 16]
        return 0

    lax.fori_loop(0, 4, keep, 0)
    for ib in range(2):
        rows = jnp.concatenate([low_back[48 * p + 16 * ib : 48 * p + 16 * ib + 16, :] for p in range(24)], 0)
        product = dot(jnp.concatenate(two_terms(rows), 1), back[...])
        for p in range(24):
            start = 48 * p + 8 + 16 * ib
            kept[start : start + 16, :] += product[16 * p : 16 * p + 16]
    tiles = beside_tiles(west, east, 32, 8)
    for p in range(24):
        turned[8 * p : 8 * p + 8, :] = tiles[p]
    for first, ib, place, row in ((0, 3, 40, 32), (7, 0, 7, 39)):
        beside = dot(jnp.concatenate(two_terms(row_of(turned, first, 8)), 1), gain_sides[ib])
        for n in range(4) if ib else (1, 3):
            own = jnp.concatenate(two_terms(row_of(flat, n * 24 * ROWS + row, ROWS)), 1)
            total = beside[:, n * NL : (n + 1) * NL] + dot(own, gain[ib, n])
            if n == 0:
                total += dot(jnp.concatenate(two_terms(row_of(low_back, row, 48)), 1), back[...])
            kept[pl.ds(n * 24 * 48 + place, 24, stride=48), :] = total


def cells_kernel(kept, out, cells, sems):
    def back_one(step, _):
        v, t = step // 4, step % 4
        pairs = {}
        for bz in range(2):
            for z in range(8):
                p = v * 8 + z
                pairs[bz, z] = unlift_rows(
                    lambda r: kept[2 * bz, p, pl.ds(8 * t + r, 8), :],
                    lambda r: kept[2 * bz + 1, p, pl.ds(8 * t + r, 8), :],
                    8,
                )
        for parity in range(2):
            planes = unlift_planes([pairs[0, z][parity] for z in range(8)], [pairs[1, z][parity] for z in range(8)])
            for z in range(NZ):
                cells[v, z, pl.ds(16 * t + parity, 8, stride=2), :] = planes[z]
        return 0

    def copy(step):
        v, rows = step // 4, pl.ds(pl.multiple_of(16 * (step % 4), 16), 16)
        return pltpu.make_async_copy(cells.at[v, :, rows], out.at[v, :, rows], sems.at[step])

    def one(step, _):
        back_one(step, 0)
        copy(step).start()
        return 0

    lax.fori_loop(0, NV * 4, one, 0)
    for step in range(NV * 4):
        copy(step).wait()


def main_specs():
    vmem = pl.BlockSpec(memory_space=pltpu.VMEM)
    return [
        vmem, vmem, vmem, vmem, vmem,
        pl.BlockSpec((1, 8, NL), lambda i: (9, 0, 0)), pl.BlockSpec((1, 8, NL), lambda i: (15, 0, 0)),
        vmem, vmem,
    ]


def main_step(flat, *operands):
    w = weights()
    return pl.pallas_call(
        main_kernel,
        grid=(1,),
        out_shape=jax.ShapeDtypeStruct((4 * NV * 8 * 48, NL), F32),
        in_specs=main_specs(),
        out_specs=pl.BlockSpec((4 * NV * 8 * 48, NL), lambda i: (0, 0)),
        scratch_shapes=[
            pltpu.VMEM((4, 4, 256, NL), BF16),
            pltpu.VMEM((NV * 8, 64, NL), F32),
            pltpu.VMEM((4, 3, NV * 32, NL), F32),
            pltpu.VMEM((4, NV * 4, 40, NL), F32),
            pltpu.VMEM((NV * 8 * 48, NL), F32),
            pltpu.VMEM((4, 4, 256, NL), BF16),
            pltpu.VMEM((4, NL, 4 * NL), F32),
            pltpu.VMEM((NV * 64, NL), F32),
        ],
        cost_estimate=cost(8),
        compiler_params=pltpu.CompilerParams(vmem_limit_bytes=VMEM_LIMIT),
    )(flat.reshape(4, NV * 8, ROWS, NL), flat, *operands, w["wide"], w["narrow"])


def cells_step(kept):
    shape = (NV, NZ, NR, NL)
    return pl.pallas_call(
        cells_kernel,
        out_shape=jax.ShapeDtypeStruct(shape, F32),
        in_specs=[pl.BlockSpec(memory_space=pltpu.VMEM)],
        out_specs=pl.BlockSpec(memory_space=pltpu.HBM),
        scratch_shapes=[pltpu.VMEM(shape, F32), pltpu.SemaphoreType.DMA((NV * 4,))],
        cost_estimate=cost(4),
        compiler_params=pltpu.CompilerParams(vmem_limit_bytes=VMEM_LIMIT),
    )(kept)


def rows_kernel(count_x, count_z, *refs):
    shares, out = refs[count_x - 1 :: -1], refs[count_x + 1]
    me, me_y = lax.axis_index("gx"), lax.axis_index("gy")
    row = lax.broadcasted_iota(jnp.int32, (8, NL), 0)
    lane = lax.broadcasted_iota(jnp.int32, (8, NL), 1)
    for r in range(count_x):
        at = pl.multiple_of(16 * (me ^ r), 16)
        for j in range(count_z):
            for z in range(4):
                start = 64 * j + 16 * z
                out[j, z, pl.ds(at, 16), :] = shares[r][start : start + 16, :]
    for j in range(count_z):
        turn = lanes_turn(me_y ^ (2 * j))
        piece = lax.rem(lane + (NL - turn), NL) // 21
        inside = [piece == p for p in range(5)]
        for r in range(count_x):
            i = me ^ r
            below = pl.multiple_of(16 * lax.rem(i + 1, count_x), 16)
            above = pl.multiple_of(16 * lax.rem(i + count_x - 1, count_x) + 8, 8)
            tiles = [shares[r][64 * j + 8 * g : 64 * j + 8 * g + 8, :] for g in range(8)]
            low, high = jnp.zeros((8, NL), F32), jnp.zeros((8, NL), F32)
            for p in range(5):
                back = (21 * p - 105) % NL
                low = jnp.where(inside[p], pltpu.roll(tiles[p], back, 1), low)
                extra = tiles[5 + p // 2]
                extra = extra if p % 2 else pltpu.roll(extra, 4, 0)
                high = jnp.where(inside[p], pltpu.roll(extra, back, 1), high)
            for z in range(4):
                first = pltpu.roll(low, 8 - 2 * z, 0) if z else low
                last = pltpu.roll(high, z, 0) if z else high
                out[j, z, pl.ds(below, 8), :] += jnp.where(row < 2, first, 0.0)
                out[j, z, pl.ds(above, 8), :] += jnp.where(row == 7, last, 0.0)


def rows_step(pieces, count_z, after):
    vmem = pl.BlockSpec(memory_space=pltpu.VMEM)
    count_x = len(pieces)
    return pl.pallas_call(
        functools.partial(rows_kernel, count_x, count_z),
        out_shape=jax.ShapeDtypeStruct((count_z, 4, 16 * count_x, NL), F32),
        in_specs=[vmem] * count_x + [pl.BlockSpec(memory_space=pl.ANY)],
        out_specs=vmem,
        compiler_params=pltpu.CompilerParams(vmem_limit_bytes=VMEM_LIMIT),
    )(*pieces[::-1], after)


def coarse_kernel(count_x, count_y, own, other, out_hbm, out, sems):
    me = lax.axis_index("gy")
    me_z, is_even = lax.shift_right_logical(me, 1), lax.rem(me, 2) == 0
    lane = lax.broadcasted_iota(jnp.int32, (8, NL), 1)
    place = [lax.rem(lane + NL - 35 * v, NL) for v in range(NV)]

    def plane(z, _):
        def block(i, _):
            rows = pl.ds(pl.multiple_of(8 * i, 8), 8)
            pieces = []
            for j in range(count_y // 2):
                mine, theirs = own[j ^ me_z, z, rows, :], other[j ^ me_z, z, rows, :]
                pieces += [jnp.where(is_even, mine, theirs), jnp.where(is_even, theirs, mine)]
            for v in range(NV):
                at = place[v]
                for t in range(count_y // 4):
                    total = jnp.where(at < 2, pieces[4 * t - 1], 0.0)
                    total += jnp.where(at == NL - 1, pieces[(4 * t + 4) % count_y], 0.0)
                    for q in range(4):
                        inside = (at >= 32 * q - 1) & (at < 32 * q + 34)
                        total += jnp.where(inside, pieces[4 * t + q], 0.0)
                    out[v, z, rows, NL * t : NL * (t + 1)] = pltpu.roll(total, NL - 35 * v, 1) if v else total
            return 0

        def four(i, _):
            for k in range(4):
                block(4 * i + k, 0)
            return 0

        lax.fori_loop(0, count_x // 2, four, 0)
        for v in range(NV):
            copy(v, z).start()
        return 0

    def copy(v, z):
        return pltpu.make_async_copy(out.at[v, z], out_hbm.at[v, z], sems.at[v, z])

    lax.fori_loop(0, 4, plane, 0)
    for v in range(NV):
        for z in range(4):
            copy(v, z).wait()


def coarse_step(own, other, count_x, count_y):
    vmem = pl.BlockSpec(memory_space=pltpu.VMEM)
    shape = (NV, 4, 16 * count_x, 32 * count_y)
    return pl.pallas_call(
        functools.partial(coarse_kernel, count_x, count_y),
        out_shape=jax.ShapeDtypeStruct(shape, F32),
        in_specs=[vmem, vmem],
        out_specs=pl.BlockSpec(memory_space=pltpu.HBM),
        scratch_shapes=[pltpu.VMEM(shape, F32), pltpu.SemaphoreType.DMA((NV, 4))],
        compiler_params=pltpu.CompilerParams(vmem_limit_bytes=VMEM_LIMIT),
    )(own, other)


def shifted(x, axis, step):
    count = lax.axis_size(axis)
    return lax.ppermute(x, axis, [(i, (i + step) % count) for i in range(count)])


def swapped(x, axis, distance):
    return lax.ppermute(x, axis, [(i, i ^ distance) for i in range(lax.axis_size(axis))])


def body(field, masks):
    count_x, count_y = lax.axis_size("gx"), lax.axis_size("gy")
    lifted, up, down, own_masks, share = first_step(field, masks)
    south = shifted(up, "gx", -1)
    north = shifted(down, "gx", 1)
    shares = [share] + [swapped(share, "gy", r) for r in range(2, count_y, 2)]
    parts, to_left, to_right = edge_step(lift_step(lifted), lifted, north, south, own_masks)
    east = shifted(to_left, "gy", -1)
    west = shifted(to_right, "gy", 1)
    joined = join_step(shares, to_left)
    pieces = [joined] + [swapped(joined, "gx", r) for r in range(1, count_x)]
    kept = main_step(parts, east, west, own_masks, north, south)
    own = rows_step(pieces, count_y // 2, kept)
    other = swapped(own, "gy", 1)
    return cells_step(kept.reshape(4, NV * 8, 48, NL)), coarse_step(own, other, count_x, count_y)


def solution(mesh):
    placed = P(None, None, "gx", "gy")
    return jax.shard_map(
        body,
        mesh=mesh,
        in_specs=(placed, placed),
        out_specs=(placed, P()),
        check_vma=False,
    )
```

```python
import functools

import jax
import jax.numpy as jnp
import ml_dtypes
import numpy as np
from jax import lax
from jax.experimental import pallas as pl
from jax.experimental.pallas import tpu as pltpu
from jax.sharding import PartitionSpec as P

F32 = jnp.float32
BF16 = jnp.bfloat16
VMEM_LIMIT = 32 * 1024 * 1024

NV, NZ, NR, NL = 3, 16, 64, 128


def detail_row(k):
    return {2 * k + 1: 1.0, 2 * k: -0.5, 2 * k + 2: -0.5}


def smooth_row(k):
    row = {2 * k: 1.0}
    for j in (k - 1, k):
        for cell, value in detail_row(j).items():
            row[cell] = row.get(cell, 0.0) + 0.25 * value
    return row


def even_row(k):
    return {("s", k): 1.0, ("d", k - 1): -0.25, ("d", k): -0.25}


def odd_row(k):
    row = {("d", k): 1.0}
    for j in (k, k + 1):
        for name, value in even_row(j).items():
            row[name] = row.get(name, 0.0) + 0.5 * value
    return row


def as_bf16(matrix):
    cast = matrix.astype(ml_dtypes.bfloat16)
    assert (cast.astype(np.float64) == matrix).all()
    return cast


def combine(*terms):
    total = {}
    for factor, row in terms:
        for cell, value in row.items():
            total[cell] = total.get(cell, 0.0) + factor * value
    return total


def level_one_columns():
    names = {("s", k): k for k in range(65)}
    names.update({("d", k): 128 + k for k in range(65)})
    names[("d", -1)] = 128 + 65
    return names


def level_two_columns():
    names = {("s", k): k for k in range(33)}
    names.update({("d", k): 64 + k for k in range(33)})
    names[("d", -1)] = 64 + 33
    return names


def smooth_place(k):
    return k + 2


def beyond(n):
    return {"cell": 40 + 16 * n, "after": 48 + 16 * n, "before": 8 * n}


BEYOND_SMOOTH = {65: 104, -1: 32}
FROM_WEST = 40


def own_row(kind, k, n):
    place = {name: 128 + lane for name, lane in beyond(n).items()}
    if kind == "d":
        if k == -1:
            return {place["before"]: 1.0, 0: -0.5}
        if k == 64:
            return {place["after"]: 1.0}
        return {(place["cell"] if y == 128 else y): value for y, value in detail_row(k).items()}
    if k in (-2, 66):
        return {}
    if k in BEYOND_SMOOTH:
        row = {128 + BEYOND_SMOOTH[k]: 1.0}
        return combine((1.0, row), (1.0, {0: -0.125})) if k == -1 else row
    even = place["cell"] if k == 64 else 2 * k
    return combine((1.0, {even: 1.0}), (0.25, own_row("d", k - 1, n)), (0.25, own_row("d", k, n)))


@functools.lru_cache(maxsize=None)
def weights():
    w = {}
    names = level_one_columns()
    forward = np.zeros((4, 256, 256))
    inverse = np.zeros((256, 128))
    for (kind, k), column in names.items():
        for n in range(4):
            for place, value in own_row(kind, k, n).items():
                forward[n, place, column] += value
    for k in range(64):
        for y, row in ((2 * k, even_row(k)), (2 * k + 1, odd_row(k))):
            for name, value in row.items():
                inverse[names[name], y] += value
    short = np.zeros((144, 256))
    short[:128] = forward[0, :128]
    for i, lane in enumerate(beyond(0).values()):
        short[128 + i] = forward[0, 128 + lane]
    smooth = np.zeros((256, 128))
    for k in range(-2, 67):
        for place, value in own_row("s", k, 0).items():
            smooth[place, smooth_place(k)] += value
    names2 = level_two_columns()
    forward2 = np.zeros((128, 128))
    inverse2 = np.zeros((128, 128))
    for (kind, k), column in names2.items():
        for cell, value in (smooth_row(k) if kind == "s" else detail_row(k)).items():
            forward2[smooth_place(cell), column] += value
    for k in range(33):
        rows = [(2 * k, even_row(k))] + ([(2 * k + 1, odd_row(k))] if k < 32 else [])
        for y, row in rows:
            for name, value in row.items():
                inverse2[names2[name], y] += value
    back = np.zeros((256, 128))
    back[:65] = inverse[:65]
    back[128 : 128 + 65] = inverse[:65]
    spread = np.zeros((3, 128, 2, 128))
    for k in range(64):
        spread[0, k, 0, k] = 1
    for k in range(32):
        spread[0, 64 + k, 1, k] = 1
        spread[0, 64 + k, 1, 64 + k] = 1
    for at in range(0, 16, 4):
        spread[1, at, 0, 64] = 1
        spread[2, at + 1, 0, 65] = 1
        for base in (0, 64):
            spread[1, at + 2, 1, base + 32] = 1
            spread[2, at + 3, 1, base + 33] = 1
    w["wide"] = np.concatenate([short, spread.reshape(384, 256)], 0)
    own, beside = smooth[:128], smooth[128:]
    w["narrow"] = np.concatenate([inverse, own, own, beside, beside, back, forward2, inverse2], 0)
    edge = np.zeros((4, 128, 128))

    def put(n, lane, row):
        for z in range(8):
            for y, value in row.items():
                j = y - 120 if y >= 120 else y + 8
                edge[n, 16 * z + j, lane + z] += value

    part = {127: 1.0, 126: -0.5}
    for n in range(4):
        put(n, beyond(n)["cell"], {0: 1.0})
        put(n, beyond(n)["after"], detail_row(0))
        put(n, beyond(n)["before"], part)
    put(0, BEYOND_SMOOTH[65], combine((1.0, smooth_row(1)), (-0.5, smooth_row(2))))
    share = combine((1.0, {126: 1.0}), (0.25, detail_row(62)), (0.25, part))
    put(0, BEYOND_SMOOTH[-1], combine((1.0, share), (-0.5, smooth_row(62))))
    w["edge"] = edge.reshape(512, 128)
    expand = np.zeros((2, 4, 128))
    for j in range(4):
        expand[0, j, 16 * j : 16 * j + 16] = 1
        expand[1, j, 64 + 8 * j : 64 + 8 * j + 8] = 1
    twice = combine(*[(value, smooth_row(k)) for k, value in smooth_row(0).items()])
    columns = np.zeros((2, 128, 128))
    for m in range(-1, 34):
        for t, value in twice.items():
            if 0 <= 4 * m + t < NL:
                columns[:, 4 * m + t, m + 1] = value
    rows = np.zeros((4, 32, 2, 64))
    for z in range(4):
        places = {m: m for m in range(16)}
        places.update({16: 16 + 2 * z, 17: 17 + 2 * z, -1: 16 + 15 - z})
        for m, place in places.items():
            for t, value in twice.items():
                if 0 <= 4 * m + t < NR:
                    rows[z, place, :, 4 * m + t] = value
    pad = np.zeros((8, 128))
    w["first"] = np.concatenate([columns.reshape(256, 128), rows.reshape(128, 128), expand.reshape(8, 128), pad], 0)
    return {name: as_bf16(matrix) for name, matrix in w.items()}


def two_terms(x):
    high = x.astype(BF16)
    low = (x - high.astype(F32)).astype(BF16)
    return high, low


def cost(gigaflops):
    return pl.CostEstimate(flops=gigaflops * 10**9, bytes_accessed=8 * 10**6, transcendentals=0)


def dot(a, b):
    return jnp.dot(a, b, preferred_element_type=F32)


def lift_planes(cells):
    half = len(cells) // 2
    even, odd = cells[0::2], cells[1::2]
    detail = [odd[k] - 0.5 * (even[k] + even[min(k + 1, half - 1)]) for k in range(half)]
    smooth = [even[k] + 0.25 * (detail[max(k - 1, 0)] + detail[k]) for k in range(half)]
    return smooth, detail


def unlift_planes(smooth, detail):
    half = len(smooth)
    even = [smooth[k] - 0.25 * (detail[max(k - 1, 0)] + detail[k]) for k in range(half)]
    out = []
    for k in range(half):
        out += [even[k], detail[k] + 0.5 * (even[k] + even[min(k + 1, half - 1)])]
    return out


def lift_rows(load, start):
    even, odd, after = load(start), load(start + 1), load(start + 2)
    before, odd_before = load(start - 2), load(start - 1)
    detail = odd - 0.5 * (even + after)
    detail_before = odd_before - 0.5 * (before + even)
    return even + 0.25 * (detail_before + detail), detail


def unlift_rows(smooth, detail, row):
    here, after = detail(row), detail(row + 1)
    even = smooth(row) - 0.25 * (detail(row - 1) + here)
    next_even = smooth(row + 1) - 0.25 * (here + after)
    return even, here + 0.5 * (even + next_even)


PITCH = 80


def lanes_turn(j):
    return lax.rem(32 * lax.rem(j, 4) + NL - 1, NL)


def first_kernel(
    field, masks_hbm, table_hbm, lifted, up, down, own_masks, share, cells, twice, masks, table, sems
):
    small = [
        pltpu.make_async_copy(masks_hbm, masks, sems.at[0]),
        pltpu.make_async_copy(table_hbm, table, sems.at[1]),
    ]
    copies = []
    for v in range(NV):
        for c in range(4):
            part = pl.ds(16 * c, 16)
            copies.append(pltpu.make_async_copy(field.at[v, :, part], cells.at[v, :, part], sems.at[2 + 4 * v + c]))
    for copy in small + copies:
        copy.start()
    for p in range(NV * NZ):
        lifted[p * PITCH : p * PITCH + 8, :] = jnp.zeros((8, NL), F32)
        lifted[p * PITCH + 72 : p * PITCH + 80, :] = jnp.zeros((8, NL), F32)
    for copy in small:
        copy.wait()
    for i, out, tile in ((0, up, 15), (1, down, 9)):
        total = jnp.zeros((7, NL), F32)
        for l in range(2):
            flags = masks[l, i].astype(F32).astype(BF16)
            spread = table[384 + 4 * l : 388 + 4 * l, :]
            total += lax.dot_general(flags, spread, (((0,), (0,)), ((), ())), preferred_element_type=F32)
        own_masks[i] = jnp.concatenate([total, jnp.zeros((1, NL), F32)], 0)
        out[tile] = own_masks[i]

    for v in range(NV):
        for t in range(8):
            if t % 2 == 0:
                copies[4 * v + t // 2].wait()
            smooth, detail = lift_planes([cells[v, z, 8 * t : 8 * t + 8, :] for z in range(NZ)])
            for k, tile in enumerate(smooth + detail):
                start = (v * NZ + k) * PITCH + 8 + 8 * t
                lifted[start : start + 8, :] = tile
            for k, tile in enumerate(lift_planes(smooth)[0]):
                twice[v * 4 + k, 8 * t : 8 * t + 8, :] = tile
        for bz in range(2):

            def row(x):
                return lifted[pl.ds((v * NZ + bz * 8) * PITCH + 8 + x, 8, stride=PITCH), :]

            x = [row(j) for j in range(7 if bz == 0 else 3)]
            first = x[1] - 0.5 * (x[0] + x[2])
            up[v * 5 + bz] = x[0]
            up[v * 5 + 2 + bz] = first
            y = {j: row(j) for j in (range(58, 64) if bz == 0 else (62, 63))}
            part = y[63] - 0.5 * y[62]
            down[v * 3 + bz] = part
            if bz == 0:
                second = x[3] - 0.5 * (x[2] + x[4])
                third = x[5] - 0.5 * (x[4] + x[6])
                up[v * 5 + 4] = x[2] + 0.25 * (first + second) - 0.5 * (x[4] + 0.25 * (second + third))
                before = y[59] - 0.5 * (y[58] + y[60])
                last = y[61] - 0.5 * (y[60] + y[62])
                down[v * 3 + 2] = y[62] + 0.25 * (last + part) - 0.5 * (y[60] + 0.25 * (before + last))

    total = jnp.zeros((80, NL), F32)
    for v in range(NV):
        main, extra = [], jnp.zeros((16, NL), F32)
        for z in range(4):
            terms = jnp.concatenate(two_terms(twice[v * 4 + z]), 0)
            part = dot(table[256 + 32 * z : 288 + 32 * z, :], terms)
            main.append(part[:16])
            extra += part[16:]
        terms = jnp.concatenate(two_terms(jnp.concatenate(main + [extra], 0)), 1)
        part = dot(terms, table[0:256, :])
        total += pltpu.roll(part, 35 * v, 1) if v else part
    turn = lanes_turn(lax.axis_index("gy"))
    lane = lax.broadcasted_iota(jnp.int32, (8, NL), 1)
    spare = (lane >= 105) & (lane < 126)
    upper = lax.broadcasted_iota(jnp.int32, (8, NL), 0) < 4
    below, above = total[64:72], total[72:80]
    pieces = [pltpu.roll(above, 105 - 21 * p, 1) for p in range(5)]
    for g in range(8):
        if g < 5:
            extra = pltpu.roll(below, 105 - 21 * g, 1)
        else:
            extra = pltpu.roll(pieces[2 * g - 10], 4, 0)
            extra = jnp.where(upper, extra, pieces[2 * g - 9] if g < 7 else 0.0)
        tile = jnp.where(spare, extra, total[8 * g : 8 * g + 8])
        share[8 * g : 8 * g + 8, :] = pltpu.roll(tile, turn, 1)


def in_hbm(x):
    return pltpu.with_memory_space_constraint(x, pltpu.HBM)


def first_step(field, masks):
    vmem = pl.BlockSpec(memory_space=pltpu.VMEM)
    shapes = [(NV * NZ * PITCH, NL), (16, 8, NL), (10, 8, NL), (2, 8, NL), (64, NL)]
    return pl.pallas_call(
        first_kernel,
        out_shape=[jax.ShapeDtypeStruct(s, F32) for s in shapes],
        in_specs=[pl.BlockSpec(memory_space=pltpu.HBM)] * 3,
        out_specs=[vmem] * 5,
        scratch_shapes=[
            pltpu.VMEM((NV, NZ, NR, NL), F32),
            pltpu.VMEM((NV * 4, NR, NL), F32),
            pltpu.VMEM((2, 2, 4, 7), jnp.int32),
            pltpu.VMEM((400, NL), BF16),
            pltpu.SemaphoreType.DMA((4 * NV + 2,)),
        ],
        compiler_params=pltpu.CompilerParams(vmem_limit_bytes=VMEM_LIMIT),
    )(*[in_hbm(x) for x in (field, masks.transpose(0, 2, 3, 1), jnp.asarray(weights()["first"]))])


ROWS = 40


def lift_kernel(lifted, parts):
    def lift(step, _):
        v, bz = step // 2, lax.rem(step, 2)
        for z in range(8):
            start = pl.multiple_of((step * 8 + z) * PITCH, 8)
            for t in range(4):
                pair = lift_rows(lambda s: lifted[pl.ds(start + 16 * t + s, 8, stride=2), :], 8)
                for bx in range(2):
                    plane = (2 * bz + bx) * 24 + v * 8 + z
                    parts[pl.ds(pl.multiple_of(plane * ROWS + 8 * t, 8), 8), :] = pair[bx]
        return 0

    lax.fori_loop(0, NV * 2, lift, 0)


def lift_step(lifted):
    vmem = pl.BlockSpec(memory_space=pltpu.VMEM)
    return pl.pallas_call(
        lift_kernel,
        out_shape=jax.ShapeDtypeStruct((4 * NV * 8 * ROWS, NL), F32),
        in_specs=[vmem],
        out_specs=vmem,
        compiler_params=pltpu.CompilerParams(vmem_limit_bytes=VMEM_LIMIT),
    )(lifted)


def edge_kernel(parts_in, lifted, north, south, own_masks, table_hbm, parts, to_left, to_right, packed, table, sem):
    copy = pltpu.make_async_copy(table_hbm, table, sem.at[0])
    copy.start()
    for p in range(4 * NV * 8):
        parts[p * ROWS + 32 : p * ROWS + 40, :] = jnp.zeros((8, NL), F32)
    for v in range(NV):
        for bz in range(2):

            def cell(x):
                return lifted[pl.ds((v * NZ + bz * 8) * PITCH + 8 + x, 8, stride=PITCH), :]

            def at(bx, r):
                return pl.ds(((2 * bz + bx) * 24 + v * 8) * ROWS + r, 8, stride=ROWS)

            before, after, detail = north[v * 3 + bz], south[v * 5 + bz], south[v * 5 + 2 + bz]
            start = cell(0)
            last = cell(63) - 0.5 * (cell(62) + after)
            parts[at(0, 0), :] = parts[at(0, 0), :] + 0.25 * before
            parts[at(0, 31), :] = parts[at(0, 31), :] - 0.125 * after
            parts[at(1, 31), :] = parts[at(1, 31), :] - 0.5 * after
            parts[at(0, 32), :] = after + 0.25 * (last + detail)
            parts[at(1, 32), :] = detail
            parts[at(1, 39), :] = before - 0.5 * start
            if bz == 0:
                parts[at(0, 33), :] = south[v * 5 + 4]
                parts[at(0, 39), :] = north[v * 3 + 2] - 0.125 * start

    lane = lax.broadcasted_iota(jnp.int32, (8, NL), 1) // 16

    def pack(v, _):
        for n in range(4):
            for t in range(5):
                tile = jnp.zeros((8, NL), F32)
                for z in range(8):
                    start = (n * 24 + v * 8 + z) * ROWS + 8 * t
                    x = parts[pl.ds(pl.multiple_of(start, 8), 8), :]
                    tile = jnp.where(lane == z, pltpu.roll(x, (8 + 16 * z) % NL, 1), tile)
                packed[pl.ds(pl.multiple_of(n * 120 + v * ROWS + 8 * t, 8), 8), :] = tile
        return 0

    for v in range(NV):
        pack(v, 0)
    copy.wait()
    terms = [two_terms(packed[n * 120 : (n + 1) * 120, :]) for n in range(4)]
    high, low = [jnp.concatenate(part, 1) for part in zip(*terms)]
    sides = dot(high, table[...]) + dot(low, table[...])
    lane = lax.broadcasted_iota(jnp.int32, (ROWS, NL), 1)
    each = [sides[v * ROWS : (v + 1) * ROWS] for v in range(NV)]
    right = jnp.where(lane < 40, each[0], pltpu.roll(each[1], 40, 1))
    to_right[0:ROWS, :] = jnp.where(lane < 80, right, pltpu.roll(each[2], 80, 1))
    last = jnp.where(lane < 32, pltpu.roll(each[2], NL - 40, 1), pltpu.roll(each[2], NL - 72, 1))
    to_left[0:ROWS, :] = jnp.where(lane < 40, last, each[0])
    to_left[ROWS : 2 * ROWS, :] = jnp.where(lane < 32, pltpu.roll(each[2], NL - 72, 1), each[1])
    lane = lax.broadcasted_iota(jnp.int32, (8, NL), 1)
    ends = jnp.zeros((8, NL), F32)
    for ib, tile in enumerate((north[9], own_masks[0], own_masks[1], south[15])):
        for j, source in enumerate((0, 63, 64, 95)):
            target = 4 * ib + j
            ends = jnp.where(lane == target, pltpu.roll(tile, (target - source) % NL, 1), ends)
    to_left[2 * ROWS : 2 * ROWS + 8, :] = ends
    to_right[ROWS : ROWS + 8, :] = ends


def edge_step(parts, lifted, north, south, own_masks):
    vmem = pl.BlockSpec(memory_space=pltpu.VMEM)
    shapes = [(4 * NV * 8 * ROWS, NL), (2 * ROWS + 8, NL), (ROWS + 8, NL)]
    return pl.pallas_call(
        edge_kernel,
        out_shape=[jax.ShapeDtypeStruct(s, F32) for s in shapes],
        in_specs=[vmem] * 5 + [pl.BlockSpec(memory_space=pltpu.HBM)],
        out_specs=[vmem] * 3,
        input_output_aliases={0: 0},
        cost_estimate=cost(20),
        scratch_shapes=[pltpu.VMEM((480, NL), F32), pltpu.VMEM((512, NL), BF16), pltpu.SemaphoreType.DMA((1,))],
        compiler_params=pltpu.CompilerParams(vmem_limit_bytes=VMEM_LIMIT),
    )(parts, lifted, north, south, own_masks, in_hbm(jnp.asarray(weights()["edge"])))


def join_kernel(*refs):
    shares, out = refs[-3::-1], refs[-1]
    for n, piece in enumerate(shares):
        out[64 * n : 64 * (n + 1), :] = piece[...]


def join_step(shares, after):
    vmem = pl.BlockSpec(memory_space=pltpu.VMEM)
    return pl.pallas_call(
        join_kernel,
        out_shape=jax.ShapeDtypeStruct((64 * len(shares), NL), F32),
        in_specs=[vmem] * len(shares) + [pl.BlockSpec(memory_space=pl.ANY)],
        out_specs=vmem,
        cost_estimate=cost(20),
        compiler_params=pltpu.CompilerParams(vmem_limit_bytes=VMEM_LIMIT),
    )(*shares[::-1], after)


def mask_lanes(west, east, own_masks, north_mask, south_mask, wide):
    group = lax.broadcasted_iota(jnp.int32, (8, NL), 1) // 4
    masks = [
        jnp.concatenate([jnp.where(group == ib, tile, 0.0) for ib in range(4)], 0)
        for tile in (east[2 * ROWS : 2 * ROWS + 8, :], west[ROWS : ROWS + 8, :])
    ]
    own = jnp.concatenate([north_mask[0], own_masks[0], own_masks[1], south_mask[0]], 0)
    flags = jnp.concatenate([own] + masks, 1).astype(BF16)
    return dot(flags, wide[144:528, :])


def beside_tiles(west, east, at, count):
    lane = lax.broadcasted_iota(jnp.int32, (count, NL), 1)
    left = west[at : at + count, :]
    first, second = east[at : at + count, :], east[ROWS + at : ROWS + at + count, :]
    third = jnp.where(lane < 104, pltpu.roll(second, 72, 1), pltpu.roll(first, 72, 1))
    third = jnp.where(lane < 72, pltpu.roll(first, 40, 1), third)
    tiles = []
    for v, right in enumerate((first, second, third)):
        beside = jnp.where(lane < FROM_WEST, pltpu.roll(left, NL - 40 * v, 1) if v else left, right)
        tiles += [pltpu.roll(beside, NL - z, 1) if z else beside for z in range(8)]
    return tiles


def beside_terms(west, east, at, count):
    return jnp.concatenate(two_terms(jnp.concatenate(beside_tiles(west, east, at, count), 0)), 1)


def own_terms(planes, at, count):
    return jnp.concatenate(two_terms(planes[:, at : at + count, :].reshape(24 * count, NL)), 1)


def main_kernel(
    parts, flat, east, west, own_masks, north_mask, south_mask, wide, narrow,
    kept,
    gain2, low, second, kept2, low_back, gain, sides_wide, turned,
):
    inverse, smooth_own, smooth_beside = narrow.at[0:256], narrow.at[256:512], narrow.at[512:768]
    back, forward2, inverse2 = narrow.at[768:1024], narrow.at[1024:1152], narrow.at[1152:1280]
    lanes = mask_lanes(west, east, own_masks, north_mask, south_mask, wide)
    lane64 = lax.broadcasted_iota(jnp.int32, (1, NL), 1) < 64
    forward2_f = forward2[...].astype(F32)
    for ib in range(4):
        for n in range(4) if ib else (1, 3):
            b = 8 * ib + 4 * (n // 2) + n % 2 - 1
            smooth_two = lanes[b : b + 1, NL:] if n else jnp.ones((1, NL), F32)
            row = jnp.where(lane64, smooth_two, lanes[b + 2 : b + 3, NL:])
            both = dot((forward2_f * row).astype(BF16), inverse2[...]).astype(BF16)
            gain2[ib, n, 0:128, :] = both
            gain2[ib, n, 128:256, :] = both

    for at, count in ((0, 16), (16, 16), (32, 8)):
        part = dot(own_terms(parts.at[0], at, count), smooth_own[...])
        part += dot(beside_terms(west, east, at, count), smooth_beside[...])
        part = part.reshape(24, count, NL)
        if at < 32:
            low[:, 8 + at : 8 + at + count, :] = part
            if at == 0:
                low[:, 56:64, :] = part[:, 0:8]
        else:
            low[:, 0:8, :] = part
            low[:, 40:48, :] = part
            low[:, 48:56, :] = part

    def rows_two(v, _):
        for t in range(3):
            lifted = [
                lift_rows(lambda s: low[v * 8 + p, pl.ds(16 * t + s, 8, stride=2), :], 8) for p in range(8)
            ]
            for bx in range(2):
                smooth, detail = lift_planes([pair[bx] for pair in lifted])
                for bz, part in ((0, smooth), (1, detail)):
                    for z in range(4):
                        second[2 * bz + bx, t, pl.ds(pl.multiple_of((v * 4 + z) * 8, 8), 8), :] = part[z]
        return 0

    for v in range(NV):
        rows_two(v, 0)
    for n in range(4):
        for t in range(3):
            terms = jnp.concatenate(two_terms(second[n, t]), 1)
            if t < 2:
                kept2[n, :, 8 + 8 * t : 16 + 8 * t, :] = dot(terms, gain2[t + 1, n]).reshape(NV * 4, 8, NL)
            else:
                if n % 2:
                    kept2[n, :, 0:8, :] = dot(terms, gain2[0, n]).reshape(NV * 4, 8, NL)
                kept2[n, :, 24:32, :] = dot(terms, gain2[3, n]).reshape(NV * 4, 8, NL)

    def back_two(v, _):
        for t in range(3):
            pairs = {}
            for bz in range(2):
                for z in range(4):
                    p = v * 4 + z
                    if t < 2:
                        pairs[bz, z] = unlift_rows(
                            lambda r: kept2[2 * bz, p, pl.ds(r, 8), :],
                            lambda r: kept2[2 * bz + 1, p, pl.ds(r, 8), :],
                            8 + 8 * t,
                        )
                    else:
                        even = kept2[2 * bz, p, 24:32, :] - 0.25 * (
                            kept2[2 * bz + 1, p, 23:31, :] + kept2[2 * bz + 1, p, 24:32, :]
                        )
                        pairs[bz, z] = (even, even)
            for parity in range(2 if t < 2 else 1):
                planes = unlift_planes([pairs[0, z][parity] for z in range(4)], [pairs[1, z][parity] for z in range(4)])
                for z in range(8):
                    low_back[pl.ds((v * 8 + z) * 48 + 16 * t + parity, 8, stride=2), :] = planes[z]
        return 0

    for v in range(NV):
        back_two(v, 0)

    forward_f = wide[0:144, :].astype(F32)
    for ib in range(4):
        sides_wide[ib] = jnp.zeros((NL, 4 * NL), F32)
    for ib in range(4):
        for n in range(4) if ib else (1, 3):
            b = 8 * ib + 4 * (n // 2) + n % 2 - 1
            smooth_one = lanes[b : b + 1, 0:NL] if n else jnp.zeros((1, NL), F32)
            row = jnp.concatenate([smooth_one, lanes[b + 2 : b + 3, 0:NL]], 1)
            both = dot((forward_f * row).astype(BF16), inverse[...])
            main = both[0:128].astype(BF16)
            gain[ib, n, 0:128, :] = main
            gain[ib, n, 128:256, :] = main
            for i in range(3):
                at = list(beyond(n).values())[i]
                sides_wide[ib, at : at + 1, n * NL : (n + 1) * NL] = both[128 + i : 129 + i]

    gain_sides = []
    for ib in range(4):
        side = sides_wide[ib].astype(BF16)
        gain_sides.append(jnp.concatenate([side, side], 0))
    def put(n, p, at, rows):
        start = pl.multiple_of((n * 24 + p) * 48 + 8 + at, 8)
        kept[pl.ds(start, rows.shape[0]), :] = rows

    def row_of(ref, first, pitch):
        return ref[pl.ds(first, 24, stride=pitch), :]

    for ib in range(2):
        product = dot(beside_terms(west, east, 16 * ib, 16), gain_sides[ib + 1])
        for n in range(4):
            for p in range(24):
                put(n, p, 16 * ib, product[16 * p : 16 * p + 16, n * NL : (n + 1) * NL])

    def keep(n, _):
        for ib in range(2):
            product = dot(own_terms(parts.at[n], 16 * ib, 16), gain[ib + 1, n])
            for p in range(24):
                start = pl.ds(pl.multiple_of((n * 24 + p) * 48 + 8 + 16 * ib, 8), 16)
                kept[start, :] += product[16 * p : 16 * p + 16]
        return 0

    for n in range(4):
        keep(n, 0)
    for ib in range(2):
        rows = jnp.concatenate([low_back[48 * p + 16 * ib : 48 * p + 16 * ib + 16, :] for p in range(24)], 0)
        product = dot(jnp.concatenate(two_terms(rows), 1), back[...])
        for p in range(24):
            start = 48 * p + 8 + 16 * ib
            kept[start : start + 16, :] += product[16 * p : 16 * p + 16]
    tiles = beside_tiles(west, east, 32, 8)
    for p in range(24):
        turned[8 * p : 8 * p + 8, :] = tiles[p]
    for first, ib, place, row in ((0, 3, 40, 32), (7, 0, 7, 39)):
        beside = dot(jnp.concatenate(two_terms(row_of(turned, first, 8)), 1), gain_sides[ib])
        for n in range(4) if ib else (1, 3):
            own = jnp.concatenate(two_terms(row_of(flat, n * 24 * ROWS + row, ROWS)), 1)
            total = beside[:, n * NL : (n + 1) * NL] + dot(own, gain[ib, n])
            if n == 0:
                total += dot(jnp.concatenate(two_terms(row_of(low_back, row, 48)), 1), back[...])
            kept[pl.ds(n * 24 * 48 + place, 24, stride=48), :] = total


def cells_kernel(kept, out, cells, sems):
    def back_one(step, _):
        v, t = step // 4, step % 4
        pairs = {}
        for bz in range(2):
            for z in range(8):
                p = v * 8 + z
                pairs[bz, z] = unlift_rows(
                    lambda r: kept[2 * bz, p, pl.ds(8 * t + r, 8), :],
                    lambda r: kept[2 * bz + 1, p, pl.ds(8 * t + r, 8), :],
                    8,
                )
        for parity in range(2):
            planes = unlift_planes([pairs[0, z][parity] for z in range(8)], [pairs[1, z][parity] for z in range(8)])
            for z in range(NZ):
                cells[v, z, pl.ds(16 * t + parity, 8, stride=2), :] = planes[z]
        return 0

    def copy(step):
        v, rows = step // 4, pl.ds(pl.multiple_of(16 * (step % 4), 16), 16)
        return pltpu.make_async_copy(cells.at[v, :, rows], out.at[v, :, rows], sems.at[step])

    def one(step, _):
        back_one(step, 0)
        copy(step).start()
        return 0

    lax.fori_loop(0, NV * 4, one, 0)
    for step in range(NV * 4):
        copy(step).wait()


def main_specs():
    vmem = pl.BlockSpec(memory_space=pltpu.VMEM)
    return [
        vmem, vmem, vmem, vmem, vmem,
        pl.BlockSpec((1, 8, NL), lambda i: (9, 0, 0)), pl.BlockSpec((1, 8, NL), lambda i: (15, 0, 0)),
        vmem, vmem,
    ]


def main_step(flat, *operands):
    w = weights()
    return pl.pallas_call(
        main_kernel,
        grid=(1,),
        out_shape=jax.ShapeDtypeStruct((4 * NV * 8 * 48, NL), F32),
        in_specs=main_specs(),
        out_specs=pl.BlockSpec((4 * NV * 8 * 48, NL), lambda i: (0, 0)),
        scratch_shapes=[
            pltpu.VMEM((4, 4, 256, NL), BF16),
            pltpu.VMEM((NV * 8, 64, NL), F32),
            pltpu.VMEM((4, 3, NV * 32, NL), F32),
            pltpu.VMEM((4, NV * 4, 40, NL), F32),
            pltpu.VMEM((NV * 8 * 48, NL), F32),
            pltpu.VMEM((4, 4, 256, NL), BF16),
            pltpu.VMEM((4, NL, 4 * NL), F32),
            pltpu.VMEM((NV * 64, NL), F32),
        ],
        cost_estimate=cost(8),
        compiler_params=pltpu.CompilerParams(vmem_limit_bytes=VMEM_LIMIT),
    )(flat.reshape(4, NV * 8, ROWS, NL), flat, *operands, w["wide"], w["narrow"])


def cells_step(kept):
    shape = (NV, NZ, NR, NL)
    return pl.pallas_call(
        cells_kernel,
        out_shape=jax.ShapeDtypeStruct(shape, F32),
        in_specs=[pl.BlockSpec(memory_space=pltpu.VMEM)],
        out_specs=pl.BlockSpec(memory_space=pltpu.HBM),
        scratch_shapes=[pltpu.VMEM(shape, F32), pltpu.SemaphoreType.DMA((NV * 4,))],
        cost_estimate=cost(4),
        compiler_params=pltpu.CompilerParams(vmem_limit_bytes=VMEM_LIMIT),
    )(kept)


def rows_kernel(count_x, count_z, *refs):
    shares, out = refs[count_x - 1 :: -1], refs[count_x + 1]
    me, me_y = lax.axis_index("gx"), lax.axis_index("gy")
    row = lax.broadcasted_iota(jnp.int32, (8, NL), 0)
    lane = lax.broadcasted_iota(jnp.int32, (8, NL), 1)
    for r in range(count_x):
        at = pl.multiple_of(16 * (me ^ r), 16)
        for j in range(count_z):
            for z in range(4):
                start = 64 * j + 16 * z
                out[j, z, pl.ds(at, 16), :] = shares[r][start : start + 16, :]
    for j in range(count_z):
        turn = lanes_turn(me_y ^ (2 * j))
        piece = lax.rem(lane + (NL - turn), NL) // 21
        inside = [piece == p for p in range(5)]
        for r in range(count_x):
            i = me ^ r
            below = pl.multiple_of(16 * lax.rem(i + 1, count_x), 16)
            above = pl.multiple_of(16 * lax.rem(i + count_x - 1, count_x) + 8, 8)
            tiles = [shares[r][64 * j + 8 * g : 64 * j + 8 * g + 8, :] for g in range(8)]
            low, high = jnp.zeros((8, NL), F32), jnp.zeros((8, NL), F32)
            for p in range(5):
                back = (21 * p - 105) % NL
                low = jnp.where(inside[p], pltpu.roll(tiles[p], back, 1), low)
                extra = tiles[5 + p // 2]
                extra = extra if p % 2 else pltpu.roll(extra, 4, 0)
                high = jnp.where(inside[p], pltpu.roll(extra, back, 1), high)
            for z in range(4):
                first = pltpu.roll(low, 8 - 2 * z, 0) if z else low
                last = pltpu.roll(high, z, 0) if z else high
                out[j, z, pl.ds(below, 8), :] += jnp.where(row < 2, first, 0.0)
                out[j, z, pl.ds(above, 8), :] += jnp.where(row == 7, last, 0.0)


def rows_step(pieces, count_z, after):
    vmem = pl.BlockSpec(memory_space=pltpu.VMEM)
    count_x = len(pieces)
    return pl.pallas_call(
        functools.partial(rows_kernel, count_x, count_z),
        out_shape=jax.ShapeDtypeStruct((count_z, 4, 16 * count_x, NL), F32),
        in_specs=[vmem] * count_x + [pl.BlockSpec(memory_space=pl.ANY)],
        out_specs=vmem,
        compiler_params=pltpu.CompilerParams(vmem_limit_bytes=VMEM_LIMIT),
    )(*pieces[::-1], after)


def coarse_kernel(count_x, count_y, own, other, out_hbm, out, sems):
    me = lax.axis_index("gy")
    me_z, is_even = lax.shift_right_logical(me, 1), lax.rem(me, 2) == 0
    lane = lax.broadcasted_iota(jnp.int32, (8, NL), 1)
    place = [lax.rem(lane + NL - 35 * v, NL) for v in range(NV)]

    def block(i, _):
        rows = pl.ds(pl.multiple_of(8 * i, 8), 8)
        for z in range(4):
            pieces = []
            for j in range(count_y // 2):
                mine, theirs = own[j ^ me_z, z, rows, :], other[j ^ me_z, z, rows, :]
                pieces += [jnp.where(is_even, mine, theirs), jnp.where(is_even, theirs, mine)]
            for v in range(NV):
                at = place[v]
                for t in range(count_y // 4):
                    total = jnp.where(at < 2, pieces[4 * t - 1], 0.0)
                    total += jnp.where(at == NL - 1, pieces[(4 * t + 4) % count_y], 0.0)
                    for q in range(4):
                        inside = (at >= 32 * q - 1) & (at < 32 * q + 34)
                        total += jnp.where(inside, pieces[4 * t + q], 0.0)
                    out[v, z, rows, NL * t : NL * (t + 1)] = pltpu.roll(total, NL - 35 * v, 1) if v else total
        return 0

    def copy(i):
        rows = pl.ds(pl.multiple_of(16 * i, 16), 16)
        return pltpu.make_async_copy(out.at[:, :, rows], out_hbm.at[:, :, rows], sems.at[i])

    group = 4 if count_x % 4 == 0 else 1

    def several(i, _):
        for k in range(group):
            block(2 * (group * i + k), 0)
            block(2 * (group * i + k) + 1, 0)
            copy(group * i + k).start()
        return 0

    lax.fori_loop(0, count_x // group, several, 0)
    for i in range(count_x):
        copy(i).wait()


def coarse_step(own, other, count_x, count_y):
    vmem = pl.BlockSpec(memory_space=pltpu.VMEM)
    shape = (NV, 4, 16 * count_x, 32 * count_y)
    return pl.pallas_call(
        functools.partial(coarse_kernel, count_x, count_y),
        out_shape=jax.ShapeDtypeStruct(shape, F32),
        in_specs=[vmem, vmem],
        out_specs=pl.BlockSpec(memory_space=pltpu.HBM),
        scratch_shapes=[pltpu.VMEM(shape, F32), pltpu.SemaphoreType.DMA((count_x,))],
        compiler_params=pltpu.CompilerParams(vmem_limit_bytes=VMEM_LIMIT),
    )(own, other)


def shifted(x, axis, step):
    count = lax.axis_size(axis)
    return lax.ppermute(x, axis, [(i, (i + step) % count) for i in range(count)])


def swapped(x, axis, distance):
    return lax.ppermute(x, axis, [(i, i ^ distance) for i in range(lax.axis_size(axis))])


def body(field, masks):
    count_x, count_y = lax.axis_size("gx"), lax.axis_size("gy")
    lifted, up, down, own_masks, share = first_step(field, masks)
    south = shifted(up, "gx", -1)
    north = shifted(down, "gx", 1)
    shares = [share] + [swapped(share, "gy", r) for r in range(2, count_y, 2)]
    parts, to_left, to_right = edge_step(lift_step(lifted), lifted, north, south, own_masks)
    east = shifted(to_left, "gy", -1)
    west = shifted(to_right, "gy", 1)
    joined = join_step(shares, to_left)
    pieces = [joined] + [swapped(joined, "gx", r) for r in range(1, count_x)]
    kept = main_step(parts, east, west, own_masks, north, south)
    own = rows_step(pieces, count_y // 2, kept)
    other = swapped(own, "gy", 1)
    return cells_step(kept.reshape(4, NV * 8, 48, NL)), coarse_step(own, other, count_x, count_y)


def solution(mesh):
    placed = P(None, None, "gx", "gy")
    return jax.shard_map(
        body,
        mesh=mesh,
        in_specs=(placed, placed),
        out_specs=(placed, P()),
        check_vma=False,
    )
```

```python
import functools

import jax
import jax.numpy as jnp
import ml_dtypes
import numpy as np
from jax import lax
from jax.experimental import pallas as pl
from jax.experimental.pallas import tpu as pltpu
from jax.sharding import PartitionSpec as P

F32 = jnp.float32
BF16 = jnp.bfloat16
VMEM_LIMIT = 32 * 1024 * 1024

NV, NZ, NR, NL = 3, 16, 64, 128


def detail_row(k):
    return {2 * k + 1: 1.0, 2 * k: -0.5, 2 * k + 2: -0.5}


def smooth_row(k):
    row = {2 * k: 1.0}
    for j in (k - 1, k):
        for cell, value in detail_row(j).items():
            row[cell] = row.get(cell, 0.0) + 0.25 * value
    return row


def even_row(k):
    return {("s", k): 1.0, ("d", k - 1): -0.25, ("d", k): -0.25}


def odd_row(k):
    row = {("d", k): 1.0}
    for j in (k, k + 1):
        for name, value in even_row(j).items():
            row[name] = row.get(name, 0.0) + 0.5 * value
    return row


def as_bf16(matrix):
    cast = matrix.astype(ml_dtypes.bfloat16)
    assert (cast.astype(np.float64) == matrix).all()
    return cast


def combine(*terms):
    total = {}
    for factor, row in terms:
        for cell, value in row.items():
            total[cell] = total.get(cell, 0.0) + factor * value
    return total


def level_one_columns():
    names = {("s", k): k for k in range(65)}
    names.update({("d", k): 128 + k for k in range(65)})
    names[("d", -1)] = 128 + 65
    return names


def level_two_columns():
    names = {("s", k): k for k in range(33)}
    names.update({("d", k): 64 + k for k in range(33)})
    names[("d", -1)] = 64 + 33
    return names


def smooth_place(k):
    return k + 2


def beyond(n):
    return {"cell": 40 + 16 * n, "after": 48 + 16 * n, "before": 8 * n}


BEYOND_SMOOTH = {65: 104, -1: 32}
FROM_WEST = 40


def own_row(kind, k, n):
    place = {name: 128 + lane for name, lane in beyond(n).items()}
    if kind == "d":
        if k == -1:
            return {place["before"]: 1.0, 0: -0.5}
        if k == 64:
            return {place["after"]: 1.0}
        return {(place["cell"] if y == 128 else y): value for y, value in detail_row(k).items()}
    if k in (-2, 66):
        return {}
    if k in BEYOND_SMOOTH:
        row = {128 + BEYOND_SMOOTH[k]: 1.0}
        return combine((1.0, row), (1.0, {0: -0.125})) if k == -1 else row
    even = place["cell"] if k == 64 else 2 * k
    return combine((1.0, {even: 1.0}), (0.25, own_row("d", k - 1, n)), (0.25, own_row("d", k, n)))


@functools.lru_cache(maxsize=None)
def weights():
    w = {}
    names = level_one_columns()
    forward = np.zeros((4, 256, 256))
    inverse = np.zeros((256, 128))
    for (kind, k), column in names.items():
        for n in range(4):
            for place, value in own_row(kind, k, n).items():
                forward[n, place, column] += value
    for k in range(64):
        for y, row in ((2 * k, even_row(k)), (2 * k + 1, odd_row(k))):
            for name, value in row.items():
                inverse[names[name], y] += value
    short = np.zeros((144, 256))
    short[:128] = forward[0, :128]
    for i, lane in enumerate(beyond(0).values()):
        short[128 + i] = forward[0, 128 + lane]
    smooth = np.zeros((256, 128))
    for k in range(-2, 67):
        for place, value in own_row("s", k, 0).items():
            smooth[place, smooth_place(k)] += value
    names2 = level_two_columns()
    forward2 = np.zeros((128, 128))
    inverse2 = np.zeros((128, 128))
    for (kind, k), column in names2.items():
        for cell, value in (smooth_row(k) if kind == "s" else detail_row(k)).items():
            forward2[smooth_place(cell), column] += value
    for k in range(33):
        rows = [(2 * k, even_row(k))] + ([(2 * k + 1, odd_row(k))] if k < 32 else [])
        for y, row in rows:
            for name, value in row.items():
                inverse2[names2[name], y] += value
    back = np.zeros((256, 128))
    back[:65] = inverse[:65]
    back[128 : 128 + 65] = inverse[:65]
    spread = np.zeros((3, 128, 2, 128))
    for k in range(64):
        spread[0, k, 0, k] = 1
    for k in range(32):
        spread[0, 64 + k, 1, k] = 1
        spread[0, 64 + k, 1, 64 + k] = 1
    for at in range(0, 16, 4):
        spread[1, at, 0, 64] = 1
        spread[2, at + 1, 0, 65] = 1
        for base in (0, 64):
            spread[1, at + 2, 1, base + 32] = 1
            spread[2, at + 3, 1, base + 33] = 1
    w["wide"] = np.concatenate([short, spread.reshape(384, 256)], 0)
    own, beside = smooth[:128], smooth[128:]
    w["narrow"] = np.concatenate([inverse, own, own, beside, beside, back, forward2, inverse2], 0)
    edge = np.zeros((4, 128, 128))

    def put(n, lane, row):
        for z in range(8):
            for y, value in row.items():
                j = y - 120 if y >= 120 else y + 8
                edge[n, 16 * z + j, lane + z] += value

    part = {127: 1.0, 126: -0.5}
    for n in range(4):
        put(n, beyond(n)["cell"], {0: 1.0})
        put(n, beyond(n)["after"], detail_row(0))
        put(n, beyond(n)["before"], part)
    put(0, BEYOND_SMOOTH[65], combine((1.0, smooth_row(1)), (-0.5, smooth_row(2))))
    share = combine((1.0, {126: 1.0}), (0.25, detail_row(62)), (0.25, part))
    put(0, BEYOND_SMOOTH[-1], combine((1.0, share), (-0.5, smooth_row(62))))
    w["edge"] = edge.reshape(512, 128)
    expand = np.zeros((2, 4, 128))
    for j in range(4):
        expand[0, j, 16 * j : 16 * j + 16] = 1
        expand[1, j, 64 + 8 * j : 64 + 8 * j + 8] = 1
    twice = combine(*[(value, smooth_row(k)) for k, value in smooth_row(0).items()])
    columns = np.zeros((2, 128, 128))
    for m in range(-1, 34):
        for t, value in twice.items():
            if 0 <= 4 * m + t < NL:
                columns[:, 4 * m + t, m + 1] = value
    rows = np.zeros((4, 32, 2, 64))
    for z in range(4):
        places = {m: m for m in range(16)}
        places.update({16: 16 + 2 * z, 17: 17 + 2 * z, -1: 16 + 15 - z})
        for m, place in places.items():
            for t, value in twice.items():
                if 0 <= 4 * m + t < NR:
                    rows[z, place, :, 4 * m + t] = value
    pad = np.zeros((8, 128))
    w["first"] = np.concatenate([columns.reshape(256, 128), rows.reshape(128, 128), expand.reshape(8, 128), pad], 0)
    return {name: as_bf16(matrix) for name, matrix in w.items()}


def two_terms(x):
    high = x.astype(BF16)
    low = (x - high.astype(F32)).astype(BF16)
    return high, low


def cost(gigaflops):
    return pl.CostEstimate(flops=gigaflops * 10**9, bytes_accessed=8 * 10**6, transcendentals=0)


def dot(a, b):
    return jnp.dot(a, b, preferred_element_type=F32)


def lift_planes(cells):
    half = len(cells) // 2
    even, odd = cells[0::2], cells[1::2]
    detail = [odd[k] - 0.5 * (even[k] + even[min(k + 1, half - 1)]) for k in range(half)]
    smooth = [even[k] + 0.25 * (detail[max(k - 1, 0)] + detail[k]) for k in range(half)]
    return smooth, detail


def unlift_planes(smooth, detail):
    half = len(smooth)
    even = [smooth[k] - 0.25 * (detail[max(k - 1, 0)] + detail[k]) for k in range(half)]
    out = []
    for k in range(half):
        out += [even[k], detail[k] + 0.5 * (even[k] + even[min(k + 1, half - 1)])]
    return out


def lift_rows(load, start):
    even, odd, after = load(start), load(start + 1), load(start + 2)
    before, odd_before = load(start - 2), load(start - 1)
    detail = odd - 0.5 * (even + after)
    detail_before = odd_before - 0.5 * (before + even)
    return even + 0.25 * (detail_before + detail), detail


def unlift_rows(smooth, detail, row):
    here, after = detail(row), detail(row + 1)
    even = smooth(row) - 0.25 * (detail(row - 1) + here)
    next_even = smooth(row + 1) - 0.25 * (here + after)
    return even, here + 0.5 * (even + next_even)


PITCH = 80


def lanes_turn(j):
    return lax.rem(32 * lax.rem(j, 4) + NL - 1, NL)


def first_kernel(
    field, masks_hbm, table_hbm, lifted, up, down, own_masks, share, cells, twice, masks, table, sems
):
    small = [
        pltpu.make_async_copy(masks_hbm, masks, sems.at[0]),
        pltpu.make_async_copy(table_hbm, table, sems.at[1]),
    ]
    copies = []
    for v in range(NV):
        for c in range(4):
            part = pl.ds(16 * c, 16)
            copies.append(pltpu.make_async_copy(field.at[v, :, part], cells.at[v, :, part], sems.at[2 + 4 * v + c]))
    for copy in small + copies:
        copy.start()
    for p in range(NV * NZ):
        lifted[p * PITCH : p * PITCH + 8, :] = jnp.zeros((8, NL), F32)
        lifted[p * PITCH + 72 : p * PITCH + 80, :] = jnp.zeros((8, NL), F32)
    for copy in small:
        copy.wait()
    for i, out, tile in ((0, up, 15), (1, down, 9)):
        total = jnp.zeros((7, NL), F32)
        for l in range(2):
            flags = masks[l, i].astype(F32).astype(BF16)
            spread = table[384 + 4 * l : 388 + 4 * l, :]
            total += lax.dot_general(flags, spread, (((0,), (0,)), ((), ())), preferred_element_type=F32)
        own_masks[i] = jnp.concatenate([total, jnp.zeros((1, NL), F32)], 0)
        out[tile] = own_masks[i]

    for v in range(NV):
        for t in range(8):
            if t % 2 == 0:
                copies[4 * v + t // 2].wait()
            smooth, detail = lift_planes([cells[v, z, 8 * t : 8 * t + 8, :] for z in range(NZ)])
            for k, tile in enumerate(smooth + detail):
                start = (v * NZ + k) * PITCH + 8 + 8 * t
                lifted[start : start + 8, :] = tile
            for k, tile in enumerate(lift_planes(smooth)[0]):
                twice[v * 4 + k, 8 * t : 8 * t + 8, :] = tile
        for bz in range(2):

            def row(x):
                return lifted[pl.ds((v * NZ + bz * 8) * PITCH + 8 + x, 8, stride=PITCH), :]

            x = [row(j) for j in range(7 if bz == 0 else 3)]
            first = x[1] - 0.5 * (x[0] + x[2])
            up[v * 5 + bz] = x[0]
            up[v * 5 + 2 + bz] = first
            y = {j: row(j) for j in (range(58, 64) if bz == 0 else (62, 63))}
            part = y[63] - 0.5 * y[62]
            down[v * 3 + bz] = part
            if bz == 0:
                second = x[3] - 0.5 * (x[2] + x[4])
                third = x[5] - 0.5 * (x[4] + x[6])
                up[v * 5 + 4] = x[2] + 0.25 * (first + second) - 0.5 * (x[4] + 0.25 * (second + third))
                before = y[59] - 0.5 * (y[58] + y[60])
                last = y[61] - 0.5 * (y[60] + y[62])
                down[v * 3 + 2] = y[62] + 0.25 * (last + part) - 0.5 * (y[60] + 0.25 * (before + last))

    total = jnp.zeros((80, NL), F32)
    for v in range(NV):
        main, extra = [], jnp.zeros((16, NL), F32)
        for z in range(4):
            terms = jnp.concatenate(two_terms(twice[v * 4 + z]), 0)
            part = dot(table[256 + 32 * z : 288 + 32 * z, :], terms)
            main.append(part[:16])
            extra += part[16:]
        terms = jnp.concatenate(two_terms(jnp.concatenate(main + [extra], 0)), 1)
        part = dot(terms, table[0:256, :])
        total += pltpu.roll(part, 35 * v, 1) if v else part
    turn = lanes_turn(lax.axis_index("gy"))
    lane = lax.broadcasted_iota(jnp.int32, (8, NL), 1)
    spare = (lane >= 105) & (lane < 126)
    upper = lax.broadcasted_iota(jnp.int32, (8, NL), 0) < 4
    below, above = total[64:72], total[72:80]
    pieces = [pltpu.roll(above, 105 - 21 * p, 1) for p in range(5)]
    for g in range(8):
        if g < 5:
            extra = pltpu.roll(below, 105 - 21 * g, 1)
        else:
            extra = pltpu.roll(pieces[2 * g - 10], 4, 0)
            extra = jnp.where(upper, extra, pieces[2 * g - 9] if g < 7 else 0.0)
        tile = jnp.where(spare, extra, total[8 * g : 8 * g + 8])
        share[8 * g : 8 * g + 8, :] = pltpu.roll(tile, turn, 1)


def in_hbm(x):
    return pltpu.with_memory_space_constraint(x, pltpu.HBM)


def first_step(field, masks):
    vmem = pl.BlockSpec(memory_space=pltpu.VMEM)
    shapes = [(NV * NZ * PITCH, NL), (16, 8, NL), (10, 8, NL), (2, 8, NL), (64, NL)]
    return pl.pallas_call(
        first_kernel,
        out_shape=[jax.ShapeDtypeStruct(s, F32) for s in shapes],
        in_specs=[pl.BlockSpec(memory_space=pltpu.HBM)] * 3,
        out_specs=[vmem] * 5,
        scratch_shapes=[
            pltpu.VMEM((NV, NZ, NR, NL), F32),
            pltpu.VMEM((NV * 4, NR, NL), F32),
            pltpu.VMEM((2, 2, 4, 7), jnp.int32),
            pltpu.VMEM((400, NL), BF16),
            pltpu.SemaphoreType.DMA((4 * NV + 2,)),
        ],
        compiler_params=pltpu.CompilerParams(vmem_limit_bytes=VMEM_LIMIT),
    )(*[in_hbm(x) for x in (field, masks.transpose(0, 2, 3, 1), jnp.asarray(weights()["first"]))])


ROWS = 40


def lift_kernel(lifted, parts):
    def lift(step, _):
        v, bz = step // 2, lax.rem(step, 2)
        for z in range(8):
            start = pl.multiple_of((step * 8 + z) * PITCH, 8)
            for t in range(4):
                pair = lift_rows(lambda s: lifted[pl.ds(start + 16 * t + s, 8, stride=2), :], 8)
                for bx in range(2):
                    plane = (2 * bz + bx) * 24 + v * 8 + z
                    parts[pl.ds(pl.multiple_of(plane * ROWS + 8 * t, 8), 8), :] = pair[bx]
        return 0

    lax.fori_loop(0, NV * 2, lift, 0)


def lift_step(lifted):
    vmem = pl.BlockSpec(memory_space=pltpu.VMEM)
    return pl.pallas_call(
        lift_kernel,
        out_shape=jax.ShapeDtypeStruct((4 * NV * 8 * ROWS, NL), F32),
        in_specs=[vmem],
        out_specs=vmem,
        compiler_params=pltpu.CompilerParams(vmem_limit_bytes=VMEM_LIMIT),
    )(lifted)


def edge_kernel(parts_in, lifted, north, south, own_masks, table_hbm, parts, to_left, to_right, packed, table, sem):
    copy = pltpu.make_async_copy(table_hbm, table, sem.at[0])
    copy.start()
    for p in range(4 * NV * 8):
        parts[p * ROWS + 32 : p * ROWS + 40, :] = jnp.zeros((8, NL), F32)
    for v in range(NV):
        for bz in range(2):

            def cell(x):
                return lifted[pl.ds((v * NZ + bz * 8) * PITCH + 8 + x, 8, stride=PITCH), :]

            def at(bx, r):
                return pl.ds(((2 * bz + bx) * 24 + v * 8) * ROWS + r, 8, stride=ROWS)

            before, after, detail = north[v * 3 + bz], south[v * 5 + bz], south[v * 5 + 2 + bz]
            start = cell(0)
            last = cell(63) - 0.5 * (cell(62) + after)
            parts[at(0, 0), :] = parts[at(0, 0), :] + 0.25 * before
            parts[at(0, 31), :] = parts[at(0, 31), :] - 0.125 * after
            parts[at(1, 31), :] = parts[at(1, 31), :] - 0.5 * after
            parts[at(0, 32), :] = after + 0.25 * (last + detail)
            parts[at(1, 32), :] = detail
            parts[at(1, 39), :] = before - 0.5 * start
            if bz == 0:
                parts[at(0, 33), :] = south[v * 5 + 4]
                parts[at(0, 39), :] = north[v * 3 + 2] - 0.125 * start

    lane = lax.broadcasted_iota(jnp.int32, (8, NL), 1) // 16

    def pack(v, _):
        for n in range(4):
            for t in range(5):
                tile = jnp.zeros((8, NL), F32)
                for z in range(8):
                    start = (n * 24 + v * 8 + z) * ROWS + 8 * t
                    x = parts[pl.ds(pl.multiple_of(start, 8), 8), :]
                    tile = jnp.where(lane == z, pltpu.roll(x, (8 + 16 * z) % NL, 1), tile)
                packed[pl.ds(pl.multiple_of(n * 120 + v * ROWS + 8 * t, 8), 8), :] = tile
        return 0

    for v in range(NV):
        pack(v, 0)
    copy.wait()
    terms = [two_terms(packed[n * 120 : (n + 1) * 120, :]) for n in range(4)]
    high, low = [jnp.concatenate(part, 1) for part in zip(*terms)]
    sides = dot(high, table[...]) + dot(low, table[...])
    lane = lax.broadcasted_iota(jnp.int32, (ROWS, NL), 1)
    each = [sides[v * ROWS : (v + 1) * ROWS] for v in range(NV)]
    right = jnp.where(lane < 40, each[0], pltpu.roll(each[1], 40, 1))
    to_right[0:ROWS, :] = jnp.where(lane < 80, right, pltpu.roll(each[2], 80, 1))
    last = jnp.where(lane < 32, pltpu.roll(each[2], NL - 40, 1), pltpu.roll(each[2], NL - 72, 1))
    to_left[0:ROWS, :] = jnp.where(lane < 40, last, each[0])
    to_left[ROWS : 2 * ROWS, :] = jnp.where(lane < 32, pltpu.roll(each[2], NL - 72, 1), each[1])
    lane = lax.broadcasted_iota(jnp.int32, (8, NL), 1)
    ends = jnp.zeros((8, NL), F32)
    for ib, tile in enumerate((north[9], own_masks[0], own_masks[1], south[15])):
        for j, source in enumerate((0, 63, 64, 95)):
            target = 4 * ib + j
            ends = jnp.where(lane == target, pltpu.roll(tile, (target - source) % NL, 1), ends)
    to_left[2 * ROWS : 2 * ROWS + 8, :] = ends
    to_right[ROWS : ROWS + 8, :] = ends


def edge_step(parts, lifted, north, south, own_masks):
    vmem = pl.BlockSpec(memory_space=pltpu.VMEM)
    shapes = [(4 * NV * 8 * ROWS, NL), (2 * ROWS + 8, NL), (ROWS + 8, NL)]
    return pl.pallas_call(
        edge_kernel,
        out_shape=[jax.ShapeDtypeStruct(s, F32) for s in shapes],
        in_specs=[vmem] * 5 + [pl.BlockSpec(memory_space=pltpu.HBM)],
        out_specs=[vmem] * 3,
        input_output_aliases={0: 0},
        cost_estimate=cost(20),
        scratch_shapes=[pltpu.VMEM((480, NL), F32), pltpu.VMEM((512, NL), BF16), pltpu.SemaphoreType.DMA((1,))],
        compiler_params=pltpu.CompilerParams(vmem_limit_bytes=VMEM_LIMIT),
    )(parts, lifted, north, south, own_masks, in_hbm(jnp.asarray(weights()["edge"])))


def join_kernel(*refs):
    shares, out = refs[-3::-1], refs[-1]
    for n, piece in enumerate(shares):
        out[64 * n : 64 * (n + 1), :] = piece[...]


def join_step(shares, after):
    vmem = pl.BlockSpec(memory_space=pltpu.VMEM)
    return pl.pallas_call(
        join_kernel,
        out_shape=jax.ShapeDtypeStruct((64 * len(shares), NL), F32),
        in_specs=[vmem] * len(shares) + [pl.BlockSpec(memory_space=pl.ANY)],
        out_specs=vmem,
        cost_estimate=cost(20),
        compiler_params=pltpu.CompilerParams(vmem_limit_bytes=VMEM_LIMIT),
    )(*shares[::-1], after)


def mask_lanes(west, east, own_masks, north_mask, south_mask, wide):
    group = lax.broadcasted_iota(jnp.int32, (8, NL), 1) // 4
    masks = [
        jnp.concatenate([jnp.where(group == ib, tile, 0.0) for ib in range(4)], 0)
        for tile in (east[2 * ROWS : 2 * ROWS + 8, :], west[ROWS : ROWS + 8, :])
    ]
    own = jnp.concatenate([north_mask[0], own_masks[0], own_masks[1], south_mask[0]], 0)
    flags = jnp.concatenate([own] + masks, 1).astype(BF16)
    return dot(flags, wide[144:528, :])


def beside_tiles(west, east, at, count):
    lane = lax.broadcasted_iota(jnp.int32, (count, NL), 1)
    left = west[at : at + count, :]
    first, second = east[at : at + count, :], east[ROWS + at : ROWS + at + count, :]
    third = jnp.where(lane < 104, pltpu.roll(second, 72, 1), pltpu.roll(first, 72, 1))
    third = jnp.where(lane < 72, pltpu.roll(first, 40, 1), third)
    tiles = []
    for v, right in enumerate((first, second, third)):
        beside = jnp.where(lane < FROM_WEST, pltpu.roll(left, NL - 40 * v, 1) if v else left, right)
        tiles += [pltpu.roll(beside, NL - z, 1) if z else beside for z in range(8)]
    return tiles


def beside_terms(west, east, at, count):
    return jnp.concatenate(two_terms(jnp.concatenate(beside_tiles(west, east, at, count), 0)), 1)


def own_terms(planes, at, count):
    return jnp.concatenate(two_terms(planes[:, at : at + count, :].reshape(24 * count, NL)), 1)


def main_kernel(
    parts, flat, east, west, own_masks, north_mask, south_mask, wide, narrow,
    kept,
    gain2, low, second, kept2, low_back, gain, sides_wide, turned,
):
    inverse, smooth_own, smooth_beside = narrow.at[0:256], narrow.at[256:512], narrow.at[512:768]
    back, forward2, inverse2 = narrow.at[768:1024], narrow.at[1024:1152], narrow.at[1152:1280]
    lanes = mask_lanes(west, east, own_masks, north_mask, south_mask, wide)
    lane64 = lax.broadcasted_iota(jnp.int32, (1, NL), 1) < 64
    forward2_f = forward2[...].astype(F32)
    for ib in range(4):
        for n in range(4) if ib else (1, 3):
            b = 8 * ib + 4 * (n // 2) + n % 2 - 1
            smooth_two = lanes[b : b + 1, NL:] if n else jnp.ones((1, NL), F32)
            row = jnp.where(lane64, smooth_two, lanes[b + 2 : b + 3, NL:])
            both = dot((forward2_f * row).astype(BF16), inverse2[...]).astype(BF16)
            gain2[ib, n, 0:128, :] = both
            gain2[ib, n, 128:256, :] = both

    for at, count in ((0, 16), (16, 16), (32, 8)):
        part = dot(own_terms(parts.at[0], at, count), smooth_own[...])
        part += dot(beside_terms(west, east, at, count), smooth_beside[...])
        part = part.reshape(24, count, NL)
        if at < 32:
            low[:, 8 + at : 8 + at + count, :] = part
            if at == 0:
                low[:, 56:64, :] = part[:, 0:8]
        else:
            low[:, 0:8, :] = part
            low[:, 40:48, :] = part
            low[:, 48:56, :] = part

    def rows_two(v, _):
        for t in range(3):
            lifted = [
                lift_rows(lambda s: low[v * 8 + p, pl.ds(16 * t + s, 8, stride=2), :], 8) for p in range(8)
            ]
            for bx in range(2):
                smooth, detail = lift_planes([pair[bx] for pair in lifted])
                for bz, part in ((0, smooth), (1, detail)):
                    for z in range(4):
                        second[2 * bz + bx, t, pl.ds(pl.multiple_of((v * 4 + z) * 8, 8), 8), :] = part[z]
        return 0

    for v in range(NV):
        rows_two(v, 0)
    for n in range(4):
        for t in range(3):
            terms = jnp.concatenate(two_terms(second[n, t]), 1)
            if t < 2:
                kept2[n, :, 8 + 8 * t : 16 + 8 * t, :] = dot(terms, gain2[t + 1, n]).reshape(NV * 4, 8, NL)
            else:
                if n % 2:
                    kept2[n, :, 0:8, :] = dot(terms, gain2[0, n]).reshape(NV * 4, 8, NL)
                kept2[n, :, 24:32, :] = dot(terms, gain2[3, n]).reshape(NV * 4, 8, NL)

    def back_two(v, _):
        for t in range(3):
            pairs = {}
            for bz in range(2):
                for z in range(4):
                    p = v * 4 + z
                    if t < 2:
                        pairs[bz, z] = unlift_rows(
                            lambda r: kept2[2 * bz, p, pl.ds(r, 8), :],
                            lambda r: kept2[2 * bz + 1, p, pl.ds(r, 8), :],
                            8 + 8 * t,
                        )
                    else:
                        even = kept2[2 * bz, p, 24:32, :] - 0.25 * (
                            kept2[2 * bz + 1, p, 23:31, :] + kept2[2 * bz + 1, p, 24:32, :]
                        )
                        pairs[bz, z] = (even, even)
            for parity in range(2 if t < 2 else 1):
                planes = unlift_planes([pairs[0, z][parity] for z in range(4)], [pairs[1, z][parity] for z in range(4)])
                for z in range(8):
                    low_back[pl.ds((v * 8 + z) * 48 + 16 * t + parity, 8, stride=2), :] = planes[z]
        return 0

    for v in range(NV):
        back_two(v, 0)

    forward_f = wide[0:144, :].astype(F32)
    for ib in range(4):
        sides_wide[ib] = jnp.zeros((NL, 4 * NL), F32)
    for ib in range(4):
        for n in range(4) if ib else (1, 3):
            b = 8 * ib + 4 * (n // 2) + n % 2 - 1
            smooth_one = lanes[b : b + 1, 0:NL] if n else jnp.zeros((1, NL), F32)
            row = jnp.concatenate([smooth_one, lanes[b + 2 : b + 3, 0:NL]], 1)
            both = dot((forward_f * row).astype(BF16), inverse[...])
            main = both[0:128].astype(BF16)
            gain[ib, n, 0:128, :] = main
            gain[ib, n, 128:256, :] = main
            for i in range(3):
                at = list(beyond(n).values())[i]
                sides_wide[ib, at : at + 1, n * NL : (n + 1) * NL] = both[128 + i : 129 + i]

    gain_sides = []
    for ib in range(4):
        side = sides_wide[ib].astype(BF16)
        gain_sides.append(jnp.concatenate([side, side], 0))
    def put(n, p, at, rows):
        start = pl.multiple_of((n * 24 + p) * 48 + 8 + at, 8)
        kept[pl.ds(start, rows.shape[0]), :] = rows

    def row_of(ref, first, pitch):
        return ref[pl.ds(first, 24, stride=pitch), :]

    for ib in range(2):
        product = dot(beside_terms(west, east, 16 * ib, 16), gain_sides[ib + 1])
        for n in range(4):
            for p in range(24):
                put(n, p, 16 * ib, product[16 * p : 16 * p + 16, n * NL : (n + 1) * NL])

    def keep(n, _):
        for ib in range(2):
            product = dot(own_terms(parts.at[n], 16 * ib, 16), gain[ib + 1, n])
            for p in range(24):
                start = pl.ds(pl.multiple_of((n * 24 + p) * 48 + 8 + 16 * ib, 8), 16)
                kept[start, :] += product[16 * p : 16 * p + 16]
        return 0

    for n in range(4):
        keep(n, 0)
    for ib in range(2):
        rows = jnp.concatenate([low_back[48 * p + 16 * ib : 48 * p + 16 * ib + 16, :] for p in range(24)], 0)
        product = dot(jnp.concatenate(two_terms(rows), 1), back[...])
        for p in range(24):
            start = 48 * p + 8 + 16 * ib
            kept[start : start + 16, :] += product[16 * p : 16 * p + 16]
    tiles = beside_tiles(west, east, 32, 8)
    for p in range(24):
        turned[8 * p : 8 * p + 8, :] = tiles[p]
    for first, ib, place, row in ((0, 3, 40, 32), (7, 0, 7, 39)):
        beside = dot(jnp.concatenate(two_terms(row_of(turned, first, 8)), 1), gain_sides[ib])
        for n in range(4) if ib else (1, 3):
            own = jnp.concatenate(two_terms(row_of(flat, n * 24 * ROWS + row, ROWS)), 1)
            total = beside[:, n * NL : (n + 1) * NL] + dot(own, gain[ib, n])
            if n == 0:
                total += dot(jnp.concatenate(two_terms(row_of(low_back, row, 48)), 1), back[...])
            kept[pl.ds(n * 24 * 48 + place, 24, stride=48), :] = total


def cells_kernel(kept, out, cells, sems):
    def back_one(step, _):
        v, t = step // 4, step % 4
        pairs = {}
        for bz in range(2):
            for z in range(8):
                p = v * 8 + z
                pairs[bz, z] = unlift_rows(
                    lambda r: kept[2 * bz, p, pl.ds(8 * t + r, 8), :],
                    lambda r: kept[2 * bz + 1, p, pl.ds(8 * t + r, 8), :],
                    8,
                )
        for parity in range(2):
            planes = unlift_planes([pairs[0, z][parity] for z in range(8)], [pairs[1, z][parity] for z in range(8)])
            for z in range(NZ):
                cells[v, z, pl.ds(16 * t + parity, 8, stride=2), :] = planes[z]
        return 0

    def copy(step):
        v, rows = step // 4, pl.ds(pl.multiple_of(16 * (step % 4), 16), 16)
        return pltpu.make_async_copy(cells.at[v, :, rows], out.at[v, :, rows], sems.at[step])

    def one(step, _):
        back_one(step, 0)
        copy(step).start()
        return 0

    lax.fori_loop(0, NV * 4, one, 0)
    for step in range(NV * 4):
        copy(step).wait()


def main_specs():
    vmem = pl.BlockSpec(memory_space=pltpu.VMEM)
    return [
        vmem, vmem, vmem, vmem, vmem,
        pl.BlockSpec((1, 8, NL), lambda i: (9, 0, 0)), pl.BlockSpec((1, 8, NL), lambda i: (15, 0, 0)),
        vmem, vmem,
    ]


def main_step(flat, *operands):
    w = weights()
    return pl.pallas_call(
        main_kernel,
        grid=(1,),
        out_shape=jax.ShapeDtypeStruct((4 * NV * 8 * 48, NL), F32),
        in_specs=main_specs(),
        out_specs=pl.BlockSpec((4 * NV * 8 * 48, NL), lambda i: (0, 0)),
        scratch_shapes=[
            pltpu.VMEM((4, 4, 256, NL), BF16),
            pltpu.VMEM((NV * 8, 64, NL), F32),
            pltpu.VMEM((4, 3, NV * 32, NL), F32),
            pltpu.VMEM((4, NV * 4, 40, NL), F32),
            pltpu.VMEM((NV * 8 * 48, NL), F32),
            pltpu.VMEM((4, 4, 256, NL), BF16),
            pltpu.VMEM((4, NL, 4 * NL), F32),
            pltpu.VMEM((NV * 64, NL), F32),
        ],
        cost_estimate=cost(8),
        compiler_params=pltpu.CompilerParams(vmem_limit_bytes=VMEM_LIMIT),
    )(flat.reshape(4, NV * 8, ROWS, NL), flat, *operands, w["wide"], w["narrow"])


def cells_step(kept):
    shape = (NV, NZ, NR, NL)
    return pl.pallas_call(
        cells_kernel,
        out_shape=jax.ShapeDtypeStruct(shape, F32),
        in_specs=[pl.BlockSpec(memory_space=pltpu.VMEM)],
        out_specs=pl.BlockSpec(memory_space=pltpu.HBM),
        scratch_shapes=[pltpu.VMEM(shape, F32), pltpu.SemaphoreType.DMA((NV * 4,))],
        cost_estimate=cost(4),
        compiler_params=pltpu.CompilerParams(vmem_limit_bytes=VMEM_LIMIT),
    )(kept)


def rows_kernel(count_x, count_z, flip, *refs):
    shares, out = refs[count_x - 1 :: -1], refs[count_x + 1]
    me, me_y = lax.axis_index("gx"), lax.axis_index("gy") ^ flip
    row = lax.broadcasted_iota(jnp.int32, (8, NL), 0)
    lane = lax.broadcasted_iota(jnp.int32, (8, NL), 1)
    for r in range(count_x):
        at = pl.multiple_of(16 * (me ^ r), 16)
        for j in range(count_z):
            for z in range(4):
                start = 64 * j + 16 * z
                out[j, z, pl.ds(at, 16), :] = shares[r][start : start + 16, :]
    for j in range(count_z):
        turn = lanes_turn(me_y ^ (2 * j))
        piece = lax.rem(lane + (NL - turn), NL) // 21
        inside = [piece == p for p in range(5)]
        for r in range(count_x):
            i = me ^ r
            below = pl.multiple_of(16 * lax.rem(i + 1, count_x), 16)
            above = pl.multiple_of(16 * lax.rem(i + count_x - 1, count_x) + 8, 8)
            tiles = [shares[r][64 * j + 8 * g : 64 * j + 8 * g + 8, :] for g in range(8)]
            low, high = jnp.zeros((8, NL), F32), jnp.zeros((8, NL), F32)
            for p in range(5):
                back = (21 * p - 105) % NL
                low = jnp.where(inside[p], pltpu.roll(tiles[p], back, 1), low)
                extra = tiles[5 + p // 2]
                extra = extra if p % 2 else pltpu.roll(extra, 4, 0)
                high = jnp.where(inside[p], pltpu.roll(extra, back, 1), high)
            for z in range(4):
                first = pltpu.roll(low, 8 - 2 * z, 0) if z else low
                last = pltpu.roll(high, z, 0) if z else high
                out[j, z, pl.ds(below, 8), :] += jnp.where(row < 2, first, 0.0)
                out[j, z, pl.ds(above, 8), :] += jnp.where(row == 7, last, 0.0)


def rows_step(pieces, count_z, flip, after):
    vmem = pl.BlockSpec(memory_space=pltpu.VMEM)
    count_x = len(pieces)
    return pl.pallas_call(
        functools.partial(rows_kernel, count_x, count_z, flip),
        out_shape=jax.ShapeDtypeStruct((count_z, 4, 16 * count_x, NL), F32),
        in_specs=[vmem] * count_x + [pl.BlockSpec(memory_space=pl.ANY)],
        out_specs=vmem,
        compiler_params=pltpu.CompilerParams(vmem_limit_bytes=VMEM_LIMIT),
    )(*pieces[::-1], after)


def coarse_kernel(count_x, count_y, own, other, out_hbm, out, sems):
    me = lax.axis_index("gy")
    me_z, is_even = lax.shift_right_logical(me, 1), lax.rem(me, 2) == 0
    lane = lax.broadcasted_iota(jnp.int32, (8, NL), 1)
    place = [lax.rem(lane + NL - 35 * v, NL) for v in range(NV)]

    def block(i, _):
        rows = pl.ds(pl.multiple_of(8 * i, 8), 8)
        for z in range(4):
            pieces = []
            for j in range(count_y // 2):
                mine, theirs = own[j ^ me_z, z, rows, :], other[j ^ me_z, z, rows, :]
                pieces += [jnp.where(is_even, mine, theirs), jnp.where(is_even, theirs, mine)]
            for v in range(NV):
                at = place[v]
                for t in range(count_y // 4):
                    total = jnp.where(at < 2, pieces[4 * t - 1], 0.0)
                    total += jnp.where(at == NL - 1, pieces[(4 * t + 4) % count_y], 0.0)
                    for q in range(4):
                        inside = (at >= 32 * q - 1) & (at < 32 * q + 34)
                        total += jnp.where(inside, pieces[4 * t + q], 0.0)
                    out[v, z, rows, NL * t : NL * (t + 1)] = pltpu.roll(total, NL - 35 * v, 1) if v else total
        return 0

    def copy(i):
        rows = pl.ds(pl.multiple_of(16 * i, 16), 16)
        return pltpu.make_async_copy(out.at[:, :, rows], out_hbm.at[:, :, rows], sems.at[i])

    group = 4 if count_x % 4 == 0 else 1

    def several(i, _):
        for k in range(group):
            block(2 * (group * i + k), 0)
            block(2 * (group * i + k) + 1, 0)
            copy(group * i + k).start()
        return 0

    lax.fori_loop(0, count_x // group, several, 0)
    for i in range(count_x):
        copy(i).wait()


def coarse_step(own, other, count_x, count_y):
    vmem = pl.BlockSpec(memory_space=pltpu.VMEM)
    shape = (NV, 4, 16 * count_x, 32 * count_y)
    return pl.pallas_call(
        functools.partial(coarse_kernel, count_x, count_y),
        out_shape=jax.ShapeDtypeStruct(shape, F32),
        in_specs=[vmem, vmem],
        out_specs=pl.BlockSpec(memory_space=pltpu.HBM),
        scratch_shapes=[pltpu.VMEM(shape, F32), pltpu.SemaphoreType.DMA((count_x,))],
        compiler_params=pltpu.CompilerParams(vmem_limit_bytes=VMEM_LIMIT),
    )(own, other)


def shifted(x, axis, step):
    count = lax.axis_size(axis)
    return lax.ppermute(x, axis, [(i, (i + step) % count) for i in range(count)])


def swapped(x, axis, distance):
    return lax.ppermute(x, axis, [(i, i ^ distance) for i in range(lax.axis_size(axis))])


def body(field, masks):
    count_x, count_y = lax.axis_size("gx"), lax.axis_size("gy")
    lifted, up, down, own_masks, share = first_step(field, masks)
    south = shifted(up, "gx", -1)
    north = shifted(down, "gx", 1)
    shares = [share] + [swapped(share, "gy", r) for r in range(2, count_y, 2)]
    parts, to_left, to_right = edge_step(lift_step(lifted), lifted, north, south, own_masks)
    east = shifted(to_left, "gy", -1)
    west = shifted(to_right, "gy", 1)
    joined = join_step(shares, to_left)
    pieces = [joined] + [swapped(joined, "gx", r) for r in range(1, count_x)]
    kept = main_step(parts, east, west, own_masks, north, south)
    restored = cells_step(kept.reshape(4, NV * 8, 48, NL))
    pieces[-1], restored = lax.optimization_barrier((pieces[-1], restored))
    others = [swapped(piece, "gy", 1) for piece in pieces]
    own = rows_step(pieces, count_y // 2, 0, kept)
    other = rows_step(others, count_y // 2, 1, own)
    return restored, coarse_step(own, other, count_x, count_y)


def solution(mesh):
    placed = P(None, None, "gx", "gy")
    return jax.shard_map(
        body,
        mesh=mesh,
        in_specs=(placed, placed),
        out_specs=(placed, P()),
        check_vma=False,
    )
```

```python
import functools

import jax
import jax.numpy as jnp
import ml_dtypes
import numpy as np
from jax import lax
from jax.experimental import pallas as pl
from jax.experimental.pallas import tpu as pltpu
from jax.sharding import PartitionSpec as P

F32 = jnp.float32
BF16 = jnp.bfloat16
VMEM_LIMIT = 32 * 1024 * 1024

NV, NZ, NR, NL = 3, 16, 64, 128


def detail_row(k):
    return {2 * k + 1: 1.0, 2 * k: -0.5, 2 * k + 2: -0.5}


def smooth_row(k):
    row = {2 * k: 1.0}
    for j in (k - 1, k):
        for cell, value in detail_row(j).items():
            row[cell] = row.get(cell, 0.0) + 0.25 * value
    return row


def even_row(k):
    return {("s", k): 1.0, ("d", k - 1): -0.25, ("d", k): -0.25}


def odd_row(k):
    row = {("d", k): 1.0}
    for j in (k, k + 1):
        for name, value in even_row(j).items():
            row[name] = row.get(name, 0.0) + 0.5 * value
    return row


def as_bf16(matrix):
    cast = matrix.astype(ml_dtypes.bfloat16)
    assert (cast.astype(np.float64) == matrix).all()
    return cast


def combine(*terms):
    total = {}
    for factor, row in terms:
        for cell, value in row.items():
            total[cell] = total.get(cell, 0.0) + factor * value
    return total


def level_one_columns():
    names = {("s", k): k for k in range(65)}
    names.update({("d", k): 128 + k for k in range(65)})
    names[("d", -1)] = 128 + 65
    return names


def level_two_columns():
    names = {("s", k): k for k in range(33)}
    names.update({("d", k): 64 + k for k in range(33)})
    names[("d", -1)] = 64 + 33
    return names


def smooth_place(k):
    return k + 2


def beyond(n):
    return {"cell": 40 + 16 * n, "after": 48 + 16 * n, "before": 8 * n}


BEYOND_SMOOTH = {65: 104, -1: 32}
FROM_WEST = 40


def own_row(kind, k, n):
    place = {name: 128 + lane for name, lane in beyond(n).items()}
    if kind == "d":
        if k == -1:
            return {place["before"]: 1.0, 0: -0.5}
        if k == 64:
            return {place["after"]: 1.0}
        return {(place["cell"] if y == 128 else y): value for y, value in detail_row(k).items()}
    if k in (-2, 66):
        return {}
    if k in BEYOND_SMOOTH:
        row = {128 + BEYOND_SMOOTH[k]: 1.0}
        return combine((1.0, row), (1.0, {0: -0.125})) if k == -1 else row
    even = place["cell"] if k == 64 else 2 * k
    return combine((1.0, {even: 1.0}), (0.25, own_row("d", k - 1, n)), (0.25, own_row("d", k, n)))


@functools.lru_cache(maxsize=None)
def weights():
    w = {}
    names = level_one_columns()
    forward = np.zeros((4, 256, 256))
    inverse = np.zeros((256, 128))
    for (kind, k), column in names.items():
        for n in range(4):
            for place, value in own_row(kind, k, n).items():
                forward[n, place, column] += value
    for k in range(64):
        for y, row in ((2 * k, even_row(k)), (2 * k + 1, odd_row(k))):
            for name, value in row.items():
                inverse[names[name], y] += value
    short = np.zeros((144, 256))
    short[:128] = forward[0, :128]
    for i, lane in enumerate(beyond(0).values()):
        short[128 + i] = forward[0, 128 + lane]
    smooth = np.zeros((256, 128))
    for k in range(-2, 67):
        for place, value in own_row("s", k, 0).items():
            smooth[place, smooth_place(k)] += value
    names2 = level_two_columns()
    forward2 = np.zeros((128, 128))
    inverse2 = np.zeros((128, 128))
    for (kind, k), column in names2.items():
        for cell, value in (smooth_row(k) if kind == "s" else detail_row(k)).items():
            forward2[smooth_place(cell), column] += value
    for k in range(33):
        rows = [(2 * k, even_row(k))] + ([(2 * k + 1, odd_row(k))] if k < 32 else [])
        for y, row in rows:
            for name, value in row.items():
                inverse2[names2[name], y] += value
    back = np.zeros((256, 128))
    back[:65] = inverse[:65]
    back[128 : 128 + 65] = inverse[:65]
    spread = np.zeros((3, 128, 2, 128))
    for k in range(64):
        spread[0, k, 0, k] = 1
    for k in range(32):
        spread[0, 64 + k, 1, k] = 1
        spread[0, 64 + k, 1, 64 + k] = 1
    for at in range(0, 16, 4):
        spread[1, at, 0, 64] = 1
        spread[2, at + 1, 0, 65] = 1
        for base in (0, 64):
            spread[1, at + 2, 1, base + 32] = 1
            spread[2, at + 3, 1, base + 33] = 1
    w["wide"] = np.concatenate([short, spread.reshape(384, 256)], 0)
    own, beside = smooth[:128], smooth[128:]
    w["narrow"] = np.concatenate([inverse, own, own, beside, beside, back, forward2, inverse2], 0)
    edge = np.zeros((4, 128, 128))

    def put(n, lane, row):
        for z in range(8):
            for y, value in row.items():
                j = y - 120 if y >= 120 else y + 8
                edge[n, 16 * z + j, lane + z] += value

    part = {127: 1.0, 126: -0.5}
    for n in range(4):
        put(n, beyond(n)["cell"], {0: 1.0})
        put(n, beyond(n)["after"], detail_row(0))
        put(n, beyond(n)["before"], part)
    put(0, BEYOND_SMOOTH[65], combine((1.0, smooth_row(1)), (-0.5, smooth_row(2))))
    share = combine((1.0, {126: 1.0}), (0.25, detail_row(62)), (0.25, part))
    put(0, BEYOND_SMOOTH[-1], combine((1.0, share), (-0.5, smooth_row(62))))
    w["edge"] = edge.reshape(512, 128)
    expand = np.zeros((2, 4, 128))
    for j in range(4):
        expand[0, j, 16 * j : 16 * j + 16] = 1
        expand[1, j, 64 + 8 * j : 64 + 8 * j + 8] = 1
    twice = combine(*[(value, smooth_row(k)) for k, value in smooth_row(0).items()])
    columns = np.zeros((2, 128, 128))
    for m in range(-1, 34):
        for t, value in twice.items():
            if 0 <= 4 * m + t < NL:
                columns[:, 4 * m + t, m + 1] = value
    rows = np.zeros((4, 32, 2, 64))
    for z in range(4):
        places = {m: m for m in range(16)}
        places.update({16: 16 + 2 * z, 17: 17 + 2 * z, -1: 16 + 15 - z})
        for m, place in places.items():
            for t, value in twice.items():
                if 0 <= 4 * m + t < NR:
                    rows[z, place, :, 4 * m + t] = value
    pad = np.zeros((8, 128))
    w["first"] = np.concatenate([columns.reshape(256, 128), rows.reshape(128, 128), expand.reshape(8, 128), pad], 0)
    return {name: as_bf16(matrix) for name, matrix in w.items()}


def two_terms(x):
    high = x.astype(BF16)
    low = (x - high.astype(F32)).astype(BF16)
    return high, low


def cost(gigaflops):
    return pl.CostEstimate(flops=gigaflops * 10**9, bytes_accessed=8 * 10**6, transcendentals=0)


def dot(a, b):
    return jnp.dot(a, b, preferred_element_type=F32)


def lift_planes(cells):
    half = len(cells) // 2
    even, odd = cells[0::2], cells[1::2]
    detail = [odd[k] - 0.5 * (even[k] + even[min(k + 1, half - 1)]) for k in range(half)]
    smooth = [even[k] + 0.25 * (detail[max(k - 1, 0)] + detail[k]) for k in range(half)]
    return smooth, detail


def unlift_planes(smooth, detail):
    half = len(smooth)
    even = [smooth[k] - 0.25 * (detail[max(k - 1, 0)] + detail[k]) for k in range(half)]
    out = []
    for k in range(half):
        out += [even[k], detail[k] + 0.5 * (even[k] + even[min(k + 1, half - 1)])]
    return out


def lift_rows(load, start):
    even, odd, after = load(start), load(start + 1), load(start + 2)
    before, odd_before = load(start - 2), load(start - 1)
    detail = odd - 0.5 * (even + after)
    detail_before = odd_before - 0.5 * (before + even)
    return even + 0.25 * (detail_before + detail), detail


def unlift_rows(smooth, detail, row):
    here, after = detail(row), detail(row + 1)
    even = smooth(row) - 0.25 * (detail(row - 1) + here)
    next_even = smooth(row + 1) - 0.25 * (here + after)
    return even, here + 0.5 * (even + next_even)


PITCH = 80


def lanes_turn(j):
    return lax.rem(32 * lax.rem(j, 4) + NL - 1, NL)


def first_kernel(
    field, masks_hbm, table_hbm, lifted, up, down, own_masks, share, cells, twice, masks, table, sems
):
    small = [
        pltpu.make_async_copy(masks_hbm, masks, sems.at[0]),
        pltpu.make_async_copy(table_hbm, table, sems.at[1]),
    ]
    copies = []
    for v in range(NV):
        for c in range(4):
            part = pl.ds(16 * c, 16)
            copies.append(pltpu.make_async_copy(field.at[v, :, part], cells.at[v, :, part], sems.at[2 + 4 * v + c]))
    for copy in small + copies:
        copy.start()
    for p in range(NV * NZ):
        lifted[p * PITCH : p * PITCH + 8, :] = jnp.zeros((8, NL), F32)
        lifted[p * PITCH + 72 : p * PITCH + 80, :] = jnp.zeros((8, NL), F32)
    for copy in small:
        copy.wait()
    for i, out, tile in ((0, up, 15), (1, down, 9)):
        total = jnp.zeros((7, NL), F32)
        for l in range(2):
            flags = masks[l, i].astype(F32).astype(BF16)
            spread = table[384 + 4 * l : 388 + 4 * l, :]
            total += lax.dot_general(flags, spread, (((0,), (0,)), ((), ())), preferred_element_type=F32)
        own_masks[i] = jnp.concatenate([total, jnp.zeros((1, NL), F32)], 0)
        out[tile] = own_masks[i]

    for v in range(NV):
        for t in range(8):
            if t % 2 == 0:
                copies[4 * v + t // 2].wait()
            smooth, detail = lift_planes([cells[v, z, 8 * t : 8 * t + 8, :] for z in range(NZ)])
            for k, tile in enumerate(smooth + detail):
                start = (v * NZ + k) * PITCH + 8 + 8 * t
                lifted[start : start + 8, :] = tile
            for k, tile in enumerate(lift_planes(smooth)[0]):
                twice[v * 4 + k, 8 * t : 8 * t + 8, :] = tile
        for bz in range(2):

            def row(x):
                return lifted[pl.ds((v * NZ + bz * 8) * PITCH + 8 + x, 8, stride=PITCH), :]

            x = [row(j) for j in range(7 if bz == 0 else 3)]
            first = x[1] - 0.5 * (x[0] + x[2])
            up[v * 5 + bz] = x[0]
            up[v * 5 + 2 + bz] = first
            y = {j: row(j) for j in (range(58, 64) if bz == 0 else (62, 63))}
            part = y[63] - 0.5 * y[62]
            down[v * 3 + bz] = part
            if bz == 0:
                second = x[3] - 0.5 * (x[2] + x[4])
                third = x[5] - 0.5 * (x[4] + x[6])
                up[v * 5 + 4] = x[2] + 0.25 * (first + second) - 0.5 * (x[4] + 0.25 * (second + third))
                before = y[59] - 0.5 * (y[58] + y[60])
                last = y[61] - 0.5 * (y[60] + y[62])
                down[v * 3 + 2] = y[62] + 0.25 * (last + part) - 0.5 * (y[60] + 0.25 * (before + last))

    total = jnp.zeros((80, NL), F32)
    for v in range(NV):
        main, extra = [], jnp.zeros((16, NL), F32)
        for z in range(4):
            terms = jnp.concatenate(two_terms(twice[v * 4 + z]), 0)
            part = dot(table[256 + 32 * z : 288 + 32 * z, :], terms)
            main.append(part[:16])
            extra += part[16:]
        terms = jnp.concatenate(two_terms(jnp.concatenate(main + [extra], 0)), 1)
        part = dot(terms, table[0:256, :])
        total += pltpu.roll(part, 35 * v, 1) if v else part
    turn = lanes_turn(lax.axis_index("gy"))
    lane = lax.broadcasted_iota(jnp.int32, (8, NL), 1)
    spare = (lane >= 105) & (lane < 126)
    upper = lax.broadcasted_iota(jnp.int32, (8, NL), 0) < 4
    below, above = total[64:72], total[72:80]
    pieces = [pltpu.roll(above, 105 - 21 * p, 1) for p in range(5)]
    for g in range(8):
        if g < 5:
            extra = pltpu.roll(below, 105 - 21 * g, 1)
        else:
            extra = pltpu.roll(pieces[2 * g - 10], 4, 0)
            extra = jnp.where(upper, extra, pieces[2 * g - 9] if g < 7 else 0.0)
        tile = jnp.where(spare, extra, total[8 * g : 8 * g + 8])
        share[8 * g : 8 * g + 8, :] = pltpu.roll(tile, turn, 1)


def in_hbm(x):
    return pltpu.with_memory_space_constraint(x, pltpu.HBM)


def first_step(field, masks):
    vmem = pl.BlockSpec(memory_space=pltpu.VMEM)
    shapes = [(NV * NZ * PITCH, NL), (16, 8, NL), (10, 8, NL), (2, 8, NL), (64, NL)]
    return pl.pallas_call(
        first_kernel,
        out_shape=[jax.ShapeDtypeStruct(s, F32) for s in shapes],
        in_specs=[pl.BlockSpec(memory_space=pltpu.HBM)] * 3,
        out_specs=[vmem] * 5,
        scratch_shapes=[
            pltpu.VMEM((NV, NZ, NR, NL), F32),
            pltpu.VMEM((NV * 4, NR, NL), F32),
            pltpu.VMEM((2, 2, 4, 7), jnp.int32),
            pltpu.VMEM((400, NL), BF16),
            pltpu.SemaphoreType.DMA((4 * NV + 2,)),
        ],
        compiler_params=pltpu.CompilerParams(vmem_limit_bytes=VMEM_LIMIT),
    )(*[in_hbm(x) for x in (field, masks.transpose(0, 2, 3, 1), jnp.asarray(weights()["first"]))])


ROWS = 40


def lift_kernel(lifted, parts):
    def lift(step, _):
        v, bz = step // 2, lax.rem(step, 2)
        for z in range(8):
            start = pl.multiple_of((step * 8 + z) * PITCH, 8)
            for t in range(4):
                pair = lift_rows(lambda s: lifted[pl.ds(start + 16 * t + s, 8, stride=2), :], 8)
                for bx in range(2):
                    plane = (2 * bz + bx) * 24 + v * 8 + z
                    parts[pl.ds(pl.multiple_of(plane * ROWS + 8 * t, 8), 8), :] = pair[bx]
        return 0

    lax.fori_loop(0, NV * 2, lift, 0)


def lift_step(lifted):
    vmem = pl.BlockSpec(memory_space=pltpu.VMEM)
    return pl.pallas_call(
        lift_kernel,
        out_shape=jax.ShapeDtypeStruct((4 * NV * 8 * ROWS, NL), F32),
        in_specs=[vmem],
        out_specs=vmem,
        compiler_params=pltpu.CompilerParams(vmem_limit_bytes=VMEM_LIMIT),
    )(lifted)


def edge_kernel(parts_in, lifted, north, south, own_masks, table_hbm, parts, to_left, to_right, packed, table, sem):
    copy = pltpu.make_async_copy(table_hbm, table, sem.at[0])
    copy.start()
    for p in range(4 * NV * 8):
        parts[p * ROWS + 32 : p * ROWS + 40, :] = jnp.zeros((8, NL), F32)
    for v in range(NV):
        for bz in range(2):

            def cell(x):
                return lifted[pl.ds((v * NZ + bz * 8) * PITCH + 8 + x, 8, stride=PITCH), :]

            def at(bx, r):
                return pl.ds(((2 * bz + bx) * 24 + v * 8) * ROWS + r, 8, stride=ROWS)

            before, after, detail = north[v * 3 + bz], south[v * 5 + bz], south[v * 5 + 2 + bz]
            start = cell(0)
            last = cell(63) - 0.5 * (cell(62) + after)
            parts[at(0, 0), :] = parts[at(0, 0), :] + 0.25 * before
            parts[at(0, 31), :] = parts[at(0, 31), :] - 0.125 * after
            parts[at(1, 31), :] = parts[at(1, 31), :] - 0.5 * after
            parts[at(0, 32), :] = after + 0.25 * (last + detail)
            parts[at(1, 32), :] = detail
            parts[at(1, 39), :] = before - 0.5 * start
            if bz == 0:
                parts[at(0, 33), :] = south[v * 5 + 4]
                parts[at(0, 39), :] = north[v * 3 + 2] - 0.125 * start

    lane = lax.broadcasted_iota(jnp.int32, (8, NL), 1) // 16

    def pack(v, _):
        for n in range(4):
            for t in range(5):
                tile = jnp.zeros((8, NL), F32)
                for z in range(8):
                    start = (n * 24 + v * 8 + z) * ROWS + 8 * t
                    x = parts[pl.ds(pl.multiple_of(start, 8), 8), :]
                    tile = jnp.where(lane == z, pltpu.roll(x, (8 + 16 * z) % NL, 1), tile)
                packed[pl.ds(pl.multiple_of(n * 120 + v * ROWS + 8 * t, 8), 8), :] = tile
        return 0

    for v in range(NV):
        pack(v, 0)
    copy.wait()
    terms = [two_terms(packed[n * 120 : (n + 1) * 120, :]) for n in range(4)]
    high, low = [jnp.concatenate(part, 1) for part in zip(*terms)]
    sides = dot(high, table[...]) + dot(low, table[...])
    lane = lax.broadcasted_iota(jnp.int32, (ROWS, NL), 1)
    each = [sides[v * ROWS : (v + 1) * ROWS] for v in range(NV)]
    right = jnp.where(lane < 40, each[0], pltpu.roll(each[1], 40, 1))
    to_right[0:ROWS, :] = jnp.where(lane < 80, right, pltpu.roll(each[2], 80, 1))
    last = jnp.where(lane < 32, pltpu.roll(each[2], NL - 40, 1), pltpu.roll(each[2], NL - 72, 1))
    to_left[0:ROWS, :] = jnp.where(lane < 40, last, each[0])
    to_left[ROWS : 2 * ROWS, :] = jnp.where(lane < 32, pltpu.roll(each[2], NL - 72, 1), each[1])
    lane = lax.broadcasted_iota(jnp.int32, (8, NL), 1)
    ends = jnp.zeros((8, NL), F32)
    for ib, tile in enumerate((north[9], own_masks[0], own_masks[1], south[15])):
        for j, source in enumerate((0, 63, 64, 95)):
            target = 4 * ib + j
            ends = jnp.where(lane == target, pltpu.roll(tile, (target - source) % NL, 1), ends)
    to_left[2 * ROWS : 2 * ROWS + 8, :] = ends
    to_right[ROWS : ROWS + 8, :] = ends


def edge_step(parts, lifted, north, south, own_masks):
    vmem = pl.BlockSpec(memory_space=pltpu.VMEM)
    shapes = [(4 * NV * 8 * ROWS, NL), (2 * ROWS + 8, NL), (ROWS + 8, NL)]
    return pl.pallas_call(
        edge_kernel,
        out_shape=[jax.ShapeDtypeStruct(s, F32) for s in shapes],
        in_specs=[vmem] * 5 + [pl.BlockSpec(memory_space=pltpu.HBM)],
        out_specs=[vmem] * 3,
        input_output_aliases={0: 0},
        cost_estimate=cost(20),
        scratch_shapes=[pltpu.VMEM((480, NL), F32), pltpu.VMEM((512, NL), BF16), pltpu.SemaphoreType.DMA((1,))],
        compiler_params=pltpu.CompilerParams(vmem_limit_bytes=VMEM_LIMIT),
    )(parts, lifted, north, south, own_masks, in_hbm(jnp.asarray(weights()["edge"])))


def join_kernel(*refs):
    shares, out = refs[-3::-1], refs[-1]
    for n, piece in enumerate(shares):
        out[64 * n : 64 * (n + 1), :] = piece[...]


def join_step(shares, after):
    vmem = pl.BlockSpec(memory_space=pltpu.VMEM)
    return pl.pallas_call(
        join_kernel,
        out_shape=jax.ShapeDtypeStruct((64 * len(shares), NL), F32),
        in_specs=[vmem] * len(shares) + [pl.BlockSpec(memory_space=pl.ANY)],
        out_specs=vmem,
        cost_estimate=cost(20),
        compiler_params=pltpu.CompilerParams(vmem_limit_bytes=VMEM_LIMIT),
    )(*shares[::-1], after)


def mask_lanes(west, east, own_masks, north_mask, south_mask, wide):
    group = lax.broadcasted_iota(jnp.int32, (8, NL), 1) // 4
    masks = [
        jnp.concatenate([jnp.where(group == ib, tile, 0.0) for ib in range(4)], 0)
        for tile in (east[2 * ROWS : 2 * ROWS + 8, :], west[ROWS : ROWS + 8, :])
    ]
    own = jnp.concatenate([north_mask[0], own_masks[0], own_masks[1], south_mask[0]], 0)
    flags = jnp.concatenate([own] + masks, 1).astype(BF16)
    return dot(flags, wide[144:528, :])


def beside_tiles(west, east, at, count):
    lane = lax.broadcasted_iota(jnp.int32, (count, NL), 1)
    left = west[at : at + count, :]
    first, second = east[at : at + count, :], east[ROWS + at : ROWS + at + count, :]
    third = jnp.where(lane < 104, pltpu.roll(second, 72, 1), pltpu.roll(first, 72, 1))
    third = jnp.where(lane < 72, pltpu.roll(first, 40, 1), third)
    tiles = []
    for v, right in enumerate((first, second, third)):
        beside = jnp.where(lane < FROM_WEST, pltpu.roll(left, NL - 40 * v, 1) if v else left, right)
        tiles += [pltpu.roll(beside, NL - z, 1) if z else beside for z in range(8)]
    return tiles


def beside_terms(west, east, at, count):
    return jnp.concatenate(two_terms(jnp.concatenate(beside_tiles(west, east, at, count), 0)), 1)


def own_terms(planes, at, count):
    return jnp.concatenate(two_terms(planes[:, at : at + count, :].reshape(24 * count, NL)), 1)


def main_kernel(
    parts, flat, east, west, own_masks, north_mask, south_mask, wide, narrow,
    kept,
    gain2, low, second, kept2, low_back, gain, sides_wide, turned,
):
    inverse, smooth_own, smooth_beside = narrow.at[0:256], narrow.at[256:512], narrow.at[512:768]
    back, forward2, inverse2 = narrow.at[768:1024], narrow.at[1024:1152], narrow.at[1152:1280]
    lanes = mask_lanes(west, east, own_masks, north_mask, south_mask, wide)
    lane64 = lax.broadcasted_iota(jnp.int32, (1, NL), 1) < 64
    forward2_f = forward2[...].astype(F32)
    for ib in range(4):
        for n in range(4) if ib else (1, 3):
            b = 8 * ib + 4 * (n // 2) + n % 2 - 1
            smooth_two = lanes[b : b + 1, NL:] if n else jnp.ones((1, NL), F32)
            row = jnp.where(lane64, smooth_two, lanes[b + 2 : b + 3, NL:])
            both = dot((forward2_f * row).astype(BF16), inverse2[...]).astype(BF16)
            gain2[ib, n, 0:128, :] = both
            gain2[ib, n, 128:256, :] = both

    for at, count in ((0, 16), (16, 16), (32, 8)):
        part = dot(own_terms(parts.at[0], at, count), smooth_own[...])
        part += dot(beside_terms(west, east, at, count), smooth_beside[...])
        part = part.reshape(24, count, NL)
        if at < 32:
            low[:, 8 + at : 8 + at + count, :] = part
            if at == 0:
                low[:, 56:64, :] = part[:, 0:8]
        else:
            low[:, 0:8, :] = part
            low[:, 40:48, :] = part
            low[:, 48:56, :] = part

    def rows_two(v, _):
        for t in range(3):
            lifted = [
                lift_rows(lambda s: low[v * 8 + p, pl.ds(16 * t + s, 8, stride=2), :], 8) for p in range(8)
            ]
            for bx in range(2):
                smooth, detail = lift_planes([pair[bx] for pair in lifted])
                for bz, part in ((0, smooth), (1, detail)):
                    for z in range(4):
                        second[2 * bz + bx, t, pl.ds(pl.multiple_of((v * 4 + z) * 8, 8), 8), :] = part[z]
        return 0

    for v in range(NV):
        rows_two(v, 0)
    for n in range(4):
        for t in range(3):
            terms = jnp.concatenate(two_terms(second[n, t]), 1)
            if t < 2:
                kept2[n, :, 8 + 8 * t : 16 + 8 * t, :] = dot(terms, gain2[t + 1, n]).reshape(NV * 4, 8, NL)
            else:
                if n % 2:
                    kept2[n, :, 0:8, :] = dot(terms, gain2[0, n]).reshape(NV * 4, 8, NL)
                kept2[n, :, 24:32, :] = dot(terms, gain2[3, n]).reshape(NV * 4, 8, NL)

    def back_two(v, _):
        for t in range(3):
            pairs = {}
            for bz in range(2):
                for z in range(4):
                    p = v * 4 + z
                    if t < 2:
                        pairs[bz, z] = unlift_rows(
                            lambda r: kept2[2 * bz, p, pl.ds(r, 8), :],
                            lambda r: kept2[2 * bz + 1, p, pl.ds(r, 8), :],
                            8 + 8 * t,
                        )
                    else:
                        even = kept2[2 * bz, p, 24:32, :] - 0.25 * (
                            kept2[2 * bz + 1, p, 23:31, :] + kept2[2 * bz + 1, p, 24:32, :]
                        )
                        pairs[bz, z] = (even, even)
            for parity in range(2 if t < 2 else 1):
                planes = unlift_planes([pairs[0, z][parity] for z in range(4)], [pairs[1, z][parity] for z in range(4)])
                for z in range(8):
                    low_back[pl.ds((v * 8 + z) * 48 + 16 * t + parity, 8, stride=2), :] = planes[z]
        return 0

    for v in range(NV):
        back_two(v, 0)

    forward_f = wide[0:144, :].astype(F32)
    for ib in range(4):
        sides_wide[ib] = jnp.zeros((NL, 4 * NL), F32)
    for ib in range(4):
        for n in range(4) if ib else (1, 3):
            b = 8 * ib + 4 * (n // 2) + n % 2 - 1
            smooth_one = lanes[b : b + 1, 0:NL] if n else jnp.zeros((1, NL), F32)
            row = jnp.concatenate([smooth_one, lanes[b + 2 : b + 3, 0:NL]], 1)
            both = dot((forward_f * row).astype(BF16), inverse[...])
            main = both[0:128].astype(BF16)
            gain[ib, n, 0:128, :] = main
            gain[ib, n, 128:256, :] = main
            for i in range(3):
                at = list(beyond(n).values())[i]
                sides_wide[ib, at : at + 1, n * NL : (n + 1) * NL] = both[128 + i : 129 + i]

    gain_sides = []
    for ib in range(4):
        side = sides_wide[ib].astype(BF16)
        gain_sides.append(jnp.concatenate([side, side], 0))
    def put(n, p, at, rows):
        start = pl.multiple_of((n * 24 + p) * 48 + 8 + at, 8)
        kept[pl.ds(start, rows.shape[0]), :] = rows

    def row_of(ref, first, pitch):
        return ref[pl.ds(first, 24, stride=pitch), :]

    for ib in range(2):
        product = dot(beside_terms(west, east, 16 * ib, 16), gain_sides[ib + 1])
        for n in range(4):
            for p in range(24):
                put(n, p, 16 * ib, product[16 * p : 16 * p + 16, n * NL : (n + 1) * NL])

    def keep(n, _):
        for ib in range(2):
            product = dot(own_terms(parts.at[n], 16 * ib, 16), gain[ib + 1, n])
            for p in range(24):
                start = pl.ds(pl.multiple_of((n * 24 + p) * 48 + 8 + 16 * ib, 8), 16)
                kept[start, :] += product[16 * p : 16 * p + 16]
        return 0

    for n in range(4):
        keep(n, 0)
    for ib in range(2):
        rows = jnp.concatenate([low_back[48 * p + 16 * ib : 48 * p + 16 * ib + 16, :] for p in range(24)], 0)
        product = dot(jnp.concatenate(two_terms(rows), 1), back[...])
        for p in range(24):
            start = 48 * p + 8 + 16 * ib
            kept[start : start + 16, :] += product[16 * p : 16 * p + 16]
    tiles = beside_tiles(west, east, 32, 8)
    for p in range(24):
        turned[8 * p : 8 * p + 8, :] = tiles[p]
    for first, ib, place, row in ((0, 3, 40, 32), (7, 0, 7, 39)):
        beside = dot(jnp.concatenate(two_terms(row_of(turned, first, 8)), 1), gain_sides[ib])
        for n in range(4) if ib else (1, 3):
            own = jnp.concatenate(two_terms(row_of(flat, n * 24 * ROWS + row, ROWS)), 1)
            total = beside[:, n * NL : (n + 1) * NL] + dot(own, gain[ib, n])
            if n == 0:
                total += dot(jnp.concatenate(two_terms(row_of(low_back, row, 48)), 1), back[...])
            kept[pl.ds(n * 24 * 48 + place, 24, stride=48), :] = total


def cells_kernel(kept, out, cells, sems):
    def back_one(step, _):
        v, t = step // 4, step % 4
        pairs = {}
        for bz in range(2):
            for z in range(8):
                p = v * 8 + z
                pairs[bz, z] = unlift_rows(
                    lambda r: kept[2 * bz, p, pl.ds(8 * t + r, 8), :],
                    lambda r: kept[2 * bz + 1, p, pl.ds(8 * t + r, 8), :],
                    8,
                )
        for parity in range(2):
            planes = unlift_planes([pairs[0, z][parity] for z in range(8)], [pairs[1, z][parity] for z in range(8)])
            for z in range(NZ):
                cells[v, z, pl.ds(16 * t + parity, 8, stride=2), :] = planes[z]
        return 0

    def copy(step):
        v, rows = step // 4, pl.ds(pl.multiple_of(16 * (step % 4), 16), 16)
        return pltpu.make_async_copy(cells.at[v, :, rows], out.at[v, :, rows], sems.at[step])

    def one(step, _):
        back_one(step, 0)
        copy(step).start()
        return 0

    def four(v, _):
        for t in range(4):
            one(4 * v + t, 0)
        return 0

    lax.fori_loop(0, NV, four, 0)
    for step in range(NV * 4):
        copy(step).wait()


def main_specs():
    vmem = pl.BlockSpec(memory_space=pltpu.VMEM)
    return [
        vmem, vmem, vmem, vmem, vmem,
        pl.BlockSpec((1, 8, NL), lambda i: (9, 0, 0)), pl.BlockSpec((1, 8, NL), lambda i: (15, 0, 0)),
        vmem, vmem,
    ]


def main_step(flat, *operands):
    w = weights()
    return pl.pallas_call(
        main_kernel,
        grid=(1,),
        out_shape=jax.ShapeDtypeStruct((4 * NV * 8 * 48, NL), F32),
        in_specs=main_specs(),
        out_specs=pl.BlockSpec((4 * NV * 8 * 48, NL), lambda i: (0, 0)),
        scratch_shapes=[
            pltpu.VMEM((4, 4, 256, NL), BF16),
            pltpu.VMEM((NV * 8, 64, NL), F32),
            pltpu.VMEM((4, 3, NV * 32, NL), F32),
            pltpu.VMEM((4, NV * 4, 40, NL), F32),
            pltpu.VMEM((NV * 8 * 48, NL), F32),
            pltpu.VMEM((4, 4, 256, NL), BF16),
            pltpu.VMEM((4, NL, 4 * NL), F32),
            pltpu.VMEM((NV * 64, NL), F32),
        ],
        cost_estimate=cost(8),
        compiler_params=pltpu.CompilerParams(vmem_limit_bytes=VMEM_LIMIT),
    )(flat.reshape(4, NV * 8, ROWS, NL), flat, *operands, w["wide"], w["narrow"])


def cells_step(kept):
    shape = (NV, NZ, NR, NL)
    return pl.pallas_call(
        cells_kernel,
        out_shape=jax.ShapeDtypeStruct(shape, F32),
        in_specs=[pl.BlockSpec(memory_space=pltpu.VMEM)],
        out_specs=pl.BlockSpec(memory_space=pltpu.HBM),
        scratch_shapes=[pltpu.VMEM(shape, F32), pltpu.SemaphoreType.DMA((NV * 4,))],
        cost_estimate=cost(4),
        compiler_params=pltpu.CompilerParams(vmem_limit_bytes=VMEM_LIMIT),
    )(kept)


def rows_kernel(count_x, count_z, flip, *refs):
    shares, out = refs[count_x - 1 :: -1], refs[count_x + 1]
    me, me_y = lax.axis_index("gx"), lax.axis_index("gy") ^ flip
    row = lax.broadcasted_iota(jnp.int32, (8, NL), 0)
    lane = lax.broadcasted_iota(jnp.int32, (8, NL), 1)
    for r in range(count_x):
        at = pl.multiple_of(16 * (me ^ r), 16)
        for j in range(count_z):
            for z in range(4):
                start = 64 * j + 16 * z
                out[j, z, pl.ds(at, 16), :] = shares[r][start : start + 16, :]
    for j in range(count_z):
        turn = lanes_turn(me_y ^ (2 * j))
        piece = lax.rem(lane + (NL - turn), NL) // 21
        inside = [piece == p for p in range(5)]
        for r in range(count_x):
            i = me ^ r
            below = pl.multiple_of(16 * lax.rem(i + 1, count_x), 16)
            above = pl.multiple_of(16 * lax.rem(i + count_x - 1, count_x) + 8, 8)
            tiles = [shares[r][64 * j + 8 * g : 64 * j + 8 * g + 8, :] for g in range(8)]
            low, high = jnp.zeros((8, NL), F32), jnp.zeros((8, NL), F32)
            for p in range(5):
                back = (21 * p - 105) % NL
                low = jnp.where(inside[p], pltpu.roll(tiles[p], back, 1), low)
                extra = tiles[5 + p // 2]
                extra = extra if p % 2 else pltpu.roll(extra, 4, 0)
                high = jnp.where(inside[p], pltpu.roll(extra, back, 1), high)
            for z in range(4):
                first = pltpu.roll(low, 8 - 2 * z, 0) if z else low
                last = pltpu.roll(high, z, 0) if z else high
                out[j, z, pl.ds(below, 8), :] += jnp.where(row < 2, first, 0.0)
                out[j, z, pl.ds(above, 8), :] += jnp.where(row == 7, last, 0.0)


def rows_step(pieces, count_z, flip, after):
    vmem = pl.BlockSpec(memory_space=pltpu.VMEM)
    count_x = len(pieces)
    return pl.pallas_call(
        functools.partial(rows_kernel, count_x, count_z, flip),
        out_shape=jax.ShapeDtypeStruct((count_z, 4, 16 * count_x, NL), F32),
        in_specs=[vmem] * count_x + [pl.BlockSpec(memory_space=pl.ANY)],
        out_specs=vmem,
        compiler_params=pltpu.CompilerParams(vmem_limit_bytes=VMEM_LIMIT),
    )(*pieces[::-1], after)


def coarse_kernel(count_x, count_y, own, other, out_hbm, out, sems):
    me = lax.axis_index("gy")
    me_z, is_even = lax.shift_right_logical(me, 1), lax.rem(me, 2) == 0
    lane = lax.broadcasted_iota(jnp.int32, (8, NL), 1)
    place = [lax.rem(lane + NL - 35 * v, NL) for v in range(NV)]

    def block(i, _):
        rows = pl.ds(pl.multiple_of(8 * i, 8), 8)
        for z in range(4):
            pieces = []
            for j in range(count_y // 2):
                mine, theirs = own[j ^ me_z, z, rows, :], other[j ^ me_z, z, rows, :]
                pieces += [jnp.where(is_even, mine, theirs), jnp.where(is_even, theirs, mine)]
            for v in range(NV):
                at = place[v]
                for t in range(count_y // 4):
                    total = jnp.where(at < 2, pieces[4 * t - 1], 0.0)
                    total += jnp.where(at == NL - 1, pieces[(4 * t + 4) % count_y], 0.0)
                    for q in range(4):
                        inside = (at >= 32 * q - 1) & (at < 32 * q + 34)
                        total += jnp.where(inside, pieces[4 * t + q], 0.0)
                    out[v, z, rows, NL * t : NL * (t + 1)] = pltpu.roll(total, NL - 35 * v, 1) if v else total
        return 0

    def copy(i):
        rows = pl.ds(pl.multiple_of(16 * i, 16), 16)
        return pltpu.make_async_copy(out.at[:, :, rows], out_hbm.at[:, :, rows], sems.at[i])

    group = 4 if count_x % 4 == 0 else 1

    def several(i, _):
        for k in range(group):
            block(2 * (group * i + k), 0)
            block(2 * (group * i + k) + 1, 0)
            copy(group * i + k).start()
        return 0

    lax.fori_loop(0, count_x // group, several, 0)
    for i in range(count_x):
        copy(i).wait()


def coarse_step(own, other, count_x, count_y):
    vmem = pl.BlockSpec(memory_space=pltpu.VMEM)
    shape = (NV, 4, 16 * count_x, 32 * count_y)
    return pl.pallas_call(
        functools.partial(coarse_kernel, count_x, count_y),
        out_shape=jax.ShapeDtypeStruct(shape, F32),
        in_specs=[vmem, vmem],
        out_specs=pl.BlockSpec(memory_space=pltpu.HBM),
        scratch_shapes=[pltpu.VMEM(shape, F32), pltpu.SemaphoreType.DMA((count_x,))],
        compiler_params=pltpu.CompilerParams(vmem_limit_bytes=VMEM_LIMIT),
    )(own, other)


def shifted(x, axis, step):
    count = lax.axis_size(axis)
    return lax.ppermute(x, axis, [(i, (i + step) % count) for i in range(count)])


def swapped(x, axis, distance):
    return lax.ppermute(x, axis, [(i, i ^ distance) for i in range(lax.axis_size(axis))])


def body(field, masks):
    count_x, count_y = lax.axis_size("gx"), lax.axis_size("gy")
    lifted, up, down, own_masks, share = first_step(field, masks)
    south = shifted(up, "gx", -1)
    north = shifted(down, "gx", 1)
    shares = [share] + [swapped(share, "gy", r) for r in range(2, count_y, 2)]
    parts, to_left, to_right = edge_step(lift_step(lifted), lifted, north, south, own_masks)
    east = shifted(to_left, "gy", -1)
    west = shifted(to_right, "gy", 1)
    joined = join_step(shares, to_left)
    pieces = [joined] + [swapped(joined, "gx", r) for r in range(1, count_x)]
    kept = main_step(parts, east, west, own_masks, north, south)
    restored = cells_step(kept.reshape(4, NV * 8, 48, NL))
    pieces[-1], restored = lax.optimization_barrier((pieces[-1], restored))
    others = [swapped(piece, "gy", 1) for piece in pieces]
    own = rows_step(pieces, count_y // 2, 0, kept)
    other = rows_step(others, count_y // 2, 1, own)
    return restored, coarse_step(own, other, count_x, count_y)


def solution(mesh):
    placed = P(None, None, "gx", "gy")
    return jax.shard_map(
        body,
        mesh=mesh,
        in_specs=(placed, placed),
        out_specs=(placed, P()),
        check_vma=False,
    )
```
